32 devices in a mesh: blk: 8 (over y, x, core), dp: 4 (over z).
Axes of the slice: x: 2, y: 2, z: 4, core: 2. Of those that a mesh axis runs over, the one named last changes fastest.
Arguments:
- tokens: bfloat16 [8, 2048, 1024], P('dp', 'blk'), may hold values from -6 to 6
- input_weight: bfloat16 [1024, 3072], P(('blk', 'dp')), may hold values from -0.1875 to 0.1875
- output_weight: bfloat16 [1024, 1024], P(('blk', 'dp')), may hold values from -3 to 3
- expand_weight: bfloat16 [1024, 4096], P(('blk', 'dp')), may hold values from -0.1875 to 0.1875
- reduce_weight: bfloat16 [4096, 1024], P(('blk', 'dp')), may hold values from -0.09375 to 0.09375
- gains: bfloat16 [2, 1024], P(None, ('blk', 'dp')), may hold values from 0.5 to 1.5
- biases: bfloat16 [6, 1024], P(None, ('blk', 'dp')), may hold values from -2 to 2
- hidden_bias: bfloat16 [4096], P(('blk', 'dp')), may hold values from -3 to 3
- segment: int32 [8, 2048], P('dp', 'blk'), may hold values from 0 to 3, as said below
- present: int32 [8, 2048], P('dp', 'blk'), may hold values from 0 to 1, as said below
- cotangent: bfloat16 [8, 2048, 1024], P('dp', 'blk'), may hold values from -6 to 6
Outputs:
- output: bfloat16 [8, 2048, 1024], P('dp', 'blk')
- grad_tokens: float32 [8, 2048, 1024], P('dp', 'blk')
- grad_input: float32 [1024, 3072], P(('blk', 'dp'))
- grad_output: float32 [1024, 1024], P(('blk', 'dp'))
- grad_expand: float32 [1024, 4096], P(('blk', 'dp'))
- grad_reduce: float32 [4096, 1024], P(('blk', 'dp'))
- grad_gains: float32 [2, 1024], P(None, ('blk', 'dp'))
- grad_biases: float32 [6, 1024], P(None, ('blk', 'dp'))
- grad_hidden: float32 [4096], P(('blk', 'dp'))
The draws below stay inside these ranges and needn't reach their ends.
Inputs may be any that keep to these rules, and one draw needn't show every extreme that they name: Each slot row holds either one protein (all segment values 0) or four consecutive ones numbered 0 to 3 in order, protein k beginning within 128 positions of k * 512. Of the 2 slots of each index of dp, one holds a single protein with every position present. Each protein has present = 1 on a leading run of at least half of its positions and 0 after it.
All inputs are finite; a program needn't handle non-finite values.
Results may differ from the reference program's by a relative error of at most 0.017.
Values may be sent and summed in bfloat16 or wider, within the bound.
A program may use at most 192 MiB of HBM per device.

```python
import jax
import jax.numpy as jnp
from jax import lax

D = 1024
HEADS = 16
FF = 4096
HEAD_DIM = 64
SEQ_LEN = 2048
SLOTS = 2
ROWS = 8
N_DP = 4


def layout(key):
    count = N_DP * SLOTS
    quarter = SEQ_LEN // 4
    jitter = quarter // 4
    kind_key = jax.random.fold_in(key, 11)
    pick_key = jax.random.fold_in(key, 12)
    span_key = jax.random.fold_in(key, 13)
    cut_key = jax.random.fold_in(key, 14)
    kinds = jax.random.randint(kind_key, (count,), 0, 2)
    picks = jax.random.randint(pick_key, (N_DP,), 0, SLOTS)
    local = jnp.arange(count) % SLOTS
    group_pick = jnp.repeat(picks, SLOTS)
    whole = local == group_pick
    short = local == (group_pick + 1) % SLOTS
    kinds = jnp.where(whole, 1, jnp.where(short, 0, kinds))
    moves = jax.random.randint(cut_key, (count, 3), -jitter, jitter + 1)
    cuts = (jnp.arange(1, 4)[None, :] * quarter + moves).astype(jnp.int32)
    starts = jnp.concatenate([jnp.zeros((count, 1), jnp.int32), cuts], axis=1)
    ends = jnp.concatenate([cuts, jnp.full((count, 1), SEQ_LEN, jnp.int32)], axis=1)
    position = jnp.arange(SEQ_LEN)
    split_segment = jnp.sum((position[None, :, None] >= cuts[:, None, :]).astype(jnp.int32), axis=-1)
    segment = jnp.where(kinds[:, None] == 1, 0, split_segment)
    spans = jnp.where(kinds[:, None] == 1, jnp.concatenate([jnp.full((count, 1), SEQ_LEN, jnp.int32), jnp.zeros((count, 3), jnp.int32)], axis=1), ends - starts)
    starts = jnp.where(kinds[:, None] == 1, 0, starts)
    lengths = jax.random.randint(span_key, (count, 4), spans // 2, spans + 1)
    lengths = jnp.where(whole[:, None], spans, lengths)
    first = jnp.arange(4)[None, :] == 0
    lengths = jnp.where(short[:, None] & first, spans // 2, lengths)
    pick = segment[:, :, None] == jnp.arange(4)[None, None, :]
    own_length = jnp.sum(jnp.where(pick, lengths[:, None, :], 0), axis=-1)
    own_start = jnp.sum(jnp.where(pick, starts[:, None, :], 0), axis=-1)
    offset = position[None, :] - own_start
    present = jnp.where(offset < own_length, 1, 0)
    return (segment.astype(jnp.int32), present.astype(jnp.int32))


def draw_segment(key, part):
    shared = layout(key)
    return shared[0]


def draw_present(key, part):
    shared = layout(key)
    return shared[1]


def draw_biases(key, part):
    key = jax.random.fold_in(key, 5)
    base = jnp.clip(jax.random.normal(key, (6, D), jnp.float32), -4.0, 4.0)
    scales = jnp.array([0.5, 0.02, 0.5, 0.5, 0.5, 0.5], jnp.float32)[:, None]
    return (base * scales).astype(jnp.bfloat16)


def shard_levels(stream_key, extent, split, least, top_value):
    level, own = 1.0, jax.random.fold_in(stream_key, 6)
    for axis_at, shards_of in split:
        heights = jnp.exp(jax.random.uniform(jax.random.fold_in(own, axis_at), (shards_of,), jnp.float32, least / len(split), top_value / len(split)))
        level = level * jnp.repeat(heights, extent[axis_at] // shards_of).reshape([-1 if axis == axis_at else 1 for axis in range(len(extent))])
    return level


def scatter_about(rng, shape, scale, reach, split=(), kind=jnp.bfloat16):
    entries = jax.random.normal(rng, shape, jnp.float32) * scale
    if len(split) > 0:
        entries = shard_levels(rng, shape, split, -0.22, 0.18) * entries
    return jnp.clip(entries, min=-reach, max=reach).astype(kind)


def setup_inputs(seed: int = 0) -> dict:
    splits = jax.random.split(jax.random.key(seed), 12)
    tokens = scatter_about(splits[0], (ROWS, SEQ_LEN, D), 1.0, 6.0, ((0, 4), (1, 8)))
    input_weight = scatter_about(splits[1], (D, 3 * D), D ** -0.5, 0.1875, ((0, 32),))
    output_weight = scatter_about(splits[2], (D, D), 4 ** -0.5, 3.0, ((0, 32),))
    expand_weight = scatter_about(splits[3], (D, FF), D ** -0.5, 0.1875, ((0, 32),))
    reduce_weight = scatter_about(splits[4], (FF, D), FF ** -0.5, 0.09375, ((0, 32),))
    gains = jnp.clip(1.0 + 0.1 * jax.random.normal(splits[5], (2, D), jnp.float32), 0.5, 1.5).astype(jnp.bfloat16)
    biases = draw_biases(jax.random.fold_in(splits[11], 71), 0)
    hidden_bias = scatter_about(splits[7], (FF,), 0.5, 3.0, ((0, 32),))
    segment = draw_segment(jax.random.fold_in(splits[11], 71), 0)
    present = draw_present(jax.random.fold_in(splits[11], 71), 0)
    cotangent = scatter_about(splits[10], (ROWS, SEQ_LEN, D), 1.0, 6.0, ((0, 4), (1, 8)))
    return dict(tokens=tokens, input_weight=input_weight, output_weight=output_weight, expand_weight=expand_weight, reduce_weight=reduce_weight, gains=gains, biases=biases, hidden_bias=hidden_bias, segment=segment, present=present, cotangent=cotangent)


EPSILON = 1e-12
HUGE = 1e+30

@jax.custom_vjp
def low(v):
    return lax.optimization_barrier(v.astype(jnp.bfloat16)).astype(jnp.float32)

@jax.custom_vjp
def low_back(v):
    return v

def low_keep(v):
    return (low(v), None)

def low_pass(kept, grad):
    return (grad,)

def back_keep(v):
    return (v, None)

def back_low(kept, grad):
    return (low(grad),)
low.defvjp(low_keep, low_pass)
low_back.defvjp(back_keep, back_low)

def product(left, right):
    return jnp.dot(left, right, precision=lax.Precision.HIGHEST, preferred_element_type=jnp.float32)

def layer_norm(values, gain, shift):
    mean = lax.optimization_barrier(jnp.mean(values, axis=-1, keepdims=True))
    centred = values - mean
    spread = lax.optimization_barrier(jnp.mean(centred * centred, axis=-1, keepdims=True))
    return centred * lax.rsqrt(spread + EPSILON) * gain + shift

def slot_attention(item):
    queries, keys, values, segment, present = item
    length = queries.shape[0]
    query_heads = queries.reshape(length, HEADS, HEAD_DIM)
    key_heads = keys.reshape(length, HEADS, HEAD_DIM)
    value_heads = values.reshape(length, HEADS, HEAD_DIM)
    scores = jnp.einsum('qhd,khd->hqk', query_heads, key_heads, precision=lax.Precision.HIGHEST) * HEAD_DIM ** (-0.5)
    scores = low_back(scores)
    allowed = (segment[:, None] == segment[None, :]) & (present[None, :] == 1)
    top = lax.optimization_barrier(jnp.max(jnp.where(allowed[None], scores, -HUGE), axis=-1, keepdims=True))
    weights = jnp.where(allowed[None], jnp.exp(scores - top), 0.0)
    probs = low(weights / lax.optimization_barrier(jnp.sum(weights, axis=-1, keepdims=True)))
    mixed = jnp.einsum('hqk,khd->qhd', probs, value_heads, precision=lax.Precision.HIGHEST)
    return mixed.reshape(length, HEADS * HEAD_DIM)

def layer(tokens, input_weight, output_weight, expand_weight, reduce_weight, gains, biases, hidden_bias, segment, present):
    slots, length, width = tokens.shape
    flattened = tokens.reshape(slots * length, width)
    mixed = product(flattened, input_weight)
    queries = low(low_back(mixed[:, :width] + biases[0]))
    keys = low(low_back(mixed[:, width:2 * width]))
    values = low(low_back(mixed[:, 2 * width:] + biases[1]))
    shape = (slots, length, width)
    attended = lax.map(jax.checkpoint(slot_attention), (queries.reshape(shape), keys.reshape(shape), values.reshape(shape), segment, present))
    attended = low(low_back(attended.reshape(slots * length, width)))
    branch = low_back(product(attended, output_weight) + biases[2])
    normed = layer_norm(flattened + branch, gains[0], biases[3])
    pre = low_back(product(low(normed), expand_weight) + hidden_bias)
    act = low(jax.nn.gelu(pre, approximate=False))
    ffn_out = low_back(product(act, reduce_weight) + biases[4])
    result = layer_norm(normed + ffn_out, gains[1], biases[5])
    return result.reshape(shape)

def reference(tokens, input_weight, output_weight, expand_weight, reduce_weight, gains, biases, hidden_bias, segment, present, cotangent):
    floats = [item.astype(jnp.float32) for item in (tokens, input_weight, output_weight, expand_weight, reduce_weight, gains, biases, hidden_bias)]

    def forward(*params):
        return layer(*params, segment, present)
    result, pullback = jax.vjp(forward, *floats)
    grads = pullback(cotangent.astype(jnp.float32))
    return (result.astype(jnp.bfloat16), grads[0], grads[1], grads[2], grads[3], grads[4], grads[5], grads[6], grads[7])
```

```python
import functools

import jax
import jax.numpy as jnp
from jax import lax
from jax.experimental import pallas as pl
from jax.experimental.pallas import tpu as pltpu
from jax.sharding import PartitionSpec as P

HEADS = 16
EPSILON = 1e-12
FAR = 2.0**60
BOTH = ("blk", "dp")
MESH = pl.DeviceIdType.MESH
LOW = jnp.bfloat16
HIGH = jnp.float32
VMEM_LIMIT = 60 * 2**20


def product(left, right):
    return jnp.dot(left, right, preferred_element_type=HIGH)


def product_nt(left, right):
    return lax.dot_general(left, right, (((1,), (1,)), ((), ())), preferred_element_type=HIGH)


def product_tn(left, right):
    return lax.dot_general(left, right, (((0,), (0,)), ((), ())), preferred_element_type=HIGH)


class Sender:
    def __init__(self, send, recv):
        self.send, self.recv, self.started = send, recv, []

    def go(self, src, dst, device, landing):
        at = len(self.started)

        def copy(a, b):
            return pltpu.make_async_remote_copy(
                src_ref=a,
                dst_ref=b,
                send_sem=self.send.at[at],
                recv_sem=self.recv.at[at],
                device_id=device,
                device_id_type=MESH,
            )

        out = copy(src, dst)
        out.start()
        self.started.append(out)
        return copy(landing, landing)

    def drain(self):
        for out in self.started:
            out.wait_send()


def greet(peers):
    barrier = pltpu.get_barrier_semaphore()
    for peer in peers:
        pl.semaphore_signal(barrier, inc=1, device_id=peer, device_id_type=MESH)
    pl.semaphore_wait(barrier, len(peers))


def half(ref, which):
    rows = ref.shape[0]
    cut = rows // 32 * 16
    return ref.at[pl.ds(0, cut)] if which == 0 else ref.at[pl.ds(cut, rows - cut)]


def position():
    return lax.axis_index("blk"), lax.axis_index("dp")


def gather_kernel(x, win, w1, w2, X, W, W1, W2, send, recv, lsem):
    b, z = position()
    bx, by, bd, bc = b ^ 2, b ^ 4, b ^ 6, b ^ 1
    greet([(b ^ d, z) for d in range(1, 8)] + [(b, z ^ d) for d in range(1, 4)])
    s = Sender(send, recv)
    locs = []

    def local(src, dst):
        copy = pltpu.make_async_copy(src, dst, lsem.at[len(locs)])
        copy.start()
        locs.append(copy)

    local(win.at[b], W.at[z, b])
    local(x, X.at[b])
    local(w1, W1.at[b, z])
    local(w2, W2.at[b, z])
    to_x, to_y, to_core = (bx, z), (by, z), (bc, z)
    cores = []

    def core(src, full, bb, zz):
        cores.append(s.go(src, full.at[bb, zz], to_core, full.at[bb ^ 1, zz]))

    def along_z(src, full):
        return [s.go(src, full.at[b, z], (b, z ^ d), full.at[b, z ^ d]) for d in (1, 2, 3)]

    def first_hop(src, full, zz):
        return [
            s.go(src, full.at[b, zz], to_x, full.at[bx, zz]),
            s.go(src, full.at[b, zz], to_y, full.at[by, zz]),
        ]

    def second_hop(full, zz, arriving):
        arriving[0].wait_recv()
        piece = half(full.at[bx, zz], 0)
        one = s.go(piece, piece, to_y, half(full.at[bd, zz], 0))
        core(full.at[bx, zz], full, bx, zz)
        arriving[1].wait_recv()
        piece = half(full.at[by, zz], 1)
        two = s.go(piece, piece, to_x, half(full.at[bd, zz], 1))
        core(full.at[by, zz], full, by, zz)
        return [one, two]

    columns = [
        s.go(win.at[b ^ d], W.at[z, b], (b ^ d, z), W.at[z, b ^ d]) for d in range(1, 8)
    ]
    token_x = s.go(x, X.at[b], to_x, X.at[bx])
    token_y = s.go(x, X.at[b], to_y, X.at[by])
    z1, z2 = along_z(w1, W1), along_z(w2, W2)
    cores.append(s.go(x, X.at[b], to_core, X.at[bc]))
    core(w1, W1, b, z)
    core(w2, W2, b, z)
    hop1, hop2 = {0: first_hop(w1, W1, z)}, {0: first_hop(w2, W2, z)}
    for copy in columns:
        copy.wait_recv()
    locs[0].wait()
    columns = [s.go(W.at[z], W.at[z], (b, z ^ d), W.at[z ^ d]) for d in (1, 2, 3)]
    token_x.wait_recv()
    piece = half(X.at[bx], 0)
    token_one = s.go(piece, piece, to_y, half(X.at[bd], 0))
    cores.append(s.go(X.at[bx], X.at[bx], to_core, X.at[bx ^ 1]))
    token_y.wait_recv()
    piece = half(X.at[by], 1)
    token_two = s.go(piece, piece, to_x, half(X.at[bd], 1))
    cores.append(s.go(X.at[by], X.at[by], to_core, X.at[by ^ 1]))
    for i, d in enumerate((1, 2, 3)):
        for hop, arriving, full in ((hop1, z1, W1), (hop2, z2, W2)):
            arriving[i].wait_recv()
            hop[d] = first_hop(full.at[b, z ^ d], full, z ^ d)
            core(full.at[b, z ^ d], full, b, z ^ d)
    last1, last2 = {}, {}
    for d in range(4):
        for hop, last, full in ((hop1, last1, W1), (hop2, last2, W2)):
            last[d] = second_hop(full, z ^ d, hop[d])
        if d == 0:
            token_one.wait_recv()
            token_two.wait_recv()
            cores.append(s.go(X.at[bd], X.at[bd], to_core, X.at[bd ^ 1]))
    for d in range(4):
        for last, full in ((last1, W1), (last2, W2)):
            for copy in last[d]:
                copy.wait_recv()
            core(full.at[bd, z ^ d], full, bd, z ^ d)
    for copy in cores + columns:
        copy.wait_recv()
    s.drain()
    for copy in locs[1:]:
        copy.wait()


def in_hbm(count):
    return [pl.BlockSpec(memory_space=pl.ANY)] * count


def pair_of_semaphores(count):
    return [pltpu.SemaphoreType.DMA((count,)), pltpu.SemaphoreType.DMA((count,))]


def gather(x, win, w1, w2):
    shape = lambda *s: jax.ShapeDtypeStruct(s, LOW)
    return pl.pallas_call(
        gather_kernel,
        out_shape=(
            shape(8, *x.shape),
            shape(4, *win.shape),
            shape(8, 4, *w1.shape),
            shape(8, 4, *w2.shape),
        ),
        in_specs=in_hbm(4),
        out_specs=tuple(in_hbm(4)),
        scratch_shapes=pair_of_semaphores(100) + [pltpu.SemaphoreType.DMA((4,))],
        compiler_params=pltpu.CompilerParams(collective_id=1, has_side_effects=True),
        name="gather",
    )(x, win, w1, w2)


def add_rows(out, one, two):
    @pl.loop(0, one.shape[0] // 16)
    def _(i):
        rows = pl.ds(pl.multiple_of(i * 16, 16), 16)
        out[rows, :] = one[rows, :] + two[rows, :]


def reduce_kernel(g1, g2, o1, o2, *scratch):
    C, S, H, Q, Z = [scratch[2 * i : 2 * i + 2] for i in range(5)]
    send, recv, lsem = scratch[10:]
    G, O = (g1, g2), (o1, o2)
    b, z = position()
    greet([(b ^ d, z) for d in (1, 2, 4)] + [(b, z ^ d) for d in (1, 2, 3)])
    to_x, to_y, to_core = (b ^ 2, z), (b ^ 4, z), (b ^ 1, z)
    s = Sender(send, recv)
    own, other = {}, {}
    order = (1, 2, 3, 0)
    for d in order:
        for e in (3, 1, 2, 0):
            for a in (0, 1):
                at = (d * 4 + e) * 2 + a
                copy = pltpu.make_async_copy(G[a].at[b ^ (2 * e), z ^ d], S[a].at[e, d], lsem.at[at])
                copy.start()
                own[a, d, e] = copy
                other[a, d, e] = s.go(
                    G[a].at[b ^ 1 ^ (2 * e), z ^ d], C[a].at[e, d], to_core, C[a].at[e, d]
                )
    halves, pieces, last = {}, {}, {}

    def fold(d):
        for e in (3, 1, 2, 0):
            for a in (0, 1):
                own[a, d, e].wait()
                other[a, d, e].wait_recv()
                add_rows(S[a].at[e, d], S[a].at[e, d], C[a].at[e, d])
                if e == 3:
                    halves[a, d] = [
                        s.go(half(S[a].at[3, d], 0), H[a].at[d, 0], to_x, H[a].at[d, 0]),
                        s.go(half(S[a].at[3, d], 1), H[a].at[d, 1], to_y, H[a].at[d, 1]),
                    ]

    def relay(d):
        for a in (0, 1):
            halves[a, d][0].wait_recv()
            part = half(S[a].at[2, d], 0)
            add_rows(part, part, H[a].at[d, 0])
            one = s.go(S[a].at[2, d], Q[a].at[d, 1], to_y, Q[a].at[d, 1])
            halves[a, d][1].wait_recv()
            part = half(S[a].at[1, d], 1)
            add_rows(part, part, H[a].at[d, 1])
            two = s.go(S[a].at[1, d], Q[a].at[d, 0], to_x, Q[a].at[d, 0])
            pieces[a, d] = [one, two]

    def collect(d):
        for a in (0, 1):
            for copy in pieces[a, d]:
                copy.wait_recv()
            add_rows(S[a].at[0, d], S[a].at[0, d], Q[a].at[d, 0])
            add_rows(S[a].at[0, d], S[a].at[0, d], Q[a].at[d, 1])
            if d:
                last[a, d] = s.go(S[a].at[0, d], Z[a].at[d - 1], (b, z ^ d), Z[a].at[d - 1])

    fold(1)
    fold(2)
    relay(1)
    fold(3)
    relay(2)
    collect(1)
    fold(0)
    relay(3)
    collect(2)
    relay(0)
    collect(3)
    collect(0)
    for a in (0, 1):
        for d in (1, 2, 3):
            last[a, d].wait_recv()

        @pl.loop(0, O[a].shape[0] // 16)
        def _(i, a=a):
            rows = pl.ds(pl.multiple_of(i * 16, 16), 16)
            total = S[a][0, 0, rows, :].astype(HIGH)
            for d in range(3):
                total = total + Z[a][d, rows, :].astype(HIGH)
            O[a][rows, :] = total

    s.drain()


def reduce(g1, g2):
    shapes = [g1.shape[2:], g2.shape[2:]]
    scratch = []
    for lead, cut in (((4, 4), 1), ((4, 4), 1), ((4, 2), 2), ((4, 2), 1), ((3,), 1)):
        for rows, columns in shapes:
            scratch.append(pltpu.VMEM((*lead, rows // cut, columns), LOW))
    return pl.pallas_call(
        reduce_kernel,
        out_shape=tuple(jax.ShapeDtypeStruct(s, HIGH) for s in shapes),
        in_specs=in_hbm(2),
        out_specs=(pl.BlockSpec(memory_space=pltpu.VMEM),) * 2,
        scratch_shapes=scratch + pair_of_semaphores(80) + [pltpu.SemaphoreType.DMA((32,))],
        compiler_params=pltpu.CompilerParams(
            collective_id=2, has_side_effects=True, vmem_limit_bytes=VMEM_LIMIT
        ),
        name="reduce",
    )(g1, g2)


def first_lanes(shape):
    return lax.broadcasted_iota(jnp.int32, shape, len(shape) - 1) < 64


def marked(block, marks, head):
    mine = first_lanes(block.shape)
    return jnp.where(mine if head == 0 else jnp.logical_not(mine), block, marks)


def rows_of(ref, slot=0):
    block = ref[:, slot]
    return block.reshape(-1, block.shape[-1])


def attend_kernel(q_ref, qm_ref, k_ref, km_ref, v_ref, out_ref, lse_ref):
    queries, q_marks = q_ref[0, 0], qm_ref[0, 0]
    keys, k_marks, values = rows_of(k_ref), rows_of(km_ref), rows_of(v_ref)
    ones = jnp.ones_like(values)
    rows = queries.shape[0]
    outs, logs = [], []
    for head in (0, 1):
        scores = product_nt(marked(queries, q_marks, head), marked(keys, k_marks, head))
        top = jnp.max(scores, axis=-1, keepdims=True)
        weights = jnp.exp(scores - top).astype(LOW)
        total = product(weights, marked(values, ones, head))
        mass = pltpu.roll(total, 64, 1)
        outs.append(total / mass)
        logs.append(top + jnp.log(mass))
    out_ref[0, 0] = jnp.where(first_lanes((rows, 128)), outs[0], outs[1]).astype(LOW)
    both = jnp.where(first_lanes((rows, 128)), logs[0], logs[1])
    flipped = both.T
    lse_ref[0, 0] = jnp.concatenate(
        [flipped[0:1], flipped[64:65], jnp.zeros((6, rows), HIGH)], axis=0
    )


def attend(q, qm, k, km, v):
    blocks, slots, rows, lanes = q.shape
    tile = pl.BlockSpec((1, 1, rows, lanes), lambda s, i: (i, s, 0, 0))
    whole = pl.BlockSpec((blocks, 1, rows, lanes), lambda s, i: (0, s, 0, 0))
    return pl.pallas_call(
        attend_kernel,
        grid=(slots, blocks),
        out_shape=(
            jax.ShapeDtypeStruct(q.shape, LOW),
            jax.ShapeDtypeStruct((slots, blocks, 8, rows), HIGH),
        ),
        in_specs=[tile, tile, whole, whole, whole],
        out_specs=(tile, pl.BlockSpec((1, 1, 8, rows), lambda s, i: (s, i, 0, 0))),
        compiler_params=pltpu.CompilerParams(vmem_limit_bytes=VMEM_LIMIT),
        name="attend",
    )(q, qm, k, km, v)


def attend_back_kernel(
    q_ref, qm_ref, o_ref, g_ref, lse_ref, k_ref, km_ref, v_ref, dq_ref, dk_ref, dv_ref, acc, delta
):
    tile = pl.program_id(1)
    blocks, _, rows, _ = q_ref.shape
    keys, k_marks, values = k_ref[0, 0], km_ref[0, 0], v_ref[0, 0]
    mine = first_lanes((rows, 128))

    @pl.when(tile == 0)
    def _():
        acc[...] = jnp.zeros_like(acc)
        pick = (lax.broadcasted_iota(jnp.int32, (8, 128), 0) == 0) == first_lanes((8, 128))
        pick = pick.astype(HIGH)
        for i in range(blocks):
            inner = o_ref[i, 0].astype(HIGH) * g_ref[i, 0].astype(HIGH)
            delta[i] = lax.dot_general(
                pick,
                inner,
                (((1,), (1,)), ((), ())),
                precision=lax.Precision.HIGHEST,
                preferred_element_type=HIGH,
            )

    zeros = jnp.zeros((rows, 128), LOW)
    key_heads = [marked(keys, k_marks, head) for head in (0, 1)]

    def step(i, carry):
        dk, dv = carry
        queries, q_marks, grads = q_ref[i, 0], qm_ref[i, 0], g_ref[i, 0]
        dk_parts, dq_parts = [], []
        for head in (0, 1):
            query = marked(queries, q_marks, head)
            grad = marked(grads, zeros, head)
            scores = product_nt(key_heads[head], query)
            probs = jnp.exp(scores - lse_ref[0, i, head : head + 1, :])
            pushed = product_nt(values, grad)
            d_scores = (probs * (pushed - delta[i, head : head + 1, :])).astype(LOW)
            dv = dv + product(probs.astype(LOW), grad)
            dk_parts.append(product(d_scores, query))
            dq_parts.append(product_tn(d_scores, keys))
        acc[i] += jnp.where(mine, dq_parts[0], dq_parts[1])
        return dk + jnp.where(mine, dk_parts[0], dk_parts[1]), dv

    start = jnp.zeros((rows, 128), HIGH)
    dk, dv = lax.fori_loop(0, blocks, step, (start, start))
    dk_ref[0, 0] = dk.astype(LOW)
    dv_ref[0, 0] = dv.astype(LOW)

    @pl.when(tile == blocks - 1)
    def _():
        for i in range(blocks):
            dq_ref[i, 0] = (acc[i] * 0.125).astype(LOW)


def attend_back(q, qm, o, g, lse, k, km, v):
    blocks, slots, rows, lanes = q.shape
    tile = pl.BlockSpec((1, 1, rows, lanes), lambda s, i: (i, s, 0, 0))
    whole = pl.BlockSpec((blocks, 1, rows, lanes), lambda s, i: (0, s, 0, 0))
    logs = pl.BlockSpec((1, blocks, 8, rows), lambda s, i: (s, 0, 0, 0))
    shape = jax.ShapeDtypeStruct(q.shape, LOW)
    return pl.pallas_call(
        attend_back_kernel,
        grid=(slots, blocks),
        out_shape=(shape,) * 3,
        in_specs=[whole, whole, whole, whole, logs, tile, tile, tile],
        out_specs=(whole, tile, tile),
        scratch_shapes=[pltpu.VMEM((blocks, rows, lanes), HIGH), pltpu.VMEM((blocks, 8, rows), HIGH)],
        compiler_params=pltpu.CompilerParams(vmem_limit_bytes=VMEM_LIMIT),
        name="attend_back",
    )(q, qm, o, g, lse, k, km, v)


def by_position(rows, cols):
    return lax.broadcasted_iota(jnp.int32, (1, cols), 1) % 64


def normalize(values):
    mean = jnp.mean(values, axis=-1, keepdims=True)
    centred = values - mean
    spread = jnp.mean(centred * centred, axis=-1, keepdims=True)
    inverse = lax.rsqrt(spread + EPSILON)
    return centred * inverse, inverse


def normalize_back(grad, normal, inverse):
    return inverse * (
        grad
        - jnp.mean(grad, axis=-1, keepdims=True)
        - normal * jnp.mean(grad * normal, axis=-1, keepdims=True)
    )


def swap(pieces):
    return lax.all_to_all(pieces, "blk", 0, 0)


def gelu_parts(pre):
    phi_sum = 0.5 * lax.erfc(-pre * (0.5**0.5))
    density = jnp.exp(-0.5 * pre * pre) * 0.3989422804014327
    return pre * phi_sum, phi_sum + pre * density


def on_device(
    tokens,
    input_weight,
    output_weight,
    expand_weight,
    reduce_weight,
    gains,
    biases,
    hidden_bias,
    segment,
    present,
    cotangent,
):
    slots, rows, width = tokens.shape
    n_blk, n_dp = lax.axis_size("blk"), lax.axis_size("dp")
    shards = n_blk * n_dp
    fast = (n_blk, n_dp) == (8, 4)
    held = width // n_blk
    shard = input_weight.shape[0]
    hidden = expand_weight.shape[1]
    count = slots * rows
    flat = tokens.reshape(count, width)

    code = segment + 4 * (1 - present)
    code_rows = jnp.zeros((16, width), LOW).at[0, :count].set(code.reshape(count).astype(LOW))
    sent_tokens = jnp.concatenate([flat, code_rows], axis=0)
    columns = input_weight.reshape(shard, 3, n_blk, held).transpose(2, 0, 1, 3)
    columns = columns.reshape(n_blk, shard, 3 * held)
    small = jnp.concatenate([gains.reshape(-1), biases.reshape(-1), hidden_bias])
    both = jnp.concatenate([expand_weight, output_weight], axis=1)
    if fast:
        small = jnp.concatenate([small[None], jnp.zeros((15, small.shape[0]), LOW)], axis=0)
        small = jnp.broadcast_to(small, (n_blk, *small.shape))
        X, W, W1, W2 = gather(
            sent_tokens, jnp.concatenate([columns, small], axis=1), both, reduce_weight
        )
        W = W.transpose(1, 0, 2, 3).reshape(shards, -1, 3 * held)
        small = W[:, shard]
        W = W[:, :shard].reshape(width, 3 * held)
        W1, W2 = W1.reshape(width, -1), W2.reshape(hidden, width)
    else:
        X = lax.all_gather(sent_tokens, "blk")
        W = lax.all_gather(swap(columns), "dp", axis=1).reshape(width, 3 * held)
        small = lax.all_gather(small, BOTH)
        W1 = lax.all_gather(both, BOTH, axis=0, tiled=True)
        W2 = lax.all_gather(reduce_weight, BOTH, axis=0, tiled=True)
    expand, out_w = W1[:, :hidden], W1[:, hidden:]
    part = width // shards
    cuts = small[:, : 8 * part].reshape(shards, 8, part).transpose(1, 0, 2).reshape(8, width)
    cuts = cuts.astype(HIGH)
    gain, bias = cuts[:2], cuts[2:]
    hidden_full = small[:, 8 * part :].reshape(hidden).astype(HIGH)

    codes = X[:, count, :count].reshape(n_blk, slots, rows, 1).astype(jnp.int32)
    lanes = lax.broadcasted_iota(jnp.int32, (1, 1, 1, 128), 3) % 64
    q_marks = jnp.where((lanes < 5) & (lanes != codes % 4), -FAR, 0.0).astype(LOW)
    k_marks = jnp.where(lanes == jnp.minimum(codes, 4), 1.0, 0.0).astype(LOW)

    all_tokens = X[:, :count]
    me = lax.axis_index("blk")
    mixed = jnp.einsum("brd,dc->brc", all_tokens, W, preferred_element_type=HIGH)
    own_bias = lax.dynamic_slice(bias[:2], (0, me * held), (2, held))
    q = (mixed[..., :held] + own_bias[0]).astype(LOW) * LOW(0.125)
    k = mixed[..., held : 2 * held].astype(LOW)
    v = (mixed[..., 2 * held :] + own_bias[1]).astype(LOW)

    def heads(block):
        block = block.reshape(n_blk, slots, rows, held)
        return jnp.pad(block, ((0, 0),) * 3 + ((0, 128 - held),))

    q, k, v = heads(q), heads(k), heads(v)
    att, lse = attend(q, q_marks, k, k_marks, v)
    rows_att = swap(att[..., :held].reshape(n_blk, count, held))
    attended = rows_att.transpose(1, 0, 2).reshape(count, width)

    branch = product(attended, out_w) + bias[2]
    n1, r1 = normalize(flat.astype(HIGH) + branch)
    normed = n1 * gain[0] + bias[3]
    normed_low = normed.astype(LOW)
    pre = product(normed_low, expand) + hidden_full
    act, slope = gelu_parts(pre)
    act = act.astype(LOW)
    ffn = product(act, W2) + bias[4]
    n2, r2 = normalize(normed + ffn)
    output = (n2 * gain[1] + bias[5]).astype(LOW).reshape(slots, rows, width)

    cot = cotangent.reshape(count, width).astype(HIGH)
    d_second = normalize_back(cot * gain[1], n2, r2)
    d_ffn = d_second.astype(LOW)
    grad_reduce = product_tn(act, d_ffn).astype(LOW)
    d_pre = (product_nt(d_ffn, W2) * slope).astype(LOW)
    grad_expand = product_tn(normed_low, d_pre).astype(LOW)
    d_normed = d_second + product_nt(d_pre, expand)
    d_first = normalize_back(d_normed * gain[0], n1, r1)
    d_branch = d_first.astype(LOW)
    grad_output = product_tn(attended, d_branch).astype(LOW)
    d_att = product_nt(d_branch, out_w).astype(LOW)

    g = swap(d_att.reshape(count, n_blk, held).transpose(1, 0, 2))
    grad_both = jnp.concatenate([grad_expand, grad_output], axis=1)
    if fast:
        sum_both, sum_reduce = reduce(
            grad_both.reshape(n_blk, n_dp, shard, -1), grad_reduce.reshape(n_blk, n_dp, -1, width)
        )
    else:
        sum_both = lax.psum_scatter(grad_both, BOTH, scatter_dimension=0, tiled=True).astype(HIGH)
        sum_reduce = lax.psum_scatter(grad_reduce, BOTH, scatter_dimension=0, tiled=True)
        sum_reduce = sum_reduce.astype(HIGH)

    dq, dk, dv = attend_back(q, q_marks, att, heads(g), lse, k, k_marks, v)
    d_mixed = jnp.concatenate([dq[..., :held], dk[..., :held], dv[..., :held]], axis=-1)
    d_mixed = d_mixed.reshape(n_blk * count, 3 * held)
    d_input = product_tn(all_tokens.reshape(n_blk * count, width), d_mixed).astype(LOW)
    d_tokens = product_nt(d_mixed, W).astype(LOW)
    d_tokens = lax.psum_scatter(d_tokens, "blk", scatter_dimension=0, tiled=True)
    grad_tokens = (d_first + d_tokens.astype(HIGH)).reshape(slots, rows, width)
    d_input = swap(d_input.reshape(n_blk, n_dp * shard, 3 * held))
    d_input = d_input.reshape(n_blk, n_dp, shard, 3, held).transpose(1, 2, 3, 0, 4)
    d_input = d_input.reshape(n_dp, shard, 3 * width).astype(HIGH)
    grad_input = lax.psum_scatter(d_input, "dp", scatter_dimension=0, tiled=False)

    col = lambda a: jnp.sum(a.astype(HIGH), axis=0)
    own_cols = jnp.stack([col(d_mixed[:, :held]), col(d_mixed[:, 2 * held :])])
    own_cols = lax.psum_scatter(own_cols, "dp", scatter_dimension=1, tiled=True)
    small_rows = jnp.stack(
        [
            col(d_normed * n1),
            col(cot * n2),
            col(d_branch),
            col(d_normed),
            col(d_ffn),
            col(cot),
        ]
    )
    small_rows = small_rows.reshape(6, shards, part).transpose(1, 0, 2).reshape(shards, 6 * part)
    small_rows = jnp.concatenate([small_rows, col(d_pre).reshape(shards, -1)], axis=1)
    small_sum = lax.psum_scatter(small_rows, BOTH, scatter_dimension=0, tiled=False)
    vectors = small_sum[: 6 * part].reshape(6, part)
    return (
        output,
        grad_tokens,
        grad_input,
        sum_both[:, hidden:],
        sum_both[:, :hidden],
        sum_reduce,
        vectors[:2],
        jnp.concatenate([own_cols, vectors[2:]], axis=0),
        small_sum[6 * part :],
    )


def solution(mesh):
    rows, sharded = P("dp", "blk", None), P(BOTH, None)
    in_specs = (rows, sharded, sharded, sharded, sharded, P(None, BOTH), P(None, BOTH), P(BOTH))
    in_specs += (P("dp", "blk"), P("dp", "blk"), rows)
    out_specs = (rows, rows, sharded, sharded, sharded, sharded)
    out_specs += (P(None, BOTH), P(None, BOTH), P(BOTH))
    return jax.shard_map(
        on_device, mesh=mesh, in_specs=in_specs, out_specs=out_specs, check_vma=False
    )
```

```python
import functools

import jax
import jax.numpy as jnp
from jax import lax
from jax.experimental import pallas as pl
from jax.experimental.pallas import tpu as pltpu
from jax.sharding import PartitionSpec as P

HEADS = 16
EPSILON = 1e-12
FAR = 2.0**60
BOTH = ("blk", "dp")
MESH = pl.DeviceIdType.MESH
LOW = jnp.bfloat16
HIGH = jnp.float32
VMEM_LIMIT = 60 * 2**20


def product(left, right):
    return jnp.dot(left, right, preferred_element_type=HIGH)


def product_nt(left, right):
    return lax.dot_general(left, right, (((1,), (1,)), ((), ())), preferred_element_type=HIGH)


def product_tn(left, right):
    return lax.dot_general(left, right, (((0,), (0,)), ((), ())), preferred_element_type=HIGH)


class Sender:
    def __init__(self, send, recv):
        self.send, self.recv, self.started = send, recv, []

    def go(self, src, dst, device, landing):
        at = len(self.started)

        def copy(a, b):
            return pltpu.make_async_remote_copy(
                src_ref=a,
                dst_ref=b,
                send_sem=self.send.at[at],
                recv_sem=self.recv.at[at],
                device_id=device,
                device_id_type=MESH,
            )

        out = copy(src, dst)
        out.start()
        self.started.append(out)
        return copy(landing, landing)

    def drain(self):
        for out in self.started:
            out.wait_send()


def greet(peers):
    barrier = pltpu.get_barrier_semaphore()
    for peer in peers:
        pl.semaphore_signal(barrier, inc=1, device_id=peer, device_id_type=MESH)
    pl.semaphore_wait(barrier, len(peers))


def half(ref, which):
    rows = ref.shape[0]
    cut = rows // 32 * 16
    return ref.at[pl.ds(0, cut)] if which == 0 else ref.at[pl.ds(cut, rows - cut)]


def position():
    return lax.axis_index("blk"), lax.axis_index("dp")


def gather_kernel(x, win, w1, w2, X, W, W1, W2, send, recv, lsem):
    b, z = position()
    bx, by, bd, bc = b ^ 2, b ^ 4, b ^ 6, b ^ 1
    greet([(b ^ d, z) for d in range(1, 8)] + [(b, z ^ d) for d in range(1, 4)])
    s = Sender(send, recv)
    locs = []

    def local(src, dst):
        copy = pltpu.make_async_copy(src, dst, lsem.at[len(locs)])
        copy.start()
        locs.append(copy)

    local(win.at[b], W.at[z, b])
    local(x, X.at[b])
    local(w1, W1.at[b, z])
    local(w2, W2.at[b, z])
    to_x, to_y, to_core = (bx, z), (by, z), (bc, z)
    cores = []

    def core(src, full, bb, zz):
        cores.append(s.go(src, full.at[bb, zz], to_core, full.at[bb ^ 1, zz]))

    def along_z(src, full):
        return [s.go(src, full.at[b, z], (b, z ^ d), full.at[b, z ^ d]) for d in (1, 2, 3)]

    def first_hop(src, full, zz):
        return [
            s.go(src, full.at[b, zz], to_x, full.at[bx, zz]),
            s.go(src, full.at[b, zz], to_y, full.at[by, zz]),
        ]

    def second_hop(full, zz, arriving):
        arriving[0].wait_recv()
        piece = half(full.at[bx, zz], 0)
        one = s.go(piece, piece, to_y, half(full.at[bd, zz], 0))
        core(full.at[bx, zz], full, bx, zz)
        arriving[1].wait_recv()
        piece = half(full.at[by, zz], 1)
        two = s.go(piece, piece, to_x, half(full.at[bd, zz], 1))
        core(full.at[by, zz], full, by, zz)
        return [one, two]

    columns = [
        s.go(win.at[b ^ d], W.at[z, b], (b ^ d, z), W.at[z, b ^ d]) for d in range(1, 8)
    ]
    token_x = s.go(x, X.at[b], to_x, X.at[bx])
    token_y = s.go(x, X.at[b], to_y, X.at[by])
    z1, z2 = along_z(w1, W1), along_z(w2, W2)
    cores.append(s.go(x, X.at[b], to_core, X.at[bc]))
    core(w1, W1, b, z)
    core(w2, W2, b, z)
    hop1, hop2 = {0: first_hop(w1, W1, z)}, {0: first_hop(w2, W2, z)}
    for copy in columns:
        copy.wait_recv()
    locs[0].wait()
    columns = [s.go(W.at[z], W.at[z], (b, z ^ d), W.at[z ^ d]) for d in (1, 2, 3)]
    token_x.wait_recv()
    piece = half(X.at[bx], 0)
    token_one = s.go(piece, piece, to_y, half(X.at[bd], 0))
    cores.append(s.go(X.at[bx], X.at[bx], to_core, X.at[bx ^ 1]))
    token_y.wait_recv()
    piece = half(X.at[by], 1)
    token_two = s.go(piece, piece, to_x, half(X.at[bd], 1))
    cores.append(s.go(X.at[by], X.at[by], to_core, X.at[by ^ 1]))
    for i, d in enumerate((1, 2, 3)):
        for hop, arriving, full in ((hop1, z1, W1), (hop2, z2, W2)):
            arriving[i].wait_recv()
            hop[d] = first_hop(full.at[b, z ^ d], full, z ^ d)
            core(full.at[b, z ^ d], full, b, z ^ d)
    last1, last2 = {}, {}
    for d in range(4):
        for hop, last, full in ((hop1, last1, W1), (hop2, last2, W2)):
            last[d] = second_hop(full, z ^ d, hop[d])
        if d == 0:
            token_one.wait_recv()
            token_two.wait_recv()
            cores.append(s.go(X.at[bd], X.at[bd], to_core, X.at[bd ^ 1]))
    for d in range(4):
        for last, full in ((last1, W1), (last2, W2)):
            for copy in last[d]:
                copy.wait_recv()
            core(full.at[bd, z ^ d], full, bd, z ^ d)
    for copy in cores + columns:
        copy.wait_recv()
    s.drain()
    for copy in locs[1:]:
        copy.wait()


def in_hbm(count):
    return [pl.BlockSpec(memory_space=pl.ANY)] * count


def pair_of_semaphores(count):
    return [pltpu.SemaphoreType.DMA((count,)), pltpu.SemaphoreType.DMA((count,))]


def gather(x, win, w1, w2):
    shape = lambda *s: jax.ShapeDtypeStruct(s, LOW)
    return pl.pallas_call(
        gather_kernel,
        out_shape=(
            shape(8, *x.shape),
            shape(4, *win.shape),
            shape(8, 4, *w1.shape),
            shape(8, 4, *w2.shape),
        ),
        in_specs=in_hbm(4),
        out_specs=tuple(in_hbm(4)),
        scratch_shapes=pair_of_semaphores(100) + [pltpu.SemaphoreType.DMA((4,))],
        compiler_params=pltpu.CompilerParams(collective_id=1, has_side_effects=True),
        name="gather",
    )(x, win, w1, w2)


def add_rows(out, one, two):
    @pl.loop(0, one.shape[0] // 16)
    def _(i):
        rows = pl.ds(pl.multiple_of(i * 16, 16), 16)
        out[rows, :] = one[rows, :] + two[rows, :]


def reduce_kernel(g1, g2, o1, o2, *scratch):
    C, S, H, Q, Z = [scratch[2 * i : 2 * i + 2] for i in range(5)]
    send, recv, lsem = scratch[10:]
    G, O = (g1, g2), (o1, o2)
    b, z = position()
    greet([(b ^ d, z) for d in (1, 2, 4)] + [(b, z ^ d) for d in (1, 2, 3)])
    to_x, to_y, to_core = (b ^ 2, z), (b ^ 4, z), (b ^ 1, z)
    s = Sender(send, recv)
    own, other = {}, {}
    order = (1, 2, 3, 0)
    for d in order:
        for e in (3, 1, 2, 0):
            for a in (0, 1):
                at = (d * 4 + e) * 2 + a
                copy = pltpu.make_async_copy(G[a].at[b ^ (2 * e), z ^ d], S[a].at[e, d], lsem.at[at])
                copy.start()
                own[a, d, e] = copy
                other[a, d, e] = s.go(
                    G[a].at[b ^ 1 ^ (2 * e), z ^ d], C[a].at[e, d], to_core, C[a].at[e, d]
                )
    halves, pieces, last = {}, {}, {}

    def fold(d):
        for e in (3, 1, 2, 0):
            for a in (0, 1):
                own[a, d, e].wait()
                other[a, d, e].wait_recv()
                add_rows(S[a].at[e, d], S[a].at[e, d], C[a].at[e, d])
                if e == 3:
                    halves[a, d] = [
                        s.go(half(S[a].at[3, d], 0), H[a].at[d, 0], to_x, H[a].at[d, 0]),
                        s.go(half(S[a].at[3, d], 1), H[a].at[d, 1], to_y, H[a].at[d, 1]),
                    ]

    def relay(d):
        for a in (0, 1):
            halves[a, d][0].wait_recv()
            part = half(S[a].at[2, d], 0)
            add_rows(part, part, H[a].at[d, 0])
            one = s.go(S[a].at[2, d], Q[a].at[d, 1], to_y, Q[a].at[d, 1])
            halves[a, d][1].wait_recv()
            part = half(S[a].at[1, d], 1)
            add_rows(part, part, H[a].at[d, 1])
            two = s.go(S[a].at[1, d], Q[a].at[d, 0], to_x, Q[a].at[d, 0])
            pieces[a, d] = [one, two]

    def collect(d):
        for a in (0, 1):
            for copy in pieces[a, d]:
                copy.wait_recv()
            add_rows(S[a].at[0, d], S[a].at[0, d], Q[a].at[d, 0])
            add_rows(S[a].at[0, d], S[a].at[0, d], Q[a].at[d, 1])
            if d:
                last[a, d] = s.go(S[a].at[0, d], Z[a].at[d - 1], (b, z ^ d), Z[a].at[d - 1])

    fold(1)
    fold(2)
    relay(1)
    fold(3)
    relay(2)
    collect(1)
    fold(0)
    relay(3)
    collect(2)
    relay(0)
    collect(3)
    collect(0)
    for a in (0, 1):
        for d in (1, 2, 3):
            last[a, d].wait_recv()

        @pl.loop(0, O[a].shape[0] // 16)
        def _(i, a=a):
            rows = pl.ds(pl.multiple_of(i * 16, 16), 16)
            total = S[a][0, 0, rows, :].astype(HIGH)
            for d in range(3):
                total = total + Z[a][d, rows, :].astype(HIGH)
            O[a][rows, :] = total

    s.drain()


def reduce(g1, g2):
    shapes = [g1.shape[2:], g2.shape[2:]]
    scratch = []
    for lead, cut in (((4, 4), 1), ((4, 4), 1), ((4, 2), 2), ((4, 2), 1), ((3,), 1)):
        for rows, columns in shapes:
            scratch.append(pltpu.VMEM((*lead, rows // cut, columns), LOW))
    return pl.pallas_call(
        reduce_kernel,
        out_shape=tuple(jax.ShapeDtypeStruct(s, HIGH) for s in shapes),
        in_specs=in_hbm(2),
        out_specs=(pl.BlockSpec(memory_space=pltpu.VMEM),) * 2,
        scratch_shapes=scratch + pair_of_semaphores(80) + [pltpu.SemaphoreType.DMA((32,))],
        compiler_params=pltpu.CompilerParams(
            collective_id=2, has_side_effects=True, vmem_limit_bytes=VMEM_LIMIT
        ),
        name="reduce",
    )(g1, g2)


def first_lanes(shape):
    return lax.broadcasted_iota(jnp.int32, shape, len(shape) - 1) < 64


def marked(block, marks, head):
    mine = first_lanes(block.shape)
    return jnp.where(mine if head == 0 else jnp.logical_not(mine), block, marks)


def rows_of(ref, slot=0):
    block = ref[:, slot]
    return block.reshape(-1, block.shape[-1])


def attend_kernel(q_ref, qm_ref, k_ref, km_ref, v_ref, out_ref, lse_ref):
    queries, q_marks = q_ref[0, 0], qm_ref[0, 0]
    keys, k_marks, values = rows_of(k_ref), rows_of(km_ref), rows_of(v_ref)
    ones = jnp.ones_like(values)
    rows = queries.shape[0]
    outs, logs = [], []
    for head in (0, 1):
        scores = product_nt(marked(queries, q_marks, head), marked(keys, k_marks, head))
        top = jnp.max(scores, axis=-1, keepdims=True)
        weights = jnp.exp(scores - top).astype(LOW)
        total = product(weights, marked(values, ones, head))
        mass = pltpu.roll(total, 64, 1)
        outs.append(total / mass)
        logs.append(top + jnp.log(mass))
    out_ref[0, 0] = jnp.where(first_lanes((rows, 128)), outs[0], outs[1]).astype(LOW)
    both = jnp.where(first_lanes((rows, 128)), logs[0], logs[1])
    flipped = both.T
    lse_ref[0] = jnp.concatenate(
        [flipped[0:1], flipped[64:65], jnp.zeros((6, rows), HIGH)], axis=0
    )


def attend(q, qm, k, km, v):
    blocks, slots, rows, lanes = q.shape
    tile = pl.BlockSpec((1, 1, rows, lanes), lambda s, i: (i, s, 0, 0))
    whole = pl.BlockSpec((blocks, 1, rows, lanes), lambda s, i: (0, s, 0, 0))
    return pl.pallas_call(
        attend_kernel,
        grid=(slots, blocks),
        out_shape=(
            jax.ShapeDtypeStruct(q.shape, LOW),
            jax.ShapeDtypeStruct((slots, 8, blocks * rows), HIGH),
        ),
        in_specs=[tile, tile, whole, whole, whole],
        out_specs=(tile, pl.BlockSpec((1, 8, rows), lambda s, i: (s, 0, i))),
        compiler_params=pltpu.CompilerParams(vmem_limit_bytes=VMEM_LIMIT),
        name="attend",
    )(q, qm, k, km, v)


def attend_back_kernel(
    q_ref, qm_ref, o_ref, g_ref, lse_ref, k_ref, km_ref, v_ref, dq_ref, dk_ref, dv_ref, acc, delta
):
    tile = pl.program_id(1)
    blocks, _, rows, _ = q_ref.shape
    count = blocks * rows
    queries, q_marks, grads = rows_of(q_ref), rows_of(qm_ref), rows_of(g_ref)
    keys, k_marks, values = k_ref[0, 0], km_ref[0, 0], v_ref[0, 0]

    @pl.when(tile == 0)
    def _():
        acc[...] = jnp.zeros_like(acc)
        pick = (lax.broadcasted_iota(jnp.int32, (8, 128), 0) == 0) == first_lanes((8, 128))
        inner = rows_of(o_ref).astype(HIGH) * grads.astype(HIGH)
        delta[...] = lax.dot_general(
            pick.astype(HIGH),
            inner,
            (((1,), (1,)), ((), ())),
            precision=lax.Precision.HIGHEST,
            preferred_element_type=HIGH,
        )

    zeros = jnp.zeros((count, 128), LOW)
    keys_t = keys.T
    dk, dv = [], 0.0
    for head in (0, 1):
        query, grad = marked(queries, q_marks, head), marked(grads, zeros, head)
        probs = jnp.exp(product_nt(marked(keys, k_marks, head), query) - lse_ref[0, head : head + 1])
        pushed = product_nt(values, grad)
        d_scores = (probs * (pushed - delta[head : head + 1])).astype(LOW)
        dv = dv + product(probs.astype(LOW), grad)
        dk.append(product(d_scores, query))
        lanes = pl.ds(head * 64, 64)
        acc[lanes, :] += product(keys_t[head * 64 : head * 64 + 64], d_scores)
    dk_ref[0, 0] = jnp.where(first_lanes((rows, 128)), dk[0], dk[1]).astype(LOW)
    dv_ref[0, 0] = dv.astype(LOW)

    @pl.when(tile == blocks - 1)
    def _():
        dq_ref[:, 0] = (acc[...].T * 0.125).astype(LOW).reshape(blocks, rows, 128)


def attend_back(q, qm, o, g, lse, k, km, v):
    blocks, slots, rows, lanes = q.shape
    tile = pl.BlockSpec((1, 1, rows, lanes), lambda s, i: (i, s, 0, 0))
    whole = pl.BlockSpec((blocks, 1, rows, lanes), lambda s, i: (0, s, 0, 0))
    logs = pl.BlockSpec((1, 8, blocks * rows), lambda s, i: (s, 0, 0))
    shape = jax.ShapeDtypeStruct(q.shape, LOW)
    return pl.pallas_call(
        attend_back_kernel,
        grid=(slots, blocks),
        out_shape=(shape,) * 3,
        in_specs=[whole, whole, whole, whole, logs, tile, tile, tile],
        out_specs=(whole, tile, tile),
        scratch_shapes=[pltpu.VMEM((lanes, blocks * rows), HIGH), pltpu.VMEM((8, blocks * rows), HIGH)],
        compiler_params=pltpu.CompilerParams(vmem_limit_bytes=VMEM_LIMIT),
        name="attend_back",
    )(q, qm, o, g, lse, k, km, v)


def normalize(values):
    mean = jnp.mean(values, axis=-1, keepdims=True)
    centred = values - mean
    spread = jnp.mean(centred * centred, axis=-1, keepdims=True)
    inverse = lax.rsqrt(spread + EPSILON)
    return centred * inverse, inverse


def normalize_back(grad, normal, inverse):
    return inverse * (
        grad
        - jnp.mean(grad, axis=-1, keepdims=True)
        - normal * jnp.mean(grad * normal, axis=-1, keepdims=True)
    )


def gelu_parts(u):
    bell = jnp.exp(-0.5 * u * u)
    t = 1.0 / (1.0 + (0.3275911 * 0.5**0.5) * jnp.abs(u))
    poly = 1.061405429 * t - 1.453152027
    poly = poly * t + 1.421413741
    poly = poly * t - 0.284496736
    poly = poly * t + 0.254829592
    tail = 0.5 * poly * t * bell
    below = jnp.where(u < 0.0, tail, 1.0 - tail)
    return u * below, below + u * bell * 0.3989422804014327


def column_sum(block):
    return jnp.sum(block.astype(HIGH), axis=0, keepdims=True)


def middle_kernel(
    chunk,
    tok_ref,
    att_ref,
    cot_ref,
    par_ref,
    hid_ref,
    w1_hbm,
    w2_hbm,
    out_ref,
    first_ref,
    d_att_ref,
    sums_ref,
    d_hid_ref,
    g1_hbm,
    g2_hbm,
    w1,
    w2,
    att,
    normed_low,
    n1,
    n2,
    act,
    slope,
    acc,
    low,
    wsem,
    gsem,
):
    hidden, width = w2.shape
    steps = hidden // chunk
    pieces, _, held = att_ref.shape

    def columns(c):
        return pl.ds(pl.multiple_of(c * chunk, chunk), chunk)

    def load1(c):
        return pltpu.make_async_copy(w1_hbm.at[:, columns(c)], w1.at[:, columns(c)], wsem.at[0, c])

    def load2(c):
        return pltpu.make_async_copy(w2_hbm.at[columns(c)], w2.at[columns(c)], wsem.at[1, c])

    last = pl.ds(hidden, width)
    load_out = pltpu.make_async_copy(w1_hbm.at[:, last], w1.at[:, last], wsem.at[0, steps])
    load_out.start()
    for c in range(steps):
        load1(c).start()
        load2(c).start()
    gain1, gain2 = par_ref[0:1], par_ref[1:2]
    bias = lambda i: par_ref[2 + i : 3 + i]
    for i in range(pieces):
        att[:, i * held : (i + 1) * held] = att_ref[i]
    load_out.wait()
    first_sum = tok_ref[...].astype(HIGH) + product(att[...], w1[:, hidden:]) + bias(2)
    normal, inverse1 = normalize(first_sum)
    n1[...] = normal
    normed = normal * gain1 + bias(3)
    normed_low[...] = normed.astype(LOW)
    acc[...] = normed + bias(4)

    @pl.loop(0, steps)
    def _(c):
        load1(c).wait()
        pre = product(normed_low[...], w1[:, columns(c)]) + hid_ref[:, columns(c)]
        value, rate = gelu_parts(pre)
        act[:, columns(c)] = value.astype(LOW)
        slope[:, columns(c)] = rate.astype(LOW)
        load2(c).wait()
        acc[...] += product(value.astype(LOW), w2[columns(c), :])

    normal, inverse2 = normalize(acc[...])
    n2[...] = normal
    out_ref[...] = (normal * gain2 + bias(5)).astype(LOW)
    cot = cot_ref[...].astype(HIGH)
    d_second = normalize_back(cot * gain2, normal, inverse2)
    low[...] = d_second.astype(LOW)
    acc[...] = d_second
    sums_ref[1:2] = column_sum(cot * normal)
    sums_ref[4:5] = column_sum(low[...])
    sums_ref[5:6] = column_sum(cot)

    def store1(c):
        return pltpu.make_async_copy(w1.at[:, columns(c)], g1_hbm.at[:, columns(c)], gsem.at[0, c])

    def store2(c):
        return pltpu.make_async_copy(w2.at[columns(c)], g2_hbm.at[columns(c)], gsem.at[1, c])

    @pl.loop(0, steps)
    def _(c):
        d_act = product_nt(low[...], w2[columns(c), :])
        d_pre = (d_act * slope[:, columns(c)].astype(HIGH)).astype(LOW)
        d_hid_ref[:, columns(c)] = column_sum(d_pre)
        acc[...] += product_nt(d_pre, w1[:, columns(c)])
        w2[columns(c), :] = product_tn(act[:, columns(c)], low[...]).astype(LOW)
        store2(c).start()
        w1[:, columns(c)] = product_tn(normed_low[...], d_pre).astype(LOW)
        store1(c).start()

    d_normed = acc[...]
    normal = n1[...]
    d_first = normalize_back(d_normed * gain1, normal, inverse1)
    first_ref[...] = d_first
    low[...] = d_first.astype(LOW)
    sums_ref[0:1] = column_sum(d_normed * normal)
    sums_ref[2:3] = column_sum(low[...])
    sums_ref[3:4] = column_sum(d_normed)
    d_att = product_nt(low[...], w1[:, hidden:]).astype(LOW)
    for i in range(pieces):
        d_att_ref[i] = d_att[:, i * held : (i + 1) * held]
    w1[:, hidden:] = product_tn(att[...], low[...]).astype(LOW)
    store_out = pltpu.make_async_copy(w1.at[:, last], g1_hbm.at[:, last], gsem.at[0, steps])
    store_out.start()
    for c in range(steps):
        store1(c).wait()
        store2(c).wait()
    store_out.wait()


def middle(tokens, att, cot, par, hid, w1, w2):
    count, width = tokens.shape
    hidden = w2.shape[0]
    pieces = att.shape[0]
    chunk = 512
    shape = jax.ShapeDtypeStruct
    vmem = pl.BlockSpec(memory_space=pltpu.VMEM)
    return pl.pallas_call(
        functools.partial(middle_kernel, chunk),
        out_shape=(
            shape((count, width), LOW),
            shape((count, width), HIGH),
            shape(att.shape, LOW),
            shape((8, width), HIGH),
            shape((1, hidden), HIGH),
            shape(w1.shape, LOW),
            shape(w2.shape, LOW),
        ),
        in_specs=[vmem] * 5 + in_hbm(2),
        out_specs=(vmem,) * 5 + tuple(in_hbm(2)),
        scratch_shapes=[
            pltpu.VMEM(w1.shape, LOW),
            pltpu.VMEM(w2.shape, LOW),
            pltpu.VMEM((count, width), LOW),
            pltpu.VMEM((count, width), LOW),
            pltpu.VMEM((count, width), HIGH),
            pltpu.VMEM((count, width), HIGH),
            pltpu.VMEM((count, hidden), LOW),
            pltpu.VMEM((count, hidden), LOW),
            pltpu.VMEM((count, width), HIGH),
            pltpu.VMEM((count, width), LOW),
            pltpu.SemaphoreType.DMA((2, hidden // chunk + 1)),
            pltpu.SemaphoreType.DMA((2, hidden // chunk + 1)),
        ],
        compiler_params=pltpu.CompilerParams(vmem_limit_bytes=VMEM_LIMIT),
        name="middle",
    )(tokens, att, cot, par, hid, w1, w2)


def finish_kernel(
    dq,
    dk,
    dv,
    w,
    d_first,
    small,
    x_hbm,
    tok_out,
    in_out,
    small_out,
    x,
    sent,
    C,
    S,
    A,
    H,
    Q,
    D,
    R,
    Z,
    M,
    N,
    T,
    send,
    recv,
    lsem,
):
    b, z = position()
    count, width = d_first.shape
    blocks = dq.shape[0]
    to_x, to_y, to_core = (b ^ 2, z), (b ^ 4, z), (b ^ 1, z)
    loads = []
    for i in range(blocks):
        load = pltpu.make_async_copy(x_hbm.at[i, pl.ds(0, count)], x.at[i], lsem.at[i])
        load.start()
        loads.append(load)
    greet([(b ^ d, z) for d in range(1, 8)] + [(b, z ^ d) for d in (1, 2, 3)])
    s = Sender(send, recv)
    small_in = [
        s.go(small.at[b ^ d], M.at[d - 1], (b ^ d, z), M.at[d - 1]) for d in range(1, 8)
    ]

    def mixed(i):
        return jnp.concatenate([ref[i].reshape(count, -1) for ref in (dq, dk, dv)], axis=-1)

    def piece(i):
        return product_nt(mixed(i), w[...])

    other = {}
    for e in (3, 1, 2, 0):
        sent[e] = piece(b ^ 1 ^ (2 * e)).astype(LOW)
        other[e] = s.go(sent.at[e], C.at[e], to_core, C.at[e])

    def own(e):
        mine = piece(b ^ (2 * e))
        other[e].wait_recv()
        return mine + C[e].astype(HIGH)

    S[3] = own(3).astype(LOW)
    halves = [
        s.go(half(S.at[3], 0), H.at[0], to_x, H.at[0]),
        s.go(half(S.at[3], 1), H.at[1], to_y, H.at[1]),
    ]
    S[2] = own(2).astype(LOW)
    pieces = [s.go(half(S.at[2], 1), half(Q.at[1], 1), to_y, half(Q.at[1], 1))]
    S[1] = own(1).astype(LOW)
    pieces.append(s.go(half(S.at[1], 0), half(Q.at[0], 0), to_x, half(Q.at[0], 0)))
    A[...] = own(0) + d_first[...]

    total = jnp.zeros((width, w.shape[1]), HIGH)
    for i in range(blocks):
        loads[i].wait()
        total = total + product_tn(x[i], mixed(i))
    D[...] = total.astype(LOW).reshape(D.shape)
    grads_in = [
        s.go(D.at[b ^ d], R.at[b], (b ^ d, z), R.at[b ^ d]) for d in range(1, 8)
    ]
    R[b] = D[b]

    halves[0].wait_recv()
    part = half(S.at[2], 0)
    part[...] = part[...] + H[0]
    pieces.append(s.go(part, half(Q.at[1], 0), to_y, half(Q.at[1], 0)))
    halves[1].wait_recv()
    part = half(S.at[1], 1)
    part[...] = part[...] + H[1]
    pieces.append(s.go(part, half(Q.at[0], 1), to_x, half(Q.at[0], 1)))

    N[...] = small[b]
    for i in range(7):
        small_in[i].wait_recv()
        N[...] += M[i]
    for row, ref in ((4, dq), (5, dv)):
        sums = jnp.zeros((1, 128), HIGH)
        for i in range(blocks):
            sums = sums + column_sum(ref[i].reshape(count, -1))
        N[row : row + 1, 0:128] = sums
    small_z = [s.go(N, T.at[d - 1], (b, z ^ d), T.at[d - 1]) for d in (1, 2, 3)]

    for copy in grads_in:
        copy.wait_recv()
    rows = R.shape[1] // 4

    def share(d):
        return R.at[:, pl.ds(pl.multiple_of((z ^ d) * rows, rows), rows)]

    in_z = [s.go(share(d), Z.at[d - 1], (b, z ^ d), Z.at[d - 1]) for d in (1, 2, 3)]
    for copy in small_z:
        copy.wait_recv()
    small_out[...] = ((N[...] + T[0]) + T[1]) + T[2]
    for copy in in_z:
        copy.wait_recv()
    in_out[...] = ((share(0)[...].astype(HIGH) + Z[0].astype(HIGH)) + Z[1].astype(HIGH)) + Z[
        2
    ].astype(HIGH)
    for copy in pieces:
        copy.wait_recv()
    tok_out[...] = A[...] + Q[0].astype(HIGH) + Q[1].astype(HIGH)
    s.drain()


def finish(dq, dk, dv, w, d_first, small, x):
    count, width = d_first.shape
    blocks, columns = dq.shape[0], w.shape[1]
    share = width // (4 * blocks)
    vmem = pl.BlockSpec(memory_space=pltpu.VMEM)
    shape = jax.ShapeDtypeStruct
    low = lambda *s: pltpu.VMEM(s, LOW)
    return pl.pallas_call(
        finish_kernel,
        out_shape=(
            shape((count, width), HIGH),
            shape((blocks, share, columns), HIGH),
            shape(small.shape[1:], HIGH),
        ),
        in_specs=[vmem] * 6 + in_hbm(1),
        out_specs=(vmem,) * 3,
        scratch_shapes=[
            low(blocks, count, width),
            low(4, count, width),
            low(4, count, width),
            low(4, count, width),
            pltpu.VMEM((count, width), HIGH),
            low(2, count // 2, width),
            low(2, count, width),
            low(blocks, 4 * share, columns),
            low(blocks, 4 * share, columns),
            low(3, blocks, share, columns),
            pltpu.VMEM((7, *small.shape[1:]), HIGH),
            pltpu.VMEM(small.shape[1:], HIGH),
            pltpu.VMEM((3, *small.shape[1:]), HIGH),
        ]
        + pair_of_semaphores(32)
        + [pltpu.SemaphoreType.DMA((blocks,))],
        compiler_params=pltpu.CompilerParams(
            collective_id=3, has_side_effects=True, vmem_limit_bytes=VMEM_LIMIT
        ),
        name="finish",
    )(dq, dk, dv, w, d_first, small, x)


def swap(pieces):
    return lax.all_to_all(pieces, "blk", 0, 0)


def on_device(
    tokens,
    input_weight,
    output_weight,
    expand_weight,
    reduce_weight,
    gains,
    biases,
    hidden_bias,
    segment,
    present,
    cotangent,
):
    slots, rows, width = tokens.shape
    n_blk, n_dp = lax.axis_size("blk"), lax.axis_size("dp")
    shards = n_blk * n_dp
    fast = (n_blk, n_dp) == (8, 4)
    held = width // n_blk
    shard = input_weight.shape[0]
    hidden = expand_weight.shape[1]
    count = slots * rows
    flat = tokens.reshape(count, width)

    code = segment + 4 * (1 - present)
    code_rows = jnp.zeros((16, width), LOW).at[0, :count].set(code.reshape(count).astype(LOW))
    sent_tokens = jnp.concatenate([flat, code_rows], axis=0)
    columns = input_weight.reshape(shard, 3, n_blk, held).transpose(2, 0, 1, 3)
    columns = columns.reshape(n_blk, shard, 3 * held)
    small = jnp.concatenate([gains.reshape(-1), biases.reshape(-1), hidden_bias])
    both = jnp.concatenate([expand_weight, output_weight], axis=1)
    if fast:
        small = jnp.concatenate([small[None], jnp.zeros((15, small.shape[0]), LOW)], axis=0)
        small = jnp.broadcast_to(small, (n_blk, *small.shape))
        X, W, W1, W2 = gather(
            sent_tokens, jnp.concatenate([columns, small], axis=1), both, reduce_weight
        )
        W = W.transpose(1, 0, 2, 3).reshape(shards, -1, 3 * held)
        small = W[:, shard]
        W = W[:, :shard].reshape(width, 3 * held)
        W1, W2 = W1.reshape(width, -1), W2.reshape(hidden, width)
    else:
        X = lax.all_gather(sent_tokens, "blk")
        W = lax.all_gather(swap(columns), "dp", axis=1).reshape(width, 3 * held)
        small = lax.all_gather(small, BOTH)
        W1 = lax.all_gather(both, BOTH, axis=0, tiled=True)
        W2 = lax.all_gather(reduce_weight, BOTH, axis=0, tiled=True)
    part = width // shards
    cuts = small[:, : 8 * part].reshape(shards, 8, part).transpose(1, 0, 2).reshape(8, width)
    cuts = cuts.astype(HIGH)
    gain, bias = cuts[:2], cuts[2:]
    hidden_full = small[:, 8 * part :].reshape(hidden).astype(HIGH)

    codes = X[:, count, :count].reshape(n_blk, slots, rows, 1).astype(jnp.int32)
    lanes = lax.broadcasted_iota(jnp.int32, (1, 1, 1, 128), 3) % 64
    q_marks = jnp.where((lanes < 5) & (lanes != codes % 4), -FAR, 0.0).astype(LOW)
    k_marks = jnp.where(lanes == jnp.minimum(codes, 4), 1.0, 0.0).astype(LOW)

    all_tokens = X[:, :count]
    me = lax.axis_index("blk")
    mixed = jnp.einsum("brd,dc->brc", all_tokens, W, preferred_element_type=HIGH)
    own_bias = lax.dynamic_slice(bias[:2], (0, me * held), (2, held))
    q = (mixed[..., :held] + own_bias[0]).astype(LOW) * LOW(0.125)
    k = mixed[..., held : 2 * held].astype(LOW)
    v = (mixed[..., 2 * held :] + own_bias[1]).astype(LOW)

    def heads(block):
        block = block.reshape(n_blk, slots, rows, held)
        return jnp.pad(block, ((0, 0),) * 3 + ((0, 128 - held),))

    q, k, v = heads(q), heads(k), heads(v)
    att, lse = attend(q, q_marks, k, k_marks, v)
    rows_att = swap(att[..., :held].reshape(n_blk, count, held))
    middle_out = middle(
        flat,
        rows_att,
        cotangent.reshape(count, width),
        cuts,
        hidden_full[None],
        W1,
        W2,
    )
    output, d_first, d_att, sums, d_hidden, grad_both, grad_reduce = middle_out
    output = output.reshape(slots, rows, width)
    g = swap(d_att)
    if fast:
        sum_both, sum_reduce = reduce(
            grad_both.reshape(n_blk, n_dp, shard, -1), grad_reduce.reshape(n_blk, n_dp, -1, width)
        )
    else:
        sum_both = lax.psum_scatter(grad_both, BOTH, scatter_dimension=0, tiled=True).astype(HIGH)
        sum_reduce = lax.psum_scatter(grad_reduce, BOTH, scatter_dimension=0, tiled=True)
        sum_reduce = sum_reduce.astype(HIGH)

    dq, dk, dv = attend_back(q, q_marks, att, heads(g), lse, k, k_marks, v)
    small_rows = sums[:6].reshape(6, shards, part).transpose(1, 0, 2).reshape(shards, 6 * part)
    small_rows = jnp.concatenate([small_rows, d_hidden.reshape(shards, -1)], axis=1)
    if fast:
        lanes = small_rows.shape[1]
        small_rows = small_rows.reshape(n_blk, n_dp, lanes)
        small_rows = jnp.pad(small_rows, ((0, 0), (0, 4), (0, 3 * held - lanes)))
        grad_tokens, d_input, small_sum = finish(dq, dk, dv, W, d_first, small_rows, X)
        grad_input = d_input.reshape(n_blk, shard, 3, held).transpose(1, 2, 0, 3)
        grad_input = grad_input.reshape(shard, 3 * width)
        me_dp = lax.axis_index("dp")
        own_cols = lax.dynamic_slice(small_sum, (4, me_dp * part), (2, part))
        small_sum = lax.dynamic_slice(small_sum, (me_dp, 0), (1, lanes))[0]
    else:
        d_mixed = jnp.concatenate([dq[..., :held], dk[..., :held], dv[..., :held]], axis=-1)
        d_mixed = d_mixed.reshape(n_blk * count, 3 * held)
        d_input = product_tn(all_tokens.reshape(n_blk * count, width), d_mixed).astype(LOW)
        d_tokens = product_nt(d_mixed, W).astype(LOW)
        d_tokens = lax.psum_scatter(d_tokens, "blk", scatter_dimension=0, tiled=True)
        grad_tokens = d_first + d_tokens.astype(HIGH)
        d_input = swap(d_input.reshape(n_blk, n_dp * shard, 3 * held))
        d_input = d_input.reshape(n_blk, n_dp, shard, 3, held).transpose(1, 2, 3, 0, 4)
        d_input = d_input.reshape(n_dp, shard, 3 * width).astype(HIGH)
        grad_input = lax.psum_scatter(d_input, "dp", scatter_dimension=0, tiled=False)
        col = lambda a: jnp.sum(a.astype(HIGH), axis=0)
        own_cols = jnp.stack([col(d_mixed[:, :held]), col(d_mixed[:, 2 * held :])])
        own_cols = lax.psum_scatter(own_cols, "dp", scatter_dimension=1, tiled=True)
        small_sum = lax.psum_scatter(small_rows, BOTH, scatter_dimension=0, tiled=False)
    vectors = small_sum[: 6 * part].reshape(6, part)
    return (
        output,
        grad_tokens.reshape(slots, rows, width),
        grad_input,
        sum_both[:, hidden:],
        sum_both[:, :hidden],
        sum_reduce,
        vectors[:2],
        jnp.concatenate([own_cols, vectors[2:]], axis=0),
        small_sum[6 * part :],
    )


def solution(mesh):
    rows, sharded = P("dp", "blk", None), P(BOTH, None)
    in_specs = (rows, sharded, sharded, sharded, sharded, P(None, BOTH), P(None, BOTH), P(BOTH))
    in_specs += (P("dp", "blk"), P("dp", "blk"), rows)
    out_specs = (rows, rows, sharded, sharded, sharded, sharded)
    out_specs += (P(None, BOTH), P(None, BOTH), P(BOTH))
    return jax.shard_map(
        on_device, mesh=mesh, in_specs=in_specs, out_specs=out_specs, check_vma=False
    )
```

```python
import functools

import jax
import jax.numpy as jnp
from jax import lax
from jax.experimental import pallas as pl
from jax.experimental.pallas import tpu as pltpu
from jax.sharding import PartitionSpec as P

HEADS = 16
EPSILON = 1e-12
FAR = 2.0**60
BOTH = ("blk", "dp")
MESH = pl.DeviceIdType.MESH
LOW = jnp.bfloat16
HIGH = jnp.float32
VMEM_LIMIT = 60 * 2**20


def product(left, right):
    return jnp.dot(left, right, preferred_element_type=HIGH)


def product_nt(left, right):
    return lax.dot_general(left, right, (((1,), (1,)), ((), ())), preferred_element_type=HIGH)


def product_tn(left, right):
    return lax.dot_general(left, right, (((0,), (0,)), ((), ())), preferred_element_type=HIGH)


class Sender:
    def __init__(self, send, recv):
        self.send, self.recv, self.planned = send, recv, []

    def plan(self, src, dst, device, landing):
        at = len(self.planned)

        def copy(a, b):
            return pltpu.make_async_remote_copy(
                src_ref=a,
                dst_ref=b,
                send_sem=self.send.at[at],
                recv_sem=self.recv.at[at],
                device_id=device,
                device_id_type=MESH,
            )

        out = copy(src, dst)
        self.planned.append(out)
        landed = copy(landing, landing)
        landed.go = out.start
        return landed

    def go(self, *what):
        landed = self.plan(*what)
        landed.go()
        return landed

    def drain(self):
        for out in self.planned:
            out.wait_send()


def greet(peers):
    barrier = pltpu.get_barrier_semaphore()
    for peer in peers:
        pl.semaphore_signal(barrier, inc=1, device_id=peer, device_id_type=MESH)
    pl.semaphore_wait(barrier, len(peers))


def half(ref, which):
    rows = ref.shape[0]
    cut = rows // 32 * 16
    return ref.at[pl.ds(0, cut)] if which == 0 else ref.at[pl.ds(cut, rows - cut)]


def position():
    return lax.axis_index("blk"), lax.axis_index("dp")


def first_lanes(shape):
    return lax.broadcasted_iota(jnp.int32, shape, len(shape) - 1) < 64


def rows_of(block):
    return block.reshape(-1, block.shape[-1])


def attend_tile(queries, keys, values):
    rows = queries[0].shape[0]
    ones = jnp.ones_like(values)
    mine = first_lanes(values.shape)
    outs, logs = [], []
    for head in (0, 1):
        scores = product_nt(queries[head], keys[head])
        top = jnp.max(scores, axis=-1, keepdims=True)
        weights = jnp.exp(scores - top).astype(LOW)
        total = product(weights, jnp.where(mine == (head == 0), values, ones))
        mass = pltpu.roll(total, 64, 1)
        outs.append(total / mass)
        logs.append(top + jnp.log(mass))
    mine = first_lanes((rows, 128))
    flipped = jnp.where(mine, logs[0], logs[1]).T
    logs = jnp.concatenate([flipped[0:1], flipped[64:65], jnp.zeros((6, rows), HIGH)], axis=0)
    return jnp.where(mine, outs[0], outs[1]).astype(LOW), logs


def split_heads(mixed, bias, codes):
    rows = mixed.shape[0]
    q = (mixed[:, :128] + bias[0]).astype(LOW) * LOW(0.125)
    k = mixed[:, 128:256].astype(LOW)
    v = (mixed[:, 256:] + bias[1]).astype(LOW)
    lanes = lax.broadcasted_iota(jnp.int32, (rows, 128), 1) % 64
    protein = jnp.where(codes >= 4, codes - 4, codes)
    q_marks = jnp.where((lanes < 5) & (lanes != protein), -FAR, 0.0).astype(LOW)
    k_marks = jnp.where(lanes == jnp.minimum(codes, 4), 1.0, 0.0).astype(LOW)
    mine = first_lanes((rows, 128))
    return (
        (jnp.where(mine, q, q_marks), jnp.where(mine, q_marks, q)),
        (jnp.where(mine, k, k_marks), jnp.where(mine, k_marks, k)),
        v,
    )


def front_kernel(
    x,
    win,
    w1,
    w2,
    X_out,
    raw,
    W1,
    W2,
    rows_att,
    wfull,
    qh,
    kh,
    v,
    att,
    lse,
    X,
    W,
    send,
    recv,
    asend,
    arecv,
    lsem,
    osem,
):
    b, z = position()
    bx, by, bd, bc = b ^ 2, b ^ 4, b ^ 6, b ^ 1
    count = X.shape[1] - 16
    slots, rows = qh.shape[2:4]
    greet([(b ^ d, z) for d in range(1, 8)] + [(b, z ^ d) for d in range(1, 4)])
    s = Sender(send, recv)
    locs = []

    def local(src, dst):
        copy = pltpu.make_async_copy(src, dst, lsem.at[len(locs)])
        copy.start()
        locs.append(copy)

    local(win.at[b], W.at[z, b])
    local(x, X.at[b])
    local(w1, W1.at[b, z])
    local(w2, W2.at[b, z])
    to_x, to_y, to_core = (bx, z), (by, z), (bc, z)

    def token_core(src, bb):
        return s.plan(src, X.at[bb], to_core, X.at[bb ^ 1])

    columns = [
        s.go(win.at[b ^ d], W.at[z, b], (b ^ d, z), W.at[z, b ^ d]) for d in range(1, 8)
    ]
    token_x = s.go(x, X.at[b], to_x, X.at[bx])
    token_y = s.go(x, X.at[b], to_y, X.at[by])
    token_c = token_core(x, b)
    token_c.go()

    own, full = (w1, w2), (W1, W2)
    ways = {}
    for a in (0, 1):
        F = full[a]
        for d in range(4):
            zz = z ^ d
            src = F.at[b, zz] if d else own[a]
            way = {}
            if d:
                way["z"] = s.plan(own[a], F.at[b, z], (b, zz), F.at[b, zz])
            way["x"] = s.plan(src, F.at[b, zz], to_x, F.at[bx, zz])
            way["y"] = s.plan(src, F.at[b, zz], to_y, F.at[by, zz])
            piece = half(F.at[bx, zz], 0)
            way["xy"] = s.plan(piece, piece, to_y, half(F.at[bd, zz], 0))
            piece = half(F.at[by, zz], 1)
            way["yx"] = s.plan(piece, piece, to_x, half(F.at[bd, zz], 1))
            way["core"] = [
                s.plan(src if bb is b else F.at[bb, zz], F.at[bb, zz], to_core, F.at[bb ^ 1, zz])
                for bb in (b, bx, by, bd)
            ]
            ways[a, d] = way
    for a in (0, 1):
        for d in (1, 2, 3):
            ways[a, d]["z"].go()

    def first(d, a):
        way = ways[a, d]
        if d:
            way["z"].wait_recv()
        way["x"].go()
        way["y"].go()
        way["core"][0].go()

    def second(d, a):
        way = ways[a, d]
        way["x"].wait_recv()
        way["xy"].go()
        way["core"][1].go()
        way["y"].wait_recv()
        way["yx"].go()
        way["core"][2].go()

    def third(d, a):
        way = ways[a, d]
        way["xy"].wait_recv()
        way["yx"].wait_recv()
        way["core"][3].go()

    def both(stage, d):
        stage(d, 0)
        stage(d, 1)

    both(first, 0)
    for copy in columns:
        copy.wait_recv()
    locs[0].wait()
    columns = [s.go(W.at[z], W.at[z], (b, z ^ d), W.at[z ^ d]) for d in (1, 2, 3)]
    token_x.wait_recv()
    piece = half(X.at[bx], 0)
    token_one = s.go(piece, piece, to_y, half(X.at[bd], 0))
    token_xc = token_core(X.at[bx], bx)
    token_xc.go()
    token_y.wait_recv()
    piece = half(X.at[by], 1)
    token_two = s.go(piece, piece, to_x, half(X.at[bd], 1))
    token_yc = token_core(X.at[by], by)
    token_yc.go()
    token_dc = token_core(X.at[bd], bd)
    both(first, 1)
    for copy in columns:
        copy.wait_recv()
    raw_copy = pltpu.make_async_copy(W, raw, lsem.at[4])
    raw_copy.start()
    for i in range(8):
        for j in range(4):
            at = (i * 4 + j) * 32
            wfull[at : at + 32] = W[j, i, 0:32]
    bias = [
        jnp.concatenate([W[j, b, 32:33, at : at + 32] for j in range(4)], axis=1).astype(HIGH)
        for at in (64, 96)
    ]

    def mix(i):
        pltpu.make_async_copy(X.at[i], X_out.at[i], osem.at[i]).start()
        mixed = product(X[i, 0:count], wfull[...])
        codes = jnp.broadcast_to(X[i, count : count + 1, 0:count].astype(HIGH), (128, count)).T
        queries, keys, values = split_heads(mixed, bias, codes.astype(jnp.int32))
        for head in (0, 1):
            qh[head, i] = queries[head].reshape(slots, rows, 128)
            kh[head, i] = keys[head].reshape(slots, rows, 128)
        v[i] = values.reshape(slots, rows, 128)

    locs[1].wait()
    mix(b)
    token_c.wait_recv()
    mix(bc)
    mix(bx)
    token_xc.wait_recv()
    mix(bx ^ 1)
    both(first, 2)
    mix(by)
    token_yc.wait_recv()
    mix(by ^ 1)
    token_one.wait_recv()
    token_two.wait_recv()
    token_dc.go()
    mix(bd)
    both(first, 3)
    token_dc.wait_recv()
    mix(bd ^ 1)
    both(second, 0)

    def piece_of(slot):
        return pl.ds(pl.multiple_of(slot * rows, rows), rows)

    def send_att(slot, d):
        return pltpu.make_async_remote_copy(
            src_ref=att.at[b ^ d, slot],
            dst_ref=rows_att.at[b, piece_of(slot)],
            send_sem=asend.at[slot * 8 + d],
            recv_sem=arecv.at[slot * 8 + d],
            device_id=(b ^ d, z),
            device_id_type=MESH,
        )

    def keep_att(slot):
        return pltpu.make_async_copy(
            att.at[b, slot], rows_att.at[b, piece_of(slot)], osem.at[8 + slot]
        )

    events = {4: (second, 1, 0), 6: (second, 1, 1), 10: (second, 2, 0), 12: (second, 2, 1)}

    @pl.loop(0, 8 * slots)
    def _(step):
        slot, d = step // 8, (step + 1) % 8
        i = b ^ d
        keys = [rows_of(kh[head, :, slot]) for head in (0, 1)]
        out, logs = attend_tile([qh[head, i, slot] for head in (0, 1)], keys, rows_of(v[:, slot]))
        att[i, slot] = out
        lse[slot, :, pl.ds(pl.multiple_of(i * rows, rows), rows)] = logs

        @pl.when(d != 0)
        def _():
            send_att(slot, d).start()

        @pl.when(d == 0)
        def _():
            keep_att(slot).start()

        for at, (event, *what) in events.items():
            pl.when(step == at)(functools.partial(event, *what))

    both(third, 0)
    both(second, 3)
    for d in (1, 2, 3):
        both(third, d)
    for way in ways.values():
        for copy in way["core"]:
            copy.wait_recv()
    for slot in range(slots):
        keep_att(slot).wait()
        for d in range(1, 8):
            copy = send_att(slot, d)
            copy.wait_send()
            pltpu.make_async_remote_copy(
                src_ref=rows_att.at[b ^ d, piece_of(slot)],
                dst_ref=rows_att.at[b ^ d, piece_of(slot)],
                send_sem=asend.at[slot * 8 + d],
                recv_sem=arecv.at[slot * 8 + d],
                device_id=(b ^ d, z),
                device_id_type=MESH,
            ).wait_recv()
    s.drain()
    for copy in locs[2:]:
        copy.wait()
    raw_copy.wait()
    for i in range(8):
        pltpu.make_async_copy(X.at[i], X_out.at[i], osem.at[i]).wait()


def in_hbm(count):
    return [pl.BlockSpec(memory_space=pl.ANY)] * count


def pair_of_semaphores(count):
    return [pltpu.SemaphoreType.DMA((count,)), pltpu.SemaphoreType.DMA((count,))]


def front(x, win, w1, w2, slots):
    count, width = x.shape[0] - 16, x.shape[1]
    rows = count // slots
    shape = lambda *s: jax.ShapeDtypeStruct(s, LOW)
    vmem = pl.BlockSpec(memory_space=pltpu.VMEM)
    return pl.pallas_call(
        front_kernel,
        out_shape=(
            shape(8, *x.shape),
            shape(4, *win.shape),
            shape(8, 4, *w1.shape),
            shape(8, 4, *w2.shape),
            shape(8, count, 128),
            shape(width, win.shape[2]),
            shape(2, 8, slots, rows, 128),
            shape(2, 8, slots, rows, 128),
            shape(8, slots, rows, 128),
            shape(8, slots, rows, 128),
            jax.ShapeDtypeStruct((slots, 8, 8 * rows), HIGH),
        ),
        in_specs=in_hbm(4),
        out_specs=tuple(in_hbm(5)) + (vmem,) * 6,
        scratch_shapes=[pltpu.VMEM((8, *x.shape), LOW), pltpu.VMEM((4, *win.shape), LOW)]
        + pair_of_semaphores(100)
        + pair_of_semaphores(8 * slots)
        + [pltpu.SemaphoreType.DMA((5,)), pltpu.SemaphoreType.DMA((8 + slots,))],
        compiler_params=pltpu.CompilerParams(
            collective_id=1, has_side_effects=True, vmem_limit_bytes=VMEM_LIMIT
        ),
        name="front",
    )(x, win, w1, w2)


def add_rows(out, one, two):
    @pl.loop(0, one.shape[0] // 16)
    def _(i):
        rows = pl.ds(pl.multiple_of(i * 16, 16), 16)
        out[rows, :] = one[rows, :] + two[rows, :]


def reduce_kernel(g1, g2, o1, o2, *scratch):
    C, S, H, Q, Z = [scratch[2 * i : 2 * i + 2] for i in range(5)]
    send, recv, lsem = scratch[10:]
    G, O = (g1, g2), (o1, o2)
    b, z = position()
    greet([(b ^ d, z) for d in (1, 2, 4)] + [(b, z ^ d) for d in (1, 2, 3)])
    to_x, to_y, to_core = (b ^ 2, z), (b ^ 4, z), (b ^ 1, z)
    s = Sender(send, recv)
    own, other = {}, {}
    order = (1, 2, 3, 0)
    for d in order:
        for e in (3, 1, 2, 0):
            for a in (0, 1):
                at = (d * 4 + e) * 2 + a
                copy = pltpu.make_async_copy(G[a].at[b ^ (2 * e), z ^ d], S[a].at[e, d], lsem.at[at])
                copy.start()
                own[a, d, e] = copy
                other[a, d, e] = s.go(
                    G[a].at[b ^ 1 ^ (2 * e), z ^ d], C[a].at[e, d], to_core, C[a].at[e, d]
                )
    halves, pieces, last = {}, {}, {}

    def fold(d):
        for e in (3, 1, 2, 0):
            for a in (0, 1):
                own[a, d, e].wait()
                other[a, d, e].wait_recv()
                add_rows(S[a].at[e, d], S[a].at[e, d], C[a].at[e, d])
                if e == 3:
                    halves[a, d] = [
                        s.go(half(S[a].at[3, d], 0), H[a].at[d, 0], to_x, H[a].at[d, 0]),
                        s.go(half(S[a].at[3, d], 1), H[a].at[d, 1], to_y, H[a].at[d, 1]),
                    ]

    def relay(d):
        for a in (0, 1):
            halves[a, d][0].wait_recv()
            part = half(S[a].at[2, d], 0)
            add_rows(part, part, H[a].at[d, 0])
            one = s.go(S[a].at[2, d], Q[a].at[d, 1], to_y, Q[a].at[d, 1])
            halves[a, d][1].wait_recv()
            part = half(S[a].at[1, d], 1)
            add_rows(part, part, H[a].at[d, 1])
            two = s.go(S[a].at[1, d], Q[a].at[d, 0], to_x, Q[a].at[d, 0])
            pieces[a, d] = [one, two]

    def collect(d):
        for a in (0, 1):
            for copy in pieces[a, d]:
                copy.wait_recv()
            add_rows(S[a].at[0, d], S[a].at[0, d], Q[a].at[d, 0])
            add_rows(S[a].at[0, d], S[a].at[0, d], Q[a].at[d, 1])
            if d:
                last[a, d] = s.go(S[a].at[0, d], Z[a].at[d - 1], (b, z ^ d), Z[a].at[d - 1])

    fold(1)
    fold(2)
    relay(1)
    fold(3)
    relay(2)
    collect(1)
    fold(0)
    relay(3)
    collect(2)
    relay(0)
    collect(3)
    collect(0)
    for a in (0, 1):
        for d in (1, 2, 3):
            last[a, d].wait_recv()

        @pl.loop(0, O[a].shape[0] // 16)
        def _(i, a=a):
            rows = pl.ds(pl.multiple_of(i * 16, 16), 16)
            total = S[a][0, 0, rows, :].astype(HIGH)
            for d in range(3):
                total = total + Z[a][d, rows, :].astype(HIGH)
            O[a][rows, :] = total

    s.drain()


def reduce(g1, g2):
    shapes = [g1.shape[2:], g2.shape[2:]]
    scratch = []
    for lead, cut in (((4, 4), 1), ((4, 4), 1), ((4, 2), 2), ((4, 2), 1), ((3,), 1)):
        for rows, columns in shapes:
            scratch.append(pltpu.VMEM((*lead, rows // cut, columns), LOW))
    return pl.pallas_call(
        reduce_kernel,
        out_shape=tuple(jax.ShapeDtypeStruct(s, HIGH) for s in shapes),
        in_specs=in_hbm(2),
        out_specs=(pl.BlockSpec(memory_space=pltpu.VMEM),) * 2,
        scratch_shapes=scratch + pair_of_semaphores(80) + [pltpu.SemaphoreType.DMA((32,))],
        compiler_params=pltpu.CompilerParams(
            collective_id=2, has_side_effects=True, vmem_limit_bytes=VMEM_LIMIT
        ),
        name="reduce",
    )(g1, g2)


def attend_kernel(qh_ref, kh_ref, v_ref, out_ref, lse_ref):
    keys = [rows_of(kh_ref[head, :, 0]) for head in (0, 1)]
    out_ref[0, 0], lse_ref[0] = attend_tile(
        [qh_ref[head, 0, 0] for head in (0, 1)], keys, rows_of(v_ref[:, 0])
    )


def attend(qh, kh, v):
    blocks, slots, rows, lanes = v.shape
    tile = pl.BlockSpec((1, 1, rows, lanes), lambda s, i: (i, s, 0, 0))
    tiles = pl.BlockSpec((2, 1, 1, rows, lanes), lambda s, i: (0, i, s, 0, 0))
    whole = pl.BlockSpec((blocks, 1, rows, lanes), lambda s, i: (0, s, 0, 0))
    wholes = pl.BlockSpec((2, blocks, 1, rows, lanes), lambda s, i: (0, 0, s, 0, 0))
    return pl.pallas_call(
        attend_kernel,
        grid=(slots, blocks),
        out_shape=(
            jax.ShapeDtypeStruct(v.shape, LOW),
            jax.ShapeDtypeStruct((slots, 8, blocks * rows), HIGH),
        ),
        in_specs=[tiles, wholes, whole],
        out_specs=(tile, pl.BlockSpec((1, 8, rows), lambda s, i: (s, 0, i))),
        compiler_params=pltpu.CompilerParams(vmem_limit_bytes=VMEM_LIMIT),
        name="attend",
    )(qh, kh, v)


def row_products(out, grad):
    pick = (lax.broadcasted_iota(jnp.int32, (8, 128), 0) == 0) == first_lanes((8, 128))
    return lax.dot_general(
        pick.astype(HIGH),
        out.astype(HIGH) * grad.astype(HIGH),
        (((1,), (1,)), ((), ())),
        precision=lax.Precision.HIGHEST,
        preferred_element_type=HIGH,
    )


def attend_back_tile(queries, keys, values, grads, logs, delta, acc):
    zeros = jnp.zeros_like(grads)
    mine = first_lanes(grads.shape)
    dk, dv = [], 0.0
    for head in (0, 1):
        grad = jnp.where(mine == (head == 0), grads, zeros)
        probs = jnp.exp(product_nt(keys[head], queries[head]) - logs[head : head + 1])
        pushed = product_nt(values, grad)
        d_scores = (probs * (pushed - delta[head : head + 1])).astype(LOW)
        dv = dv + product(probs.astype(LOW), grad)
        dk.append(product(d_scores, queries[head]))
        keys_t = keys[head].T[head * 64 : head * 64 + 64]
        acc[head * 64 : head * 64 + 64, :] += product(keys_t, d_scores)
    return jnp.where(first_lanes(dk[0].shape), dk[0], dk[1]).astype(LOW), dv.astype(LOW)


def attend_back_kernel(
    qh_ref, o_ref, g_ref, lse_ref, kh_ref, v_ref, dq_ref, dk_ref, dv_ref, acc, delta
):
    tile = pl.program_id(1)
    blocks, _, rows, _ = g_ref.shape
    grads = rows_of(g_ref[:, 0])

    @pl.when(tile == 0)
    def _():
        acc[...] = jnp.zeros_like(acc)
        delta[...] = row_products(rows_of(o_ref[:, 0]), grads)

    dk_ref[0, 0], dv_ref[0, 0] = attend_back_tile(
        [rows_of(qh_ref[head, :, 0]) for head in (0, 1)],
        [kh_ref[head, 0, 0] for head in (0, 1)],
        v_ref[0, 0],
        grads,
        lse_ref[0],
        delta[...],
        acc,
    )

    @pl.when(tile == blocks - 1)
    def _():
        dq_ref[:, 0] = (acc[...].T * 0.125).astype(LOW).reshape(blocks, rows, 128)


def attend_back(qh, o, g, lse, kh, v):
    blocks, slots, rows, lanes = v.shape
    tile = pl.BlockSpec((1, 1, rows, lanes), lambda s, i: (i, s, 0, 0))
    tiles = pl.BlockSpec((2, 1, 1, rows, lanes), lambda s, i: (0, i, s, 0, 0))
    whole = pl.BlockSpec((blocks, 1, rows, lanes), lambda s, i: (0, s, 0, 0))
    wholes = pl.BlockSpec((2, blocks, 1, rows, lanes), lambda s, i: (0, 0, s, 0, 0))
    logs = pl.BlockSpec((1, 8, blocks * rows), lambda s, i: (s, 0, 0))
    shape = jax.ShapeDtypeStruct(v.shape, LOW)
    return pl.pallas_call(
        attend_back_kernel,
        grid=(slots, blocks),
        out_shape=(shape,) * 3,
        in_specs=[wholes, whole, whole, logs, tiles, tile],
        out_specs=(whole, tile, tile),
        scratch_shapes=[pltpu.VMEM((lanes, blocks * rows), HIGH), pltpu.VMEM((8, blocks * rows), HIGH)],
        compiler_params=pltpu.CompilerParams(vmem_limit_bytes=VMEM_LIMIT),
        name="attend_back",
    )(qh, o, g, lse, kh, v)


def normalize(values):
    mean = jnp.mean(values, axis=-1, keepdims=True)
    centred = values - mean
    spread = jnp.mean(centred * centred, axis=-1, keepdims=True)
    inverse = lax.rsqrt(spread + EPSILON)
    return centred * inverse, inverse


def normalize_back(grad, normal, inverse):
    return inverse * (
        grad
        - jnp.mean(grad, axis=-1, keepdims=True)
        - normal * jnp.mean(grad * normal, axis=-1, keepdims=True)
    )


def gelu_parts(u):
    bell = jnp.exp(-0.5 * u * u)
    t = 1.0 / (1.0 + (0.3275911 * 0.5**0.5) * jnp.abs(u))
    poly = 1.061405429 * t - 1.453152027
    poly = poly * t + 1.421413741
    poly = poly * t - 0.284496736
    poly = poly * t + 0.254829592
    tail = 0.5 * poly * t * bell
    below = jnp.where(u < 0.0, tail, 1.0 - tail)
    return u * below, below + u * bell * 0.3989422804014327


def column_sum(block):
    return jnp.sum(block.astype(HIGH), axis=0, keepdims=True)


def middle_kernel(
    chunk,
    tok_ref,
    att_ref,
    cot_ref,
    par_ref,
    hid_ref,
    w1_hbm,
    w2_hbm,
    out_ref,
    first_ref,
    d_att_ref,
    sums_ref,
    d_hid_ref,
    g1_hbm,
    g2_hbm,
    w1,
    w2,
    att,
    normed_low,
    n1,
    n2,
    act,
    slope,
    acc,
    low,
    wsem,
    gsem,
):
    hidden, width = w2.shape
    steps = hidden // chunk
    pieces, _, held = att_ref.shape

    def columns(c):
        return pl.ds(pl.multiple_of(c * chunk, chunk), chunk)

    def load1(c):
        return pltpu.make_async_copy(w1_hbm.at[:, columns(c)], w1.at[:, columns(c)], wsem.at[0, c])

    def load2(c):
        return pltpu.make_async_copy(w2_hbm.at[columns(c)], w2.at[columns(c)], wsem.at[1, c])

    last = pl.ds(hidden, width)
    load_out = pltpu.make_async_copy(w1_hbm.at[:, last], w1.at[:, last], wsem.at[0, steps])
    load_out.start()
    for c in range(steps):
        load1(c).start()
        load2(c).start()
    gain1, gain2 = par_ref[0:1], par_ref[1:2]
    bias = lambda i: par_ref[2 + i : 3 + i]
    for i in range(pieces):
        att[:, i * held : (i + 1) * held] = att_ref[i]
    load_out.wait()
    first_sum = tok_ref[...].astype(HIGH) + product(att[...], w1[:, hidden:]) + bias(2)
    normal, inverse1 = normalize(first_sum)
    n1[...] = normal
    normed = normal * gain1 + bias(3)
    normed_low[...] = normed.astype(LOW)
    acc[...] = normed + bias(4)

    @pl.loop(0, steps)
    def _(c):
        load1(c).wait()
        pre = product(normed_low[...], w1[:, columns(c)]) + hid_ref[:, columns(c)]
        value, rate = gelu_parts(pre)
        act[:, columns(c)] = value.astype(LOW)
        slope[:, columns(c)] = rate.astype(LOW)
        load2(c).wait()
        acc[...] += product(value.astype(LOW), w2[columns(c), :])

    normal, inverse2 = normalize(acc[...])
    n2[...] = normal
    out_ref[...] = (normal * gain2 + bias(5)).astype(LOW)
    cot = cot_ref[...].astype(HIGH)
    d_second = normalize_back(cot * gain2, normal, inverse2)
    low[...] = d_second.astype(LOW)
    acc[...] = d_second
    sums_ref[1:2] = column_sum(cot * normal)
    sums_ref[4:5] = column_sum(low[...])
    sums_ref[5:6] = column_sum(cot)

    def store1(c):
        return pltpu.make_async_copy(w1.at[:, columns(c)], g1_hbm.at[:, columns(c)], gsem.at[0, c])

    def store2(c):
        return pltpu.make_async_copy(w2.at[columns(c)], g2_hbm.at[columns(c)], gsem.at[1, c])

    @pl.loop(0, steps)
    def _(c):
        d_act = product_nt(low[...], w2[columns(c), :])
        d_pre = (d_act * slope[:, columns(c)].astype(HIGH)).astype(LOW)
        d_hid_ref[:, columns(c)] = column_sum(d_pre)
        acc[...] += product_nt(d_pre, w1[:, columns(c)])
        w2[columns(c), :] = product_tn(act[:, columns(c)], low[...]).astype(LOW)
        store2(c).start()
        w1[:, columns(c)] = product_tn(normed_low[...], d_pre).astype(LOW)
        store1(c).start()

    d_normed = acc[...]
    normal = n1[...]
    d_first = normalize_back(d_normed * gain1, normal, inverse1)
    first_ref[...] = d_first
    low[...] = d_first.astype(LOW)
    sums_ref[0:1] = column_sum(d_normed * normal)
    sums_ref[2:3] = column_sum(low[...])
    sums_ref[3:4] = column_sum(d_normed)
    d_att = product_nt(low[...], w1[:, hidden:]).astype(LOW)
    for i in range(pieces):
        d_att_ref[i] = d_att[:, i * held : (i + 1) * held]
    w1[:, hidden:] = product_tn(att[...], low[...]).astype(LOW)
    store_out = pltpu.make_async_copy(w1.at[:, last], g1_hbm.at[:, last], gsem.at[0, steps])
    store_out.start()
    for c in range(steps):
        store1(c).wait()
        store2(c).wait()
    store_out.wait()


def middle(tokens, att, cot, par, hid, w1, w2):
    count, width = tokens.shape
    hidden = w2.shape[0]
    pieces = att.shape[0]
    chunk = 512
    shape = jax.ShapeDtypeStruct
    vmem = pl.BlockSpec(memory_space=pltpu.VMEM)
    return pl.pallas_call(
        functools.partial(middle_kernel, chunk),
        out_shape=(
            shape((count, width), LOW),
            shape((count, width), HIGH),
            shape(att.shape, LOW),
            shape((8, width), HIGH),
            shape((1, hidden), HIGH),
            shape(w1.shape, LOW),
            shape(w2.shape, LOW),
        ),
        in_specs=[vmem] * 5 + in_hbm(2),
        out_specs=(vmem,) * 5 + tuple(in_hbm(2)),
        scratch_shapes=[
            pltpu.VMEM(w1.shape, LOW),
            pltpu.VMEM(w2.shape, LOW),
            pltpu.VMEM((count, width), LOW),
            pltpu.VMEM((count, width), LOW),
            pltpu.VMEM((count, width), HIGH),
            pltpu.VMEM((count, width), HIGH),
            pltpu.VMEM((count, hidden), LOW),
            pltpu.VMEM((count, hidden), LOW),
            pltpu.VMEM((count, width), HIGH),
            pltpu.VMEM((count, width), LOW),
            pltpu.SemaphoreType.DMA((2, hidden // chunk + 1)),
            pltpu.SemaphoreType.DMA((2, hidden // chunk + 1)),
        ],
        compiler_params=pltpu.CompilerParams(vmem_limit_bytes=VMEM_LIMIT),
        name="middle",
    )(tokens, att, cot, par, hid, w1, w2)


def finish_kernel(
    dq,
    dk,
    dv,
    w,
    d_first,
    small,
    x_hbm,
    tok_out,
    in_out,
    small_out,
    x,
    sent,
    C,
    S,
    A,
    H,
    Q,
    D,
    R,
    Z,
    M,
    N,
    T,
    send,
    recv,
    lsem,
):
    b, z = position()
    count, width = d_first.shape
    blocks = dq.shape[0]
    to_x, to_y, to_core = (b ^ 2, z), (b ^ 4, z), (b ^ 1, z)
    loads = []
    for i in range(blocks):
        load = pltpu.make_async_copy(x_hbm.at[i, pl.ds(0, count)], x.at[i], lsem.at[i])
        load.start()
        loads.append(load)
    greet([(b ^ d, z) for d in range(1, 8)] + [(b, z ^ d) for d in (1, 2, 3)])
    s = Sender(send, recv)
    small_in = [
        s.go(small.at[b ^ d], M.at[d - 1], (b ^ d, z), M.at[d - 1]) for d in range(1, 8)
    ]

    def mixed(i):
        return jnp.concatenate([ref[i].reshape(count, -1) for ref in (dq, dk, dv)], axis=-1)

    def piece(i):
        return product_nt(mixed(i), w[...])

    other = {}
    for e in (3, 1, 2, 0):
        sent[e] = piece(b ^ 1 ^ (2 * e)).astype(LOW)
        other[e] = s.go(sent.at[e], C.at[e], to_core, C.at[e])

    def own(e):
        mine = piece(b ^ (2 * e))
        other[e].wait_recv()
        return mine + C[e].astype(HIGH)

    S[3] = own(3).astype(LOW)
    halves = [
        s.go(half(S.at[3], 0), H.at[0], to_x, H.at[0]),
        s.go(half(S.at[3], 1), H.at[1], to_y, H.at[1]),
    ]
    S[2] = own(2).astype(LOW)
    pieces = [s.go(half(S.at[2], 1), half(Q.at[1], 1), to_y, half(Q.at[1], 1))]
    S[1] = own(1).astype(LOW)
    pieces.append(s.go(half(S.at[1], 0), half(Q.at[0], 0), to_x, half(Q.at[0], 0)))
    A[...] = own(0) + d_first[...]

    total = jnp.zeros((width, w.shape[1]), HIGH)
    for i in range(blocks):
        loads[i].wait()
        total = total + product_tn(x[i], mixed(i))
    D[...] = total.astype(LOW).reshape(D.shape)
    grads_in = [
        s.go(D.at[b ^ d], R.at[b], (b ^ d, z), R.at[b ^ d]) for d in range(1, 8)
    ]
    R[b] = D[b]

    halves[0].wait_recv()
    part = half(S.at[2], 0)
    part[...] = part[...] + H[0]
    pieces.append(s.go(part, half(Q.at[1], 0), to_y, half(Q.at[1], 0)))
    halves[1].wait_recv()
    part = half(S.at[1], 1)
    part[...] = part[...] + H[1]
    pieces.append(s.go(part, half(Q.at[0], 1), to_x, half(Q.at[0], 1)))

    N[...] = small[b]
    for i in range(7):
        small_in[i].wait_recv()
        N[...] += M[i]
    for row, ref in ((4, dq), (5, dv)):
        sums = jnp.zeros((1, 128), HIGH)
        for i in range(blocks):
            sums = sums + column_sum(ref[i].reshape(count, -1))
        N[row : row + 1, 0:128] = sums
    small_z = [s.go(N, T.at[d - 1], (b, z ^ d), T.at[d - 1]) for d in (1, 2, 3)]

    for copy in grads_in:
        copy.wait_recv()
    rows = R.shape[1] // 4

    def share(d):
        return R.at[:, pl.ds(pl.multiple_of((z ^ d) * rows, rows), rows)]

    in_z = [s.go(share(d), Z.at[d - 1], (b, z ^ d), Z.at[d - 1]) for d in (1, 2, 3)]
    for copy in small_z:
        copy.wait_recv()
    small_out[...] = ((N[...] + T[0]) + T[1]) + T[2]
    for copy in in_z:
        copy.wait_recv()
    in_out[...] = ((share(0)[...].astype(HIGH) + Z[0].astype(HIGH)) + Z[1].astype(HIGH)) + Z[
        2
    ].astype(HIGH)
    for copy in pieces:
        copy.wait_recv()
    tok_out[...] = A[...] + Q[0].astype(HIGH) + Q[1].astype(HIGH)
    s.drain()


def finish(dq, dk, dv, w, d_first, small, x):
    count, width = d_first.shape
    blocks, columns = dq.shape[0], w.shape[1]
    share = width // (4 * blocks)
    vmem = pl.BlockSpec(memory_space=pltpu.VMEM)
    shape = jax.ShapeDtypeStruct
    low = lambda *s: pltpu.VMEM(s, LOW)
    return pl.pallas_call(
        finish_kernel,
        out_shape=(
            shape((count, width), HIGH),
            shape((blocks, share, columns), HIGH),
            shape(small.shape[1:], HIGH),
        ),
        in_specs=[vmem] * 6 + in_hbm(1),
        out_specs=(vmem,) * 3,
        scratch_shapes=[
            low(blocks, count, width),
            low(4, count, width),
            low(4, count, width),
            low(4, count, width),
            pltpu.VMEM((count, width), HIGH),
            low(2, count // 2, width),
            low(2, count, width),
            low(blocks, 4 * share, columns),
            low(blocks, 4 * share, columns),
            low(3, blocks, share, columns),
            pltpu.VMEM((7, *small.shape[1:]), HIGH),
            pltpu.VMEM(small.shape[1:], HIGH),
            pltpu.VMEM((3, *small.shape[1:]), HIGH),
        ]
        + pair_of_semaphores(32)
        + [pltpu.SemaphoreType.DMA((blocks,))],
        compiler_params=pltpu.CompilerParams(
            collective_id=3, has_side_effects=True, vmem_limit_bytes=VMEM_LIMIT
        ),
        name="finish",
    )(dq, dk, dv, w, d_first, small, x)


def swap(pieces):
    return lax.all_to_all(pieces, "blk", 0, 0)


def by_slot(block, slots):
    blocks, count, held = block.shape
    block = block.reshape(blocks, slots, count // slots, held)
    return jnp.pad(block, ((0, 0),) * 3 + ((0, 128 - held),))


def front_apart(X, W, bias, slots):
    n_blk, count = X.shape[0], X.shape[1] - 16
    held = W.shape[1] // 3
    mixed = jnp.einsum("brd,dc->brc", X[:, :count], W, preferred_element_type=HIGH)
    parts = [mixed[..., i * held : (i + 1) * held] for i in range(3)]
    parts = [jnp.pad(p, ((0, 0), (0, 0), (0, 128 - held))).reshape(-1, 128) for p in parts]
    own = lax.dynamic_slice(bias[:2], (0, lax.axis_index("blk") * held), (2, held))
    own = jnp.pad(own, ((0, 0), (0, 128 - held)))
    codes = X[:, count, :count].reshape(-1, 1).astype(jnp.int32)
    codes = jnp.broadcast_to(codes, (n_blk * count, 128))
    queries, keys, values = split_heads(jnp.concatenate(parts, axis=1), (own[0], own[1]), codes)
    shape = (n_blk, slots, count // slots, 128)
    qh = jnp.stack(queries).reshape(2, *shape)
    kh = jnp.stack(keys).reshape(2, *shape)
    v = values.reshape(shape)
    att, lse = attend(qh, kh, v)
    rows_att = swap(att[..., :held].reshape(n_blk, count, held))
    return qh, kh, v, att, lse, rows_att


def on_device(
    tokens,
    input_weight,
    output_weight,
    expand_weight,
    reduce_weight,
    gains,
    biases,
    hidden_bias,
    segment,
    present,
    cotangent,
):
    slots, rows, width = tokens.shape
    n_blk, n_dp = lax.axis_size("blk"), lax.axis_size("dp")
    shards = n_blk * n_dp
    fast = (n_blk, n_dp) == (8, 4)
    held = width // n_blk
    shard = input_weight.shape[0]
    hidden = expand_weight.shape[1]
    count = slots * rows
    flat = tokens.reshape(count, width)

    code = segment + 4 * (1 - present)
    code_rows = jnp.zeros((16, width), LOW).at[0, :count].set(code.reshape(count).astype(LOW))
    sent_tokens = jnp.concatenate([flat, code_rows], axis=0)
    columns = input_weight.reshape(shard, 3, n_blk, held).transpose(2, 0, 1, 3)
    columns = columns.reshape(n_blk, shard, 3 * held)
    small = jnp.concatenate([gains.reshape(-1), biases.reshape(-1), hidden_bias])
    both = jnp.concatenate([expand_weight, output_weight], axis=1)
    if fast:
        small = jnp.concatenate([small[None], jnp.zeros((15, small.shape[0]), LOW)], axis=0)
        small = jnp.broadcast_to(small, (n_blk, *small.shape))
        win = jnp.concatenate([columns, small], axis=1)
        X, raw, W1, W2, rows_att, W, qh, kh, v, att, lse = front(
            sent_tokens, win, both, reduce_weight, slots
        )
        small = raw[:, :, shard].transpose(1, 0, 2).reshape(shards, 3 * held)
        W1, W2 = W1.reshape(width, -1), W2.reshape(hidden, width)
    else:
        X = lax.all_gather(sent_tokens, "blk")
        W = lax.all_gather(swap(columns), "dp", axis=1).reshape(width, 3 * held)
        small = lax.all_gather(small, BOTH)
        W1 = lax.all_gather(both, BOTH, axis=0, tiled=True)
        W2 = lax.all_gather(reduce_weight, BOTH, axis=0, tiled=True)
    part = width // shards
    cuts = small[:, : 8 * part].reshape(shards, 8, part).transpose(1, 0, 2).reshape(8, width)
    cuts = cuts.astype(HIGH)
    gain, bias = cuts[:2], cuts[2:]
    hidden_full = small[:, 8 * part :].reshape(hidden).astype(HIGH)

    all_tokens = X[:, :count]
    if not fast:
        qh, kh, v, att, lse, rows_att = front_apart(X, W, bias, slots)
    middle_out = middle(
        flat,
        rows_att,
        cotangent.reshape(count, width),
        cuts,
        hidden_full[None],
        W1,
        W2,
    )
    output, d_first, d_att, sums, d_hidden, grad_both, grad_reduce = middle_out
    output = output.reshape(slots, rows, width)
    g = swap(d_att)
    if fast:
        sum_both, sum_reduce = reduce(
            grad_both.reshape(n_blk, n_dp, shard, -1), grad_reduce.reshape(n_blk, n_dp, -1, width)
        )
    else:
        sum_both = lax.psum_scatter(grad_both, BOTH, scatter_dimension=0, tiled=True).astype(HIGH)
        sum_reduce = lax.psum_scatter(grad_reduce, BOTH, scatter_dimension=0, tiled=True)
        sum_reduce = sum_reduce.astype(HIGH)

    g = by_slot(g, slots)
    dq, dk, dv = attend_back(qh, att, g, lse, kh, v)
    small_rows = sums[:6].reshape(6, shards, part).transpose(1, 0, 2).reshape(shards, 6 * part)
    small_rows = jnp.concatenate([small_rows, d_hidden.reshape(shards, -1)], axis=1)
    if fast:
        lanes = small_rows.shape[1]
        small_rows = small_rows.reshape(n_blk, n_dp, lanes)
        small_rows = jnp.pad(small_rows, ((0, 0), (0, 4), (0, 3 * held - lanes)))
        grad_tokens, d_input, small_sum = finish(dq, dk, dv, W, d_first, small_rows, X)
        grad_input = d_input.reshape(n_blk, shard, 3, held).transpose(1, 2, 0, 3)
        grad_input = grad_input.reshape(shard, 3 * width)
        me_dp = lax.axis_index("dp")
        own_cols = lax.dynamic_slice(small_sum, (4, me_dp * part), (2, part))
        small_sum = lax.dynamic_slice(small_sum, (me_dp, 0), (1, lanes))[0]
    else:
        d_mixed = jnp.concatenate([dq[..., :held], dk[..., :held], dv[..., :held]], axis=-1)
        d_mixed = d_mixed.reshape(n_blk * count, 3 * held)
        d_input = product_tn(all_tokens.reshape(n_blk * count, width), d_mixed).astype(LOW)
        d_tokens = product_nt(d_mixed, W).astype(LOW)
        d_tokens = lax.psum_scatter(d_tokens, "blk", scatter_dimension=0, tiled=True)
        grad_tokens = d_first + d_tokens.astype(HIGH)
        d_input = swap(d_input.reshape(n_blk, n_dp * shard, 3 * held))
        d_input = d_input.reshape(n_blk, n_dp, shard, 3, held).transpose(1, 2, 3, 0, 4)
        d_input = d_input.reshape(n_dp, shard, 3 * width).astype(HIGH)
        grad_input = lax.psum_scatter(d_input, "dp", scatter_dimension=0, tiled=False)
        col = lambda a: jnp.sum(a.astype(HIGH), axis=0)
        own_cols = jnp.stack([col(d_mixed[:, :held]), col(d_mixed[:, 2 * held :])])
        own_cols = lax.psum_scatter(own_cols, "dp", scatter_dimension=1, tiled=True)
        small_sum = lax.psum_scatter(small_rows, BOTH, scatter_dimension=0, tiled=False)
    vectors = small_sum[: 6 * part].reshape(6, part)
    return (
        output,
        grad_tokens.reshape(slots, rows, width),
        grad_input,
        sum_both[:, hidden:],
        sum_both[:, :hidden],
        sum_reduce,
        vectors[:2],
        jnp.concatenate([own_cols, vectors[2:]], axis=0),
        small_sum[6 * part :],
    )


def solution(mesh):
    rows, sharded = P("dp", "blk", None), P(BOTH, None)
    in_specs = (rows, sharded, sharded, sharded, sharded, P(None, BOTH), P(None, BOTH), P(BOTH))
    in_specs += (P("dp", "blk"), P("dp", "blk"), rows)
    out_specs = (rows, rows, sharded, sharded, sharded, sharded)
    out_specs += (P(None, BOTH), P(None, BOTH), P(BOTH))
    return jax.shard_map(
        on_device, mesh=mesh, in_specs=in_specs, out_specs=out_specs, check_vma=False
    )
```

```python
import functools

import jax
import jax.numpy as jnp
from jax import lax
from jax.experimental import pallas as pl
from jax.experimental.pallas import tpu as pltpu
from jax.sharding import PartitionSpec as P

HEADS = 16
EPSILON = 1e-12
FAR = 2.0**60
BOTH = ("blk", "dp")
MESH = pl.DeviceIdType.MESH
LOW = jnp.bfloat16
HIGH = jnp.float32
VMEM_LIMIT = 60 * 2**20


def product(left, right):
    return jnp.dot(left, right, preferred_element_type=HIGH)


def product_nt(left, right):
    return lax.dot_general(left, right, (((1,), (1,)), ((), ())), preferred_element_type=HIGH)


def product_tn(left, right):
    return lax.dot_general(left, right, (((0,), (0,)), ((), ())), preferred_element_type=HIGH)


class Sender:
    def __init__(self, send, recv):
        self.send, self.recv, self.planned = send, recv, []

    def plan(self, src, dst, device, landing):
        at = len(self.planned)

        def copy(a, b):
            return pltpu.make_async_remote_copy(
                src_ref=a,
                dst_ref=b,
                send_sem=self.send.at[at],
                recv_sem=self.recv.at[at],
                device_id=device,
                device_id_type=MESH,
            )

        out = copy(src, dst)
        self.planned.append(out)
        landed = copy(landing, landing)
        landed.go = out.start
        return landed

    def go(self, *what):
        landed = self.plan(*what)
        landed.go()
        return landed

    def drain(self):
        for out in self.planned:
            out.wait_send()


def greet(peers):
    barrier = pltpu.get_barrier_semaphore()
    for peer in peers:
        pl.semaphore_signal(barrier, inc=1, device_id=peer, device_id_type=MESH)
    pl.semaphore_wait(barrier, len(peers))


def half(ref, which):
    rows = ref.shape[0]
    cut = rows // 32 * 16
    return ref.at[pl.ds(0, cut)] if which == 0 else ref.at[pl.ds(cut, rows - cut)]


def position():
    return lax.axis_index("blk"), lax.axis_index("dp")


def first_lanes(shape):
    return lax.broadcasted_iota(jnp.int32, shape, len(shape) - 1) < 64


def rows_of(block):
    return block.reshape(-1, block.shape[-1])


def attend_tile(queries, keys, values):
    rows = queries[0].shape[0]
    ones = jnp.ones_like(values)
    mine = first_lanes(values.shape)
    outs, logs = [], []
    for head in (0, 1):
        scores = product_nt(queries[head], keys[head])
        top = jnp.max(scores, axis=-1, keepdims=True)
        weights = jnp.exp(scores - top).astype(LOW)
        total = product(weights, jnp.where(mine == (head == 0), values, ones))
        mass = pltpu.roll(total, 64, 1)
        outs.append(total / mass)
        logs.append(top + jnp.log(mass))
    mine = first_lanes((rows, 128))
    flipped = jnp.where(mine, logs[0], logs[1]).T
    logs = jnp.concatenate([flipped[0:1], flipped[64:65], jnp.zeros((6, rows), HIGH)], axis=0)
    return jnp.where(mine, outs[0], outs[1]).astype(LOW), logs


def split_heads(mixed, bias, codes):
    rows = mixed.shape[0]
    q = (mixed[:, :128] + bias[0]).astype(LOW) * LOW(0.125)
    k = mixed[:, 128:256].astype(LOW)
    v = (mixed[:, 256:] + bias[1]).astype(LOW)
    lanes = lax.broadcasted_iota(jnp.int32, (rows, 128), 1) % 64
    protein = jnp.where(codes >= 4, codes - 4, codes)
    q_marks = jnp.where((lanes < 5) & (lanes != protein), -FAR, 0.0).astype(LOW)
    k_marks = jnp.where(lanes == jnp.minimum(codes, 4), 1.0, 0.0).astype(LOW)
    mine = first_lanes((rows, 128))
    return (
        (jnp.where(mine, q, q_marks), jnp.where(mine, q_marks, q)),
        (jnp.where(mine, k, k_marks), jnp.where(mine, k_marks, k)),
        v,
    )


def front_kernel(
    x,
    win,
    w1,
    w2,
    X_out,
    raw,
    W1,
    W2,
    rows_att,
    wfull,
    qh,
    kh,
    v,
    att,
    lse,
    X,
    W,
    send,
    recv,
    asend,
    arecv,
    lsem,
    osem,
):
    b, z = position()
    bx, by, bd, bc = b ^ 2, b ^ 4, b ^ 6, b ^ 1
    count = X.shape[1] - 16
    slots, rows = qh.shape[2:4]
    greet([(b ^ d, z) for d in range(1, 8)] + [(b, z ^ d) for d in range(1, 4)])
    s = Sender(send, recv)
    locs = []

    def local(src, dst):
        copy = pltpu.make_async_copy(src, dst, lsem.at[len(locs)])
        copy.start()
        locs.append(copy)

    local(win.at[b], W.at[z, b])
    local(x, X.at[b])
    local(w1, W1.at[b, z])
    local(w2, W2.at[b, z])
    to_x, to_y, to_core = (bx, z), (by, z), (bc, z)

    def token_core(src, bb):
        return s.plan(src, X.at[bb], to_core, X.at[bb ^ 1])

    columns = [
        s.go(win.at[b ^ d], W.at[z, b], (b ^ d, z), W.at[z, b ^ d]) for d in range(1, 8)
    ]
    token_x = s.go(x, X.at[b], to_x, X.at[bx])
    token_y = s.go(x, X.at[b], to_y, X.at[by])
    token_c = token_core(x, b)
    token_c.go()

    own, full = (w1, w2), (W1, W2)
    ways = {}
    for a in (0, 1):
        F = full[a]
        for d in range(4):
            zz = z ^ d
            src = F.at[b, zz] if d else own[a]
            way = {}
            if d:
                way["z"] = s.plan(own[a], F.at[b, z], (b, zz), F.at[b, zz])
            way["x"] = s.plan(src, F.at[b, zz], to_x, F.at[bx, zz])
            way["y"] = s.plan(src, F.at[b, zz], to_y, F.at[by, zz])
            piece = half(F.at[bx, zz], 0)
            way["xy"] = s.plan(piece, piece, to_y, half(F.at[bd, zz], 0))
            piece = half(F.at[by, zz], 1)
            way["yx"] = s.plan(piece, piece, to_x, half(F.at[bd, zz], 1))
            way["core"] = [
                s.plan(src if bb is b else F.at[bb, zz], F.at[bb, zz], to_core, F.at[bb ^ 1, zz])
                for bb in (b, bx, by, bd)
            ]
            ways[a, d] = way
    for a in (0, 1):
        for d in (1, 2, 3):
            ways[a, d]["z"].go()

    def first(d, a):
        way = ways[a, d]
        if d:
            way["z"].wait_recv()
        way["x"].go()
        way["y"].go()
        way["core"][0].go()

    def second(d, a):
        way = ways[a, d]
        way["x"].wait_recv()
        way["xy"].go()
        way["core"][1].go()
        way["y"].wait_recv()
        way["yx"].go()
        way["core"][2].go()

    def third(d, a):
        way = ways[a, d]
        way["xy"].wait_recv()
        way["yx"].wait_recv()
        way["core"][3].go()

    def both(stage, d):
        stage(d, 0)
        stage(d, 1)

    both(first, 0)
    for copy in columns:
        copy.wait_recv()
    locs[0].wait()
    columns = [s.go(W.at[z], W.at[z], (b, z ^ d), W.at[z ^ d]) for d in (1, 2, 3)]
    token_x.wait_recv()
    piece = half(X.at[bx], 0)
    token_one = s.go(piece, piece, to_y, half(X.at[bd], 0))
    token_xc = token_core(X.at[bx], bx)
    token_xc.go()
    token_y.wait_recv()
    piece = half(X.at[by], 1)
    token_two = s.go(piece, piece, to_x, half(X.at[bd], 1))
    token_yc = token_core(X.at[by], by)
    token_yc.go()
    token_dc = token_core(X.at[bd], bd)
    both(first, 1)
    for copy in columns:
        copy.wait_recv()
    raw_copy = pltpu.make_async_copy(W, raw, lsem.at[4])
    raw_copy.start()
    for i in range(8):
        for j in range(4):
            at = (i * 4 + j) * 32
            wfull[at : at + 32] = W[j, i, 0:32]
    bias = [
        jnp.concatenate([W[j, b, 32:33, at : at + 32] for j in range(4)], axis=1).astype(HIGH)
        for at in (64, 96)
    ]

    def mix(i):
        pltpu.make_async_copy(X.at[i], X_out.at[i], osem.at[i]).start()
        mixed = product(X[i, 0:count], wfull[...])
        codes = jnp.broadcast_to(X[i, count : count + 1, 0:count].astype(HIGH), (128, count)).T
        queries, keys, values = split_heads(mixed, bias, codes.astype(jnp.int32))
        for head in (0, 1):
            qh[head, i] = queries[head].reshape(slots, rows, 128)
            kh[head, i] = keys[head].reshape(slots, rows, 128)
        v[i] = values.reshape(slots, rows, 128)

    locs[1].wait()
    mix(b)
    token_c.wait_recv()
    mix(bc)
    mix(bx)
    token_xc.wait_recv()
    mix(bx ^ 1)
    both(first, 2)
    mix(by)
    token_yc.wait_recv()
    mix(by ^ 1)
    token_one.wait_recv()
    token_two.wait_recv()
    token_dc.go()
    mix(bd)
    both(first, 3)
    token_dc.wait_recv()
    mix(bd ^ 1)
    both(second, 0)

    def piece_of(slot):
        return pl.ds(pl.multiple_of(slot * rows, rows), rows)

    def send_att(slot, d):
        return pltpu.make_async_remote_copy(
            src_ref=att.at[b ^ d, slot],
            dst_ref=rows_att.at[b, piece_of(slot)],
            send_sem=asend.at[slot * 8 + d],
            recv_sem=arecv.at[slot * 8 + d],
            device_id=(b ^ d, z),
            device_id_type=MESH,
        )

    def keep_att(slot):
        return pltpu.make_async_copy(
            att.at[b, slot], rows_att.at[b, piece_of(slot)], osem.at[8 + slot]
        )

    events = {4: (second, 1, 0), 6: (second, 1, 1), 10: (second, 2, 0), 12: (second, 2, 1)}

    @pl.loop(0, 8 * slots)
    def _(step):
        slot, d = step // 8, (step + 1) % 8
        i = b ^ d
        keys = [rows_of(kh[head, :, slot]) for head in (0, 1)]
        out, logs = attend_tile([qh[head, i, slot] for head in (0, 1)], keys, rows_of(v[:, slot]))
        att[i, slot] = out
        lse[slot, :, pl.ds(pl.multiple_of(i * rows, rows), rows)] = logs

        @pl.when(d != 0)
        def _():
            send_att(slot, d).start()

        @pl.when(d == 0)
        def _():
            keep_att(slot).start()

        for at, (event, *what) in events.items():
            pl.when(step == at)(functools.partial(event, *what))

    both(third, 0)
    both(second, 3)
    for d in (1, 2, 3):
        both(third, d)
    for way in ways.values():
        for copy in way["core"]:
            copy.wait_recv()
    for slot in range(slots):
        keep_att(slot).wait()
        for d in range(1, 8):
            copy = send_att(slot, d)
            copy.wait_send()
            pltpu.make_async_remote_copy(
                src_ref=rows_att.at[b ^ d, piece_of(slot)],
                dst_ref=rows_att.at[b ^ d, piece_of(slot)],
                send_sem=asend.at[slot * 8 + d],
                recv_sem=arecv.at[slot * 8 + d],
                device_id=(b ^ d, z),
                device_id_type=MESH,
            ).wait_recv()
    s.drain()
    for copy in locs[2:]:
        copy.wait()
    raw_copy.wait()
    for i in range(8):
        pltpu.make_async_copy(X.at[i], X_out.at[i], osem.at[i]).wait()


def in_hbm(count):
    return [pl.BlockSpec(memory_space=pl.ANY)] * count


def pair_of_semaphores(count):
    return [pltpu.SemaphoreType.DMA((count,)), pltpu.SemaphoreType.DMA((count,))]


def front(x, win, w1, w2, slots):
    count, width = x.shape[0] - 16, x.shape[1]
    rows = count // slots
    shape = lambda *s: jax.ShapeDtypeStruct(s, LOW)
    vmem = pl.BlockSpec(memory_space=pltpu.VMEM)
    return pl.pallas_call(
        front_kernel,
        out_shape=(
            shape(8, *x.shape),
            shape(4, *win.shape),
            shape(8, 4, *w1.shape),
            shape(8, 4, *w2.shape),
            shape(8, count, 128),
            shape(width, win.shape[2]),
            shape(2, 8, slots, rows, 128),
            shape(2, 8, slots, rows, 128),
            shape(8, slots, rows, 128),
            shape(8, slots, rows, 128),
            jax.ShapeDtypeStruct((slots, 8, 8 * rows), HIGH),
        ),
        in_specs=in_hbm(4),
        out_specs=tuple(in_hbm(5)) + (vmem,) * 6,
        scratch_shapes=[pltpu.VMEM((8, *x.shape), LOW), pltpu.VMEM((4, *win.shape), LOW)]
        + pair_of_semaphores(100)
        + pair_of_semaphores(8 * slots)
        + [pltpu.SemaphoreType.DMA((5,)), pltpu.SemaphoreType.DMA((8 + slots,))],
        compiler_params=pltpu.CompilerParams(
            collective_id=1, has_side_effects=True, vmem_limit_bytes=VMEM_LIMIT
        ),
        name="front",
    )(x, win, w1, w2)


def add_rows(out, one, two):
    @pl.loop(0, one.shape[0] // 16)
    def _(i):
        rows = pl.ds(pl.multiple_of(i * 16, 16), 16)
        out[rows, :] = one[rows, :] + two[rows, :]


class Reducer:
    ORDER = (1, 2, 3, 0)

    def __init__(self, s, g, out, C, S, H, Q, Z, lsem):
        b, z = position()
        to_x, to_y, to_core = (b ^ 2, z), (b ^ 4, z), (b ^ 1, z)
        self.out, self.C, self.S, self.H, self.Q, self.Z = out, C, S, H, Q, Z
        self.mine, self.other, self.halves, self.ahead, self.rest, self.last = ({} for _ in range(6))
        for d in self.ORDER:
            for e in (3, 1, 2, 0):
                self.mine[d, e] = pltpu.make_async_copy(
                    g.at[b ^ (2 * e), z ^ d], S.at[e, d], lsem.at[d * 4 + e]
                )
                self.other[d, e] = s.plan(
                    g.at[b ^ 1 ^ (2 * e), z ^ d], C.at[e, d], to_core, C.at[e, d]
                )

            def send(e, part, to, where):
                return s.plan(half(S.at[e, d], part), where, to, where)

            self.halves[d] = [send(3, 0, to_x, H.at[d, 0]), send(3, 1, to_y, H.at[d, 1])]
            self.ahead[d] = [
                send(2, 1, to_y, half(Q.at[d, 1], 1)),
                send(1, 0, to_x, half(Q.at[d, 0], 0)),
            ]
            self.rest[d] = [
                send(2, 0, to_y, half(Q.at[d, 1], 0)),
                send(1, 1, to_x, half(Q.at[d, 0], 1)),
            ]
            if d:
                self.last[d] = s.plan(S.at[0, d], Z.at[d - 1], (b, z ^ d), Z.at[d - 1])

    def start(self):
        for d in self.ORDER:
            for e in (3, 1, 2, 0):
                self.mine[d, e].start()
                self.other[d, e].go()

    def fold(self, d):
        for e in (3, 1, 2, 0):
            self.mine[d, e].wait()
            self.other[d, e].wait_recv()
            add_rows(self.S.at[e, d], self.S.at[e, d], self.C.at[e, d])
            for copy in {3: self.halves[d], 1: self.ahead[d][1:], 2: self.ahead[d][:1], 0: []}[e]:
                copy.go()

    def relay(self, d):
        for i, e in ((0, 2), (1, 1)):
            self.halves[d][i].wait_recv()
            part = half(self.S.at[e, d], i)
            add_rows(part, part, self.H.at[d, i])
            self.rest[d][i].go()

    def collect(self, d):
        for copy in self.ahead[d] + self.rest[d]:
            copy.wait_recv()
        for i in (0, 1):
            add_rows(self.S.at[0, d], self.S.at[0, d], self.Q.at[d, i])
        if d:
            self.last[d].go()

    def total(self):
        for d in (1, 2, 3):
            self.last[d].wait_recv()
        S, Z, out = self.S, self.Z, self.out

        @pl.loop(0, out.shape[0] // 16)
        def _(i):
            rows = pl.ds(pl.multiple_of(i * 16, 16), 16)
            total = S[0, 0, rows, :].astype(HIGH)
            for d in range(3):
                total = total + Z[d, rows, :].astype(HIGH)
            out[rows, :] = total

    @staticmethod
    def scratch(rows, columns):
        lead = (((4, 4), 1), ((4, 4), 1), ((4, 2), 2), ((4, 2), 1), ((3,), 1))
        shapes = [pltpu.VMEM((*n, rows // cut, columns), LOW) for n, cut in lead]
        return shapes + [pltpu.SemaphoreType.DMA((16,))]

    COPIES = 16 + 4 * 6 + 3


def attend_kernel(qh_ref, kh_ref, v_ref, out_ref, lse_ref):
    keys = [rows_of(kh_ref[head, :, 0]) for head in (0, 1)]
    out_ref[0, 0], lse_ref[0] = attend_tile(
        [qh_ref[head, 0, 0] for head in (0, 1)], keys, rows_of(v_ref[:, 0])
    )


def attend(qh, kh, v):
    blocks, slots, rows, lanes = v.shape
    tile = pl.BlockSpec((1, 1, rows, lanes), lambda s, i: (i, s, 0, 0))
    tiles = pl.BlockSpec((2, 1, 1, rows, lanes), lambda s, i: (0, i, s, 0, 0))
    whole = pl.BlockSpec((blocks, 1, rows, lanes), lambda s, i: (0, s, 0, 0))
    wholes = pl.BlockSpec((2, blocks, 1, rows, lanes), lambda s, i: (0, 0, s, 0, 0))
    return pl.pallas_call(
        attend_kernel,
        grid=(slots, blocks),
        out_shape=(
            jax.ShapeDtypeStruct(v.shape, LOW),
            jax.ShapeDtypeStruct((slots, 8, blocks * rows), HIGH),
        ),
        in_specs=[tiles, wholes, whole],
        out_specs=(tile, pl.BlockSpec((1, 8, rows), lambda s, i: (s, 0, i))),
        compiler_params=pltpu.CompilerParams(vmem_limit_bytes=VMEM_LIMIT),
        name="attend",
    )(qh, kh, v)


def row_products(out, grad):
    pick = (lax.broadcasted_iota(jnp.int32, (8, 128), 0) == 0) == first_lanes((8, 128))
    return lax.dot_general(
        pick.astype(HIGH),
        out.astype(HIGH) * grad.astype(HIGH),
        (((1,), (1,)), ((), ())),
        precision=lax.Precision.HIGHEST,
        preferred_element_type=HIGH,
    )


def attend_back_tile(queries, keys, values, grads, logs, delta, acc):
    zeros = jnp.zeros_like(grads)
    mine = first_lanes(grads.shape)
    dk, dv = [], 0.0
    for head in (0, 1):
        grad = jnp.where(mine == (head == 0), grads, zeros)
        probs = jnp.exp(product_nt(keys[head], queries[head]) - logs[head : head + 1])
        pushed = product_nt(values, grad)
        d_scores = (probs * (pushed - delta[head : head + 1])).astype(LOW)
        dv = dv + product(probs.astype(LOW), grad)
        dk.append(product(d_scores, queries[head]))
        keys_t = keys[head].T[head * 64 : head * 64 + 64]
        acc[head * 64 : head * 64 + 64, :] += product(keys_t, d_scores)
    return jnp.where(first_lanes(dk[0].shape), dk[0], dk[1]).astype(LOW), dv.astype(LOW)


def attend_back_kernel(
    qh_ref, o_ref, g_ref, lse_ref, kh_ref, v_ref, dq_ref, dk_ref, dv_ref, acc, delta
):
    tile = pl.program_id(1)
    blocks, _, rows, _ = g_ref.shape
    grads = rows_of(g_ref[:, 0])

    @pl.when(tile == 0)
    def _():
        acc[...] = jnp.zeros_like(acc)
        delta[...] = row_products(rows_of(o_ref[:, 0]), grads)

    dk_ref[0, 0], dv_ref[0, 0] = attend_back_tile(
        [rows_of(qh_ref[head, :, 0]) for head in (0, 1)],
        [kh_ref[head, 0, 0] for head in (0, 1)],
        v_ref[0, 0],
        grads,
        lse_ref[0],
        delta[...],
        acc,
    )

    @pl.when(tile == blocks - 1)
    def _():
        dq_ref[:, 0] = (acc[...].T * 0.125).astype(LOW).reshape(blocks, rows, 128)


def attend_back(qh, o, g, lse, kh, v):
    blocks, slots, rows, lanes = v.shape
    tile = pl.BlockSpec((1, 1, rows, lanes), lambda s, i: (i, s, 0, 0))
    tiles = pl.BlockSpec((2, 1, 1, rows, lanes), lambda s, i: (0, i, s, 0, 0))
    whole = pl.BlockSpec((blocks, 1, rows, lanes), lambda s, i: (0, s, 0, 0))
    wholes = pl.BlockSpec((2, blocks, 1, rows, lanes), lambda s, i: (0, 0, s, 0, 0))
    logs = pl.BlockSpec((1, 8, blocks * rows), lambda s, i: (s, 0, 0))
    shape = jax.ShapeDtypeStruct(v.shape, LOW)
    return pl.pallas_call(
        attend_back_kernel,
        grid=(slots, blocks),
        out_shape=(shape,) * 3,
        in_specs=[wholes, whole, whole, logs, tiles, tile],
        out_specs=(whole, tile, tile),
        scratch_shapes=[pltpu.VMEM((lanes, blocks * rows), HIGH), pltpu.VMEM((8, blocks * rows), HIGH)],
        compiler_params=pltpu.CompilerParams(vmem_limit_bytes=VMEM_LIMIT),
        name="attend_back",
    )(qh, o, g, lse, kh, v)


def back_kernel(
    d_att, qh, kh, v, att, lse, g1, dq, dk, dv, o1, grads, acc, delta, C, S, H, Q, Z, lsem, send, recv
):
    b, z = position()
    blocks, slots, rows, _ = v.shape
    count = slots * rows
    greet([(b ^ d, z) for d in range(1, 8)] + [(b, z ^ d) for d in (1, 2, 3)])
    s = Sender(send, recv)
    arriving = [
        s.go(d_att.at[b ^ d], grads.at[b], (b ^ d, z), grads.at[b ^ d]) for d in range(1, 8)
    ]
    sums = Reducer(s, g1, o1, C, S, H, Q, Z, lsem)
    sums.start()
    grads[b] = d_att[b]
    sums.fold(1)
    sums.fold(2)
    for copy in arriving:
        copy.wait_recv()

    def grad_rows(slot):
        part = pl.ds(pl.multiple_of(slot * rows, rows), rows)
        return rows_of(grads[:, part])

    events = {
        1: (sums.relay, 1),
        3: (sums.fold, 3),
        4: (sums.relay, 2),
        5: (sums.collect, 1),
        6: (sums.fold, 0),
        8: (sums.relay, 3),
        9: (sums.collect, 2),
        11: (sums.relay, 0),
        13: (sums.collect, 3),
    }

    @pl.loop(0, blocks * slots)
    def _(step):
        slot, tile = step // blocks, step % blocks
        slot_grads = grad_rows(slot)

        @pl.when(tile == 0)
        def _():
            acc[...] = jnp.zeros_like(acc)
            delta[...] = row_products(rows_of(att[:, slot]), slot_grads)

        dk[tile, slot], dv[tile, slot] = attend_back_tile(
            [rows_of(qh[head, :, slot]) for head in (0, 1)],
            [kh[head, tile, slot] for head in (0, 1)],
            v[tile, slot],
            slot_grads,
            lse[slot],
            delta[...],
            acc,
        )

        @pl.when(tile == blocks - 1)
        def _():
            dq[:, slot] = (acc[...].T * 0.125).astype(LOW).reshape(blocks, rows, 128)

        for at, (event, what) in events.items():
            pl.when(step == at)(functools.partial(event, what))

    sums.collect(0)
    sums.total()
    s.drain()


def back(d_att, qh, kh, v, att, lse, g1):
    blocks, slots, rows, lanes = v.shape
    shape = jax.ShapeDtypeStruct
    vmem = pl.BlockSpec(memory_space=pltpu.VMEM)
    return pl.pallas_call(
        back_kernel,
        out_shape=(shape(v.shape, LOW),) * 3 + (shape(g1.shape[2:], HIGH),),
        in_specs=[vmem] * 6 + in_hbm(1),
        out_specs=(vmem,) * 4,
        scratch_shapes=[
            pltpu.VMEM(d_att.shape, LOW),
            pltpu.VMEM((lanes, blocks * rows), HIGH),
            pltpu.VMEM((8, blocks * rows), HIGH),
        ]
        + Reducer.scratch(*g1.shape[2:])
        + pair_of_semaphores(7 + Reducer.COPIES),
        compiler_params=pltpu.CompilerParams(
            collective_id=2, has_side_effects=True, vmem_limit_bytes=VMEM_LIMIT
        ),
        name="back",
    )(d_att, qh, kh, v, att, lse, g1)


def normalize(values):
    mean = jnp.mean(values, axis=-1, keepdims=True)
    centred = values - mean
    spread = jnp.mean(centred * centred, axis=-1, keepdims=True)
    inverse = lax.rsqrt(spread + EPSILON)
    return centred * inverse, inverse


def normalize_back(grad, normal, inverse):
    return inverse * (
        grad
        - jnp.mean(grad, axis=-1, keepdims=True)
        - normal * jnp.mean(grad * normal, axis=-1, keepdims=True)
    )


def gelu_parts(u):
    bell = jnp.exp(-0.5 * u * u)
    t = 1.0 / (1.0 + (0.3275911 * 0.5**0.5) * jnp.abs(u))
    poly = 1.061405429 * t - 1.453152027
    poly = poly * t + 1.421413741
    poly = poly * t - 0.284496736
    poly = poly * t + 0.254829592
    tail = 0.5 * poly * t * bell
    below = jnp.where(u < 0.0, tail, 1.0 - tail)
    return u * below, below + u * bell * 0.3989422804014327


def column_sum(block):
    return jnp.sum(block.astype(HIGH), axis=0, keepdims=True)


def middle_kernel(
    chunk,
    tok_ref,
    att_ref,
    cot_ref,
    par_ref,
    hid_ref,
    w1_hbm,
    w2_hbm,
    out_ref,
    first_ref,
    d_att_ref,
    sums_ref,
    d_hid_ref,
    g1_hbm,
    g2_hbm,
    w1,
    w2,
    att,
    normed_low,
    n1,
    n2,
    act,
    slope,
    acc,
    low,
    wsem,
    gsem,
):
    hidden, width = w2.shape
    steps = hidden // chunk
    pieces, _, held = att_ref.shape

    def columns(c):
        return pl.ds(pl.multiple_of(c * chunk, chunk), chunk)

    def load1(c):
        return pltpu.make_async_copy(w1_hbm.at[:, columns(c)], w1.at[:, columns(c)], wsem.at[0, c])

    def load2(c):
        return pltpu.make_async_copy(w2_hbm.at[columns(c)], w2.at[columns(c)], wsem.at[1, c])

    last = pl.ds(hidden, width)
    load_out = pltpu.make_async_copy(w1_hbm.at[:, last], w1.at[:, last], wsem.at[0, steps])
    load_out.start()
    for c in range(steps):
        load1(c).start()
        load2(c).start()
    gain1, gain2 = par_ref[0:1], par_ref[1:2]
    bias = lambda i: par_ref[2 + i : 3 + i]
    for i in range(pieces):
        att[:, i * held : (i + 1) * held] = att_ref[i]
    load_out.wait()
    first_sum = tok_ref[...].astype(HIGH) + product(att[...], w1[:, hidden:]) + bias(2)
    normal, inverse1 = normalize(first_sum)
    n1[...] = normal
    normed = normal * gain1 + bias(3)
    normed_low[...] = normed.astype(LOW)
    acc[...] = normed + bias(4)

    @pl.loop(0, steps)
    def _(c):
        load1(c).wait()
        pre = product(normed_low[...], w1[:, columns(c)]) + hid_ref[:, columns(c)]
        value, rate = gelu_parts(pre)
        act[:, columns(c)] = value.astype(LOW)
        slope[:, columns(c)] = rate.astype(LOW)
        load2(c).wait()
        acc[...] += product(value.astype(LOW), w2[columns(c), :])

    normal, inverse2 = normalize(acc[...])
    n2[...] = normal
    out_ref[...] = (normal * gain2 + bias(5)).astype(LOW)
    cot = cot_ref[...].astype(HIGH)
    d_second = normalize_back(cot * gain2, normal, inverse2)
    low[...] = d_second.astype(LOW)
    acc[...] = d_second
    sums_ref[1:2] = column_sum(cot * normal)
    sums_ref[4:5] = column_sum(low[...])
    sums_ref[5:6] = column_sum(cot)

    def store1(c):
        return pltpu.make_async_copy(w1.at[:, columns(c)], g1_hbm.at[:, columns(c)], gsem.at[0, c])

    def store2(c):
        return pltpu.make_async_copy(w2.at[columns(c)], g2_hbm.at[columns(c)], gsem.at[1, c])

    @pl.loop(0, steps)
    def _(c):
        d_act = product_nt(low[...], w2[columns(c), :])
        d_pre = (d_act * slope[:, columns(c)].astype(HIGH)).astype(LOW)
        d_hid_ref[:, columns(c)] = column_sum(d_pre)
        acc[...] += product_nt(d_pre, w1[:, columns(c)])
        w2[columns(c), :] = product_tn(act[:, columns(c)], low[...]).astype(LOW)
        store2(c).start()
        w1[:, columns(c)] = product_tn(normed_low[...], d_pre).astype(LOW)
        store1(c).start()

    d_normed = acc[...]
    normal = n1[...]
    d_first = normalize_back(d_normed * gain1, normal, inverse1)
    first_ref[...] = d_first
    low[...] = d_first.astype(LOW)
    sums_ref[0:1] = column_sum(d_normed * normal)
    sums_ref[2:3] = column_sum(low[...])
    sums_ref[3:4] = column_sum(d_normed)
    d_att = product_nt(low[...], w1[:, hidden:]).astype(LOW)
    for i in range(pieces):
        d_att_ref[i] = d_att[:, i * held : (i + 1) * held]
    w1[:, hidden:] = product_tn(att[...], low[...]).astype(LOW)
    store_out = pltpu.make_async_copy(w1.at[:, last], g1_hbm.at[:, last], gsem.at[0, steps])
    store_out.start()
    for c in range(steps):
        store1(c).wait()
        store2(c).wait()
    store_out.wait()


def middle(tokens, att, cot, par, hid, w1, w2):
    count, width = tokens.shape
    hidden = w2.shape[0]
    pieces = att.shape[0]
    chunk = 512
    shape = jax.ShapeDtypeStruct
    vmem = pl.BlockSpec(memory_space=pltpu.VMEM)
    return pl.pallas_call(
        functools.partial(middle_kernel, chunk),
        out_shape=(
            shape((count, width), LOW),
            shape((count, width), HIGH),
            shape(att.shape, LOW),
            shape((8, width), HIGH),
            shape((1, hidden), HIGH),
            shape(w1.shape, LOW),
            shape(w2.shape, LOW),
        ),
        in_specs=[vmem] * 5 + in_hbm(2),
        out_specs=(vmem,) * 5 + tuple(in_hbm(2)),
        scratch_shapes=[
            pltpu.VMEM(w1.shape, LOW),
            pltpu.VMEM(w2.shape, LOW),
            pltpu.VMEM((count, width), LOW),
            pltpu.VMEM((count, width), LOW),
            pltpu.VMEM((count, width), HIGH),
            pltpu.VMEM((count, width), HIGH),
            pltpu.VMEM((count, hidden), LOW),
            pltpu.VMEM((count, hidden), LOW),
            pltpu.VMEM((count, width), HIGH),
            pltpu.VMEM((count, width), LOW),
            pltpu.SemaphoreType.DMA((2, hidden // chunk + 1)),
            pltpu.SemaphoreType.DMA((2, hidden // chunk + 1)),
        ],
        compiler_params=pltpu.CompilerParams(vmem_limit_bytes=VMEM_LIMIT),
        name="middle",
    )(tokens, att, cot, par, hid, w1, w2)


def finish_kernel(
    dq,
    dk,
    dv,
    w,
    d_first,
    small,
    x_hbm,
    g2,
    tok_out,
    in_out,
    small_out,
    o2,
    x,
    sent,
    C,
    S,
    A,
    H,
    Q,
    D,
    R,
    Z,
    M,
    N,
    T,
    C2,
    S2,
    H2,
    Q2,
    Z2,
    lsem2,
    send,
    recv,
    lsem,
):
    b, z = position()
    count, width = d_first.shape
    blocks = dq.shape[0]
    to_x, to_y, to_core = (b ^ 2, z), (b ^ 4, z), (b ^ 1, z)
    loads = []
    for i in range(blocks):
        load = pltpu.make_async_copy(x_hbm.at[i, pl.ds(0, count)], x.at[i], lsem.at[i])
        load.start()
        loads.append(load)
    greet([(b ^ d, z) for d in range(1, 8)] + [(b, z ^ d) for d in (1, 2, 3)])
    s = Sender(send, recv)
    sums = Reducer(s, g2, o2, C2, S2, H2, Q2, Z2, lsem2)
    small_in = [
        s.go(small.at[b ^ d], M.at[d - 1], (b ^ d, z), M.at[d - 1]) for d in range(1, 8)
    ]

    def mixed(i):
        return jnp.concatenate([ref[i].reshape(count, -1) for ref in (dq, dk, dv)], axis=-1)

    def piece(i):
        return product_nt(mixed(i), w[...])

    other = {}
    for e in (3, 1, 2, 0):
        sent[e] = piece(b ^ 1 ^ (2 * e)).astype(LOW)
        other[e] = s.go(sent.at[e], C.at[e], to_core, C.at[e])
        if e == 3:
            sums.start()
    sums.fold(1)

    def own(e):
        mine = piece(b ^ (2 * e))
        other[e].wait_recv()
        return mine + C[e].astype(HIGH)

    S[3] = own(3).astype(LOW)
    halves = [
        s.go(half(S.at[3], 0), H.at[0], to_x, H.at[0]),
        s.go(half(S.at[3], 1), H.at[1], to_y, H.at[1]),
    ]
    sums.fold(2)
    S[2] = own(2).astype(LOW)
    pieces = [s.go(half(S.at[2], 1), half(Q.at[1], 1), to_y, half(Q.at[1], 1))]
    sums.relay(1)
    S[1] = own(1).astype(LOW)
    pieces.append(s.go(half(S.at[1], 0), half(Q.at[0], 0), to_x, half(Q.at[0], 0)))
    A[...] = own(0) + d_first[...]
    sums.fold(3)
    sums.relay(2)

    total = jnp.zeros((width, w.shape[1]), HIGH)
    for i in range(blocks):
        loads[i].wait()
        total = total + product_tn(x[i], mixed(i))
    D[...] = total.astype(LOW).reshape(D.shape)
    grads_in = [
        s.go(D.at[b ^ d], R.at[b], (b ^ d, z), R.at[b ^ d]) for d in range(1, 8)
    ]
    R[b] = D[b]
    sums.collect(1)
    sums.fold(0)

    halves[0].wait_recv()
    part = half(S.at[2], 0)
    part[...] = part[...] + H[0]
    pieces.append(s.go(part, half(Q.at[1], 0), to_y, half(Q.at[1], 0)))
    halves[1].wait_recv()
    part = half(S.at[1], 1)
    part[...] = part[...] + H[1]
    pieces.append(s.go(part, half(Q.at[0], 1), to_x, half(Q.at[0], 1)))

    sums.relay(3)
    sums.collect(2)

    N[...] = small[b]
    for i in range(7):
        small_in[i].wait_recv()
        N[...] += M[i]
    for row, ref in ((4, dq), (5, dv)):
        whole = jnp.zeros((1, 128), HIGH)
        for i in range(blocks):
            whole = whole + column_sum(ref[i].reshape(count, -1))
        N[row : row + 1, 0:128] = whole
    small_z = [s.go(N, T.at[d - 1], (b, z ^ d), T.at[d - 1]) for d in (1, 2, 3)]

    sums.relay(0)
    for copy in grads_in:
        copy.wait_recv()
    rows = R.shape[1] // 4

    def share(d):
        return R.at[:, pl.ds(pl.multiple_of((z ^ d) * rows, rows), rows)]

    in_z = [s.go(share(d), Z.at[d - 1], (b, z ^ d), Z.at[d - 1]) for d in (1, 2, 3)]
    sums.collect(3)
    for copy in small_z:
        copy.wait_recv()
    small_out[...] = ((N[...] + T[0]) + T[1]) + T[2]
    for copy in in_z:
        copy.wait_recv()
    in_out[...] = ((share(0)[...].astype(HIGH) + Z[0].astype(HIGH)) + Z[1].astype(HIGH)) + Z[
        2
    ].astype(HIGH)
    for copy in pieces:
        copy.wait_recv()
    tok_out[...] = A[...] + Q[0].astype(HIGH) + Q[1].astype(HIGH)
    sums.collect(0)
    sums.total()
    s.drain()


def finish(dq, dk, dv, w, d_first, small, x, g2):
    count, width = d_first.shape
    blocks, columns = dq.shape[0], w.shape[1]
    share = width // (4 * blocks)
    vmem = pl.BlockSpec(memory_space=pltpu.VMEM)
    shape = jax.ShapeDtypeStruct
    low = lambda *s: pltpu.VMEM(s, LOW)
    return pl.pallas_call(
        finish_kernel,
        out_shape=(
            shape((count, width), HIGH),
            shape((blocks, share, columns), HIGH),
            shape(small.shape[1:], HIGH),
            shape(g2.shape[2:], HIGH),
        ),
        in_specs=[vmem] * 6 + in_hbm(2),
        out_specs=(vmem,) * 4,
        scratch_shapes=[
            low(blocks, count, width),
            low(4, count, width),
            low(4, count, width),
            low(4, count, width),
            pltpu.VMEM((count, width), HIGH),
            low(2, count // 2, width),
            low(2, count, width),
            low(blocks, 4 * share, columns),
            low(blocks, 4 * share, columns),
            low(3, blocks, share, columns),
            pltpu.VMEM((7, *small.shape[1:]), HIGH),
            pltpu.VMEM(small.shape[1:], HIGH),
            pltpu.VMEM((3, *small.shape[1:]), HIGH),
        ]
        + Reducer.scratch(*g2.shape[2:])
        + pair_of_semaphores(32 + Reducer.COPIES)
        + [pltpu.SemaphoreType.DMA((blocks,))],
        compiler_params=pltpu.CompilerParams(
            collective_id=3, has_side_effects=True, vmem_limit_bytes=VMEM_LIMIT
        ),
        name="finish",
    )(dq, dk, dv, w, d_first, small, x, g2)


def swap(pieces):
    return lax.all_to_all(pieces, "blk", 0, 0)


def by_slot(block, slots):
    blocks, count, held = block.shape
    block = block.reshape(blocks, slots, count // slots, held)
    return jnp.pad(block, ((0, 0),) * 3 + ((0, 128 - held),))


def front_apart(X, W, bias, slots):
    n_blk, count = X.shape[0], X.shape[1] - 16
    held = W.shape[1] // 3
    mixed = jnp.einsum("brd,dc->brc", X[:, :count], W, preferred_element_type=HIGH)
    parts = [mixed[..., i * held : (i + 1) * held] for i in range(3)]
    parts = [jnp.pad(p, ((0, 0), (0, 0), (0, 128 - held))).reshape(-1, 128) for p in parts]
    own = lax.dynamic_slice(bias[:2], (0, lax.axis_index("blk") * held), (2, held))
    own = jnp.pad(own, ((0, 0), (0, 128 - held)))
    codes = X[:, count, :count].reshape(-1, 1).astype(jnp.int32)
    codes = jnp.broadcast_to(codes, (n_blk * count, 128))
    queries, keys, values = split_heads(jnp.concatenate(parts, axis=1), (own[0], own[1]), codes)
    shape = (n_blk, slots, count // slots, 128)
    qh = jnp.stack(queries).reshape(2, *shape)
    kh = jnp.stack(keys).reshape(2, *shape)
    v = values.reshape(shape)
    att, lse = attend(qh, kh, v)
    rows_att = swap(att[..., :held].reshape(n_blk, count, held))
    return qh, kh, v, att, lse, rows_att


def on_device(
    tokens,
    input_weight,
    output_weight,
    expand_weight,
    reduce_weight,
    gains,
    biases,
    hidden_bias,
    segment,
    present,
    cotangent,
):
    slots, rows, width = tokens.shape
    n_blk, n_dp = lax.axis_size("blk"), lax.axis_size("dp")
    shards = n_blk * n_dp
    fast = (n_blk, n_dp) == (8, 4)
    held = width // n_blk
    shard = input_weight.shape[0]
    hidden = expand_weight.shape[1]
    count = slots * rows
    flat = tokens.reshape(count, width)

    code = segment + 4 * (1 - present)
    code_rows = jnp.zeros((16, width), LOW).at[0, :count].set(code.reshape(count).astype(LOW))
    sent_tokens = jnp.concatenate([flat, code_rows], axis=0)
    columns = input_weight.reshape(shard, 3, n_blk, held).transpose(2, 0, 1, 3)
    columns = columns.reshape(n_blk, shard, 3 * held)
    small = jnp.concatenate([gains.reshape(-1), biases.reshape(-1), hidden_bias])
    both = jnp.concatenate([expand_weight, output_weight], axis=1)
    if fast:
        small = jnp.concatenate([small[None], jnp.zeros((15, small.shape[0]), LOW)], axis=0)
        small = jnp.broadcast_to(small, (n_blk, *small.shape))
        win = jnp.concatenate([columns, small], axis=1)
        X, raw, W1, W2, rows_att, W, qh, kh, v, att, lse = front(
            sent_tokens, win, both, reduce_weight, slots
        )
        small = raw[:, :, shard].transpose(1, 0, 2).reshape(shards, 3 * held)
        W1, W2 = W1.reshape(width, -1), W2.reshape(hidden, width)
    else:
        X = lax.all_gather(sent_tokens, "blk")
        W = lax.all_gather(swap(columns), "dp", axis=1).reshape(width, 3 * held)
        small = lax.all_gather(small, BOTH)
        W1 = lax.all_gather(both, BOTH, axis=0, tiled=True)
        W2 = lax.all_gather(reduce_weight, BOTH, axis=0, tiled=True)
    part = width // shards
    cuts = small[:, : 8 * part].reshape(shards, 8, part).transpose(1, 0, 2).reshape(8, width)
    cuts = cuts.astype(HIGH)
    gain, bias = cuts[:2], cuts[2:]
    hidden_full = small[:, 8 * part :].reshape(hidden).astype(HIGH)

    all_tokens = X[:, :count]
    if not fast:
        qh, kh, v, att, lse, rows_att = front_apart(X, W, bias, slots)
    middle_out = middle(
        flat,
        rows_att,
        cotangent.reshape(count, width),
        cuts,
        hidden_full[None],
        W1,
        W2,
    )
    output, d_first, d_att, sums, d_hidden, grad_both, grad_reduce = middle_out
    output = output.reshape(slots, rows, width)
    if fast:
        dq, dk, dv, sum_both = back(
            d_att, qh, kh, v, att, lse, grad_both.reshape(n_blk, n_dp, shard, -1)
        )
        grad_reduce = grad_reduce.reshape(n_blk, n_dp, -1, width)
    else:
        sum_both = lax.psum_scatter(grad_both, BOTH, scatter_dimension=0, tiled=True).astype(HIGH)
        sum_reduce = lax.psum_scatter(grad_reduce, BOTH, scatter_dimension=0, tiled=True)
        sum_reduce = sum_reduce.astype(HIGH)
        dq, dk, dv = attend_back(qh, att, by_slot(swap(d_att), slots), lse, kh, v)
    small_rows = sums[:6].reshape(6, shards, part).transpose(1, 0, 2).reshape(shards, 6 * part)
    small_rows = jnp.concatenate([small_rows, d_hidden.reshape(shards, -1)], axis=1)
    if fast:
        lanes = small_rows.shape[1]
        small_rows = small_rows.reshape(n_blk, n_dp, lanes)
        small_rows = jnp.pad(small_rows, ((0, 0), (0, 4), (0, 3 * held - lanes)))
        grad_tokens, d_input, small_sum, sum_reduce = finish(
            dq, dk, dv, W, d_first, small_rows, X, grad_reduce
        )
        grad_input = d_input.reshape(n_blk, shard, 3, held).transpose(1, 2, 0, 3)
        grad_input = grad_input.reshape(shard, 3 * width)
        me_dp = lax.axis_index("dp")
        own_cols = lax.dynamic_slice(small_sum, (4, me_dp * part), (2, part))
        small_sum = lax.dynamic_slice(small_sum, (me_dp, 0), (1, lanes))[0]
    else:
        d_mixed = jnp.concatenate([dq[..., :held], dk[..., :held], dv[..., :held]], axis=-1)
        d_mixed = d_mixed.reshape(n_blk * count, 3 * held)
        d_input = product_tn(all_tokens.reshape(n_blk * count, width), d_mixed).astype(LOW)
        d_tokens = product_nt(d_mixed, W).astype(LOW)
        d_tokens = lax.psum_scatter(d_tokens, "blk", scatter_dimension=0, tiled=True)
        grad_tokens = d_first + d_tokens.astype(HIGH)
        d_input = swap(d_input.reshape(n_blk, n_dp * shard, 3 * held))
        d_input = d_input.reshape(n_blk, n_dp, shard, 3, held).transpose(1, 2, 3, 0, 4)
        d_input = d_input.reshape(n_dp, shard, 3 * width).astype(HIGH)
        grad_input = lax.psum_scatter(d_input, "dp", scatter_dimension=0, tiled=False)
        col = lambda a: jnp.sum(a.astype(HIGH), axis=0)
        own_cols = jnp.stack([col(d_mixed[:, :held]), col(d_mixed[:, 2 * held :])])
        own_cols = lax.psum_scatter(own_cols, "dp", scatter_dimension=1, tiled=True)
        small_sum = lax.psum_scatter(small_rows, BOTH, scatter_dimension=0, tiled=False)
    vectors = small_sum[: 6 * part].reshape(6, part)
    return (
        output,
        grad_tokens.reshape(slots, rows, width),
        grad_input,
        sum_both[:, hidden:],
        sum_both[:, :hidden],
        sum_reduce,
        vectors[:2],
        jnp.concatenate([own_cols, vectors[2:]], axis=0),
        small_sum[6 * part :],
    )


def solution(mesh):
    rows, sharded = P("dp", "blk", None), P(BOTH, None)
    in_specs = (rows, sharded, sharded, sharded, sharded, P(None, BOTH), P(None, BOTH), P(BOTH))
    in_specs += (P("dp", "blk"), P("dp", "blk"), rows)
    out_specs = (rows, rows, sharded, sharded, sharded, sharded)
    out_specs += (P(None, BOTH), P(None, BOTH), P(BOTH))
    return jax.shard_map(
        on_device, mesh=mesh, in_specs=in_specs, out_specs=out_specs, check_vma=False
    )
```

```python
import functools

import jax
import jax.numpy as jnp
from jax import lax
from jax.experimental import pallas as pl
from jax.experimental.pallas import tpu as pltpu
from jax.sharding import PartitionSpec as P

HEADS = 16
EPSILON = 1e-12
FAR = 2.0**60
BOTH = ("blk", "dp")
MESH = pl.DeviceIdType.MESH
LOW = jnp.bfloat16
HIGH = jnp.float32
VMEM_LIMIT = 60 * 2**20


def product(left, right):
    return jnp.dot(left, right, preferred_element_type=HIGH)


def product_nt(left, right):
    return lax.dot_general(left, right, (((1,), (1,)), ((), ())), preferred_element_type=HIGH)


def product_tn(left, right):
    return lax.dot_general(left, right, (((0,), (0,)), ((), ())), preferred_element_type=HIGH)


class Sender:
    def __init__(self, send, recv):
        self.send, self.recv, self.planned = send, recv, []

    def plan(self, src, dst, device, landing):
        at = len(self.planned)

        def copy(a, b):
            return pltpu.make_async_remote_copy(
                src_ref=a,
                dst_ref=b,
                send_sem=self.send.at[at],
                recv_sem=self.recv.at[at],
                device_id=device,
                device_id_type=MESH,
            )

        out = copy(src, dst)
        self.planned.append(out)
        landed = copy(landing, landing)
        landed.go = out.start
        return landed

    def go(self, *what):
        landed = self.plan(*what)
        landed.go()
        return landed

    def drain(self):
        for out in self.planned:
            out.wait_send()


def greet(peers):
    barrier = pltpu.get_barrier_semaphore()
    for peer in peers:
        pl.semaphore_signal(barrier, inc=1, device_id=peer, device_id_type=MESH)
    pl.semaphore_wait(barrier, len(peers))


def half(ref, which):
    rows = ref.shape[0]
    cut = rows // 32 * 16
    return ref.at[pl.ds(0, cut)] if which == 0 else ref.at[pl.ds(cut, rows - cut)]


def position():
    return lax.axis_index("blk"), lax.axis_index("dp")


def first_lanes(shape):
    return lax.broadcasted_iota(jnp.int32, shape, len(shape) - 1) < 64


def rows_of(block):
    return block.reshape(-1, block.shape[-1])


def attend_tile(queries, keys, values):
    rows = queries[0].shape[0]
    ones = jnp.ones_like(values)
    mine = first_lanes(values.shape)
    outs, logs = [], []
    for head in (0, 1):
        scores = product_nt(queries[head], keys[head])
        top = jnp.max(scores, axis=-1, keepdims=True)
        weights = jnp.exp(scores - top).astype(LOW)
        total = product(weights, jnp.where(mine == (head == 0), values, ones))
        mass = pltpu.roll(total, 64, 1)
        outs.append(total / mass)
        logs.append(top + jnp.log(mass))
    mine = first_lanes((rows, 128))
    flipped = jnp.where(mine, logs[0], logs[1]).T
    logs = jnp.concatenate([flipped[0:1], flipped[64:65], jnp.zeros((6, rows), HIGH)], axis=0)
    return jnp.where(mine, outs[0], outs[1]).astype(LOW), logs


def split_heads(mixed, bias, codes):
    rows = mixed.shape[0]
    q = (mixed[:, :128] + bias[0]).astype(LOW) * LOW(0.125)
    k = mixed[:, 128:256].astype(LOW)
    v = (mixed[:, 256:] + bias[1]).astype(LOW)
    lanes = lax.broadcasted_iota(jnp.int32, (rows, 128), 1) % 64
    protein = jnp.where(codes >= 4, codes - 4, codes)
    q_marks = jnp.where((lanes < 5) & (lanes != protein), -FAR, 0.0).astype(LOW)
    k_marks = jnp.where(lanes == jnp.minimum(codes, 4), 1.0, 0.0).astype(LOW)
    mine = first_lanes((rows, 128))
    return (
        (jnp.where(mine, q, q_marks), jnp.where(mine, q_marks, q)),
        (jnp.where(mine, k, k_marks), jnp.where(mine, k_marks, k)),
        v,
    )


def front_kernel(
    x,
    win,
    w1,
    w2,
    X_out,
    W1,
    W2,
    rows_att,
    wfull,
    small,
    qh,
    kh,
    v,
    att,
    lse,
    X,
    W,
    send,
    recv,
    asend,
    arecv,
    lsem,
    osem,
):
    b, z = position()
    bx, by, bd, bc = b ^ 2, b ^ 4, b ^ 6, b ^ 1
    count = X.shape[1] - 16
    slots, rows = qh.shape[2:4]
    greet([(b ^ d, z) for d in range(1, 8)] + [(b, z ^ d) for d in range(1, 4)])
    s = Sender(send, recv)
    locs = []

    def local(src, dst):
        copy = pltpu.make_async_copy(src, dst, lsem.at[len(locs)])
        copy.start()
        locs.append(copy)

    local(win.at[b], W.at[z, b])
    local(x, X.at[b])
    local(w1, W1.at[b, z])
    local(w2, W2.at[b, z])
    to_x, to_y, to_core = (bx, z), (by, z), (bc, z)

    def token_core(src, bb):
        return s.plan(src, X.at[bb], to_core, X.at[bb ^ 1])

    def to_z(d):
        return b, z ^ d

    def hops(F, src, zz):
        near = [
            s.plan(src, F.at[b, zz], to_x, F.at[bx, zz]),
            s.plan(src, F.at[b, zz], to_y, F.at[by, zz]),
        ]
        one, two = half(F.at[bx, zz], 0), half(F.at[by, zz], 1)
        far = [
            s.plan(one, one, to_y, half(F.at[bd, zz], 0)),
            s.plan(two, two, to_x, half(F.at[bd, zz], 1)),
        ]
        return near, far

    def planes(F, src, bb):
        pair = [s.plan(src, F.at[bb, z], to_z(d), F.at[bb, z ^ d]) for d in (1, 2)]
        on = F.at[bb, z ^ 2]
        return pair + [s.plan(on, on, to_z(1), F.at[bb, z ^ 3])]

    def to_sibling(F, src, bb, zz):
        return s.plan(src, F.at[bb, zz], to_core, F.at[bb ^ 1, zz])

    places = (b, bx, by, bd)
    z1 = planes(W1, w1, b)
    hop1 = [hops(W1, W1.at[b, z ^ d] if d else w1, z ^ d) for d in range(4)]
    hop2 = hops(W2, w2, z)
    z2 = [planes(W2, W2.at[bb, z] if i else w2, bb) for i, bb in enumerate(places)]
    core1, core2 = (
        {
            (i, d): to_sibling(F, F.at[bb, z ^ d] if i or d else own, bb, z ^ d)
            for i, bb in enumerate(places)
            for d in range(4)
        }
        for F, own in ((W1, w1), (W2, w2))
    )

    def start(*copies):
        for copy in copies:
            copy.go()

    def first(d):
        if d:
            z1[d - 1].wait_recv()
        if d == 2:
            z1[2].go()
        start(*hop1[d][0], core1[0, d])

    def second(d):
        near, far = hop1[d]
        for i in (0, 1):
            near[i].wait_recv()
            start(far[i], core1[1 + i, d])

    def third(d):
        for copy in hop1[d][1]:
            copy.wait_recv()
        core1[3, d].go()

    def spread(i):
        start(z2[i][0], z2[i][1], core2[i, 0])

    def second2():
        near, far = hop2
        for i in (0, 1):
            near[i].wait_recv()
            far[i].go()
            spread(1 + i)

    def third2():
        for copy in hop2[1]:
            copy.wait_recv()
        spread(3)

    def arrive2(i):
        z2[i][1].wait_recv()
        start(z2[i][2], core2[i, 2])
        z2[i][0].wait_recv()
        core2[i, 1].go()

    def last2(i):
        z2[i][2].wait_recv()
        core2[i, 3].go()

    columns = [
        s.go(win.at[b ^ d], W.at[z, b], (b ^ d, z), W.at[z, b ^ d]) for d in range(1, 8)
    ]
    start(*hop2[0])
    token_x = s.go(x, X.at[b], to_x, X.at[bx])
    token_y = s.go(x, X.at[b], to_y, X.at[by])
    token_c = token_core(x, b)
    token_c.go()
    start(z1[0], z1[1])
    spread(0)
    first(0)
    for copy in columns:
        copy.wait_recv()
    locs[0].wait()
    for i in range(8):
        small[z, i : i + 1] = W[z, i, 32:33]
    trimmed = lambda zz: W.at[zz, :, pl.ds(0, 32)]
    columns, vectors = (
        [s.plan(at(z), at(z), to_z(d), at(z ^ d)) for d in (1, 2)]
        + [s.plan(at(z ^ 2), at(z ^ 2), to_z(1), at(z ^ 3))]
        for at in (trimmed, lambda zz: small.at[zz])
    )
    start(*columns[:2], *vectors[:2])
    second2()
    token_x.wait_recv()
    piece = half(X.at[bx], 0)
    token_one = s.go(piece, piece, to_y, half(X.at[bd], 0))
    token_xc = token_core(X.at[bx], bx)
    token_xc.go()
    token_y.wait_recv()
    piece = half(X.at[by], 1)
    token_two = s.go(piece, piece, to_x, half(X.at[bd], 1))
    token_yc = token_core(X.at[by], by)
    token_yc.go()
    token_dc = token_core(X.at[bd], bd)
    first(2)
    first(1)
    columns[1].wait_recv()
    columns[2].go()
    vectors[1].wait_recv()
    vectors[2].go()
    third2()
    for copy in (columns[0], columns[2], vectors[0], vectors[2]):
        copy.wait_recv()
    for i in range(8):
        for j in range(4):
            at = (i * 4 + j) * 32
            wfull[at : at + 32] = W[j, i, 0:32]
    chosen = lax.broadcasted_iota(jnp.int32, (16, 128), 0) == b
    bias = [[], []]
    for j in range(4):
        row = jnp.where(chosen, small[j, :, 0:128].astype(HIGH), 0.0)
        row = jnp.sum(row, axis=0, keepdims=True)
        bias[0].append(row[:, 64:96])
        bias[1].append(row[:, 96:128])
    bias = [jnp.concatenate(parts, axis=1) for parts in bias]

    def mix(i):
        pltpu.make_async_copy(X.at[i], X_out.at[i], osem.at[i]).start()
        mixed = product(X[i, 0:count], wfull[...])
        codes = jnp.broadcast_to(X[i, count : count + 1, 0:count].astype(HIGH), (128, count)).T
        queries, keys, values = split_heads(mixed, bias, codes.astype(jnp.int32))
        for head in (0, 1):
            qh[head, i] = queries[head].reshape(slots, rows, 128)
            kh[head, i] = keys[head].reshape(slots, rows, 128)
        v[i] = values.reshape(slots, rows, 128)

    locs[1].wait()
    mix(b)
    token_c.wait_recv()
    mix(bc)
    mix(bx)
    token_xc.wait_recv()
    mix(bx ^ 1)
    first(3)
    mix(by)
    token_yc.wait_recv()
    mix(by ^ 1)
    token_one.wait_recv()
    token_two.wait_recv()
    token_dc.go()
    arrive2(0)
    mix(bd)
    token_dc.wait_recv()
    mix(bd ^ 1)
    second(0)

    def piece_of(slot):
        return pl.ds(pl.multiple_of(slot * rows, rows), rows)

    def send_att(slot, d):
        return pltpu.make_async_remote_copy(
            src_ref=att.at[b ^ d, slot],
            dst_ref=rows_att.at[b, piece_of(slot)],
            send_sem=asend.at[slot * 8 + d],
            recv_sem=arecv.at[slot * 8 + d],
            device_id=(b ^ d, z),
            device_id_type=MESH,
        )

    def keep_att(slot):
        return pltpu.make_async_copy(
            att.at[b, slot], rows_att.at[b, piece_of(slot)], osem.at[8 + slot]
        )

    events = {
        0: (second, 1),
        1: (arrive2, 1),
        2: (arrive2, 2),
        3: (second, 2),
        4: (third, 0),
        5: (second, 3),
        6: (arrive2, 3),
        8: (third, 1),
        9: (last2, 0),
        10: (third, 2),
        12: (last2, 1),
        13: (last2, 2),
        14: (last2, 3),
        15: (third, 3),
    }

    @pl.loop(0, 8 * slots)
    def _(step):
        slot, d = step // 8, (step + 1) % 8
        i = b ^ d
        keys = [rows_of(kh[head, :, slot]) for head in (0, 1)]
        out, logs = attend_tile([qh[head, i, slot] for head in (0, 1)], keys, rows_of(v[:, slot]))
        att[i, slot] = out
        lse[slot, :, pl.ds(pl.multiple_of(i * rows, rows), rows)] = logs

        @pl.when(d != 0)
        def _():
            send_att(slot, d).start()

        @pl.when(d == 0)
        def _():
            keep_att(slot).start()

        for at, (event, *what) in events.items():
            pl.when(step == at)(functools.partial(event, *what))

    for copy in [*core1.values(), *core2.values()]:
        copy.wait_recv()
    for slot in range(slots):
        keep_att(slot).wait()
        for d in range(1, 8):
            copy = send_att(slot, d)
            copy.wait_send()
            pltpu.make_async_remote_copy(
                src_ref=rows_att.at[b ^ d, piece_of(slot)],
                dst_ref=rows_att.at[b ^ d, piece_of(slot)],
                send_sem=asend.at[slot * 8 + d],
                recv_sem=arecv.at[slot * 8 + d],
                device_id=(b ^ d, z),
                device_id_type=MESH,
            ).wait_recv()
    s.drain()
    for copy in locs[2:]:
        copy.wait()
    for i in range(8):
        pltpu.make_async_copy(X.at[i], X_out.at[i], osem.at[i]).wait()


def in_hbm(count):
    return [pl.BlockSpec(memory_space=pl.ANY)] * count


def pair_of_semaphores(count):
    return [pltpu.SemaphoreType.DMA((count,)), pltpu.SemaphoreType.DMA((count,))]


def front(x, win, w1, w2, slots):
    count, width = x.shape[0] - 16, x.shape[1]
    rows = count // slots
    shape = lambda *s: jax.ShapeDtypeStruct(s, LOW)
    vmem = pl.BlockSpec(memory_space=pltpu.VMEM)
    return pl.pallas_call(
        front_kernel,
        out_shape=(
            shape(8, *x.shape),
            shape(8, 4, *w1.shape),
            shape(8, 4, *w2.shape),
            shape(8, count, 128),
            shape(width, win.shape[2]),
            shape(4, 16, win.shape[2]),
            shape(2, 8, slots, rows, 128),
            shape(2, 8, slots, rows, 128),
            shape(8, slots, rows, 128),
            shape(8, slots, rows, 128),
            jax.ShapeDtypeStruct((slots, 8, 8 * rows), HIGH),
        ),
        in_specs=in_hbm(4),
        out_specs=tuple(in_hbm(4)) + (vmem,) * 7,
        scratch_shapes=[pltpu.VMEM((8, *x.shape), LOW), pltpu.VMEM((4, *win.shape), LOW)]
        + pair_of_semaphores(116)
        + pair_of_semaphores(8 * slots)
        + [pltpu.SemaphoreType.DMA((4,)), pltpu.SemaphoreType.DMA((8 + slots,))],
        compiler_params=pltpu.CompilerParams(
            collective_id=1, has_side_effects=True, vmem_limit_bytes=VMEM_LIMIT
        ),
        name="front",
    )(x, win, w1, w2)


def add_rows(out, one, two):
    @pl.loop(0, one.shape[0] // 16)
    def _(i):
        rows = pl.ds(pl.multiple_of(i * 16, 16), 16)
        out[rows, :] = one[rows, :] + two[rows, :]


def sum_rows(out, *terms):
    @pl.loop(0, out.shape[0] // 16)
    def _(i):
        rows = pl.ds(pl.multiple_of(i * 16, 16), 16)
        total = terms[0][rows, :].astype(HIGH)
        for term in terms[1:]:
            total = total + term[rows, :].astype(HIGH)
        out[rows, :] = total


class Reducer:
    ORDER = (3, 2, 1, 0)
    COPIES = 16 + 4 * 6 + 3

    def __init__(self, s, share, out, C, S, H, Q, Z, lsem):
        b, z = position()
        to_x, to_y, to_core = (b ^ 2, z), (b ^ 4, z), (b ^ 1, z)
        self.out, self.C, self.S, self.H, self.Q, self.Z = out, C, S, H, Q, Z
        self.mine, self.other, self.halves, self.ahead, self.rest, self.last = ({} for _ in range(6))
        for d in self.ORDER:
            for e in (3, 1, 2, 0):
                self.mine[d, e] = pltpu.make_async_copy(
                    share(b ^ (2 * e), z ^ d), S.at[e, d], lsem.at[d * 4 + e]
                )
                self.other[d, e] = s.plan(
                    share(b ^ 1 ^ (2 * e), z ^ d), C.at[e, d], to_core, C.at[e, d]
                )

            def send(e, part, to, where):
                return s.plan(half(S.at[e, d], part), where, to, where)

            self.halves[d] = [send(3, 0, to_x, H.at[d, 0]), send(3, 1, to_y, H.at[d, 1])]
            self.ahead[d] = [
                send(2, 1, to_y, half(Q.at[d, 1], 1)),
                send(1, 0, to_x, half(Q.at[d, 0], 0)),
            ]
            self.rest[d] = [
                send(2, 0, to_y, half(Q.at[d, 1], 0)),
                send(1, 1, to_x, half(Q.at[d, 0], 1)),
            ]
            if d:
                to = (b, z ^ (2 if d == 2 else 1))
                self.last[d] = s.plan(S.at[0, d], Z.at[d - 1], to, Z.at[d - 1])

    def start(self):
        for d in self.ORDER:
            for e in (3, 1, 2, 0):
                self.mine[d, e].start()
                self.other[d, e].go()

    def fold(self, d):
        for e in (3, 1, 2, 0):
            self.mine[d, e].wait()
            self.other[d, e].wait_recv()
            add_rows(self.S.at[e, d], self.S.at[e, d], self.C.at[e, d])
            for copy in {3: self.halves[d], 1: self.ahead[d][1:], 2: self.ahead[d][:1], 0: []}[e]:
                copy.go()

    def relay(self, d):
        for i, e in ((0, 2), (1, 1)):
            self.halves[d][i].wait_recv()
            part = half(self.S.at[e, d], i)
            add_rows(part, part, self.H.at[d, i])
            self.rest[d][i].go()

    def collect(self, d):
        for copy in self.ahead[d] + self.rest[d]:
            copy.wait_recv()
        total = self.S.at[0, d]
        for i in (0, 1):
            add_rows(total, total, self.Q.at[d, i])
        if d == 2:
            self.last[3].wait_recv()
            add_rows(total, total, self.Z.at[2])
        if d:
            self.last[d].go()

    def total(self):
        for d in (1, 2):
            self.last[d].wait_recv()
        sum_rows(self.out, self.S.at[0, 0], self.Z.at[0], self.Z.at[1])

    @staticmethod
    def scratch(rows, columns):
        lead = (((4, 4), 1), ((4, 4), 1), ((4, 2), 2), ((4, 2), 1), ((3,), 1))
        shapes = [pltpu.VMEM((*n, rows // cut, columns), LOW) for n, cut in lead]
        return shapes + [pltpu.SemaphoreType.DMA((16,))]


class ReducerAlongZ:
    COPIES = 16 + 4 * 3 + 6

    def __init__(self, s, share, out, C, S, H, Q, Z, lsem):
        b, z = position()
        to_x, to_y, to_core = (b ^ 2, z), (b ^ 4, z), (b ^ 1, z)
        self.out, self.C, self.S, self.H, self.Q, self.Z = out, C, S, H, Q, Z
        self.mine, self.other, self.along = {}, {}, {}
        for e in (3, 1, 2, 0):
            for d in (3, 2, 1, 0):
                self.mine[e, d] = pltpu.make_async_copy(
                    share(b ^ (2 * e), z ^ d), S.at[e, d], lsem.at[d * 4 + e]
                )
                self.other[e, d] = s.plan(
                    share(b ^ 1 ^ (2 * e), z ^ d), C.at[e, d], to_core, C.at[e, d]
                )
                if d:
                    to = (b, z ^ (2 if d == 2 else 1))
                    self.along[e, d] = s.plan(S.at[e, d], Z.at[e, d - 1], to, Z.at[e, d - 1])

        def send(e, part, to, where):
            return s.plan(half(S.at[e, 0], part), where, to, where)

        self.halves = [send(3, 0, to_x, H.at[0]), send(3, 1, to_y, H.at[1])]
        self.ahead = [
            send(2, 1, to_y, half(Q.at[1], 1)),
            send(1, 0, to_x, half(Q.at[0], 0)),
        ]
        self.rest = [
            send(2, 0, to_y, half(Q.at[1], 0)),
            send(1, 1, to_x, half(Q.at[0], 1)),
        ]

    def start(self):
        for at in self.mine:
            self.mine[at].start()
            self.other[at].go()

    def fold(self, e):
        for d in (3, 1, 2, 0):
            self.mine[e, d].wait()
            self.other[e, d].wait_recv()
            add_rows(self.S.at[e, d], self.S.at[e, d], self.C.at[e, d])
            if d in (1, 3):
                self.along[e, d].go()

    def relay(self, e):
        self.along[e, 3].wait_recv()
        add_rows(self.S.at[e, 2], self.S.at[e, 2], self.Z.at[e, 2])
        self.along[e, 2].go()

    def collect(self, e):
        total = self.S.at[e, 0]
        for d in (1, 2):
            self.along[e, d].wait_recv()
            add_rows(total, total, self.Z.at[e, d - 1])
        for copy in {3: self.halves, 1: self.ahead[1:], 2: self.ahead[:1], 0: []}[e]:
            copy.go()

    def cross(self):
        for i, e in ((0, 2), (1, 1)):
            self.halves[i].wait_recv()
            part = half(self.S.at[e, 0], i)
            add_rows(part, part, self.H.at[i])
            self.rest[i].go()

    def total(self):
        for copy in self.ahead + self.rest:
            copy.wait_recv()
        sum_rows(self.out, self.S.at[0, 0], self.Q.at[0], self.Q.at[1])

    @staticmethod
    def scratch(rows, columns):
        lead = (((4, 4), 1), ((4, 4), 1), ((2,), 2), ((2,), 1), ((4, 3), 1))
        shapes = [pltpu.VMEM((*n, rows // cut, columns), LOW) for n, cut in lead]
        return shapes + [pltpu.SemaphoreType.DMA((16,))]


def attend_kernel(qh_ref, kh_ref, v_ref, out_ref, lse_ref):
    keys = [rows_of(kh_ref[head, :, 0]) for head in (0, 1)]
    out_ref[0, 0], lse_ref[0] = attend_tile(
        [qh_ref[head, 0, 0] for head in (0, 1)], keys, rows_of(v_ref[:, 0])
    )


def attend(qh, kh, v):
    blocks, slots, rows, lanes = v.shape
    tile = pl.BlockSpec((1, 1, rows, lanes), lambda s, i: (i, s, 0, 0))
    tiles = pl.BlockSpec((2, 1, 1, rows, lanes), lambda s, i: (0, i, s, 0, 0))
    whole = pl.BlockSpec((blocks, 1, rows, lanes), lambda s, i: (0, s, 0, 0))
    wholes = pl.BlockSpec((2, blocks, 1, rows, lanes), lambda s, i: (0, 0, s, 0, 0))
    return pl.pallas_call(
        attend_kernel,
        grid=(slots, blocks),
        out_shape=(
            jax.ShapeDtypeStruct(v.shape, LOW),
            jax.ShapeDtypeStruct((slots, 8, blocks * rows), HIGH),
        ),
        in_specs=[tiles, wholes, whole],
        out_specs=(tile, pl.BlockSpec((1, 8, rows), lambda s, i: (s, 0, i))),
        compiler_params=pltpu.CompilerParams(vmem_limit_bytes=VMEM_LIMIT),
        name="attend",
    )(qh, kh, v)


def row_products(out, grad):
    pick = (lax.broadcasted_iota(jnp.int32, (8, 128), 0) == 0) == first_lanes((8, 128))
    return lax.dot_general(
        pick.astype(HIGH),
        out.astype(HIGH) * grad.astype(HIGH),
        (((1,), (1,)), ((), ())),
        precision=lax.Precision.HIGHEST,
        preferred_element_type=HIGH,
    )


def attend_back_tile(queries, keys, values, grads, logs, delta, acc):
    zeros = jnp.zeros_like(grads)
    mine = first_lanes(grads.shape)
    dk, dv = [], 0.0
    for head in (0, 1):
        grad = jnp.where(mine == (head == 0), grads, zeros)
        probs = jnp.exp(product_nt(keys[head], queries[head]) - logs[head : head + 1])
        pushed = product_nt(values, grad)
        d_scores = (probs * (pushed - delta[head : head + 1])).astype(LOW)
        dv = dv + product(probs.astype(LOW), grad)
        dk.append(product(d_scores, queries[head]))
        keys_t = keys[head].T[head * 64 : head * 64 + 64]
        acc[head * 64 : head * 64 + 64, :] += product(keys_t, d_scores)
    return jnp.where(first_lanes(dk[0].shape), dk[0], dk[1]).astype(LOW), dv.astype(LOW)


def attend_back_kernel(
    qh_ref, o_ref, g_ref, lse_ref, kh_ref, v_ref, dq_ref, dk_ref, dv_ref, acc, delta
):
    tile = pl.program_id(1)
    blocks, _, rows, _ = g_ref.shape
    grads = rows_of(g_ref[:, 0])

    @pl.when(tile == 0)
    def _():
        acc[...] = jnp.zeros_like(acc)
        delta[...] = row_products(rows_of(o_ref[:, 0]), grads)

    dk_ref[0, 0], dv_ref[0, 0] = attend_back_tile(
        [rows_of(qh_ref[head, :, 0]) for head in (0, 1)],
        [kh_ref[head, 0, 0] for head in (0, 1)],
        v_ref[0, 0],
        grads,
        lse_ref[0],
        delta[...],
        acc,
    )

    @pl.when(tile == blocks - 1)
    def _():
        dq_ref[:, 0] = (acc[...].T * 0.125).astype(LOW).reshape(blocks, rows, 128)


def attend_back(qh, o, g, lse, kh, v):
    blocks, slots, rows, lanes = v.shape
    tile = pl.BlockSpec((1, 1, rows, lanes), lambda s, i: (i, s, 0, 0))
    tiles = pl.BlockSpec((2, 1, 1, rows, lanes), lambda s, i: (0, i, s, 0, 0))
    whole = pl.BlockSpec((blocks, 1, rows, lanes), lambda s, i: (0, s, 0, 0))
    wholes = pl.BlockSpec((2, blocks, 1, rows, lanes), lambda s, i: (0, 0, s, 0, 0))
    logs = pl.BlockSpec((1, 8, blocks * rows), lambda s, i: (s, 0, 0))
    shape = jax.ShapeDtypeStruct(v.shape, LOW)
    return pl.pallas_call(
        attend_back_kernel,
        grid=(slots, blocks),
        out_shape=(shape,) * 3,
        in_specs=[wholes, whole, whole, logs, tiles, tile],
        out_specs=(whole, tile, tile),
        scratch_shapes=[pltpu.VMEM((lanes, blocks * rows), HIGH), pltpu.VMEM((8, blocks * rows), HIGH)],
        compiler_params=pltpu.CompilerParams(vmem_limit_bytes=VMEM_LIMIT),
        name="attend_back",
    )(qh, o, g, lse, kh, v)


def back_kernel(
    d_att, qh, kh, v, att, lse, g1, dq, dk, dv, o1, grads, acc, delta, C, S, H, Q, Z, lsem, send, recv
):
    b, z = position()
    blocks, slots, rows, _ = v.shape
    count = slots * rows
    greet([(b ^ d, z) for d in range(1, 8)] + [(b, z ^ d) for d in (1, 2, 3)])
    s = Sender(send, recv)
    arriving = [
        s.go(d_att.at[b ^ d], grads.at[b], (b ^ d, z), grads.at[b ^ d]) for d in range(1, 8)
    ]
    sums = Reducer(s, lambda bb, zz: g1.at[bb, zz], o1, C, S, H, Q, Z, lsem)
    sums.start()
    grads[b] = d_att[b]
    sums.fold(3)
    sums.fold(2)
    for copy in arriving:
        copy.wait_recv()

    def grad_rows(slot):
        part = pl.ds(pl.multiple_of(slot * rows, rows), rows)
        return rows_of(grads[:, part])

    events = {
        1: (sums.relay, 3),
        3: (sums.fold, 1),
        4: (sums.relay, 2),
        5: (sums.collect, 3),
        6: (sums.fold, 0),
        8: (sums.relay, 1),
        9: (sums.collect, 2),
        11: (sums.relay, 0),
        13: (sums.collect, 1),
    }

    @pl.loop(0, blocks * slots)
    def _(step):
        slot, tile = step // blocks, step % blocks
        slot_grads = grad_rows(slot)

        @pl.when(tile == 0)
        def _():
            acc[...] = jnp.zeros_like(acc)
            delta[...] = row_products(rows_of(att[:, slot]), slot_grads)

        dk[tile, slot], dv[tile, slot] = attend_back_tile(
            [rows_of(qh[head, :, slot]) for head in (0, 1)],
            [kh[head, tile, slot] for head in (0, 1)],
            v[tile, slot],
            slot_grads,
            lse[slot],
            delta[...],
            acc,
        )

        @pl.when(tile == blocks - 1)
        def _():
            dq[:, slot] = (acc[...].T * 0.125).astype(LOW).reshape(blocks, rows, 128)

        for at, (event, what) in events.items():
            pl.when(step == at)(functools.partial(event, what))

    sums.collect(0)
    sums.total()
    s.drain()


def back(d_att, qh, kh, v, att, lse, g1):
    blocks, slots, rows, lanes = v.shape
    shape = jax.ShapeDtypeStruct
    vmem = pl.BlockSpec(memory_space=pltpu.VMEM)
    return pl.pallas_call(
        back_kernel,
        out_shape=(shape(v.shape, LOW),) * 3 + (shape(g1.shape[2:], HIGH),),
        in_specs=[vmem] * 6 + in_hbm(1),
        out_specs=(vmem,) * 4,
        scratch_shapes=[
            pltpu.VMEM(d_att.shape, LOW),
            pltpu.VMEM((lanes, blocks * rows), HIGH),
            pltpu.VMEM((8, blocks * rows), HIGH),
        ]
        + Reducer.scratch(*g1.shape[2:])
        + pair_of_semaphores(7 + Reducer.COPIES),
        compiler_params=pltpu.CompilerParams(
            collective_id=2, has_side_effects=True, vmem_limit_bytes=VMEM_LIMIT
        ),
        name="back",
    )(d_att, qh, kh, v, att, lse, g1)


def normalize(values):
    mean = jnp.mean(values, axis=-1, keepdims=True)
    centred = values - mean
    spread = jnp.mean(centred * centred, axis=-1, keepdims=True)
    inverse = lax.rsqrt(spread + EPSILON)
    return centred * inverse, inverse


def normalize_back(grad, normal, inverse):
    return inverse * (
        grad
        - jnp.mean(grad, axis=-1, keepdims=True)
        - normal * jnp.mean(grad * normal, axis=-1, keepdims=True)
    )


def gelu_parts(u):
    bell = jnp.exp(-0.5 * u * u)
    t = 1.0 / (1.0 + (0.3275911 * 0.5**0.5) * jnp.abs(u))
    poly = 1.061405429 * t - 1.453152027
    poly = poly * t + 1.421413741
    poly = poly * t - 0.284496736
    poly = poly * t + 0.254829592
    tail = 0.5 * poly * t * bell
    below = jnp.where(u < 0.0, tail, 1.0 - tail)
    return u * below, below + u * bell * 0.3989422804014327


def column_sum(block):
    return jnp.sum(block.astype(HIGH), axis=0, keepdims=True)


def middle_kernel(
    chunk,
    tok_ref,
    att_ref,
    cot_ref,
    par_ref,
    hid_ref,
    w1_hbm,
    w2_hbm,
    out_ref,
    first_ref,
    d_att_ref,
    sums_ref,
    d_hid_ref,
    g1_hbm,
    g2_hbm,
    w1,
    w2,
    att,
    normed_low,
    n1,
    n2,
    act,
    slope,
    acc,
    low,
    wsem,
    gsem,
):
    hidden, width = w2.shape
    steps = hidden // chunk
    pieces, _, held = att_ref.shape

    def columns(c):
        return pl.ds(pl.multiple_of(c * chunk, chunk), chunk)

    def load1(c):
        return pltpu.make_async_copy(w1_hbm.at[:, columns(c)], w1.at[:, columns(c)], wsem.at[0, c])

    def load2(c):
        return pltpu.make_async_copy(w2_hbm.at[columns(c)], w2.at[columns(c)], wsem.at[1, c])

    last = pl.ds(hidden, width)
    load_out = pltpu.make_async_copy(w1_hbm.at[:, last], w1.at[:, last], wsem.at[0, steps])
    load_out.start()
    for c in range(steps):
        load1(c).start()
        load2(c).start()
    gain1, gain2 = par_ref[0:1], par_ref[1:2]
    bias = lambda i: par_ref[2 + i : 3 + i]
    for i in range(pieces):
        att[:, i * held : (i + 1) * held] = att_ref[i]
    load_out.wait()
    first_sum = tok_ref[...].astype(HIGH) + product(att[...], w1[:, hidden:]) + bias(2)
    normal, inverse1 = normalize(first_sum)
    n1[...] = normal
    normed = normal * gain1 + bias(3)
    normed_low[...] = normed.astype(LOW)
    acc[...] = normed + bias(4)

    @pl.loop(0, steps)
    def _(c):
        load1(c).wait()
        pre = product(normed_low[...], w1[:, columns(c)]) + hid_ref[:, columns(c)]
        value, rate = gelu_parts(pre)
        act[:, columns(c)] = value.astype(LOW)
        slope[:, columns(c)] = rate.astype(LOW)
        load2(c).wait()
        acc[...] += product(value.astype(LOW), w2[columns(c), :])

    normal, inverse2 = normalize(acc[...])
    n2[...] = normal
    out_ref[...] = (normal * gain2 + bias(5)).astype(LOW)
    cot = cot_ref[...].astype(HIGH)
    d_second = normalize_back(cot * gain2, normal, inverse2)
    low[...] = d_second.astype(LOW)
    acc[...] = d_second
    sums_ref[1:2] = column_sum(cot * normal)
    sums_ref[4:5] = column_sum(low[...])
    sums_ref[5:6] = column_sum(cot)

    def store1(c):
        return pltpu.make_async_copy(w1.at[:, columns(c)], g1_hbm.at[:, columns(c)], gsem.at[0, c])

    def store2(c):
        return pltpu.make_async_copy(w2.at[columns(c)], g2_hbm.at[columns(c)], gsem.at[1, c])

    @pl.loop(0, steps)
    def _(c):
        d_act = product_nt(low[...], w2[columns(c), :])
        d_pre = (d_act * slope[:, columns(c)].astype(HIGH)).astype(LOW)
        d_hid_ref[:, columns(c)] = column_sum(d_pre)
        acc[...] += product_nt(d_pre, w1[:, columns(c)])
        w2[columns(c), :] = product_tn(act[:, columns(c)], low[...]).astype(LOW)
        store2(c).start()
        w1[:, columns(c)] = product_tn(normed_low[...], d_pre).astype(LOW)
        store1(c).start()

    d_normed = acc[...]
    normal = n1[...]
    d_first = normalize_back(d_normed * gain1, normal, inverse1)
    first_ref[...] = d_first
    low[...] = d_first.astype(LOW)
    sums_ref[0:1] = column_sum(d_normed * normal)
    sums_ref[2:3] = column_sum(low[...])
    sums_ref[3:4] = column_sum(d_normed)
    d_att = product_nt(low[...], w1[:, hidden:]).astype(LOW)
    for i in range(pieces):
        d_att_ref[i] = d_att[:, i * held : (i + 1) * held]
    w1[:, hidden:] = product_tn(att[...], low[...]).astype(LOW)
    store_out = pltpu.make_async_copy(w1.at[:, last], g1_hbm.at[:, last], gsem.at[0, steps])
    store_out.start()
    for c in range(steps):
        store1(c).wait()
        store2(c).wait()
    store_out.wait()


def middle(tokens, att, cot, par, hid, w1, w2):
    count, width = tokens.shape
    hidden = w2.shape[0]
    pieces = att.shape[0]
    chunk = 512
    shape = jax.ShapeDtypeStruct
    vmem = pl.BlockSpec(memory_space=pltpu.VMEM)
    return pl.pallas_call(
        functools.partial(middle_kernel, chunk),
        out_shape=(
            shape((count, width), LOW),
            shape((count, width), HIGH),
            shape(att.shape, LOW),
            shape((8, width), HIGH),
            shape((1, hidden), HIGH),
            shape(w1.shape, LOW),
            shape(w2.shape, LOW),
        ),
        in_specs=[vmem] * 5 + in_hbm(2),
        out_specs=(vmem,) * 5 + tuple(in_hbm(2)),
        scratch_shapes=[
            pltpu.VMEM(w1.shape, LOW),
            pltpu.VMEM(w2.shape, LOW),
            pltpu.VMEM((count, width), LOW),
            pltpu.VMEM((count, width), LOW),
            pltpu.VMEM((count, width), HIGH),
            pltpu.VMEM((count, width), HIGH),
            pltpu.VMEM((count, hidden), LOW),
            pltpu.VMEM((count, hidden), LOW),
            pltpu.VMEM((count, width), HIGH),
            pltpu.VMEM((count, width), LOW),
            pltpu.SemaphoreType.DMA((2, hidden // chunk + 1)),
            pltpu.SemaphoreType.DMA((2, hidden // chunk + 1)),
        ],
        compiler_params=pltpu.CompilerParams(vmem_limit_bytes=VMEM_LIMIT),
        name="middle",
    )(tokens, att, cot, par, hid, w1, w2)


def finish_kernel(
    dq,
    dk,
    dv,
    w,
    d_first,
    small,
    x_hbm,
    g2,
    tok_out,
    in_out,
    small_out,
    o2,
    x,
    sent,
    C,
    S,
    A,
    H,
    Q,
    D,
    R,
    Z,
    M,
    N,
    T,
    lsem,
    send,
    recv,
    *reducing,
):
    b, z = position()
    count, width = d_first.shape
    blocks = dq.shape[0]
    to_x, to_y, to_core = (b ^ 2, z), (b ^ 4, z), (b ^ 1, z)
    loads = []
    for i in range(blocks):
        load = pltpu.make_async_copy(x_hbm.at[i, pl.ds(0, count)], x.at[i], lsem.at[i])
        load.start()
        loads.append(load)
    greet([(b ^ d, z) for d in range(1, 8)] + [(b, z ^ d) for d in (1, 2, 3)])
    s = Sender(send, recv)
    cut = o2.shape[0] // 2
    lower, upper = pl.ds(0, cut), pl.ds(cut, cut)
    sums = Reducer(s, lambda bb, zz: g2.at[bb, zz, lower], o2.at[lower], *reducing[:6])
    late = ReducerAlongZ(s, lambda bb, zz: g2.at[bb, zz, upper], o2.at[upper], *reducing[6:])
    small_in = [
        s.go(small.at[b ^ d], M.at[d - 1], (b ^ d, z), M.at[d - 1]) for d in range(1, 8)
    ]

    def mixed(i):
        return jnp.concatenate([ref[i].reshape(count, -1) for ref in (dq, dk, dv)], axis=-1)

    def piece(i):
        return product_nt(mixed(i), w[...])

    other = {}
    for e in (3, 1, 2, 0):
        sent[e] = piece(b ^ 1 ^ (2 * e)).astype(LOW)
        other[e] = s.go(sent.at[e], C.at[e], to_core, C.at[e])
        if e == 3:
            late.start()
        if e == 1:
            sums.start()
    late.fold(3)
    sums.fold(3)
    late.fold(1)

    def own(e):
        mine = piece(b ^ (2 * e))
        other[e].wait_recv()
        return mine + C[e].astype(HIGH)

    S[3] = own(3).astype(LOW)
    halves = [
        s.go(half(S.at[3], 0), H.at[0], to_x, H.at[0]),
        s.go(half(S.at[3], 1), H.at[1], to_y, H.at[1]),
    ]
    late.relay(3)
    late.fold(2)
    sums.fold(2)
    S[2] = own(2).astype(LOW)
    pieces = [s.go(half(S.at[2], 1), half(Q.at[1], 1), to_y, half(Q.at[1], 1))]
    sums.relay(3)
    late.fold(0)
    late.relay(1)
    S[1] = own(1).astype(LOW)
    pieces.append(s.go(half(S.at[1], 0), half(Q.at[0], 0), to_x, half(Q.at[0], 0)))
    A[...] = own(0) + d_first[...]
    sums.fold(1)
    sums.relay(2)
    late.relay(2)
    late.collect(3)

    total = jnp.zeros((width, w.shape[1]), HIGH)
    for i in range(blocks):
        loads[i].wait()
        total = total + product_tn(x[i], mixed(i))
    D[...] = total.astype(LOW).reshape(D.shape)
    grads_in = [
        s.go(D.at[b ^ d], R.at[b], (b ^ d, z), R.at[b ^ d]) for d in range(1, 8)
    ]
    R[b] = D[b]
    sums.collect(3)
    sums.fold(0)
    late.relay(0)

    halves[0].wait_recv()
    part = half(S.at[2], 0)
    part[...] = part[...] + H[0]
    pieces.append(s.go(part, half(Q.at[1], 0), to_y, half(Q.at[1], 0)))
    halves[1].wait_recv()
    part = half(S.at[1], 1)
    part[...] = part[...] + H[1]
    pieces.append(s.go(part, half(Q.at[0], 1), to_x, half(Q.at[0], 1)))

    sums.relay(1)
    late.collect(1)
    sums.collect(2)
    late.collect(2)

    N[...] = small[b]
    for i in range(7):
        small_in[i].wait_recv()
        N[...] += M[i]
    for row, ref in ((4, dq), (5, dv)):
        whole = jnp.zeros((1, 128), HIGH)
        for i in range(blocks):
            whole = whole + column_sum(ref[i].reshape(count, -1))
        N[row : row + 1, 0:128] = whole
    small_z = [s.go(N, T.at[d - 1], (b, z ^ d), T.at[d - 1]) for d in (1, 2, 3)]

    sums.relay(0)
    late.cross()
    for copy in grads_in:
        copy.wait_recv()
    rows = R.shape[1] // 4

    def share(d):
        return R.at[:, pl.ds(pl.multiple_of((z ^ d) * rows, rows), rows)]

    in_z = [s.go(share(d), Z.at[d - 1], (b, z ^ d), Z.at[d - 1]) for d in (1, 2, 3)]
    sums.collect(1)
    for copy in small_z:
        copy.wait_recv()
    small_out[...] = ((N[...] + T[0]) + T[1]) + T[2]
    for copy in in_z:
        copy.wait_recv()
    in_out[...] = ((share(0)[...].astype(HIGH) + Z[0].astype(HIGH)) + Z[1].astype(HIGH)) + Z[
        2
    ].astype(HIGH)
    for copy in pieces:
        copy.wait_recv()
    tok_out[...] = A[...] + Q[0].astype(HIGH) + Q[1].astype(HIGH)
    late.collect(0)
    sums.collect(0)
    sums.total()
    late.total()
    s.drain()


def finish(dq, dk, dv, w, d_first, small, x, g2):
    count, width = d_first.shape
    blocks, columns = dq.shape[0], w.shape[1]
    share = width // (4 * blocks)
    vmem = pl.BlockSpec(memory_space=pltpu.VMEM)
    shape = jax.ShapeDtypeStruct
    low = lambda *s: pltpu.VMEM(s, LOW)
    return pl.pallas_call(
        finish_kernel,
        out_shape=(
            shape((count, width), HIGH),
            shape((blocks, share, columns), HIGH),
            shape(small.shape[1:], HIGH),
            shape(g2.shape[2:], HIGH),
        ),
        in_specs=[vmem] * 6 + in_hbm(2),
        out_specs=(vmem,) * 4,
        scratch_shapes=[
            low(blocks, count, width),
            low(4, count, width),
            low(4, count, width),
            low(4, count, width),
            pltpu.VMEM((count, width), HIGH),
            low(2, count // 2, width),
            low(2, count, width),
            low(blocks, 4 * share, columns),
            low(blocks, 4 * share, columns),
            low(3, blocks, share, columns),
            pltpu.VMEM((7, *small.shape[1:]), HIGH),
            pltpu.VMEM(small.shape[1:], HIGH),
            pltpu.VMEM((3, *small.shape[1:]), HIGH),
        ]
        + [pltpu.SemaphoreType.DMA((blocks,))]
        + pair_of_semaphores(32 + Reducer.COPIES + ReducerAlongZ.COPIES)
        + Reducer.scratch(g2.shape[2] // 2, width)
        + ReducerAlongZ.scratch(g2.shape[2] // 2, width),
        compiler_params=pltpu.CompilerParams(
            collective_id=3, has_side_effects=True, vmem_limit_bytes=VMEM_LIMIT
        ),
        name="finish",
    )(dq, dk, dv, w, d_first, small, x, g2)


def swap(pieces):
    return lax.all_to_all(pieces, "blk", 0, 0)


def by_slot(block, slots):
    blocks, count, held = block.shape
    block = block.reshape(blocks, slots, count // slots, held)
    return jnp.pad(block, ((0, 0),) * 3 + ((0, 128 - held),))


def front_apart(X, W, bias, slots):
    n_blk, count = X.shape[0], X.shape[1] - 16
    held = W.shape[1] // 3
    mixed = jnp.einsum("brd,dc->brc", X[:, :count], W, preferred_element_type=HIGH)
    parts = [mixed[..., i * held : (i + 1) * held] for i in range(3)]
    parts = [jnp.pad(p, ((0, 0), (0, 0), (0, 128 - held))).reshape(-1, 128) for p in parts]
    own = lax.dynamic_slice(bias[:2], (0, lax.axis_index("blk") * held), (2, held))
    own = jnp.pad(own, ((0, 0), (0, 128 - held)))
    codes = X[:, count, :count].reshape(-1, 1).astype(jnp.int32)
    codes = jnp.broadcast_to(codes, (n_blk * count, 128))
    queries, keys, values = split_heads(jnp.concatenate(parts, axis=1), (own[0], own[1]), codes)
    shape = (n_blk, slots, count // slots, 128)
    qh = jnp.stack(queries).reshape(2, *shape)
    kh = jnp.stack(keys).reshape(2, *shape)
    v = values.reshape(shape)
    att, lse = attend(qh, kh, v)
    rows_att = swap(att[..., :held].reshape(n_blk, count, held))
    return qh, kh, v, att, lse, rows_att


def on_device(
    tokens,
    input_weight,
    output_weight,
    expand_weight,
    reduce_weight,
    gains,
    biases,
    hidden_bias,
    segment,
    present,
    cotangent,
):
    slots, rows, width = tokens.shape
    n_blk, n_dp = lax.axis_size("blk"), lax.axis_size("dp")
    shards = n_blk * n_dp
    fast = (n_blk, n_dp) == (8, 4)
    held = width // n_blk
    shard = input_weight.shape[0]
    hidden = expand_weight.shape[1]
    count = slots * rows
    flat = tokens.reshape(count, width)

    code = segment + 4 * (1 - present)
    code_rows = jnp.zeros((16, width), LOW).at[0, :count].set(code.reshape(count).astype(LOW))
    sent_tokens = jnp.concatenate([flat, code_rows], axis=0)
    columns = input_weight.reshape(shard, 3, n_blk, held).transpose(2, 0, 1, 3)
    columns = columns.reshape(n_blk, shard, 3 * held)
    small = jnp.concatenate([gains.reshape(-1), biases.reshape(-1), hidden_bias])
    both = jnp.concatenate([expand_weight, output_weight], axis=1)
    if fast:
        small = jnp.concatenate([small[None], jnp.zeros((15, small.shape[0]), LOW)], axis=0)
        small = jnp.broadcast_to(small, (n_blk, *small.shape))
        win = jnp.concatenate([columns, small], axis=1)
        X, W1, W2, rows_att, W, small, qh, kh, v, att, lse = front(
            sent_tokens, win, both, reduce_weight, slots
        )
        small = small[:, :n_blk].transpose(1, 0, 2).reshape(shards, 3 * held)
        W1, W2 = W1.reshape(width, -1), W2.reshape(hidden, width)
    else:
        X = lax.all_gather(sent_tokens, "blk")
        W = lax.all_gather(swap(columns), "dp", axis=1).reshape(width, 3 * held)
        small = lax.all_gather(small, BOTH)
        W1 = lax.all_gather(both, BOTH, axis=0, tiled=True)
        W2 = lax.all_gather(reduce_weight, BOTH, axis=0, tiled=True)
    part = width // shards
    cuts = small[:, : 8 * part].reshape(shards, 8, part).transpose(1, 0, 2).reshape(8, width)
    cuts = cuts.astype(HIGH)
    gain, bias = cuts[:2], cuts[2:]
    hidden_full = small[:, 8 * part :].reshape(hidden).astype(HIGH)

    all_tokens = X[:, :count]
    if not fast:
        qh, kh, v, att, lse, rows_att = front_apart(X, W, bias, slots)
    middle_out = middle(
        flat,
        rows_att,
        cotangent.reshape(count, width),
        cuts,
        hidden_full[None],
        W1,
        W2,
    )
    output, d_first, d_att, sums, d_hidden, grad_both, grad_reduce = middle_out
    output = output.reshape(slots, rows, width)
    if fast:
        dq, dk, dv, sum_both = back(
            d_att, qh, kh, v, att, lse, grad_both.reshape(n_blk, n_dp, shard, -1)
        )
        grad_reduce = grad_reduce.reshape(n_blk, n_dp, -1, width)
    else:
        sum_both = lax.psum_scatter(grad_both, BOTH, scatter_dimension=0, tiled=True).astype(HIGH)
        sum_reduce = lax.psum_scatter(grad_reduce, BOTH, scatter_dimension=0, tiled=True)
        sum_reduce = sum_reduce.astype(HIGH)
        dq, dk, dv = attend_back(qh, att, by_slot(swap(d_att), slots), lse, kh, v)
    small_rows = sums[:6].reshape(6, shards, part).transpose(1, 0, 2).reshape(shards, 6 * part)
    small_rows = jnp.concatenate([small_rows, d_hidden.reshape(shards, -1)], axis=1)
    if fast:
        lanes = small_rows.shape[1]
        small_rows = small_rows.reshape(n_blk, n_dp, lanes)
        small_rows = jnp.pad(small_rows, ((0, 0), (0, 4), (0, 3 * held - lanes)))
        grad_tokens, d_input, small_sum, sum_reduce = finish(
            dq, dk, dv, W, d_first, small_rows, X, grad_reduce
        )
        grad_input = d_input.reshape(n_blk, shard, 3, held).transpose(1, 2, 0, 3)
        grad_input = grad_input.reshape(shard, 3 * width)
        me_dp = lax.axis_index("dp")
        own_cols = lax.dynamic_slice(small_sum, (4, me_dp * part), (2, part))
        small_sum = lax.dynamic_slice(small_sum, (me_dp, 0), (1, lanes))[0]
    else:
        d_mixed = jnp.concatenate([dq[..., :held], dk[..., :held], dv[..., :held]], axis=-1)
        d_mixed = d_mixed.reshape(n_blk * count, 3 * held)
        d_input = product_tn(all_tokens.reshape(n_blk * count, width), d_mixed).astype(LOW)
        d_tokens = product_nt(d_mixed, W).astype(LOW)
        d_tokens = lax.psum_scatter(d_tokens, "blk", scatter_dimension=0, tiled=True)
        grad_tokens = d_first + d_tokens.astype(HIGH)
        d_input = swap(d_input.reshape(n_blk, n_dp * shard, 3 * held))
        d_input = d_input.reshape(n_blk, n_dp, shard, 3, held).transpose(1, 2, 3, 0, 4)
        d_input = d_input.reshape(n_dp, shard, 3 * width).astype(HIGH)
        grad_input = lax.psum_scatter(d_input, "dp", scatter_dimension=0, tiled=False)
        col = lambda a: jnp.sum(a.astype(HIGH), axis=0)
        own_cols = jnp.stack([col(d_mixed[:, :held]), col(d_mixed[:, 2 * held :])])
        own_cols = lax.psum_scatter(own_cols, "dp", scatter_dimension=1, tiled=True)
        small_sum = lax.psum_scatter(small_rows, BOTH, scatter_dimension=0, tiled=False)
    vectors = small_sum[: 6 * part].reshape(6, part)
    return (
        output,
        grad_tokens.reshape(slots, rows, width),
        grad_input,
        sum_both[:, hidden:],
        sum_both[:, :hidden],
        sum_reduce,
        vectors[:2],
        jnp.concatenate([own_cols, vectors[2:]], axis=0),
        small_sum[6 * part :],
    )


def solution(mesh):
    rows, sharded = P("dp", "blk", None), P(BOTH, None)
    in_specs = (rows, sharded, sharded, sharded, sharded, P(None, BOTH), P(None, BOTH), P(BOTH))
    in_specs += (P("dp", "blk"), P("dp", "blk"), rows)
    out_specs = (rows, rows, sharded, sharded, sharded, sharded)
    out_specs += (P(None, BOTH), P(None, BOTH), P(BOTH))
    return jax.shard_map(
        on_device, mesh=mesh, in_specs=in_specs, out_specs=out_specs, check_vma=False
    )
```

```python
import functools

import jax
import jax.numpy as jnp
from jax import lax
from jax.experimental import pallas as pl
from jax.experimental.pallas import tpu as pltpu
from jax.sharding import PartitionSpec as P

HEADS = 16
EPSILON = 1e-12
FAR = 2.0**60
BOTH = ("blk", "dp")
MESH = pl.DeviceIdType.MESH
LOW = jnp.bfloat16
HIGH = jnp.float32
VMEM_LIMIT = 60 * 2**20


def product(left, right):
    return jnp.dot(left, right, preferred_element_type=HIGH)


def product_nt(left, right):
    return lax.dot_general(left, right, (((1,), (1,)), ((), ())), preferred_element_type=HIGH)


def product_tn(left, right):
    return lax.dot_general(left, right, (((0,), (0,)), ((), ())), preferred_element_type=HIGH)


def normalize(values):
    mean = jnp.mean(values, axis=-1, keepdims=True)
    centred = values - mean
    spread = jnp.mean(centred * centred, axis=-1, keepdims=True)
    inverse = lax.rsqrt(spread + EPSILON)
    return centred * inverse, inverse


def normalize_back(grad, normal, inverse):
    return inverse * (
        grad
        - jnp.mean(grad, axis=-1, keepdims=True)
        - normal * jnp.mean(grad * normal, axis=-1, keepdims=True)
    )


def gelu_parts(u):
    bell = jnp.exp(-0.5 * u * u)
    t = 1.0 / (1.0 + (0.3275911 * 0.5**0.5) * jnp.abs(u))
    poly = 1.061405429 * t - 1.453152027
    poly = poly * t + 1.421413741
    poly = poly * t - 0.284496736
    poly = poly * t + 0.254829592
    tail = 0.5 * poly * t * bell
    below = jnp.where(u < 0.0, tail, 1.0 - tail)
    return u * below, below + u * bell * 0.3989422804014327


class Sender:
    def __init__(self, send, recv):
        self.send, self.recv, self.planned = send, recv, []

    def plan(self, src, dst, device, landing):
        at = len(self.planned)

        def copy(a, b):
            return pltpu.make_async_remote_copy(
                src_ref=a,
                dst_ref=b,
                send_sem=self.send.at[at],
                recv_sem=self.recv.at[at],
                device_id=device,
                device_id_type=MESH,
            )

        out = copy(src, dst)
        self.planned.append(out)
        landed = copy(landing, landing)
        landed.go = out.start
        return landed

    def go(self, *what):
        landed = self.plan(*what)
        landed.go()
        return landed

    def drain(self):
        for out in self.planned:
            out.wait_send()


def greet(peers):
    barrier = pltpu.get_barrier_semaphore()
    for peer in peers:
        pl.semaphore_signal(barrier, inc=1, device_id=peer, device_id_type=MESH)
    pl.semaphore_wait(barrier, len(peers))


def half(ref, which):
    rows = ref.shape[0]
    cut = rows // 32 * 16
    return ref.at[pl.ds(0, cut)] if which == 0 else ref.at[pl.ds(cut, rows - cut)]


def position():
    return lax.axis_index("blk"), lax.axis_index("dp")


def first_lanes(shape):
    return lax.broadcasted_iota(jnp.int32, shape, len(shape) - 1) < 64


def rows_of(block):
    return block.reshape(-1, block.shape[-1])


def attend_tile(queries, keys, values):
    rows = queries[0].shape[0]
    ones = jnp.ones_like(values)
    mine = first_lanes(values.shape)
    outs, logs = [], []
    for head in (0, 1):
        scores = product_nt(queries[head], keys[head])
        top = jnp.max(scores, axis=-1, keepdims=True)
        weights = jnp.exp(scores - top).astype(LOW)
        total = product(weights, jnp.where(mine == (head == 0), values, ones))
        mass = pltpu.roll(total, 64, 1)
        outs.append(total / mass)
        logs.append(top + jnp.log(mass))
    mine = first_lanes((rows, 128))
    flipped = jnp.where(mine, logs[0], logs[1]).T
    logs = jnp.concatenate([flipped[0:1], flipped[64:65], jnp.zeros((6, rows), HIGH)], axis=0)
    return jnp.where(mine, outs[0], outs[1]).astype(LOW), logs


def split_heads(mixed, bias, codes):
    rows = mixed.shape[0]
    q = (mixed[:, :128] + bias[0]).astype(LOW) * LOW(0.125)
    k = mixed[:, 128:256].astype(LOW)
    v = (mixed[:, 256:] + bias[1]).astype(LOW)
    lanes = lax.broadcasted_iota(jnp.int32, (rows, 128), 1) % 64
    protein = jnp.where(codes >= 4, codes - 4, codes)
    q_marks = jnp.where((lanes < 5) & (lanes != protein), -FAR, 0.0).astype(LOW)
    k_marks = jnp.where(lanes == jnp.minimum(codes, 4), 1.0, 0.0).astype(LOW)
    mine = first_lanes((rows, 128))
    return (
        (jnp.where(mine, q, q_marks), jnp.where(mine, q_marks, q)),
        (jnp.where(mine, k, k_marks), jnp.where(mine, k_marks, k)),
        v,
    )


def spread_vectors(small, par, hid):
    for i in range(8):
        for j in range(4):
            row = small[j, i : i + 1].astype(HIGH)
            at = (i * 4 + j) * 32
            for k in range(8):
                par[k : k + 1, at : at + 32] = row[:, k * 32 : k * 32 + 32]
            hid[:, at * 4 : at * 4 + 128] = row[:, 256:384]


def front_kernel(
    x,
    segment,
    present,
    input_weight,
    gains,
    biases,
    hidden_bias,
    expand,
    out_w_in,
    w2,
    X_out,
    W1,
    W2,
    act_out,
    slope_out,
    wfull,
    small,
    qh,
    kh,
    v,
    att,
    lse,
    branch_in,
    n1,
    r1,
    normed_low,
    par,
    X,
    W,
    win,
    w1,
    rows_att,
    w1v,
    act,
    slope,
    hid,
    send,
    recv,
    asend,
    arecv,
    lsem,
    osem,
    wsem,
    csem,
):
    b, z = position()
    bx, by, bd, bc = b ^ 2, b ^ 4, b ^ 6, b ^ 1
    count = X.shape[1] - 16
    hidden, width = expand.shape[1], x.shape[1]
    slots, rows = qh.shape[2:4]
    locs = []

    def local(src, dst):
        copy = pltpu.make_async_copy(src, dst, lsem.at[len(locs)])
        copy.start()
        locs.append(copy)

    local(x, X.at[b, pl.ds(0, count)])
    local(expand, w1.at[:, pl.ds(0, hidden)])
    local(out_w_in, w1.at[:, pl.ds(hidden, width)])
    local(w2, W2.at[b, z])
    shard = input_weight.shape[0]
    n = gains.shape[1]
    win[...] = jnp.zeros_like(win)
    for i in range(8):
        for k in range(3):
            at = k * width + i * 128
            win[i, 0:shard, k * 128 : (k + 1) * 128] = input_weight[:, at : at + 128]
    rows_small = [gains[k : k + 1] for k in range(2)] + [biases[k : k + 1] for k in range(6)]
    line = jnp.concatenate(rows_small + [hidden_bias[...]], axis=1)
    for i in range(8):
        win[i, shard : shard + 16] = jnp.broadcast_to(line, (16, line.shape[1]))
    W[z, b] = win[b]
    codes = (segment[...] + 4 * (1 - present[...])).astype(HIGH).astype(LOW)
    codes = jnp.concatenate([codes[k : k + 1] for k in range(slots)], axis=1)
    X[b, pl.ds(count, 16), 0:count] = jnp.broadcast_to(codes, (16, count))
    X[b, pl.ds(count, 16), count:width] = jnp.zeros((16, width - count), LOW)
    greet([(b ^ d, z) for d in range(1, 8)] + [(b, z ^ d) for d in range(1, 4)])
    s = Sender(send, recv)
    to_x, to_y, to_core = (bx, z), (by, z), (bc, z)

    def token_core(src, bb):
        return s.plan(src, X.at[bb], to_core, X.at[bb ^ 1])

    def to_z(d):
        return b, z ^ d

    def hops(F, src, zz):
        near = [
            s.plan(src, F.at[b, zz], to_x, F.at[bx, zz]),
            s.plan(src, F.at[b, zz], to_y, F.at[by, zz]),
        ]
        one, two = half(F.at[bx, zz], 0), half(F.at[by, zz], 1)
        far = [
            s.plan(one, one, to_y, half(F.at[bd, zz], 0)),
            s.plan(two, two, to_x, half(F.at[bd, zz], 1)),
        ]
        return near, far

    def planes(F, src, bb):
        pair = [s.plan(src, F.at[bb, z], to_z(d), F.at[bb, z ^ d]) for d in (1, 2)]
        on = F.at[bb, z ^ 2]
        return pair + [s.plan(on, on, to_z(1), F.at[bb, z ^ 3])]

    def to_sibling(F, src, bb, zz):
        return s.plan(src, F.at[bb, zz], to_core, F.at[bb ^ 1, zz])

    places = (b, bx, by, bd)
    z1 = planes(W1, w1, b)
    hop1 = [hops(W1, W1.at[b, z ^ d] if d else w1, z ^ d) for d in range(4)]
    hop2 = hops(W2, w2, z)
    z2 = [planes(W2, W2.at[bb, z] if i else w2, bb) for i, bb in enumerate(places)]
    core1, core2 = (
        {
            (i, d): to_sibling(F, F.at[bb, z ^ d] if i or d else own, bb, z ^ d)
            for i, bb in enumerate(places)
            for d in range(4)
        }
        for F, own in ((W1, w1), (W2, w2))
    )

    def start(*copies):
        for copy in copies:
            copy.go()

    def first(d):
        if d in (1, 3):
            z1[d - 1].wait_recv()
        start(*hop1[d][0], core1[0, d])

    def second(d):
        near, far = hop1[d]
        for i in (0, 1):
            near[i].wait_recv()
            start(far[i], core1[1 + i, d])

    def third(d):
        for copy in hop1[d][1]:
            copy.wait_recv()
        core1[3, d].go()

    def spread(i):
        start(z2[i][0], z2[i][1], core2[i, 0])

    def second2():
        near, far = hop2
        for i in (0, 1):
            near[i].wait_recv()
            far[i].go()
            spread(1 + i)

    def third2():
        for copy in hop2[1]:
            copy.wait_recv()
        spread(3)

    def arrive2(i):
        z2[i][1].wait_recv()
        start(z2[i][2], core2[i, 2])
        z2[i][0].wait_recv()
        core2[i, 1].go()

    def last2(i):
        z2[i][2].wait_recv()
        core2[i, 3].go()

    columns = [
        s.go(win.at[b ^ d], W.at[z, b], (b ^ d, z), W.at[z, b ^ d]) for d in range(1, 8)
    ]
    locs[0].wait()
    token_x = s.go(X.at[b], X.at[b], to_x, X.at[bx])
    token_y = s.go(X.at[b], X.at[b], to_y, X.at[by])
    token_c = token_core(X.at[b], b)
    token_c.go()
    for copy in locs[1:3]:
        copy.wait()
    local(w1, W1.at[b, z])
    start(z1[0], z1[1])
    for copy in columns:
        copy.wait_recv()
    for i in range(8):
        small[z, i : i + 1] = W[z, i, 32:33]
    trimmed = lambda zz: W.at[zz, :, pl.ds(0, 32)]
    columns, vectors = (
        [s.plan(at(z), at(z), to_z(d), at(z ^ d)) for d in (1, 2)]
        + [s.plan(at(z ^ 2), at(z ^ 2), to_z(1), at(z ^ 3))]
        for at in (trimmed, lambda zz: small.at[zz])
    )
    start(*columns[:2], *vectors[:2])
    spread(0)
    token_x.wait_recv()
    piece = half(X.at[bx], 0)
    token_one = s.go(piece, piece, to_y, half(X.at[bd], 0))
    token_xc = token_core(X.at[bx], bx)
    token_xc.go()
    token_y.wait_recv()
    piece = half(X.at[by], 1)
    token_two = s.go(piece, piece, to_x, half(X.at[bd], 1))
    token_yc = token_core(X.at[by], by)
    token_yc.go()
    token_dc = token_core(X.at[bd], bd)
    start(*hop2[0])
    columns[1].wait_recv()
    columns[2].go()
    vectors[1].wait_recv()
    vectors[2].go()
    z1[1].wait_recv()
    z1[2].go()
    for copy in (columns[0], columns[2], vectors[0], vectors[2]):
        copy.wait_recv()
    for i in range(8):
        for j in range(4):
            at = (i * 4 + j) * 32
            wfull[at : at + 32] = W[j, i, 0:32]
    spread_vectors(small, par, hid)
    chosen = lax.broadcasted_iota(jnp.int32, (16, 128), 0) == b
    bias = [[], []]
    for j in range(4):
        row = jnp.where(chosen, small[j, :, 0:128].astype(HIGH), 0.0)
        row = jnp.sum(row, axis=0, keepdims=True)
        bias[0].append(row[:, 64:96])
        bias[1].append(row[:, 96:128])
    bias = [jnp.concatenate(parts, axis=1) for parts in bias]

    def mix(i):
        pltpu.make_async_copy(X.at[i], X_out.at[i], osem.at[i]).start()
        mixed = product(X[i, 0:count], wfull[...])
        codes = jnp.broadcast_to(X[i, count : count + 1, 0:count].astype(HIGH), (128, count)).T
        queries, keys, values = split_heads(mixed, bias, codes.astype(jnp.int32))
        for head in (0, 1):
            qh[head, i] = queries[head].reshape(slots, rows, 128)
            kh[head, i] = keys[head].reshape(slots, rows, 128)
        v[i] = values.reshape(slots, rows, 128)

    mix(b)
    token_c.wait_recv()
    mix(bc)
    mix(bx)
    token_xc.wait_recv()
    mix(bx ^ 1)
    mix(by)
    token_one.wait_recv()
    token_two.wait_recv()
    token_dc.go()
    first(0)
    first(2)
    first(1)
    second2()
    first(3)
    token_yc.wait_recv()
    mix(by ^ 1)
    mix(bd)
    token_dc.wait_recv()
    mix(bd ^ 1)
    arrive2(0)

    def piece_of(slot):
        return pl.ds(pl.multiple_of(slot * rows, rows), rows)

    def send_att(slot, d):
        return pltpu.make_async_remote_copy(
            src_ref=att.at[b ^ d, slot],
            dst_ref=rows_att.at[b, piece_of(slot)],
            send_sem=asend.at[slot * 8 + d],
            recv_sem=arecv.at[slot * 8 + d],
            device_id=(b ^ d, z),
            device_id_type=MESH,
        )

    def keep_att(slot):
        return pltpu.make_async_copy(
            att.at[b, slot], rows_att.at[b, piece_of(slot)], osem.at[8 + slot]
        )

    events = {
        0: (second, 0),
        1: (third2,),
        2: (second, 2),
        4: (second, 1),
        5: (arrive2, 1),
        6: (arrive2, 2),
        7: (third, 0),
        9: (second, 3),
        10: (arrive2, 3),
        12: (third, 2),
        14: (third, 1),
    }
    late_events = {1: (last2, 0), 3: (last2, 1), 5: (last2, 2), 7: (last2, 3)}

    @pl.loop(0, 8 * slots)
    def _(step):
        slot, d = step // 8, (step + 1) % 8
        i = b ^ d
        keys = [rows_of(kh[head, :, slot]) for head in (0, 1)]
        out, logs = attend_tile([qh[head, i, slot] for head in (0, 1)], keys, rows_of(v[:, slot]))
        att[i, slot] = out
        lse[slot, :, pl.ds(pl.multiple_of(i * rows, rows), rows)] = logs

        @pl.when(d != 0)
        def _():
            send_att(slot, d).start()

        @pl.when(d == 0)
        def _():
            keep_att(slot).start()

        for at, (event, *what) in events.items():
            pl.when(step == at)(functools.partial(event, *what))

    third(3)
    for copy in core1.values():
        copy.wait_recv()
    locs[4].wait()
    chunk = 512
    steps = hidden // chunk

    def load(c, size=chunk):
        cols = pl.ds(pl.multiple_of(c * chunk, chunk), size)
        return pltpu.make_async_copy(W1.at[:, :, :, cols], w1v.at[:, :, :, cols], wsem.at[c])

    load(steps, width).start()
    for c in range(steps):
        load(c).start()
    for slot in range(slots):
        keep_att(slot).wait()
        for d in range(1, 8):
            pltpu.make_async_remote_copy(
                src_ref=rows_att.at[b ^ d, piece_of(slot)],
                dst_ref=rows_att.at[b ^ d, piece_of(slot)],
                send_sem=asend.at[slot * 8 + d],
                recv_sem=arecv.at[slot * 8 + d],
                device_id=(b ^ d, z),
                device_id_type=MESH,
            ).wait_recv()
    branch_in[...] = jnp.concatenate([rows_att[i] for i in range(8)], axis=1)
    load(steps, width).wait()
    out_w = w1v[:, :, :, hidden:].reshape(width, width)
    branch = product(branch_in[...], out_w) + par[4:5]
    normal, inverse = normalize(X[b, 0:count].astype(HIGH) + branch)
    n1[...] = normal
    r1[...] = jnp.broadcast_to(inverse, r1.shape)
    normed_low[...] = (normal * par[0:1] + par[5:6]).astype(LOW)

    def store(c, ref, out, which):
        cols = pl.ds(pl.multiple_of(c * chunk, chunk), chunk)
        return pltpu.make_async_copy(ref.at[:, cols], out.at[:, cols], csem.at[which, c])

    @pl.loop(0, steps)
    def _(c):
        cols = pl.ds(pl.multiple_of(c * chunk, chunk), chunk)
        load(c).wait()
        pre = product(normed_low[...], w1v[:, :, :, cols].reshape(width, chunk))
        value, rate = gelu_parts(pre + hid[:, cols])
        act[:, cols] = value.astype(LOW)
        slope[:, cols] = rate.astype(LOW)
        store(c, act, act_out, 0).start()
        store(c, slope, slope_out, 1).start()
        for at, (event, *what) in late_events.items():
            pl.when(c == at)(functools.partial(event, *what))

    for copy in core2.values():
        copy.wait_recv()
    for slot in range(slots):
        for d in range(1, 8):
            send_att(slot, d).wait_send()
    for c in range(steps):
        store(c, act, act_out, 0).wait()
        store(c, slope, slope_out, 1).wait()
    s.drain()
    locs[3].wait()
    for i in range(8):
        pltpu.make_async_copy(X.at[i], X_out.at[i], osem.at[i]).wait()


def in_hbm(count):
    return [pl.BlockSpec(memory_space=pl.ANY)] * count


def pair_of_semaphores(count):
    return [pltpu.SemaphoreType.DMA((count,)), pltpu.SemaphoreType.DMA((count,))]


def front(x, segment, present, input_weight, gains, biases, hidden_bias, expand, out_w, w2):
    slots = segment.shape[0]
    count, width = x.shape
    rows, hidden = count // slots, expand.shape[1]
    shard = expand.shape[0]
    shape = lambda *s: jax.ShapeDtypeStruct(s, LOW)
    wide = lambda *s: jax.ShapeDtypeStruct(s, HIGH)
    vmem = pl.BlockSpec(memory_space=pltpu.VMEM)
    return pl.pallas_call(
        front_kernel,
        out_shape=(
            shape(8, count + 16, width),
            shape(8, 4, shard, hidden + width),
            shape(8, 4, *w2.shape),
            shape(count, hidden),
            shape(count, hidden),
            shape(width, 384),
            shape(4, 16, 384),
            shape(2, 8, slots, rows, 128),
            shape(2, 8, slots, rows, 128),
            shape(8, slots, rows, 128),
            shape(8, slots, rows, 128),
            wide(slots, 8, 8 * rows),
            shape(count, width),
            wide(count, width),
            wide(count, 128),
            shape(count, width),
            wide(8, width),
        ),
        in_specs=in_hbm(1) + [vmem] * 6 + in_hbm(3),
        out_specs=tuple(in_hbm(5)) + (vmem,) * 12,
        scratch_shapes=[
            pltpu.VMEM((8, count + 16, width), LOW),
            pltpu.VMEM((4, 8, shard + 16, 384), LOW),
            pltpu.VMEM((8, shard + 16, 384), LOW),
            pltpu.VMEM((shard, hidden + width), LOW),
            pltpu.VMEM((8, count, 128), LOW),
            pltpu.VMEM((8, 4, shard, hidden + width), LOW),
            pltpu.VMEM((count, hidden), LOW),
            pltpu.VMEM((count, hidden), LOW),
            pltpu.VMEM((1, hidden), HIGH),
        ]
        + pair_of_semaphores(116)
        + pair_of_semaphores(8 * slots)
        + [pltpu.SemaphoreType.DMA((5,)), pltpu.SemaphoreType.DMA((8 + slots,))]
        + [pltpu.SemaphoreType.DMA((hidden // 512 + 1,)), pltpu.SemaphoreType.DMA((2, hidden // 512))],
        compiler_params=pltpu.CompilerParams(
            collective_id=1, has_side_effects=True, vmem_limit_bytes=VMEM_LIMIT
        ),
        name="front",
    )(x, segment, present, input_weight, gains, biases, hidden_bias, expand, out_w, w2)


def add_rows(out, one, two):
    @pl.loop(0, one.shape[0] // 16)
    def _(i):
        rows = pl.ds(pl.multiple_of(i * 16, 16), 16)
        out[rows, :] = one[rows, :] + two[rows, :]


def sum_rows(out, *terms):
    @pl.loop(0, out.shape[0] // 16)
    def _(i):
        rows = pl.ds(pl.multiple_of(i * 16, 16), 16)
        total = terms[0][rows, :].astype(HIGH)
        for term in terms[1:]:
            total = total + term[rows, :].astype(HIGH)
        out[rows, :] = total


class Reducer:
    ORDER = (3, 2, 1, 0)
    COPIES = 16 + 4 * 6 + 3

    def __init__(self, s, share, out, C, S, H, Q, Z, lsem):
        b, z = position()
        to_x, to_y, to_core = (b ^ 2, z), (b ^ 4, z), (b ^ 1, z)
        self.out, self.C, self.S, self.H, self.Q, self.Z = out, C, S, H, Q, Z
        self.mine, self.other, self.halves, self.ahead, self.rest, self.last = ({} for _ in range(6))
        for d in self.ORDER:
            for e in (3, 1, 2, 0):
                self.mine[d, e] = pltpu.make_async_copy(
                    share(b ^ (2 * e), z ^ d), S.at[e, d], lsem.at[d * 4 + e]
                )
                self.other[d, e] = s.plan(
                    share(b ^ 1 ^ (2 * e), z ^ d), C.at[e, d], to_core, C.at[e, d]
                )

            def send(e, part, to, where):
                return s.plan(half(S.at[e, d], part), where, to, where)

            self.halves[d] = [send(3, 0, to_x, H.at[d, 0]), send(3, 1, to_y, H.at[d, 1])]
            self.ahead[d] = [
                send(2, 1, to_y, half(Q.at[d, 1], 1)),
                send(1, 0, to_x, half(Q.at[d, 0], 0)),
            ]
            self.rest[d] = [
                send(2, 0, to_y, half(Q.at[d, 1], 0)),
                send(1, 1, to_x, half(Q.at[d, 0], 1)),
            ]
            if d:
                to = (b, z ^ (2 if d == 2 else 1))
                self.last[d] = s.plan(S.at[0, d], Z.at[d - 1], to, Z.at[d - 1])

    def start(self):
        for d in self.ORDER:
            for e in (3, 1, 2, 0):
                self.mine[d, e].start()
                self.other[d, e].go()

    def fold(self, d):
        for e in (3, 1, 2, 0):
            self.mine[d, e].wait()
            self.other[d, e].wait_recv()
            add_rows(self.S.at[e, d], self.S.at[e, d], self.C.at[e, d])
            for copy in {3: self.halves[d], 1: self.ahead[d][1:], 2: self.ahead[d][:1], 0: []}[e]:
                copy.go()

    def relay(self, d):
        for i, e in ((0, 2), (1, 1)):
            self.halves[d][i].wait_recv()
            part = half(self.S.at[e, d], i)
            add_rows(part, part, self.H.at[d, i])
            self.rest[d][i].go()

    def collect(self, d):
        for copy in self.ahead[d] + self.rest[d]:
            copy.wait_recv()
        total = self.S.at[0, d]
        for i in (0, 1):
            add_rows(total, total, self.Q.at[d, i])
        if d == 2:
            self.last[3].wait_recv()
            add_rows(total, total, self.Z.at[2])
        if d:
            self.last[d].go()

    def total(self):
        for d in (1, 2):
            self.last[d].wait_recv()
        sum_rows(self.out, self.S.at[0, 0], self.Z.at[0], self.Z.at[1])

    @staticmethod
    def scratch(rows, columns):
        lead = (((4, 4), 1), ((4, 4), 1), ((4, 2), 2), ((4, 2), 1), ((3,), 1))
        shapes = [pltpu.VMEM((*n, rows // cut, columns), LOW) for n, cut in lead]
        return shapes + [pltpu.SemaphoreType.DMA((16,))]


class ReducerAlongZ:
    COPIES = 16 + 4 * 3 + 6

    def __init__(self, s, share, out, C, S, H, Q, Z, lsem):
        b, z = position()
        to_x, to_y, to_core = (b ^ 2, z), (b ^ 4, z), (b ^ 1, z)
        self.out, self.C, self.S, self.H, self.Q, self.Z = out, C, S, H, Q, Z
        self.mine, self.other, self.along = {}, {}, {}
        for e in (3, 1, 2, 0):
            for d in (3, 2, 1, 0):
                self.mine[e, d] = pltpu.make_async_copy(
                    share(b ^ (2 * e), z ^ d), S.at[e, d], lsem.at[d * 4 + e]
                )
                self.other[e, d] = s.plan(
                    share(b ^ 1 ^ (2 * e), z ^ d), C.at[e, d], to_core, C.at[e, d]
                )
                if d:
                    to = (b, z ^ (2 if d == 2 else 1))
                    self.along[e, d] = s.plan(S.at[e, d], Z.at[e, d - 1], to, Z.at[e, d - 1])

        def send(e, part, to, where):
            return s.plan(half(S.at[e, 0], part), where, to, where)

        self.halves = [send(3, 0, to_x, H.at[0]), send(3, 1, to_y, H.at[1])]
        self.ahead = [
            send(2, 1, to_y, half(Q.at[1], 1)),
            send(1, 0, to_x, half(Q.at[0], 0)),
        ]
        self.rest = [
            send(2, 0, to_y, half(Q.at[1], 0)),
            send(1, 1, to_x, half(Q.at[0], 1)),
        ]

    def start(self):
        for at in self.mine:
            self.mine[at].start()
            self.other[at].go()

    def fold(self, e):
        for d in (3, 1, 2, 0):
            self.mine[e, d].wait()
            self.other[e, d].wait_recv()
            add_rows(self.S.at[e, d], self.S.at[e, d], self.C.at[e, d])
            if d in (1, 3):
                self.along[e, d].go()

    def relay(self, e):
        self.along[e, 3].wait_recv()
        add_rows(self.S.at[e, 2], self.S.at[e, 2], self.Z.at[e, 2])
        self.along[e, 2].go()

    def collect(self, e):
        total = self.S.at[e, 0]
        for d in (1, 2):
            self.along[e, d].wait_recv()
            add_rows(total, total, self.Z.at[e, d - 1])
        for copy in {3: self.halves, 1: self.ahead[1:], 2: self.ahead[:1], 0: []}[e]:
            copy.go()

    def cross(self):
        for i, e in ((0, 2), (1, 1)):
            self.halves[i].wait_recv()
            part = half(self.S.at[e, 0], i)
            add_rows(part, part, self.H.at[i])
            self.rest[i].go()

    def total(self):
        for copy in self.ahead + self.rest:
            copy.wait_recv()
        sum_rows(self.out, self.S.at[0, 0], self.Q.at[0], self.Q.at[1])

    @staticmethod
    def scratch(rows, columns):
        lead = (((4, 4), 1), ((4, 4), 1), ((2,), 2), ((2,), 1), ((4, 3), 1))
        shapes = [pltpu.VMEM((*n, rows // cut, columns), LOW) for n, cut in lead]
        return shapes + [pltpu.SemaphoreType.DMA((16,))]


def attend_kernel(qh_ref, kh_ref, v_ref, out_ref, lse_ref):
    keys = [rows_of(kh_ref[head, :, 0]) for head in (0, 1)]
    out_ref[0, 0], lse_ref[0] = attend_tile(
        [qh_ref[head, 0, 0] for head in (0, 1)], keys, rows_of(v_ref[:, 0])
    )


def attend(qh, kh, v):
    blocks, slots, rows, lanes = v.shape
    tile = pl.BlockSpec((1, 1, rows, lanes), lambda s, i: (i, s, 0, 0))
    tiles = pl.BlockSpec((2, 1, 1, rows, lanes), lambda s, i: (0, i, s, 0, 0))
    whole = pl.BlockSpec((blocks, 1, rows, lanes), lambda s, i: (0, s, 0, 0))
    wholes = pl.BlockSpec((2, blocks, 1, rows, lanes), lambda s, i: (0, 0, s, 0, 0))
    return pl.pallas_call(
        attend_kernel,
        grid=(slots, blocks),
        out_shape=(
            jax.ShapeDtypeStruct(v.shape, LOW),
            jax.ShapeDtypeStruct((slots, 8, blocks * rows), HIGH),
        ),
        in_specs=[tiles, wholes, whole],
        out_specs=(tile, pl.BlockSpec((1, 8, rows), lambda s, i: (s, 0, i))),
        compiler_params=pltpu.CompilerParams(vmem_limit_bytes=VMEM_LIMIT),
        name="attend",
    )(qh, kh, v)


def row_products(out, grad):
    pick = (lax.broadcasted_iota(jnp.int32, (8, 128), 0) == 0) == first_lanes((8, 128))
    return lax.dot_general(
        pick.astype(HIGH),
        out.astype(HIGH) * grad.astype(HIGH),
        (((1,), (1,)), ((), ())),
        precision=lax.Precision.HIGHEST,
        preferred_element_type=HIGH,
    )


def attend_back_tile(queries, keys, values, grads, logs, delta, acc):
    zeros = jnp.zeros_like(grads)
    mine = first_lanes(grads.shape)
    dk, dv = [], 0.0
    for head in (0, 1):
        grad = jnp.where(mine == (head == 0), grads, zeros)
        probs = jnp.exp(product_nt(keys[head], queries[head]) - logs[head : head + 1])
        pushed = product_nt(values, grad)
        d_scores = (probs * (pushed - delta[head : head + 1])).astype(LOW)
        dv = dv + product(probs.astype(LOW), grad)
        dk.append(product(d_scores, queries[head]))
        keys_t = keys[head].T[head * 64 : head * 64 + 64]
        acc[head * 64 : head * 64 + 64, :] += product(keys_t, d_scores)
    return jnp.where(first_lanes(dk[0].shape), dk[0], dk[1]).astype(LOW), dv.astype(LOW)


def attend_back_kernel(
    qh_ref, o_ref, g_ref, lse_ref, kh_ref, v_ref, dq_ref, dk_ref, dv_ref, acc, delta
):
    tile = pl.program_id(1)
    blocks, _, rows, _ = g_ref.shape
    grads = rows_of(g_ref[:, 0])

    @pl.when(tile == 0)
    def _():
        acc[...] = jnp.zeros_like(acc)
        delta[...] = row_products(rows_of(o_ref[:, 0]), grads)

    dk_ref[0, 0], dv_ref[0, 0] = attend_back_tile(
        [rows_of(qh_ref[head, :, 0]) for head in (0, 1)],
        [kh_ref[head, 0, 0] for head in (0, 1)],
        v_ref[0, 0],
        grads,
        lse_ref[0],
        delta[...],
        acc,
    )

    @pl.when(tile == blocks - 1)
    def _():
        dq_ref[:, 0] = (acc[...].T * 0.125).astype(LOW).reshape(blocks, rows, 128)


def attend_back(qh, o, g, lse, kh, v):
    blocks, slots, rows, lanes = v.shape
    tile = pl.BlockSpec((1, 1, rows, lanes), lambda s, i: (i, s, 0, 0))
    tiles = pl.BlockSpec((2, 1, 1, rows, lanes), lambda s, i: (0, i, s, 0, 0))
    whole = pl.BlockSpec((blocks, 1, rows, lanes), lambda s, i: (0, s, 0, 0))
    wholes = pl.BlockSpec((2, blocks, 1, rows, lanes), lambda s, i: (0, 0, s, 0, 0))
    logs = pl.BlockSpec((1, 8, blocks * rows), lambda s, i: (s, 0, 0))
    shape = jax.ShapeDtypeStruct(v.shape, LOW)
    return pl.pallas_call(
        attend_back_kernel,
        grid=(slots, blocks),
        out_shape=(shape,) * 3,
        in_specs=[wholes, whole, whole, logs, tiles, tile],
        out_specs=(whole, tile, tile),
        scratch_shapes=[pltpu.VMEM((lanes, blocks * rows), HIGH), pltpu.VMEM((8, blocks * rows), HIGH)],
        compiler_params=pltpu.CompilerParams(vmem_limit_bytes=VMEM_LIMIT),
        name="attend_back",
    )(qh, o, g, lse, kh, v)


class TokenSums:
    COPIES = 4 + 2 + 4

    def __init__(self, s, piece, sent, C, S, H, Q, A):
        b, z = position()
        to_x, to_y, to_core = (b ^ 2, z), (b ^ 4, z), (b ^ 1, z)
        self.b, self.piece = b, piece
        self.sent, self.C, self.S, self.H, self.Q, self.A = sent, C, S, H, Q, A
        self.other = [s.plan(sent.at[e], C.at[e], to_core, C.at[e]) for e in range(4)]

        def send(e, part, to, where):
            return s.plan(half(S.at[e - 1], part), where, to, where)

        self.halves = [send(3, 0, to_x, H.at[0]), send(3, 1, to_y, H.at[1])]
        self.ahead = [
            send(2, 1, to_y, half(Q.at[1], 1)),
            send(1, 0, to_x, half(Q.at[0], 0)),
        ]
        self.rest = [
            send(2, 0, to_y, half(Q.at[1], 0)),
            send(1, 1, to_x, half(Q.at[0], 1)),
        ]

    def give(self, e):
        self.sent[e] = self.piece(self.b ^ 1 ^ (2 * e)).astype(LOW)
        self.other[e].go()

    def take(self, e):
        mine = self.piece(self.b ^ (2 * e))
        self.other[e].wait_recv()
        mine = mine + self.C[e].astype(HIGH)
        if e:
            self.S[e - 1] = mine.astype(LOW)
        else:
            self.A[...] = mine
        for copy in {3: self.halves, 1: self.ahead[1:], 2: self.ahead[:1], 0: []}[e]:
            copy.go()

    def relay(self):
        for i, e in ((0, 2), (1, 1)):
            self.halves[i].wait_recv()
            part = half(self.S.at[e - 1], i)
            add_rows(part, part, self.H.at[i])
            self.rest[i].go()

    def total(self):
        for copy in self.ahead + self.rest:
            copy.wait_recv()
        return self.A[...] + self.Q[0].astype(HIGH) + self.Q[1].astype(HIGH)

    @staticmethod
    def scratch(rows, width):
        low = lambda *s: pltpu.VMEM((*s, width), LOW)
        return [low(4, rows), low(4, rows), low(3, rows), low(2, rows // 2), low(2, rows)] + [
            pltpu.VMEM((rows, width), HIGH)
        ]


def back_kernel(
    d_att,
    qh_in,
    kh_in,
    v_in,
    att_in,
    lse_in,
    w_in,
    first,
    g1,
    dq,
    dk,
    dv,
    o1,
    out_o,
    tok,
    qh,
    kh,
    v,
    att,
    lse,
    w,
    first_rows,
    tail,
    grads,
    acc,
    delta,
    lsem,
    send,
    recv,
    *buffers,
):
    b, z = position()
    blocks, slots, rows, _ = v.shape
    loads = [
        pltpu.make_async_copy(src, dst, lsem.at[i])
        for i, (src, dst) in enumerate(
            (
                (d_att.at[b], grads.at[b]),
                (qh_in, qh),
                (kh_in, kh),
                (v_in, v),
                (att_in, att),
                (lse_in, lse),
                (w_in, w),
                (first.at[pl.ds(0, rows)], first_rows),
            )
        )
    ]
    for load in loads:
        load.start()
    greet([(b ^ d, z) for d in range(1, 8)] + [(b, z ^ d) for d in (1, 2, 3)])
    s = Sender(send, recv)
    arriving = [
        [
            s.go(d_att.at[b ^ d, part], grads.at[b, part], (b ^ d, z), grads.at[b ^ d, part])
            for d in range(1, 8)
        ]
        for part in (pl.ds(slot * rows, rows) for slot in range(slots))
    ]

    def arrive(slot):
        for copy in arriving[slot]:
            copy.wait_recv()

    most = o1.shape[1] - tail.shape[1] + out_o.shape[1]
    sums = Reducer(
        s, lambda bb, zz: g1.at[bb, zz, :, pl.ds(0, most)], o1.at[:, pl.ds(0, most)], *buffers[:6]
    )
    late = ReducerAlongZ(
        s, lambda bb, zz: g1.at[bb, zz, :, pl.ds(most, tail.shape[1])], tail, *buffers[6:12]
    )

    def piece(i):
        mixed = jnp.concatenate([ref[i, 0] for ref in (dq, dk, dv)], axis=-1)
        return product_nt(mixed, w[...])

    tokens = TokenSums(s, piece, *buffers[12:])
    late.start()
    sums.start()
    late.fold(3)
    late.fold(1)
    sums.fold(3)
    late.fold(2)
    late.fold(0)
    sums.fold(2)
    arrive(0)
    for load in loads:
        load.wait()

    def grad_rows(slot):
        part = pl.ds(pl.multiple_of(slot * rows, rows), rows)
        return rows_of(grads[:, part])

    events = {
        0: [(late.relay, 3), (late.relay, 1)],
        1: [(sums.relay, 3)],
        2: [(late.relay, 2), (late.relay, 0)],
        3: [(sums.fold, 1)],
        4: [(sums.relay, 2), (late.collect, 3)],
        5: [(sums.collect, 3)],
        6: [(sums.fold, 0), (late.collect, 1)],
        7: [(late.collect, 2), (arrive, 1)],
        8: [(tokens.give, 3), (sums.relay, 1)],
        9: [(tokens.give, 2), (tokens.take, 3), (sums.collect, 2)],
        10: [(tokens.give, 1), (tokens.take, 2)],
        11: [(tokens.give, 0), (tokens.take, 1), (sums.relay, 0)],
        12: [(tokens.take, 0), (late.cross,)],
        13: [(sums.collect, 1), (tokens.relay,)],
        14: [(late.collect, 0)],
    }

    @pl.loop(0, blocks * slots)
    def _(step):
        slot, tile = step // blocks, step % blocks
        slot_grads = grad_rows(slot)

        @pl.when(tile == 0)
        def _():
            acc[...] = jnp.zeros_like(acc)
            delta[...] = row_products(rows_of(att[:, slot]), slot_grads)

        dk[tile, slot], dv[tile, slot] = attend_back_tile(
            [rows_of(qh[head, :, slot]) for head in (0, 1)],
            [kh[head, tile, slot] for head in (0, 1)],
            v[tile, slot],
            slot_grads,
            lse[slot],
            delta[...],
            acc,
        )

        @pl.when(tile == blocks - 1)
        def _():
            dq[:, slot] = (acc[...].T * 0.125).astype(LOW).reshape(blocks, rows, 128)

        for at, some in events.items():

            @pl.when(step == at)
            def _(some=some):
                for event, *what in some:
                    event(*what)

    sums.collect(0)
    late.total()
    rest = o1.shape[1] - most
    o1[:, most:] = tail[:, :rest]
    out_o[...] = tail[:, rest:]
    sums.total()
    tok[...] = first_rows[...] + tokens.total()
    s.drain()


def back(d_att, qh, kh, v, att, lse, w, d_first, g1):
    blocks, slots, rows, lanes = v.shape
    shape = jax.ShapeDtypeStruct
    shard, total = g1.shape[2:]
    width = w.shape[0]
    late = 2 * width
    vmem = pl.BlockSpec(memory_space=pltpu.VMEM)
    scratch = lambda a: pltpu.VMEM(a.shape, a.dtype)
    return pl.pallas_call(
        back_kernel,
        out_shape=(shape(v.shape, LOW),) * 3
        + (
            shape((shard, total - width), HIGH),
            shape((shard, width), HIGH),
            shape((rows, width), HIGH),
        ),
        in_specs=in_hbm(9),
        out_specs=(vmem,) * 6,
        scratch_shapes=[scratch(a) for a in (qh, kh, v, att, lse, w)]
        + [
            pltpu.VMEM((rows, width), HIGH),
            pltpu.VMEM((shard, late), HIGH),
            pltpu.VMEM(d_att.shape, LOW),
            pltpu.VMEM((lanes, blocks * rows), HIGH),
            pltpu.VMEM((8, blocks * rows), HIGH),
            pltpu.SemaphoreType.DMA((8,)),
        ]
        + pair_of_semaphores(7 * slots + Reducer.COPIES + ReducerAlongZ.COPIES + TokenSums.COPIES)
        + Reducer.scratch(shard, total - late)
        + ReducerAlongZ.scratch(shard, late)
        + TokenSums.scratch(rows, width),
        compiler_params=pltpu.CompilerParams(
            collective_id=2, has_side_effects=True, vmem_limit_bytes=VMEM_LIMIT
        ),
        name="back",
    )(d_att, qh, kh, v, att, lse, w, d_first, g1)


def column_sum(block):
    return jnp.sum(block.astype(HIGH), axis=0, keepdims=True)


def middle_kernel(
    chunk,
    small_rows,
    att,
    n1,
    r1,
    normed_low,
    cot_ref,
    par_ref,
    act_hbm,
    slope_hbm,
    w1_hbm,
    w2_hbm,
    out_ref,
    first_ref,
    d_att_ref,
    small_ref,
    g1_hbm,
    g2_hbm,
    w1,
    w2,
    act,
    slope,
    acc,
    low,
    sums_ref,
    d_hid_ref,
    wsem,
    gsem,
):
    hidden, width = w2.shape
    steps = hidden // chunk
    pieces, _, held = d_att_ref.shape

    def columns(c):
        return pl.ds(pl.multiple_of(c * chunk, chunk), chunk)

    def load1(c):
        return pltpu.make_async_copy(w1_hbm.at[:, columns(c)], w1.at[:, columns(c)], wsem.at[0, c])

    def load2(c):
        return pltpu.make_async_copy(w2_hbm.at[columns(c)], w2.at[columns(c)], wsem.at[1, c])

    def load_act(c):
        return pltpu.make_async_copy(act_hbm.at[:, columns(c)], act.at[:, columns(c)], wsem.at[2, c])

    def load_slope(c):
        return pltpu.make_async_copy(
            slope_hbm.at[:, columns(c)], slope.at[:, columns(c)], wsem.at[3, c]
        )

    last = pl.ds(hidden, width)
    for c in range(steps):
        load_act(c).start()
        load2(c).start()
    for c in range(steps):
        load_slope(c).start()
        load1(c).start()
    load_out = pltpu.make_async_copy(w1_hbm.at[:, last], w1.at[:, last], wsem.at[0, steps])
    load_out.start()
    gain1, gain2 = par_ref[0:1], par_ref[1:2]
    bias = lambda i: par_ref[2 + i : 3 + i]
    acc[...] = n1[...] * gain1 + (bias(3) + bias(4))

    @pl.loop(0, steps)
    def _(c):
        load_act(c).wait()
        load2(c).wait()
        acc[...] += product(act[:, columns(c)], w2[columns(c), :])

    normal, inverse2 = normalize(acc[...])
    out_ref[...] = (normal * gain2 + bias(5)).astype(LOW)
    cot = cot_ref[...].astype(HIGH)
    d_second = normalize_back(cot * gain2, normal, inverse2)
    low[...] = d_second.astype(LOW)
    acc[...] = d_second
    sums_ref[1:2] = column_sum(cot * normal)
    sums_ref[4:5] = column_sum(low[...])
    sums_ref[5:6] = column_sum(cot)

    def store1(c):
        return pltpu.make_async_copy(w1.at[:, columns(c)], g1_hbm.at[:, columns(c)], gsem.at[0, c])

    def store2(c):
        return pltpu.make_async_copy(w2.at[columns(c)], g2_hbm.at[columns(c)], gsem.at[1, c])

    @pl.loop(0, steps)
    def _(c):
        load_slope(c).wait()
        load1(c).wait()
        d_act = product_nt(low[...], w2[columns(c), :])
        d_pre = (d_act * slope[:, columns(c)].astype(HIGH)).astype(LOW)
        d_hid_ref[:, columns(c)] = column_sum(d_pre)
        acc[...] += product_nt(d_pre, w1[:, columns(c)])
        w2[columns(c), :] = product_tn(act[:, columns(c)], low[...]).astype(LOW)
        store2(c).start()
        w1[:, columns(c)] = product_tn(normed_low[...], d_pre).astype(LOW)
        store1(c).start()

    d_normed = acc[...]
    normal = n1[...]
    d_first = normalize_back(d_normed * gain1, normal, r1[:, 0:1])
    first_ref[...] = d_first
    low[...] = d_first.astype(LOW)
    sums_ref[0:1] = column_sum(d_normed * normal)
    sums_ref[2:3] = column_sum(low[...])
    sums_ref[3:4] = column_sum(d_normed)
    load_out.wait()
    d_att = product_nt(low[...], w1[:, hidden:]).astype(LOW)
    for i in range(pieces):
        d_att_ref[i] = d_att[:, i * held : (i + 1) * held]
    w1[:, hidden:] = product_tn(att[...], low[...]).astype(LOW)
    store_out = pltpu.make_async_copy(w1.at[:, last], g1_hbm.at[:, last], gsem.at[0, steps])
    store_out.start()
    blocks, planes, _ = small_ref.shape
    small_ref[...] = jnp.zeros_like(small_ref)
    owners = [(i, j) for i in range(blocks) for j in range(width // (blocks * small_rows))]
    for at, (i, j) in enumerate(owners):
        for k in range(6):
            small_ref[i, j : j + 1, k * small_rows : (k + 1) * small_rows] = sums_ref[
                k : k + 1, at * small_rows : (at + 1) * small_rows
            ]
        part = hidden // len(owners)
        small_ref[i, j : j + 1, 6 * small_rows : 6 * small_rows + part] = d_hid_ref[
            :, at * part : (at + 1) * part
        ]
    for c in range(steps):
        store1(c).wait()
        store2(c).wait()
    store_out.wait()


def middle(att, n1, r1, normed_low, cot, par, act, slope, w1, w2, pieces, planes):
    count, width = cot.shape
    hidden = w2.shape[0]
    chunk = 512
    shape = jax.ShapeDtypeStruct
    vmem = pl.BlockSpec(memory_space=pltpu.VMEM)
    return pl.pallas_call(
        functools.partial(middle_kernel, chunk, width // (pieces * planes)),
        out_shape=(
            shape((count, width), LOW),
            shape((count, width), HIGH),
            shape((pieces, count, width // pieces), LOW),
            shape((pieces, -(-planes // 8) * 8, 384), HIGH),
            shape(w1.shape, LOW),
            shape(w2.shape, LOW),
        ),
        in_specs=[vmem] * 6 + in_hbm(4),
        out_specs=(vmem,) * 4 + tuple(in_hbm(2)),
        scratch_shapes=[
            pltpu.VMEM(w1.shape, LOW),
            pltpu.VMEM(w2.shape, LOW),
            pltpu.VMEM((count, hidden), LOW),
            pltpu.VMEM((count, hidden), LOW),
            pltpu.VMEM((count, width), HIGH),
            pltpu.VMEM((count, width), LOW),
            pltpu.VMEM((8, width), HIGH),
            pltpu.VMEM((1, hidden), HIGH),
            pltpu.SemaphoreType.DMA((4, hidden // chunk + 1)),
            pltpu.SemaphoreType.DMA((2, hidden // chunk + 1)),
        ],
        compiler_params=pltpu.CompilerParams(vmem_limit_bytes=VMEM_LIMIT),
        name="middle",
    )(att, n1, r1, normed_low, cot, par, act, slope, w1, w2)


def finish_kernel(
    dq,
    dk,
    dv,
    w,
    first,
    tok0,
    small,
    x_hbm,
    g2,
    tok_out,
    in_out,
    gains_out,
    biases_out,
    hidden_out,
    o2,
    first_rows,
    x,
    D,
    R,
    Z,
    M,
    N,
    T,
    lsem,
    send,
    recv,
    *buffers,
):
    b, z = position()
    rows, width = tok0.shape
    blocks = dq.shape[0]
    count = 2 * rows
    loads = [
        pltpu.make_async_copy(x_hbm.at[i, pl.ds(0, count)], x.at[i], lsem.at[i])
        for i in range(blocks)
    ]
    loads.append(pltpu.make_async_copy(first.at[pl.ds(rows, rows)], first_rows, lsem.at[blocks]))
    loads.append(pltpu.make_async_copy(tok0, tok_out.at[pl.ds(0, rows)], lsem.at[blocks + 1]))
    for load in loads:
        load.start()
    greet([(b ^ d, z) for d in range(1, 8)] + [(b, z ^ d) for d in (1, 2, 3)])
    s = Sender(send, recv)
    cut = buffers[0].shape[2]
    lower, upper = pl.ds(0, cut), pl.ds(cut, o2.shape[0] - cut)
    sums = Reducer(s, lambda bb, zz: g2.at[bb, zz, lower], o2.at[lower], *buffers[:6])
    late = ReducerAlongZ(s, lambda bb, zz: g2.at[bb, zz, upper], o2.at[upper], *buffers[6:12])

    def piece(i):
        mixed = jnp.concatenate([ref[i, 1] for ref in (dq, dk, dv)], axis=-1)
        return product_nt(mixed, w[...])

    tokens = TokenSums(s, piece, *buffers[12:])
    small_in = [
        s.go(small.at[b ^ d], M.at[d - 1], (b ^ d, z), M.at[d - 1]) for d in range(1, 8)
    ]
    late.start()
    tokens.give(3)
    sums.start()
    tokens.give(2)
    tokens.give(1)
    tokens.give(0)
    late.fold(3)
    late.fold(1)
    tokens.take(3)
    sums.fold(3)
    late.relay(3)
    late.fold(2)
    sums.fold(2)
    tokens.take(2)
    sums.relay(3)
    late.fold(0)
    late.relay(1)
    tokens.take(1)
    tokens.take(0)
    sums.fold(1)
    sums.relay(2)
    late.relay(2)
    late.collect(3)

    total = jnp.zeros((width, w.shape[1]), HIGH)
    for i in range(blocks):
        loads[i].wait()
        mixed = jnp.concatenate([ref[i].reshape(count, -1) for ref in (dq, dk, dv)], axis=-1)
        total = total + product_tn(x[i], mixed)
    D[...] = total.astype(LOW).reshape(D.shape)
    grads_in = [
        s.go(D.at[b ^ d], R.at[b], (b ^ d, z), R.at[b ^ d]) for d in range(1, 8)
    ]
    R[b] = D[b]
    sums.collect(3)
    sums.fold(0)
    late.relay(0)
    tokens.relay()
    sums.relay(1)
    late.collect(1)
    sums.collect(2)
    late.collect(2)

    N[...] = small[b]
    for i in range(7):
        small_in[i].wait_recv()
        N[...] += M[i]
    for row, ref in ((4, dq), (5, dv)):
        whole = jnp.zeros((1, 128), HIGH)
        for i in range(blocks):
            whole = whole + column_sum(ref[i].reshape(count, -1))
        N[row : row + 1, 0:128] = whole
    small_z = [s.go(N, T.at[d - 1], (b, z ^ d), T.at[d - 1]) for d in (1, 2, 3)]

    sums.relay(0)
    late.cross()
    for copy in grads_in:
        copy.wait_recv()
    share_rows = R.shape[1] // 4

    def share(d):
        return R.at[:, pl.ds(pl.multiple_of((z ^ d) * share_rows, share_rows), share_rows)]

    in_z = [s.go(share(d), Z.at[d - 1], (b, z ^ d), Z.at[d - 1]) for d in (1, 2, 3)]
    sums.collect(1)
    for copy in small_z:
        copy.wait_recv()
    vectors = ((N[...] + T[0]) + T[1]) + T[2]
    planes = lax.broadcasted_iota(jnp.int32, vectors.shape, 0)
    row = jnp.sum(jnp.where(planes == z, vectors, 0.0), axis=0, keepdims=True)
    n = gains_out.shape[1]
    for k in range(2):
        gains_out[k : k + 1] = row[:, k * n : (k + 1) * n]
        own = vectors[4 + k : 5 + k]
        parts = [jnp.where(z == j, own[:, j * n : (j + 1) * n], 0.0) for j in range(4)]
        biases_out[k : k + 1] = (parts[0] + parts[1]) + (parts[2] + parts[3])
    for k in range(2, 6):
        biases_out[k : k + 1] = row[:, k * n : (k + 1) * n]
    hidden_out[...] = row[:, 6 * n : 6 * n + hidden_out.shape[1]]
    for copy in in_z:
        copy.wait_recv()
    terms = [share(0), Z.at[0], Z.at[1], Z.at[2]]
    for i in range(blocks):
        block = terms[0][i].astype(HIGH)
        for term in terms[1:]:
            block = block + term[i].astype(HIGH)
        for k in range(3):
            at = k * width + i * 128
            in_out[:, at : at + 128] = block[:, k * 128 : (k + 1) * 128]
    late.collect(0)
    sums.collect(0)
    sums.total()
    late.total()
    for load in loads[blocks:]:
        load.wait()
    tok_out[rows:] = first_rows[...] + tokens.total()
    s.drain()


def finish(dq, dk, dv, w, d_first, tok0, small, x, g2):
    rows, width = tok0.shape
    blocks, columns = dq.shape[0], w.shape[1]
    share = width // (4 * blocks)
    shard = g2.shape[2]
    late = shard // 4
    vmem = pl.BlockSpec(memory_space=pltpu.VMEM)
    shape = lambda *s: jax.ShapeDtypeStruct(s, HIGH)
    low = lambda *s: pltpu.VMEM(s, LOW)
    wide = lambda *s: pltpu.VMEM(s, HIGH)
    tile = small.shape[1:]
    return pl.pallas_call(
        finish_kernel,
        out_shape=(
            shape(2 * rows, width),
            shape(share, 3 * width),
            shape(2, share),
            shape(6, share),
            shape(1, shard),
            shape(shard, width),
        ),
        in_specs=[vmem] * 4 + in_hbm(2) + [vmem] + in_hbm(2),
        out_specs=(vmem,) * 6,
        scratch_shapes=[
            wide(rows, width),
            low(blocks, 2 * rows, width),
            low(blocks, 4 * share, columns),
            low(blocks, 4 * share, columns),
            low(3, blocks, share, columns),
            wide(7, *tile),
            wide(*tile),
            wide(3, *tile),
            pltpu.SemaphoreType.DMA((blocks + 2,)),
        ]
        + pair_of_semaphores(
            20 + Reducer.COPIES + ReducerAlongZ.COPIES + TokenSums.COPIES
        )
        + Reducer.scratch(shard - late, width)
        + ReducerAlongZ.scratch(late, width)
        + TokenSums.scratch(rows, width),
        compiler_params=pltpu.CompilerParams(
            collective_id=3, has_side_effects=True, vmem_limit_bytes=VMEM_LIMIT
        ),
        name="finish",
    )(dq, dk, dv, w, d_first, tok0, small, x, g2)


def swap(pieces):
    return lax.all_to_all(pieces, "blk", 0, 0)


def by_slot(block, slots):
    blocks, count, held = block.shape
    block = block.reshape(blocks, slots, count // slots, held)
    return jnp.pad(block, ((0, 0),) * 3 + ((0, 128 - held),))


def front_apart(X, W, bias, slots):
    n_blk, count = X.shape[0], X.shape[1] - 16
    held = W.shape[1] // 3
    mixed = jnp.einsum("brd,dc->brc", X[:, :count], W, preferred_element_type=HIGH)
    parts = [mixed[..., i * held : (i + 1) * held] for i in range(3)]
    parts = [jnp.pad(p, ((0, 0), (0, 0), (0, 128 - held))).reshape(-1, 128) for p in parts]
    own = lax.dynamic_slice(bias[:2], (0, lax.axis_index("blk") * held), (2, held))
    own = jnp.pad(own, ((0, 0), (0, 128 - held)))
    codes = X[:, count, :count].reshape(-1, 1).astype(jnp.int32)
    codes = jnp.broadcast_to(codes, (n_blk * count, 128))
    queries, keys, values = split_heads(jnp.concatenate(parts, axis=1), (own[0], own[1]), codes)
    shape = (n_blk, slots, count // slots, 128)
    qh = jnp.stack(queries).reshape(2, *shape)
    kh = jnp.stack(keys).reshape(2, *shape)
    v = values.reshape(shape)
    att, lse = attend(qh, kh, v)
    rows_att = swap(att[..., :held].reshape(n_blk, count, held))
    return qh, kh, v, att, lse, rows_att


def on_device(
    tokens,
    input_weight,
    output_weight,
    expand_weight,
    reduce_weight,
    gains,
    biases,
    hidden_bias,
    segment,
    present,
    cotangent,
):
    slots, rows, width = tokens.shape
    n_blk, n_dp = lax.axis_size("blk"), lax.axis_size("dp")
    shards = n_blk * n_dp
    fast = (n_blk, n_dp) == (8, 4)
    held = width // n_blk
    shard = input_weight.shape[0]
    hidden = expand_weight.shape[1]
    count = slots * rows
    flat = tokens.reshape(count, width)

    if fast:
        front_out = front(
            flat,
            segment,
            present,
            input_weight,
            gains,
            biases,
            hidden_bias[None],
            expand_weight,
            output_weight,
            reduce_weight,
        )
        X, W1, W2, act, slope, W, _, qh, kh, v, att, lse = front_out[:12]
        attended, n1, r1, normed_low, cuts = front_out[12:]
        W1, W2 = W1.reshape(width, -1), W2.reshape(hidden, width)
    else:
        code = (segment + 4 * (1 - present)).reshape(1, count).astype(LOW)
        code_rows = jnp.pad(jnp.broadcast_to(code, (16, count)), ((0, 0), (0, width - count)))
        columns = input_weight.reshape(shard, 3, n_blk, held).transpose(2, 0, 1, 3)
        columns = columns.reshape(n_blk, shard, 3 * held)
        small = jnp.concatenate([gains.reshape(-1), biases.reshape(-1), hidden_bias])
        X = lax.all_gather(jnp.concatenate([flat, code_rows], axis=0), "blk")
        W = lax.all_gather(swap(columns), "dp", axis=1).reshape(width, 3 * held)
        small = lax.all_gather(small, BOTH)
        W1 = jnp.concatenate([expand_weight, output_weight], axis=1)
        W1 = lax.all_gather(W1, BOTH, axis=0, tiled=True)
        W2 = lax.all_gather(reduce_weight, BOTH, axis=0, tiled=True)
        part = width // shards
        cuts = small[:, : 8 * part].reshape(shards, 8, part).transpose(1, 0, 2)
        cuts = cuts.reshape(8, width).astype(HIGH)
        hidden_full = small[:, 8 * part :].reshape(hidden).astype(HIGH)
        gain, bias = cuts[:2], cuts[2:]
        qh, kh, v, att, lse, rows_att = front_apart(X, W, bias, slots)
        attended = rows_att.transpose(1, 0, 2).reshape(count, width)
        branch = product(attended, W1[:, hidden:]) + bias[2]
        n1, r1 = normalize(flat.astype(HIGH) + branch)
        r1 = jnp.broadcast_to(r1, (count, 128))
        normed_low = (n1 * gain[0] + bias[3]).astype(LOW)
        act, slope = gelu_parts(product(normed_low, W1[:, :hidden]) + hidden_full)
        act, slope = act.astype(LOW), slope.astype(LOW)
    cot = cotangent.reshape(count, width)
    middle_out = middle(
        attended, n1, r1, normed_low, cot, cuts, act, slope, W1, W2, n_blk, n_dp
    )
    output, d_first, d_att, small_rows, grad_both, grad_reduce = middle_out
    output = output.reshape(slots, rows, width)
    if fast:
        grad_both = grad_both.reshape(n_blk, n_dp, shard, -1)
        grad_reduce = grad_reduce.reshape(n_blk, n_dp, -1, width)
        dq, dk, dv, sum_expand, sum_output, tok0 = back(
            d_att, qh, kh, v, att, lse, W, d_first, grad_both
        )
        grad_tokens, grad_input, d_gains, d_biases, d_hidden, sum_reduce = finish(
            dq, dk, dv, W, d_first, tok0, small_rows, X, grad_reduce
        )
        return (
            output,
            grad_tokens.reshape(slots, rows, width),
            grad_input,
            sum_output,
            sum_expand,
            sum_reduce,
            d_gains,
            d_biases,
            d_hidden.reshape(-1),
        )
    sum_both = lax.psum_scatter(grad_both, BOTH, scatter_dimension=0, tiled=True).astype(HIGH)
    sum_reduce = lax.psum_scatter(grad_reduce, BOTH, scatter_dimension=0, tiled=True)
    dq, dk, dv = attend_back(qh, att, by_slot(swap(d_att), slots), lse, kh, v)
    d_mixed = jnp.concatenate([dq[..., :held], dk[..., :held], dv[..., :held]], axis=-1)
    d_mixed = d_mixed.reshape(n_blk * count, 3 * held)
    all_tokens = X[:, :count].reshape(n_blk * count, width)
    d_input = product_tn(all_tokens, d_mixed).astype(LOW)
    d_tokens = product_nt(d_mixed, W).astype(LOW)
    d_tokens = lax.psum_scatter(d_tokens, "blk", scatter_dimension=0, tiled=True)
    grad_tokens = d_first + d_tokens.astype(HIGH)
    d_input = swap(d_input.reshape(n_blk, n_dp * shard, 3 * held))
    d_input = d_input.reshape(n_blk, n_dp, shard, 3, held).transpose(1, 2, 3, 0, 4)
    d_input = d_input.reshape(n_dp, shard, 3 * width).astype(HIGH)
    grad_input = lax.psum_scatter(d_input, "dp", scatter_dimension=0, tiled=False)
    col = lambda a: jnp.sum(a.astype(HIGH), axis=0)
    own_cols = jnp.stack([col(d_mixed[:, :held]), col(d_mixed[:, 2 * held :])])
    own_cols = lax.psum_scatter(own_cols, "dp", scatter_dimension=1, tiled=True)
    small_rows = small_rows[:, :n_dp].reshape(shards, -1)
    small_sum = lax.psum_scatter(small_rows, BOTH, scatter_dimension=0, tiled=False)
    vectors = small_sum[: 6 * part].reshape(6, part)
    return (
        output,
        grad_tokens.reshape(slots, rows, width),
        grad_input,
        sum_both[:, hidden:],
        sum_both[:, :hidden],
        sum_reduce.astype(HIGH),
        vectors[:2],
        jnp.concatenate([own_cols, vectors[2:]], axis=0),
        small_sum[6 * part : 6 * part + hidden // shards],
    )


def solution(mesh):
    rows, sharded = P("dp", "blk", None), P(BOTH, None)
    in_specs = (rows, sharded, sharded, sharded, sharded, P(None, BOTH), P(None, BOTH), P(BOTH))
    in_specs += (P("dp", "blk"), P("dp", "blk"), rows)
    out_specs = (rows, rows, sharded, sharded, sharded, sharded)
    out_specs += (P(None, BOTH), P(None, BOTH), P(BOTH))
    return jax.shard_map(
        on_device, mesh=mesh, in_specs=in_specs, out_specs=out_specs, check_vma=False
    )
```

```python
import functools

import jax
import jax.numpy as jnp
from jax import lax
from jax.experimental import pallas as pl
from jax.experimental.pallas import tpu as pltpu
from jax.sharding import PartitionSpec as P

HEADS = 16
EPSILON = 1e-12
FAR = 2.0**60
BOTH = ("blk", "dp")
MESH = pl.DeviceIdType.MESH
LOW = jnp.bfloat16
HIGH = jnp.float32
VMEM_LIMIT = 60 * 2**20


def product(left, right):
    return jnp.dot(left, right, preferred_element_type=HIGH)


def product_nt(left, right):
    return lax.dot_general(left, right, (((1,), (1,)), ((), ())), preferred_element_type=HIGH)


def product_tn(left, right):
    return lax.dot_general(left, right, (((0,), (0,)), ((), ())), preferred_element_type=HIGH)


def normalize(values):
    mean = jnp.mean(values, axis=-1, keepdims=True)
    centred = values - mean
    spread = jnp.mean(centred * centred, axis=-1, keepdims=True)
    inverse = lax.rsqrt(spread + EPSILON)
    return centred * inverse, inverse


def normalize_back(grad, normal, inverse):
    return inverse * (
        grad
        - jnp.mean(grad, axis=-1, keepdims=True)
        - normal * jnp.mean(grad * normal, axis=-1, keepdims=True)
    )


def quick_reciprocal(x):
    first = pl.reciprocal(x, approx=True)
    return first * (2.0 - x * first)


def gelu_parts(u, reciprocal=lambda x: 1.0 / x):
    bell = jnp.exp(-0.5 * u * u)
    below = 1.0 + (0.3275911 * 0.5**0.5) * jnp.abs(u)
    t = reciprocal(below)
    poly = 1.061405429 * t - 1.453152027
    poly = poly * t + 1.421413741
    poly = poly * t - 0.284496736
    poly = poly * t + 0.254829592
    tail = 0.5 * poly * t * bell
    below = jnp.where(u < 0.0, tail, 1.0 - tail)
    return u * below, below + u * bell * 0.3989422804014327


class Sender:
    def __init__(self, send, recv):
        self.send, self.recv, self.planned = send, recv, []

    def plan(self, src, dst, device, landing):
        at = len(self.planned)

        def copy(a, b):
            return pltpu.make_async_remote_copy(
                src_ref=a,
                dst_ref=b,
                send_sem=self.send.at[at],
                recv_sem=self.recv.at[at],
                device_id=device,
                device_id_type=MESH,
            )

        out = copy(src, dst)
        self.planned.append(out)
        landed = copy(landing, landing)
        landed.go = out.start
        return landed

    def go(self, *what):
        landed = self.plan(*what)
        landed.go()
        return landed

    def drain(self):
        for out in self.planned:
            out.wait_send()


def greet(peers):
    barrier = pltpu.get_barrier_semaphore()
    for peer in peers:
        pl.semaphore_signal(barrier, inc=1, device_id=peer, device_id_type=MESH)
    pl.semaphore_wait(barrier, len(peers))


def half(ref, which):
    rows = ref.shape[0]
    cut = rows // 32 * 16
    return ref.at[pl.ds(0, cut)] if which == 0 else ref.at[pl.ds(cut, rows - cut)]


def position():
    return lax.axis_index("blk"), lax.axis_index("dp")


def first_lanes(shape):
    return lax.broadcasted_iota(jnp.int32, shape, len(shape) - 1) < 64


def rows_of(block):
    return block.reshape(-1, block.shape[-1])


def attend_tile(queries, keys, values):
    rows = queries[0].shape[0]
    ones = jnp.ones_like(values)
    mine = first_lanes(values.shape)
    outs, logs = [], []
    for head in (0, 1):
        scores = product_nt(queries[head], keys[head])
        top = jnp.max(scores, axis=-1, keepdims=True)
        weights = jnp.exp(scores - top).astype(LOW)
        total = product(weights, jnp.where(mine == (head == 0), values, ones))
        mass = pltpu.roll(total, 64, 1)
        outs.append(total / mass)
        logs.append(top + jnp.log(mass))
    mine = first_lanes((rows, 128))
    flipped = jnp.where(mine, logs[0], logs[1]).T
    logs = jnp.concatenate([flipped[0:1], flipped[64:65], jnp.zeros((6, rows), HIGH)], axis=0)
    return jnp.where(mine, outs[0], outs[1]).astype(LOW), logs


def split_heads(mixed, bias, codes):
    rows = mixed.shape[0]
    q = (mixed[:, :128] + bias[0]).astype(LOW) * LOW(0.125)
    k = mixed[:, 128:256].astype(LOW)
    v = (mixed[:, 256:] + bias[1]).astype(LOW)
    lanes = lax.broadcasted_iota(jnp.int32, (rows, 128), 1) % 64
    protein = jnp.where(codes >= 4, codes - 4, codes)
    q_marks = jnp.where((lanes < 5) & (lanes != protein), -FAR, 0.0).astype(LOW)
    k_marks = jnp.where(lanes == jnp.minimum(codes, 4), 1.0, 0.0).astype(LOW)
    mine = first_lanes((rows, 128))
    return (
        (jnp.where(mine, q, q_marks), jnp.where(mine, q_marks, q)),
        (jnp.where(mine, k, k_marks), jnp.where(mine, k_marks, k)),
        v,
    )


def spread_vectors(small, par, hid):
    for i in range(8):
        for j in range(4):
            row = small[j, i : i + 1].astype(HIGH)
            at = (i * 4 + j) * 32
            for k in range(8):
                par[k : k + 1, at : at + 32] = row[:, k * 32 : k * 32 + 32]
            hid[:, at * 4 : at * 4 + 128] = row[:, 256:384]


def front_kernel(
    x,
    segment,
    present,
    input_weight,
    gains,
    biases,
    hidden_bias,
    expand,
    out_w_in,
    w2,
    X_out,
    W1,
    W2,
    act_out,
    slope_out,
    wfull,
    small,
    qh,
    kh,
    v,
    att,
    lse,
    branch_in,
    n1,
    r1,
    normed_t,
    par,
    normed_low,
    X,
    W,
    win,
    w1,
    rows_att,
    w1v,
    act,
    slope,
    hid,
    send,
    recv,
    asend,
    arecv,
    lsem,
    osem,
    wsem,
    csem,
):
    b, z = position()
    bx, by, bd, bc = b ^ 2, b ^ 4, b ^ 6, b ^ 1
    count = X.shape[1] - 16
    hidden, width = expand.shape[1], x.shape[1]
    slots, rows = qh.shape[2:4]
    locs = []

    def local(src, dst):
        copy = pltpu.make_async_copy(src, dst, lsem.at[len(locs)])
        copy.start()
        locs.append(copy)

    local(x, X.at[b, pl.ds(0, count)])
    local(expand, w1.at[:, pl.ds(0, hidden)])
    local(out_w_in, w1.at[:, pl.ds(hidden, width)])
    local(w2, W2.at[b, z])
    shard = input_weight.shape[0]
    n = gains.shape[1]
    win[...] = jnp.zeros_like(win)
    for i in range(8):
        for k in range(3):
            at = k * width + i * 128
            win[i, 0:shard, k * 128 : (k + 1) * 128] = input_weight[:, at : at + 128]
    rows_small = [gains[k : k + 1] for k in range(2)] + [biases[k : k + 1] for k in range(6)]
    line = jnp.concatenate(rows_small + [hidden_bias[...]], axis=1)
    for i in range(8):
        win[i, shard : shard + 16] = jnp.broadcast_to(line, (16, line.shape[1]))
    W[z, b] = win[b]
    codes = (segment[...] + 4 * (1 - present[...])).astype(HIGH).astype(LOW)
    codes = jnp.concatenate([codes[k : k + 1] for k in range(slots)], axis=1)
    X[b, pl.ds(count, 16), 0:count] = jnp.broadcast_to(codes, (16, count))
    X[b, pl.ds(count, 16), count:width] = jnp.zeros((16, width - count), LOW)
    greet([(b ^ d, z) for d in range(1, 8)] + [(b, z ^ d) for d in range(1, 4)])
    s = Sender(send, recv)
    to_x, to_y, to_core = (bx, z), (by, z), (bc, z)

    def token_core(src, bb):
        return s.plan(src, X.at[bb], to_core, X.at[bb ^ 1])

    def to_z(d):
        return b, z ^ d

    def hops(F, src, zz):
        near = [
            s.plan(src, F.at[b, zz], to_x, F.at[bx, zz]),
            s.plan(src, F.at[b, zz], to_y, F.at[by, zz]),
        ]
        one, two = half(F.at[bx, zz], 0), half(F.at[by, zz], 1)
        far = [
            s.plan(one, one, to_y, half(F.at[bd, zz], 0)),
            s.plan(two, two, to_x, half(F.at[bd, zz], 1)),
        ]
        return near, far

    def planes(F, src, bb):
        pair = [s.plan(src, F.at[bb, z], to_z(d), F.at[bb, z ^ d]) for d in (1, 2)]
        on = F.at[bb, z ^ 2]
        return pair + [s.plan(on, on, to_z(1), F.at[bb, z ^ 3])]

    def to_sibling(F, src, bb, zz):
        return s.plan(src, F.at[bb, zz], to_core, F.at[bb ^ 1, zz])

    places = (b, bx, by, bd)
    z1 = planes(W1, w1, b)
    hop1 = [hops(W1, W1.at[b, z ^ d] if d else w1, z ^ d) for d in range(4)]
    hop2 = hops(W2, w2, z)
    z2 = [planes(W2, W2.at[bb, z] if i else w2, bb) for i, bb in enumerate(places)]
    core1, core2 = (
        {
            (i, d): to_sibling(F, F.at[bb, z ^ d] if i or d else own, bb, z ^ d)
            for i, bb in enumerate(places)
            for d in range(4)
        }
        for F, own in ((W1, w1), (W2, w2))
    )

    def start(*copies):
        for copy in copies:
            copy.go()

    def first(d):
        if d in (1, 3):
            z1[d - 1].wait_recv()
        start(*hop1[d][0], core1[0, d])

    def second(d):
        near, far = hop1[d]
        for i in (0, 1):
            near[i].wait_recv()
            start(far[i], core1[1 + i, d])

    def third(d):
        for copy in hop1[d][1]:
            copy.wait_recv()
        core1[3, d].go()

    def spread(i):
        start(z2[i][0], z2[i][1], core2[i, 0])

    def second2():
        near, far = hop2
        for i in (0, 1):
            near[i].wait_recv()
            far[i].go()
            spread(1 + i)

    def third2():
        for copy in hop2[1]:
            copy.wait_recv()
        spread(3)

    def arrive2(i):
        z2[i][1].wait_recv()
        start(z2[i][2], core2[i, 2])
        z2[i][0].wait_recv()
        core2[i, 1].go()

    def last2(i):
        z2[i][2].wait_recv()
        core2[i, 3].go()

    columns = [
        s.go(win.at[b ^ d], W.at[z, b], (b ^ d, z), W.at[z, b ^ d]) for d in range(1, 8)
    ]
    locs[0].wait()
    token_x = s.go(X.at[b], X.at[b], to_x, X.at[bx])
    token_y = s.go(X.at[b], X.at[b], to_y, X.at[by])
    token_c = token_core(X.at[b], b)
    token_c.go()
    for copy in locs[1:3]:
        copy.wait()
    local(w1, W1.at[b, z])
    start(z1[0], z1[1])
    for copy in columns:
        copy.wait_recv()
    for i in range(8):
        small[z, i : i + 1] = W[z, i, 32:33]
    trimmed = lambda zz: W.at[zz, :, pl.ds(0, 32)]
    columns, vectors = (
        [s.plan(at(z), at(z), to_z(d), at(z ^ d)) for d in (1, 2)]
        + [s.plan(at(z ^ 2), at(z ^ 2), to_z(1), at(z ^ 3))]
        for at in (trimmed, lambda zz: small.at[zz])
    )
    start(*columns[:2], *vectors[:2])
    spread(0)
    token_x.wait_recv()
    piece = half(X.at[bx], 0)
    token_one = s.go(piece, piece, to_y, half(X.at[bd], 0))
    token_xc = token_core(X.at[bx], bx)
    token_xc.go()
    token_y.wait_recv()
    piece = half(X.at[by], 1)
    token_two = s.go(piece, piece, to_x, half(X.at[bd], 1))
    token_yc = token_core(X.at[by], by)
    token_yc.go()
    token_dc = token_core(X.at[bd], bd)
    start(*hop2[0])
    columns[1].wait_recv()
    columns[2].go()
    vectors[1].wait_recv()
    vectors[2].go()
    z1[1].wait_recv()
    z1[2].go()
    for copy in (columns[0], columns[2], vectors[0], vectors[2]):
        copy.wait_recv()
    for i in range(8):
        for j in range(4):
            at = (i * 4 + j) * 32
            wfull[at : at + 32] = W[j, i, 0:32]
    spread_vectors(small, par, hid)
    chosen = lax.broadcasted_iota(jnp.int32, (16, 128), 0) == b
    bias = [[], []]
    for j in range(4):
        row = jnp.where(chosen, small[j, :, 0:128].astype(HIGH), 0.0)
        row = jnp.sum(row, axis=0, keepdims=True)
        bias[0].append(row[:, 64:96])
        bias[1].append(row[:, 96:128])
    bias = [jnp.concatenate(parts, axis=1) for parts in bias]

    def mix(i):
        pltpu.make_async_copy(X.at[i], X_out.at[i], osem.at[i]).start()
        mixed = product(X[i, 0:count], wfull[...])
        codes = jnp.broadcast_to(X[i, count : count + 1, 0:count].astype(HIGH), (128, count)).T
        queries, keys, values = split_heads(mixed, bias, codes.astype(jnp.int32))
        for head in (0, 1):
            qh[head, i] = queries[head].reshape(slots, rows, 128)
            kh[head, i] = keys[head].reshape(slots, rows, 128)
        v[i] = values.reshape(slots, rows, 128)

    mix(b)
    token_c.wait_recv()
    mix(bc)
    mix(bx)
    token_xc.wait_recv()
    mix(bx ^ 1)
    mix(by)
    token_one.wait_recv()
    token_two.wait_recv()
    token_dc.go()
    first(0)
    first(2)
    first(1)
    second2()
    first(3)
    token_yc.wait_recv()
    mix(by ^ 1)
    mix(bd)
    token_dc.wait_recv()
    mix(bd ^ 1)
    arrive2(0)

    def piece_of(slot):
        return pl.ds(pl.multiple_of(slot * rows, rows), rows)

    def send_att(slot, d):
        return pltpu.make_async_remote_copy(
            src_ref=att.at[b ^ d, slot],
            dst_ref=rows_att.at[b, piece_of(slot)],
            send_sem=asend.at[slot * 8 + d],
            recv_sem=arecv.at[slot * 8 + d],
            device_id=(b ^ d, z),
            device_id_type=MESH,
        )

    def keep_att(slot):
        return pltpu.make_async_copy(
            att.at[b, slot], rows_att.at[b, piece_of(slot)], osem.at[8 + slot]
        )

    events = {
        0: (second, 0),
        1: (third2,),
        2: (second, 2),
        4: (second, 1),
        5: (arrive2, 1),
        6: (arrive2, 2),
        7: (third, 0),
        9: (second, 3),
        10: (arrive2, 3),
        12: (third, 2),
        14: (third, 1),
    }
    late_events = {1: (last2, 0), 3: (last2, 1), 5: (last2, 2), 7: (last2, 3)}

    @pl.loop(0, 8 * slots)
    def _(step):
        slot, d = step // 8, (step + 1) % 8
        i = b ^ d
        keys = [rows_of(kh[head, :, slot]) for head in (0, 1)]
        out, logs = attend_tile([qh[head, i, slot] for head in (0, 1)], keys, rows_of(v[:, slot]))
        att[i, slot] = out
        lse[slot, :, pl.ds(pl.multiple_of(i * rows, rows), rows)] = logs

        @pl.when(d != 0)
        def _():
            send_att(slot, d).start()

        @pl.when(d == 0)
        def _():
            keep_att(slot).start()

        for at, (event, *what) in events.items():
            pl.when(step == at)(functools.partial(event, *what))

    third(3)
    for copy in core1.values():
        copy.wait_recv()
    locs[4].wait()
    chunk = 512
    steps = hidden // chunk

    def load(c, size=chunk):
        cols = pl.ds(pl.multiple_of(c * chunk, chunk), size)
        return pltpu.make_async_copy(W1.at[:, :, :, cols], w1v.at[:, :, :, cols], wsem.at[c])

    load(steps, width).start()
    for c in range(steps):
        load(c).start()
    for slot in range(slots):
        keep_att(slot).wait()
        for d in range(1, 8):
            pltpu.make_async_remote_copy(
                src_ref=rows_att.at[b ^ d, piece_of(slot)],
                dst_ref=rows_att.at[b ^ d, piece_of(slot)],
                send_sem=asend.at[slot * 8 + d],
                recv_sem=arecv.at[slot * 8 + d],
                device_id=(b ^ d, z),
                device_id_type=MESH,
            ).wait_recv()
    branch_in[...] = jnp.concatenate([rows_att[i] for i in range(8)], axis=1)
    load(steps, width).wait()
    out_w = w1v[:, :, :, hidden:].reshape(width, width)
    branch = product(branch_in[...], out_w) + par[4:5]
    normal, inverse = normalize(X[b, 0:count].astype(HIGH) + branch)
    n1[...] = normal
    r1[...] = jnp.broadcast_to(inverse, r1.shape)
    normed = (normal * par[0:1] + par[5:6]).astype(LOW)
    normed_low[...] = normed
    normed_t[...] = normed.T

    def store(c, ref, out, which):
        cols = pl.ds(pl.multiple_of(c * chunk, chunk), chunk)
        return pltpu.make_async_copy(ref.at[:, cols], out.at[:, cols], csem.at[which, c])

    @pl.loop(0, steps)
    def _(c):
        cols = pl.ds(pl.multiple_of(c * chunk, chunk), chunk)
        load(c).wait()
        pre = product(normed_low[...], w1v[:, :, :, cols].reshape(width, chunk))
        value, rate = gelu_parts(pre + hid[:, cols], quick_reciprocal)
        act[:, cols] = value.astype(LOW)
        slope[:, cols] = rate.astype(LOW)
        store(c, act, act_out, 0).start()
        store(c, slope, slope_out, 1).start()
        for at, (event, *what) in late_events.items():
            pl.when(c == at)(functools.partial(event, *what))

    for copy in core2.values():
        copy.wait_recv()
    for slot in range(slots):
        for d in range(1, 8):
            send_att(slot, d).wait_send()
    for c in range(steps):
        store(c, act, act_out, 0).wait()
        store(c, slope, slope_out, 1).wait()
    s.drain()
    locs[3].wait()
    for i in range(8):
        pltpu.make_async_copy(X.at[i], X_out.at[i], osem.at[i]).wait()


def in_hbm(count):
    return [pl.BlockSpec(memory_space=pl.ANY)] * count


def pair_of_semaphores(count):
    return [pltpu.SemaphoreType.DMA((count,)), pltpu.SemaphoreType.DMA((count,))]


def front(x, segment, present, input_weight, gains, biases, hidden_bias, expand, out_w, w2):
    slots = segment.shape[0]
    count, width = x.shape
    rows, hidden = count // slots, expand.shape[1]
    shard = expand.shape[0]
    shape = lambda *s: jax.ShapeDtypeStruct(s, LOW)
    wide = lambda *s: jax.ShapeDtypeStruct(s, HIGH)
    vmem = pl.BlockSpec(memory_space=pltpu.VMEM)
    return pl.pallas_call(
        front_kernel,
        out_shape=(
            shape(8, count + 16, width),
            shape(8, 4, shard, hidden + width),
            shape(8, 4, *w2.shape),
            shape(count, hidden),
            shape(count, hidden),
            shape(width, 384),
            shape(4, 16, 384),
            shape(2, 8, slots, rows, 128),
            shape(2, 8, slots, rows, 128),
            shape(8, slots, rows, 128),
            shape(8, slots, rows, 128),
            wide(slots, 8, 8 * rows),
            shape(count, width),
            wide(count, width),
            wide(count, 128),
            shape(width, count),
            wide(8, width),
        ),
        in_specs=in_hbm(1) + [vmem] * 6 + in_hbm(3),
        out_specs=tuple(in_hbm(5)) + (vmem,) * 12,
        scratch_shapes=[
            pltpu.VMEM((count, width), LOW),
            pltpu.VMEM((8, count + 16, width), LOW),
            pltpu.VMEM((4, 8, shard + 16, 384), LOW),
            pltpu.VMEM((8, shard + 16, 384), LOW),
            pltpu.VMEM((shard, hidden + width), LOW),
            pltpu.VMEM((8, count, 128), LOW),
            pltpu.VMEM((8, 4, shard, hidden + width), LOW),
            pltpu.VMEM((count, hidden), LOW),
            pltpu.VMEM((count, hidden), LOW),
            pltpu.VMEM((1, hidden), HIGH),
        ]
        + pair_of_semaphores(116)
        + pair_of_semaphores(8 * slots)
        + [pltpu.SemaphoreType.DMA((5,)), pltpu.SemaphoreType.DMA((8 + slots,))]
        + [pltpu.SemaphoreType.DMA((hidden // 512 + 1,)), pltpu.SemaphoreType.DMA((2, hidden // 512))],
        compiler_params=pltpu.CompilerParams(
            collective_id=1, has_side_effects=True, vmem_limit_bytes=VMEM_LIMIT
        ),
        name="front",
    )(x, segment, present, input_weight, gains, biases, hidden_bias, expand, out_w, w2)


def add_rows(out, one, two):
    @pl.loop(0, one.shape[0] // 16)
    def _(i):
        rows = pl.ds(pl.multiple_of(i * 16, 16), 16)
        out[rows, :] = one[rows, :] + two[rows, :]


def sum_rows(out, *terms):
    @pl.loop(0, out.shape[0] // 16)
    def _(i):
        rows = pl.ds(pl.multiple_of(i * 16, 16), 16)
        total = terms[0][rows, :].astype(HIGH)
        for term in terms[1:]:
            total = total + term[rows, :].astype(HIGH)
        out[rows, :] = total


class Reducer:
    ORDER = (3, 2, 1, 0)
    COPIES = 16 + 4 * 6 + 3

    def __init__(self, s, share, out, C, H, Q, Z, S=None, lsem=None):
        b, z = position()
        to_x, to_y, to_core = (b ^ 2, z), (b ^ 4, z), (b ^ 1, z)
        self.out, self.C, self.H, self.Q, self.Z = out, C, H, Q, Z
        self.at = at = lambda e, d: share(b ^ (2 * e), z ^ d) if S is None else S.at[e, d]
        self.mine, self.other, self.halves, self.ahead, self.rest, self.last = ({} for _ in range(6))
        for d in self.ORDER:
            for e in (3, 1, 2, 0):
                if S is not None:
                    self.mine[d, e] = pltpu.make_async_copy(
                        share(b ^ (2 * e), z ^ d), S.at[e, d], lsem.at[d * 4 + e]
                    )
                self.other[d, e] = s.plan(
                    share(b ^ 1 ^ (2 * e), z ^ d), C.at[e, d], to_core, C.at[e, d]
                )

            def send(e, part, to, where):
                return s.plan(half(at(e, d), part), where, to, where)

            self.halves[d] = [send(3, 0, to_x, H.at[d, 0]), send(3, 1, to_y, H.at[d, 1])]
            self.ahead[d] = [
                send(2, 1, to_y, half(Q.at[d, 1], 1)),
                send(1, 0, to_x, half(Q.at[d, 0], 0)),
            ]
            self.rest[d] = [
                send(2, 0, to_y, half(Q.at[d, 1], 0)),
                send(1, 1, to_x, half(Q.at[d, 0], 1)),
            ]
            if d:
                to = (b, z ^ (2 if d == 2 else 1))
                self.last[d] = s.plan(at(0, d), Z.at[d - 1], to, Z.at[d - 1])

    def start(self):
        for d in self.ORDER:
            for e in (3, 1, 2, 0):
                self.mine[d, e].start()
                self.other[d, e].go()

    def give(self, e):
        for d in self.ORDER:
            self.other[d, e].go()

    def fold(self, d, chips=(3, 1, 2, 0)):
        for e in chips:
            if self.mine:
                self.mine[d, e].wait()
            self.other[d, e].wait_recv()
            add_rows(self.at(e, d), self.at(e, d), self.C.at[e, d])
            for copy in {3: self.halves[d], 1: self.ahead[d][1:], 2: self.ahead[d][:1], 0: []}[e]:
                copy.go()

    def fold_chip(self, e):
        for d in self.ORDER:
            self.fold(d, (e,))

    def relay(self, d):
        for i, e in ((0, 2), (1, 1)):
            self.halves[d][i].wait_recv()
            part = half(self.at(e, d), i)
            add_rows(part, part, self.H.at[d, i])
            self.rest[d][i].go()

    def collect(self, d):
        for copy in self.ahead[d] + self.rest[d]:
            copy.wait_recv()
        total = self.at(0, d)
        for i in (0, 1):
            add_rows(total, total, self.Q.at[d, i])
        if d == 2:
            self.last[3].wait_recv()
            add_rows(total, total, self.Z.at[2])
        if d:
            self.last[d].go()

    def total(self):
        for d in (1, 2):
            self.last[d].wait_recv()
        sum_rows(self.out, self.at(0, 0), self.Z.at[0], self.Z.at[1])

    LEAD = (((4, 4), 1), ((4, 2), 2), ((4, 2), 1), ((3,), 1))

    @classmethod
    def scratch(cls, rows, columns, in_place=False):
        shapes = [pltpu.VMEM((*n, rows // cut, columns), LOW) for n, cut in cls.LEAD]
        if in_place:
            return shapes
        return shapes + [pltpu.VMEM((4, 4, rows, columns), LOW), pltpu.SemaphoreType.DMA((16,))]


class ReducerAlongZ(Reducer):
    COPIES = 16 + 4 * 3 + 6

    def __init__(self, s, share, out, C, H, Q, Z, S=None, lsem=None):
        b, z = position()
        to_x, to_y, to_core = (b ^ 2, z), (b ^ 4, z), (b ^ 1, z)
        self.out, self.C, self.H, self.Q, self.Z = out, C, H, Q, Z
        self.at = at = lambda e, d: share(b ^ (2 * e), z ^ d) if S is None else S.at[e, d]
        self.mine, self.other, self.along = {}, {}, {}
        for e in (3, 1, 2, 0):
            for d in (3, 2, 1, 0):
                if S is not None:
                    self.mine[e, d] = pltpu.make_async_copy(
                        share(b ^ (2 * e), z ^ d), S.at[e, d], lsem.at[d * 4 + e]
                    )
                self.other[e, d] = s.plan(
                    share(b ^ 1 ^ (2 * e), z ^ d), C.at[e, d], to_core, C.at[e, d]
                )
                if d:
                    to = (b, z ^ (2 if d == 2 else 1))
                    self.along[e, d] = s.plan(at(e, d), Z.at[e, d - 1], to, Z.at[e, d - 1])

        def send(e, part, to, where):
            return s.plan(half(at(e, 0), part), where, to, where)

        self.halves = [send(3, 0, to_x, H.at[0]), send(3, 1, to_y, H.at[1])]
        self.ahead = [
            send(2, 1, to_y, half(Q.at[1], 1)),
            send(1, 0, to_x, half(Q.at[0], 0)),
        ]
        self.rest = [
            send(2, 0, to_y, half(Q.at[1], 0)),
            send(1, 1, to_x, half(Q.at[0], 1)),
        ]

    def start(self):
        for at in self.mine:
            self.mine[at].start()
            self.other[at].go()

    def give(self, e):
        for d in (3, 2, 1, 0):
            self.other[e, d].go()

    def fold(self, e):
        for d in (3, 1, 2, 0):
            if self.mine:
                self.mine[e, d].wait()
            self.other[e, d].wait_recv()
            add_rows(self.at(e, d), self.at(e, d), self.C.at[e, d])
            if d in (1, 3):
                self.along[e, d].go()

    def relay(self, e):
        self.along[e, 3].wait_recv()
        add_rows(self.at(e, 2), self.at(e, 2), self.Z.at[e, 2])
        self.along[e, 2].go()

    def collect(self, e):
        total = self.at(e, 0)
        for d in (1, 2):
            self.along[e, d].wait_recv()
            add_rows(total, total, self.Z.at[e, d - 1])
        for copy in {3: self.halves, 1: self.ahead[1:], 2: self.ahead[:1], 0: []}[e]:
            copy.go()

    def cross(self):
        for i, e in ((0, 2), (1, 1)):
            self.halves[i].wait_recv()
            part = half(self.at(e, 0), i)
            add_rows(part, part, self.H.at[i])
            self.rest[i].go()

    def total(self):
        for copy in self.ahead + self.rest:
            copy.wait_recv()
        sum_rows(self.out, self.at(0, 0), self.Q.at[0], self.Q.at[1])

    LEAD = (((4, 4), 1), ((2,), 2), ((2,), 1), ((4, 3), 1))


def attend_kernel(qh_ref, kh_ref, v_ref, out_ref, lse_ref):
    keys = [rows_of(kh_ref[head, :, 0]) for head in (0, 1)]
    out_ref[0, 0], lse_ref[0] = attend_tile(
        [qh_ref[head, 0, 0] for head in (0, 1)], keys, rows_of(v_ref[:, 0])
    )


def attend(qh, kh, v):
    blocks, slots, rows, lanes = v.shape
    tile = pl.BlockSpec((1, 1, rows, lanes), lambda s, i: (i, s, 0, 0))
    tiles = pl.BlockSpec((2, 1, 1, rows, lanes), lambda s, i: (0, i, s, 0, 0))
    whole = pl.BlockSpec((blocks, 1, rows, lanes), lambda s, i: (0, s, 0, 0))
    wholes = pl.BlockSpec((2, blocks, 1, rows, lanes), lambda s, i: (0, 0, s, 0, 0))
    return pl.pallas_call(
        attend_kernel,
        grid=(slots, blocks),
        out_shape=(
            jax.ShapeDtypeStruct(v.shape, LOW),
            jax.ShapeDtypeStruct((slots, 8, blocks * rows), HIGH),
        ),
        in_specs=[tiles, wholes, whole],
        out_specs=(tile, pl.BlockSpec((1, 8, rows), lambda s, i: (s, 0, i))),
        compiler_params=pltpu.CompilerParams(vmem_limit_bytes=VMEM_LIMIT),
        name="attend",
    )(qh, kh, v)


def row_products(out, grad):
    pick = (lax.broadcasted_iota(jnp.int32, (8, 128), 0) == 0) == first_lanes((8, 128))
    return lax.dot_general(
        pick.astype(HIGH),
        out.astype(HIGH) * grad.astype(HIGH),
        (((1,), (1,)), ((), ())),
        precision=lax.Precision.HIGHEST,
        preferred_element_type=HIGH,
    )


def attend_back_tile(queries, keys, values, grads, logs, delta, acc):
    zeros = jnp.zeros_like(grads)
    mine = first_lanes(grads.shape)
    dk, dv = [], 0.0
    for head in (0, 1):
        grad = jnp.where(mine == (head == 0), grads, zeros)
        probs = jnp.exp(product_nt(keys[head], queries[head]) - logs[head : head + 1])
        pushed = product_nt(values, grad)
        d_scores = (probs * (pushed - delta[head : head + 1])).astype(LOW)
        dv = dv + product(probs.astype(LOW), grad)
        dk.append(product(d_scores, queries[head]))
        keys_t = keys[head].T[head * 64 : head * 64 + 64]
        acc[head * 64 : head * 64 + 64, :] += product(keys_t, d_scores)
    return jnp.where(first_lanes(dk[0].shape), dk[0], dk[1]).astype(LOW), dv.astype(LOW)


def attend_back_kernel(
    qh_ref, o_ref, g_ref, lse_ref, kh_ref, v_ref, dq_ref, dk_ref, dv_ref, acc, delta
):
    tile = pl.program_id(1)
    blocks, _, rows, _ = g_ref.shape
    grads = rows_of(g_ref[:, 0])

    @pl.when(tile == 0)
    def _():
        acc[...] = jnp.zeros_like(acc)
        delta[...] = row_products(rows_of(o_ref[:, 0]), grads)

    dk_ref[0, 0], dv_ref[0, 0] = attend_back_tile(
        [rows_of(qh_ref[head, :, 0]) for head in (0, 1)],
        [kh_ref[head, 0, 0] for head in (0, 1)],
        v_ref[0, 0],
        grads,
        lse_ref[0],
        delta[...],
        acc,
    )

    @pl.when(tile == blocks - 1)
    def _():
        dq_ref[:, 0] = (acc[...].T * 0.125).astype(LOW).reshape(blocks, rows, 128)


def attend_back(qh, o, g, lse, kh, v):
    blocks, slots, rows, lanes = v.shape
    tile = pl.BlockSpec((1, 1, rows, lanes), lambda s, i: (i, s, 0, 0))
    tiles = pl.BlockSpec((2, 1, 1, rows, lanes), lambda s, i: (0, i, s, 0, 0))
    whole = pl.BlockSpec((blocks, 1, rows, lanes), lambda s, i: (0, s, 0, 0))
    wholes = pl.BlockSpec((2, blocks, 1, rows, lanes), lambda s, i: (0, 0, s, 0, 0))
    logs = pl.BlockSpec((1, 8, blocks * rows), lambda s, i: (s, 0, 0))
    shape = jax.ShapeDtypeStruct(v.shape, LOW)
    return pl.pallas_call(
        attend_back_kernel,
        grid=(slots, blocks),
        out_shape=(shape,) * 3,
        in_specs=[wholes, whole, whole, logs, tiles, tile],
        out_specs=(whole, tile, tile),
        scratch_shapes=[pltpu.VMEM((lanes, blocks * rows), HIGH), pltpu.VMEM((8, blocks * rows), HIGH)],
        compiler_params=pltpu.CompilerParams(vmem_limit_bytes=VMEM_LIMIT),
        name="attend_back",
    )(qh, o, g, lse, kh, v)


class TokenSums:
    COPIES = 4 + 2 + 4

    def __init__(self, s, piece, sent, C, S, H, Q, A):
        b, z = position()
        to_x, to_y, to_core = (b ^ 2, z), (b ^ 4, z), (b ^ 1, z)
        self.b, self.piece = b, piece
        self.sent, self.C, self.S, self.H, self.Q, self.A = sent, C, S, H, Q, A
        self.other = [s.plan(sent.at[e], C.at[e], to_core, C.at[e]) for e in range(4)]

        def send(e, part, to, where):
            return s.plan(half(S.at[e - 1], part), where, to, where)

        self.halves = [send(3, 0, to_x, H.at[0]), send(3, 1, to_y, H.at[1])]
        self.ahead = [
            send(2, 1, to_y, half(Q.at[1], 1)),
            send(1, 0, to_x, half(Q.at[0], 0)),
        ]
        self.rest = [
            send(2, 0, to_y, half(Q.at[1], 0)),
            send(1, 1, to_x, half(Q.at[0], 1)),
        ]

    def give(self, e):
        self.sent[e] = self.piece(self.b ^ 1 ^ (2 * e)).astype(LOW)
        self.other[e].go()

    def take(self, e):
        mine = self.piece(self.b ^ (2 * e))
        self.other[e].wait_recv()
        mine = mine + self.C[e].astype(HIGH)
        if e:
            self.S[e - 1] = mine.astype(LOW)
        else:
            self.A[...] = mine
        for copy in {3: self.halves, 1: self.ahead[1:], 2: self.ahead[:1], 0: []}[e]:
            copy.go()

    def relay(self):
        for i, e in ((0, 2), (1, 1)):
            self.halves[i].wait_recv()
            part = half(self.S.at[e - 1], i)
            add_rows(part, part, self.H.at[i])
            self.rest[i].go()

    def total(self):
        for copy in self.ahead + self.rest:
            copy.wait_recv()
        return self.A[...] + self.Q[0].astype(HIGH) + self.Q[1].astype(HIGH)

    @staticmethod
    def scratch(rows, width):
        low = lambda *s: pltpu.VMEM((*s, width), LOW)
        return [low(4, rows), low(4, rows), low(3, rows), low(2, rows // 2), low(2, rows)] + [
            pltpu.VMEM((rows, width), HIGH)
        ]


def back_kernel(
    d_att,
    qh_in,
    kh_in,
    v_in,
    att_in,
    lse_in,
    w_in,
    first,
    g1,
    dq,
    dk,
    dv,
    o1,
    out_o,
    tok,
    qh,
    kh,
    v,
    att,
    lse,
    w,
    first_rows,
    tail,
    grads,
    acc,
    delta,
    lsem,
    send,
    recv,
    *buffers,
):
    b, z = position()
    blocks, slots, rows, _ = v.shape
    loads = [
        pltpu.make_async_copy(src, dst, lsem.at[i])
        for i, (src, dst) in enumerate(
            (
                (d_att.at[b], grads.at[b]),
                (qh_in, qh),
                (kh_in, kh),
                (v_in, v),
                (att_in, att),
                (lse_in, lse),
                (w_in, w),
                (first.at[pl.ds(0, rows)], first_rows),
            )
        )
    ]
    for load in loads:
        load.start()
    greet([(b ^ d, z) for d in range(1, 8)] + [(b, z ^ d) for d in (1, 2, 3)])
    s = Sender(send, recv)
    arriving = [
        [
            s.go(d_att.at[b ^ d, part], grads.at[b, part], (b ^ d, z), grads.at[b ^ d, part])
            for d in range(1, 8)
        ]
        for part in (pl.ds(slot * rows, rows) for slot in range(slots))
    ]

    def arrive(slot):
        for copy in arriving[slot]:
            copy.wait_recv()

    most = o1.shape[1] - tail.shape[1] + out_o.shape[1]
    sums = Reducer(
        s, lambda bb, zz: g1.at[bb, zz, :, pl.ds(0, most)], o1.at[:, pl.ds(0, most)], *buffers[:6]
    )
    late = ReducerAlongZ(
        s, lambda bb, zz: g1.at[bb, zz, :, pl.ds(most, tail.shape[1])], tail, *buffers[6:12]
    )

    def piece(i):
        mixed = jnp.concatenate([ref[i, 0] for ref in (dq, dk, dv)], axis=-1)
        return product_nt(mixed, w[...])

    tokens = TokenSums(s, piece, *buffers[12:])
    late.start()
    sums.start()
    late.fold(3)
    late.fold(1)
    late.fold(2)
    sums.fold(3)
    arrive(0)
    for load in loads:
        load.wait()

    def grad_rows(slot):
        part = pl.ds(pl.multiple_of(slot * rows, rows), rows)
        return rows_of(grads[:, part])

    events = {
        0: [(late.fold, 0)],
        1: [(sums.fold, 2), (late.relay, 3)],
        2: [(late.relay, 1)],
        3: [(sums.fold, 1), (sums.relay, 3)],
        4: [(late.relay, 2)],
        5: [(late.relay, 0), (sums.relay, 2)],
        6: [(sums.fold, 0), (late.collect, 3), (arrive, 1)],
        7: [(sums.collect, 3), (late.collect, 1)],
        8: [(sums.relay, 1), (late.collect, 2), (tokens.give, 3), (tokens.give, 2)],
        9: [(sums.collect, 2), (tokens.give, 1), (tokens.take, 3)],
        10: [(tokens.give, 0), (tokens.take, 2)],
        11: [(sums.relay, 0), (late.cross,), (tokens.take, 1)],
        12: [(tokens.take, 0)],
        13: [(sums.collect, 1), (tokens.relay,)],
        15: [(late.collect, 0)],
    }

    @pl.loop(0, blocks * slots)
    def _(step):
        slot, tile = step // blocks, step % blocks
        slot_grads = grad_rows(slot)

        @pl.when(tile == 0)
        def _():
            acc[...] = jnp.zeros_like(acc)
            delta[...] = row_products(rows_of(att[:, slot]), slot_grads)

        dk[tile, slot], dv[tile, slot] = attend_back_tile(
            [rows_of(qh[head, :, slot]) for head in (0, 1)],
            [kh[head, tile, slot] for head in (0, 1)],
            v[tile, slot],
            slot_grads,
            lse[slot],
            delta[...],
            acc,
        )

        @pl.when(tile == blocks - 1)
        def _():
            dq[:, slot] = (acc[...].T * 0.125).astype(LOW).reshape(blocks, rows, 128)

        for at, some in events.items():

            @pl.when(step == at)
            def _(some=some):
                for event, *what in some:
                    event(*what)

    sums.collect(0)
    late.total()
    rest = o1.shape[1] - most
    o1[:, most:] = tail[:, :rest]
    out_o[...] = tail[:, rest:]
    sums.total()
    tok[...] = first_rows[...] + tokens.total()
    s.drain()


def back(d_att, qh, kh, v, att, lse, w, d_first, g1):
    blocks, slots, rows, lanes = v.shape
    shape = jax.ShapeDtypeStruct
    shard, total = g1.shape[2:]
    width = w.shape[0]
    late = 2 * width
    vmem = pl.BlockSpec(memory_space=pltpu.VMEM)
    scratch = lambda a: pltpu.VMEM(a.shape, a.dtype)
    return pl.pallas_call(
        back_kernel,
        out_shape=(shape(v.shape, LOW),) * 3
        + (
            shape((shard, total - width), HIGH),
            shape((shard, width), HIGH),
            shape((rows, width), HIGH),
        ),
        in_specs=in_hbm(9),
        out_specs=(vmem,) * 6,
        scratch_shapes=[scratch(a) for a in (qh, kh, v, att, lse, w)]
        + [
            pltpu.VMEM((rows, width), HIGH),
            pltpu.VMEM((shard, late), HIGH),
            pltpu.VMEM(d_att.shape, LOW),
            pltpu.VMEM((lanes, blocks * rows), HIGH),
            pltpu.VMEM((8, blocks * rows), HIGH),
            pltpu.SemaphoreType.DMA((8,)),
        ]
        + pair_of_semaphores(7 * slots + Reducer.COPIES + ReducerAlongZ.COPIES + TokenSums.COPIES)
        + Reducer.scratch(shard, total - late)
        + ReducerAlongZ.scratch(shard, late)
        + TokenSums.scratch(rows, width),
        compiler_params=pltpu.CompilerParams(
            collective_id=2, has_side_effects=True, vmem_limit_bytes=VMEM_LIMIT
        ),
        name="back",
    )(d_att, qh, kh, v, att, lse, w, d_first, g1)


def column_sum(block):
    return jnp.sum(block.astype(HIGH), axis=0, keepdims=True)


def middle_kernel(
    chunk,
    small_rows,
    remote,
    att,
    n1,
    r1,
    normed_t,
    cot_ref,
    par_ref,
    act_hbm,
    slope_hbm,
    w1_hbm,
    w2_hbm,
    out_ref,
    first_ref,
    d_att_ref,
    small_ref,
    g1_hbm,
    g2_out,
    w1,
    w2,
    act,
    slope,
    acc,
    low,
    sums_ref,
    d_hid_ref,
    wsem,
    gsem,
    *buffers,
):
    hidden, width = w2.shape
    steps = hidden // chunk
    pieces, _, held = d_att_ref.shape

    def columns(c):
        return pl.ds(pl.multiple_of(c * chunk, chunk), chunk)

    def load1(c):
        return pltpu.make_async_copy(w1_hbm.at[:, columns(c)], w1.at[:, columns(c)], wsem.at[0, c])

    def load2(c):
        return pltpu.make_async_copy(w2_hbm.at[columns(c)], w2.at[columns(c)], wsem.at[1, c])

    def load_act(c):
        return pltpu.make_async_copy(act_hbm.at[:, columns(c)], act.at[:, columns(c)], wsem.at[2, c])

    def load_slope(c):
        return pltpu.make_async_copy(
            slope_hbm.at[:, columns(c)], slope.at[:, columns(c)], wsem.at[3, c]
        )

    if remote:
        b, z = position()
        barrier = pltpu.get_barrier_semaphore()
        peers = [(b ^ d, z) for d in (1, 2, 4)] + [(b, z ^ d) for d in (1, 2)]
        for peer in peers:
            pl.semaphore_signal(barrier, inc=1, device_id=peer, device_id_type=MESH)
    last = pl.ds(hidden, width)
    for c in range(steps):
        load_act(c).start()
        load2(c).start()
    for c in range(steps):
        load_slope(c).start()
        load1(c).start()
    load_out = pltpu.make_async_copy(w1_hbm.at[:, last], w1.at[:, last], wsem.at[0, steps])
    load_out.start()
    gain1, gain2 = par_ref[0:1], par_ref[1:2]
    bias = lambda i: par_ref[2 + i : 3 + i]
    acc[...] = n1[...] * gain1 + (bias(3) + bias(4))

    @pl.loop(0, steps)
    def _(c):
        load_act(c).wait()
        load2(c).wait()
        acc[...] += product(act[:, columns(c)], w2[columns(c), :])

    normal, inverse2 = normalize(acc[...])
    out_ref[...] = (normal * gain2 + bias(5)).astype(LOW)
    cot = cot_ref[...].astype(HIGH)
    d_second = normalize_back(cot * gain2, normal, inverse2)
    low[...] = d_second.astype(LOW)
    acc[...] = d_second
    sums_ref[1:2] = column_sum(cot * normal)
    sums_ref[4:5] = column_sum(low[...])
    sums_ref[5:6] = column_sum(cot)

    def store1(c):
        return pltpu.make_async_copy(w1.at[:, columns(c)], g1_hbm.at[:, columns(c)], gsem.at[0, c])

    def store2(c):
        return pltpu.make_async_copy(w2.at[columns(c)], g2_out.at[columns(c)], gsem.at[1, c])

    first_events, second_events = {}, {}
    if remote:
        pl.semaphore_wait(barrier, len(peers))
        s = Sender(*buffers[:2])
        each = w2.shape[0] // (8 * 4)
        cut = buffers[2].shape[2]
        plain = lambda bb, zz: w2.at[pl.ds(pl.multiple_of((bb * 4 + zz) * each, each), cut)]
        upper = lambda bb, zz: w2.at[
            pl.ds(pl.multiple_of((bb * 4 + zz) * each + cut, 16), each - cut)
        ]
        sums = Reducer(s, plain, g2_out.at[pl.ds(0, cut)], *buffers[2:6])
        late = ReducerAlongZ(s, upper, g2_out.at[pl.ds(cut, each - cut)], *buffers[6:])
        first_events = {
            0: [(late.give, 3), (sums.give, 3)],
            2: [(late.give, 2), (sums.give, 2)],
            3: [(late.fold, 3), (sums.fold_chip, 3)],
            4: [(late.give, 1), (sums.give, 1)],
            6: [(late.give, 0), (sums.give, 0), (late.relay, 3)],
            7: [(late.fold, 2), (sums.fold_chip, 2)],
        }
        second_events = {
            0: [(late.fold, 1), (sums.fold_chip, 1)],
            1: [(late.relay, 2), (sums.relay, 3)],
            2: [(late.relay, 1), (sums.relay, 2)],
            3: [(late.fold, 0), (sums.fold_chip, 0), (late.collect, 3)],
            4: [(late.relay, 0), (sums.relay, 1), (sums.collect, 3)],
            5: [(late.collect, 2), (sums.relay, 0)],
            6: [(sums.collect, 2), (late.collect, 1)],
            7: [(late.cross,)],
        }

    def run(events, step):
        for at, some in events.items():

            @pl.when(step == at)
            def _(some=some):
                for event, *what in some:
                    event(*what)

    @pl.loop(0, steps)
    def _(step):
        c = b ^ (7 - step) if remote else step
        load_slope(c).wait()
        d_act = product_nt(low[...], w2[columns(c), :])
        d_pre = (d_act * slope[:, columns(c)].astype(HIGH)).astype(LOW)
        d_hid_ref[:, columns(c)] = column_sum(d_pre)
        slope[:, columns(c)] = d_pre
        w2[columns(c), :] = product_tn(act[:, columns(c)], low[...]).astype(LOW)
        if not remote:
            store2(c).start()
        run(first_events, step)

    @pl.loop(0, steps)
    def _(c):
        load1(c).wait()
        d_pre = slope[:, columns(c)]
        acc[...] += product_nt(d_pre, w1[:, columns(c)])
        w1[:, columns(c)] = product(normed_t[...], d_pre).astype(LOW)
        store1(c).start()
        run(second_events, c)

    d_normed = acc[...]
    normal = n1[...]
    d_first = normalize_back(d_normed * gain1, normal, r1[:, 0:1])
    first_ref[...] = d_first
    low[...] = d_first.astype(LOW)
    sums_ref[0:1] = column_sum(d_normed * normal)
    sums_ref[2:3] = column_sum(low[...])
    sums_ref[3:4] = column_sum(d_normed)
    load_out.wait()
    d_att = product_nt(low[...], w1[:, hidden:]).astype(LOW)
    for i in range(pieces):
        d_att_ref[i] = d_att[:, i * held : (i + 1) * held]
    w1[:, hidden:] = product_tn(att[...], low[...]).astype(LOW)
    store_out = pltpu.make_async_copy(w1.at[:, last], g1_hbm.at[:, last], gsem.at[0, steps])
    store_out.start()
    blocks, planes, _ = small_ref.shape
    small_ref[...] = jnp.zeros_like(small_ref)
    owners = [(i, j) for i in range(blocks) for j in range(width // (blocks * small_rows))]
    for at, (i, j) in enumerate(owners):
        for k in range(6):
            small_ref[i, j : j + 1, k * small_rows : (k + 1) * small_rows] = sums_ref[
                k : k + 1, at * small_rows : (at + 1) * small_rows
            ]
        part = hidden // len(owners)
        small_ref[i, j : j + 1, 6 * small_rows : 6 * small_rows + part] = d_hid_ref[
            :, at * part : (at + 1) * part
        ]
    if remote:
        sums.collect(1)
        late.collect(0)
        sums.collect(0)
        sums.total()
        late.total()
        s.drain()
    for c in range(steps):
        store1(c).wait()
        if not remote:
            store2(c).wait()
    store_out.wait()


def middle(att, n1, r1, normed_t, cot, par, act, slope, w1, w2, pieces, planes, remote):
    count, width = cot.shape
    hidden = w2.shape[0]
    chunk = 512
    shape = jax.ShapeDtypeStruct
    vmem = pl.BlockSpec(memory_space=pltpu.VMEM)
    shard = hidden // (pieces * planes)
    late = shard // 4
    buffers, params = [], {}
    if remote:
        buffers = pair_of_semaphores(Reducer.COPIES + ReducerAlongZ.COPIES)
        buffers += Reducer.scratch(shard - late, width, in_place=True)
        buffers += ReducerAlongZ.scratch(late, width, in_place=True)
        params = dict(collective_id=4, has_side_effects=True)
    return pl.pallas_call(
        functools.partial(middle_kernel, chunk, width // (pieces * planes), remote),
        out_shape=(
            shape((count, width), LOW),
            shape((count, width), HIGH),
            shape((pieces, count, width // pieces), LOW),
            shape((pieces, -(-planes // 8) * 8, 384), HIGH),
            shape(w1.shape, LOW),
            shape((shard, width), HIGH) if remote else shape(w2.shape, LOW),
        ),
        in_specs=[vmem] * 6 + in_hbm(4),
        out_specs=(vmem,) * 4 + tuple(in_hbm(1)) + ((vmem,) if remote else tuple(in_hbm(1))),
        scratch_shapes=[
            pltpu.VMEM(w1.shape, LOW),
            pltpu.VMEM(w2.shape, LOW),
            pltpu.VMEM((count, hidden), LOW),
            pltpu.VMEM((count, hidden), LOW),
            pltpu.VMEM((count, width), HIGH),
            pltpu.VMEM((count, width), LOW),
            pltpu.VMEM((8, width), HIGH),
            pltpu.VMEM((1, hidden), HIGH),
            pltpu.SemaphoreType.DMA((4, hidden // chunk + 1)),
            pltpu.SemaphoreType.DMA((2, hidden // chunk + 1)),
        ]
        + buffers,
        compiler_params=pltpu.CompilerParams(vmem_limit_bytes=VMEM_LIMIT, **params),
        name="middle",
    )(att, n1, r1, normed_t, cot, par, act, slope, w1, w2)


def finish_kernel(
    dq,
    dk,
    dv,
    w,
    first,
    tok0,
    small,
    x_hbm,
    tok_out,
    in_out,
    gains_out,
    biases_out,
    hidden_out,
    first_rows,
    x,
    D,
    P,
    R,
    Z,
    M,
    N,
    T,
    lsem,
    send,
    recv,
    *buffers,
):
    b, z = position()
    rows, width = tok0.shape
    blocks = dq.shape[0]
    count = 2 * rows
    loads = [
        pltpu.make_async_copy(x_hbm.at[i, pl.ds(0, count)], x.at[i], lsem.at[i])
        for i in range(blocks)
    ]
    loads.append(pltpu.make_async_copy(first.at[pl.ds(rows, rows)], first_rows, lsem.at[blocks]))
    loads.append(pltpu.make_async_copy(tok0, tok_out.at[pl.ds(0, rows)], lsem.at[blocks + 1]))
    for load in loads:
        load.start()
    greet([(b ^ d, z) for d in range(1, 8)] + [(b, z ^ d) for d in (1, 2, 3)])
    s = Sender(send, recv)

    def piece(i):
        mixed = jnp.concatenate([ref[i, 1] for ref in (dq, dk, dv)], axis=-1)
        return product_nt(mixed, w[...])

    tokens = TokenSums(s, piece, *buffers)
    small_in = [
        s.go(small.at[b ^ d], M.at[d - 1], (b ^ d, z), M.at[d - 1]) for d in range(1, 8)
    ]
    total = jnp.zeros((width, w.shape[1]), HIGH)
    for i in range(blocks):
        loads[i].wait()
        mixed = jnp.concatenate([ref[i].reshape(count, -1) for ref in (dq, dk, dv)], axis=-1)
        total = total + product_tn(x[i], mixed)
    D[...] = total.astype(LOW).reshape(D.shape)
    share_rows = D.shape[1] // 4

    def share(d):
        return D.at[:, pl.ds(pl.multiple_of((z ^ d) * share_rows, share_rows), share_rows)]

    in_z = [s.go(share(d), Z.at[d - 1], (b, z ^ d), Z.at[d - 1]) for d in (1, 2, 3)]
    for e in (3, 2, 1, 0):
        tokens.give(e)
    for e in (3, 2, 1, 0):
        tokens.take(e)

    N[...] = small[b]
    for i in range(7):
        small_in[i].wait_recv()
        N[...] += M[i]
    for row, ref in ((4, dq), (5, dv)):
        whole = jnp.zeros((1, 128), HIGH)
        for i in range(blocks):
            whole = whole + column_sum(ref[i].reshape(count, -1))
        N[row : row + 1, 0:128] = whole
    small_z = [s.go(N, T.at[d - 1], (b, z ^ d), T.at[d - 1]) for d in (1, 2, 3)]

    for copy in in_z:
        copy.wait_recv()
    plane = share(0)[...].astype(HIGH)
    for i in range(3):
        plane = plane + Z[i].astype(HIGH)
    P[...] = plane
    grads_in = [
        s.go(P.at[b ^ d], R.at[b], (b ^ d, z), R.at[b ^ d]) for d in range(1, 8)
    ]
    R[b] = P[b]
    tokens.relay()
    for copy in small_z:
        copy.wait_recv()
    vectors = ((N[...] + T[0]) + T[1]) + T[2]
    planes = lax.broadcasted_iota(jnp.int32, vectors.shape, 0)
    row = jnp.sum(jnp.where(planes == z, vectors, 0.0), axis=0, keepdims=True)
    n = gains_out.shape[1]
    for k in range(2):
        gains_out[k : k + 1] = row[:, k * n : (k + 1) * n]
        own = vectors[4 + k : 5 + k]
        parts = [jnp.where(z == j, own[:, j * n : (j + 1) * n], 0.0) for j in range(4)]
        biases_out[k : k + 1] = (parts[0] + parts[1]) + (parts[2] + parts[3])
    for k in range(2, 6):
        biases_out[k : k + 1] = row[:, k * n : (k + 1) * n]
    hidden_out[...] = row[:, 6 * n : 6 * n + hidden_out.shape[1]]
    for copy in grads_in:
        copy.wait_recv()
    for i in range(blocks):
        for k in range(3):
            at = k * width + i * 128
            in_out[:, at : at + 128] = R[i, :, k * 128 : (k + 1) * 128]
    for load in loads[blocks:]:
        load.wait()
    tok_out[rows:] = first_rows[...] + tokens.total()
    s.drain()


def finish(dq, dk, dv, w, d_first, tok0, small, x):
    rows, width = tok0.shape
    blocks, columns = dq.shape[0], w.shape[1]
    share = width // (4 * blocks)
    vmem = pl.BlockSpec(memory_space=pltpu.VMEM)
    shape = lambda *s: jax.ShapeDtypeStruct(s, HIGH)
    low = lambda *s: pltpu.VMEM(s, LOW)
    wide = lambda *s: pltpu.VMEM(s, HIGH)
    tile = small.shape[1:]
    return pl.pallas_call(
        finish_kernel,
        out_shape=(
            shape(2 * rows, width),
            shape(share, 3 * width),
            shape(2, share),
            shape(6, share),
            shape(1, 4 * share),
        ),
        in_specs=[vmem] * 4 + in_hbm(2) + [vmem] + in_hbm(1),
        out_specs=(vmem,) * 5,
        scratch_shapes=[
            wide(rows, width),
            low(blocks, 2 * rows, width),
            low(blocks, 4 * share, columns),
            wide(blocks, share, columns),
            wide(blocks, share, columns),
            low(3, blocks, share, columns),
            wide(7, *tile),
            wide(*tile),
            wide(3, *tile),
            pltpu.SemaphoreType.DMA((blocks + 2,)),
        ]
        + pair_of_semaphores(20 + TokenSums.COPIES)
        + TokenSums.scratch(rows, width),
        compiler_params=pltpu.CompilerParams(
            collective_id=3, has_side_effects=True, vmem_limit_bytes=VMEM_LIMIT
        ),
        name="finish",
    )(dq, dk, dv, w, d_first, tok0, small, x)


def swap(pieces):
    return lax.all_to_all(pieces, "blk", 0, 0)


def by_slot(block, slots):
    blocks, count, held = block.shape
    block = block.reshape(blocks, slots, count // slots, held)
    return jnp.pad(block, ((0, 0),) * 3 + ((0, 128 - held),))


def front_apart(X, W, bias, slots):
    n_blk, count = X.shape[0], X.shape[1] - 16
    held = W.shape[1] // 3
    mixed = jnp.einsum("brd,dc->brc", X[:, :count], W, preferred_element_type=HIGH)
    parts = [mixed[..., i * held : (i + 1) * held] for i in range(3)]
    parts = [jnp.pad(p, ((0, 0), (0, 0), (0, 128 - held))).reshape(-1, 128) for p in parts]
    own = lax.dynamic_slice(bias[:2], (0, lax.axis_index("blk") * held), (2, held))
    own = jnp.pad(own, ((0, 0), (0, 128 - held)))
    codes = X[:, count, :count].reshape(-1, 1).astype(jnp.int32)
    codes = jnp.broadcast_to(codes, (n_blk * count, 128))
    queries, keys, values = split_heads(jnp.concatenate(parts, axis=1), (own[0], own[1]), codes)
    shape = (n_blk, slots, count // slots, 128)
    qh = jnp.stack(queries).reshape(2, *shape)
    kh = jnp.stack(keys).reshape(2, *shape)
    v = values.reshape(shape)
    att, lse = attend(qh, kh, v)
    rows_att = swap(att[..., :held].reshape(n_blk, count, held))
    return qh, kh, v, att, lse, rows_att


def on_device(
    tokens,
    input_weight,
    output_weight,
    expand_weight,
    reduce_weight,
    gains,
    biases,
    hidden_bias,
    segment,
    present,
    cotangent,
):
    slots, rows, width = tokens.shape
    n_blk, n_dp = lax.axis_size("blk"), lax.axis_size("dp")
    shards = n_blk * n_dp
    fast = (n_blk, n_dp) == (8, 4)
    held = width // n_blk
    shard = input_weight.shape[0]
    hidden = expand_weight.shape[1]
    count = slots * rows
    flat = tokens.reshape(count, width)

    if fast:
        front_out = front(
            flat,
            segment,
            present,
            input_weight,
            gains,
            biases,
            hidden_bias[None],
            expand_weight,
            output_weight,
            reduce_weight,
        )
        X, W1, W2, act, slope, W, _, qh, kh, v, att, lse = front_out[:12]
        attended, n1, r1, normed_t, cuts = front_out[12:]
        W1, W2 = W1.reshape(width, -1), W2.reshape(hidden, width)
    else:
        code = (segment + 4 * (1 - present)).reshape(1, count).astype(LOW)
        code_rows = jnp.pad(jnp.broadcast_to(code, (16, count)), ((0, 0), (0, width - count)))
        columns = input_weight.reshape(shard, 3, n_blk, held).transpose(2, 0, 1, 3)
        columns = columns.reshape(n_blk, shard, 3 * held)
        small = jnp.concatenate([gains.reshape(-1), biases.reshape(-1), hidden_bias])
        X = lax.all_gather(jnp.concatenate([flat, code_rows], axis=0), "blk")
        W = lax.all_gather(swap(columns), "dp", axis=1).reshape(width, 3 * held)
        small = lax.all_gather(small, BOTH)
        W1 = jnp.concatenate([expand_weight, output_weight], axis=1)
        W1 = lax.all_gather(W1, BOTH, axis=0, tiled=True)
        W2 = lax.all_gather(reduce_weight, BOTH, axis=0, tiled=True)
        part = width // shards
        cuts = small[:, : 8 * part].reshape(shards, 8, part).transpose(1, 0, 2)
        cuts = cuts.reshape(8, width).astype(HIGH)
        hidden_full = small[:, 8 * part :].reshape(hidden).astype(HIGH)
        gain, bias = cuts[:2], cuts[2:]
        qh, kh, v, att, lse, rows_att = front_apart(X, W, bias, slots)
        attended = rows_att.transpose(1, 0, 2).reshape(count, width)
        branch = product(attended, W1[:, hidden:]) + bias[2]
        n1, r1 = normalize(flat.astype(HIGH) + branch)
        r1 = jnp.broadcast_to(r1, (count, 128))
        normed_low = (n1 * gain[0] + bias[3]).astype(LOW)
        act, slope = gelu_parts(product(normed_low, W1[:, :hidden]) + hidden_full)
        act, slope = act.astype(LOW), slope.astype(LOW)
        normed_t = normed_low.T
    cot = cotangent.reshape(count, width)
    middle_out = middle(
        attended, n1, r1, normed_t, cot, cuts, act, slope, W1, W2, n_blk, n_dp, fast
    )
    output, d_first, d_att, small_rows, grad_both, grad_reduce = middle_out
    output = output.reshape(slots, rows, width)
    if fast:
        grad_both = grad_both.reshape(n_blk, n_dp, shard, -1)
        dq, dk, dv, sum_expand, sum_output, tok0 = back(
            d_att, qh, kh, v, att, lse, W, d_first, grad_both
        )
        grad_tokens, grad_input, d_gains, d_biases, d_hidden = finish(
            dq, dk, dv, W, d_first, tok0, small_rows, X
        )
        return (
            output,
            grad_tokens.reshape(slots, rows, width),
            grad_input,
            sum_output,
            sum_expand,
            grad_reduce,
            d_gains,
            d_biases,
            d_hidden.reshape(-1),
        )
    sum_both = lax.psum_scatter(grad_both, BOTH, scatter_dimension=0, tiled=True).astype(HIGH)
    sum_reduce = lax.psum_scatter(grad_reduce, BOTH, scatter_dimension=0, tiled=True)
    dq, dk, dv = attend_back(qh, att, by_slot(swap(d_att), slots), lse, kh, v)
    d_mixed = jnp.concatenate([dq[..., :held], dk[..., :held], dv[..., :held]], axis=-1)
    d_mixed = d_mixed.reshape(n_blk * count, 3 * held)
    all_tokens = X[:, :count].reshape(n_blk * count, width)
    d_input = product_tn(all_tokens, d_mixed).astype(LOW)
    d_tokens = product_nt(d_mixed, W).astype(LOW)
    d_tokens = lax.psum_scatter(d_tokens, "blk", scatter_dimension=0, tiled=True)
    grad_tokens = d_first + d_tokens.astype(HIGH)
    d_input = swap(d_input.reshape(n_blk, n_dp * shard, 3 * held))
    d_input = d_input.reshape(n_blk, n_dp, shard, 3, held).transpose(1, 2, 3, 0, 4)
    d_input = d_input.reshape(n_dp, shard, 3 * width).astype(HIGH)
    grad_input = lax.psum_scatter(d_input, "dp", scatter_dimension=0, tiled=False)
    col = lambda a: jnp.sum(a.astype(HIGH), axis=0)
    own_cols = jnp.stack([col(d_mixed[:, :held]), col(d_mixed[:, 2 * held :])])
    own_cols = lax.psum_scatter(own_cols, "dp", scatter_dimension=1, tiled=True)
    small_rows = small_rows[:, :n_dp].reshape(shards, -1)
    small_sum = lax.psum_scatter(small_rows, BOTH, scatter_dimension=0, tiled=False)
    vectors = small_sum[: 6 * part].reshape(6, part)
    return (
        output,
        grad_tokens.reshape(slots, rows, width),
        grad_input,
        sum_both[:, hidden:],
        sum_both[:, :hidden],
        sum_reduce.astype(HIGH),
        vectors[:2],
        jnp.concatenate([own_cols, vectors[2:]], axis=0),
        small_sum[6 * part : 6 * part + hidden // shards],
    )


def solution(mesh):
    rows, sharded = P("dp", "blk", None), P(BOTH, None)
    in_specs = (rows, sharded, sharded, sharded, sharded, P(None, BOTH), P(None, BOTH), P(BOTH))
    in_specs += (P("dp", "blk"), P("dp", "blk"), rows)
    out_specs = (rows, rows, sharded, sharded, sharded, sharded)
    out_specs += (P(None, BOTH), P(None, BOTH), P(BOTH))
    return jax.shard_map(
        on_device, mesh=mesh, in_specs=in_specs, out_specs=out_specs, check_vma=False
    )
```

```python
import functools

import jax
import jax.numpy as jnp
from jax import lax
from jax.experimental import pallas as pl
from jax.experimental.pallas import tpu as pltpu
from jax.sharding import PartitionSpec as P

HEADS = 16
EPSILON = 1e-12
FAR = 2.0**60
BOTH = ("blk", "dp")
MESH = pl.DeviceIdType.MESH
LOW = jnp.bfloat16
HIGH = jnp.float32
VMEM_LIMIT = 60 * 2**20


def product(left, right):
    return jnp.dot(left, right, preferred_element_type=HIGH)


def product_nt(left, right):
    return lax.dot_general(left, right, (((1,), (1,)), ((), ())), preferred_element_type=HIGH)


def product_tn(left, right):
    return lax.dot_general(left, right, (((0,), (0,)), ((), ())), preferred_element_type=HIGH)


def normalize(values):
    mean = jnp.mean(values, axis=-1, keepdims=True)
    centred = values - mean
    spread = jnp.mean(centred * centred, axis=-1, keepdims=True)
    inverse = lax.rsqrt(spread + EPSILON)
    return centred * inverse, inverse


def normalize_back(grad, normal, inverse):
    return inverse * (
        grad
        - jnp.mean(grad, axis=-1, keepdims=True)
        - normal * jnp.mean(grad * normal, axis=-1, keepdims=True)
    )


def quick_reciprocal(x):
    first = pl.reciprocal(x, approx=True)
    return first * (2.0 - x * first)


def gelu_parts(u, reciprocal=lambda x: 1.0 / x):
    bell = jnp.exp(-0.5 * u * u)
    below = 1.0 + (0.3275911 * 0.5**0.5) * jnp.abs(u)
    t = reciprocal(below)
    poly = 1.061405429 * t - 1.453152027
    poly = poly * t + 1.421413741
    poly = poly * t - 0.284496736
    poly = poly * t + 0.254829592
    tail = 0.5 * poly * t * bell
    below = jnp.where(u < 0.0, tail, 1.0 - tail)
    return u * below, below + u * bell * 0.3989422804014327


class Sender:
    def __init__(self, send, recv):
        self.send, self.recv, self.planned = send, recv, []

    def plan(self, src, dst, device, landing):
        at = len(self.planned)

        def copy(a, b):
            return pltpu.make_async_remote_copy(
                src_ref=a,
                dst_ref=b,
                send_sem=self.send.at[at],
                recv_sem=self.recv.at[at],
                device_id=device,
                device_id_type=MESH,
            )

        out = copy(src, dst)
        self.planned.append(out)
        landed = copy(landing, landing)
        landed.go = out.start
        return landed

    def go(self, *what):
        landed = self.plan(*what)
        landed.go()
        return landed

    def drain(self):
        for out in self.planned:
            out.wait_send()


def greet(peers):
    barrier = pltpu.get_barrier_semaphore()
    for peer in peers:
        pl.semaphore_signal(barrier, inc=1, device_id=peer, device_id_type=MESH)
    pl.semaphore_wait(barrier, len(peers))


def half(ref, which):
    rows = ref.shape[0]
    cut = rows // 32 * 16
    return ref.at[pl.ds(0, cut)] if which == 0 else ref.at[pl.ds(cut, rows - cut)]


def position():
    return lax.axis_index("blk"), lax.axis_index("dp")


def first_lanes(shape):
    return lax.broadcasted_iota(jnp.int32, shape, len(shape) - 1) < 64


def rows_of(block):
    return block.reshape(-1, block.shape[-1])


def attend_tile(queries, keys, values):
    rows = queries[0].shape[0]
    ones = jnp.ones_like(values)
    mine = first_lanes(values.shape)
    outs, logs = [], []
    for head in (0, 1):
        scores = product_nt(queries[head], keys[head])
        top = jnp.max(scores, axis=-1, keepdims=True)
        weights = jnp.exp(scores - top).astype(LOW)
        total = product(weights, jnp.where(mine == (head == 0), values, ones))
        mass = pltpu.roll(total, 64, 1)
        outs.append(total / mass)
        logs.append(top + jnp.log(mass))
    mine = first_lanes((rows, 128))
    flipped = jnp.where(mine, logs[0], logs[1]).T
    logs = jnp.concatenate([flipped[0:1], flipped[64:65], jnp.zeros((6, rows), HIGH)], axis=0)
    return jnp.where(mine, outs[0], outs[1]).astype(LOW), logs


def split_heads(mixed, bias, codes):
    rows = mixed.shape[0]
    q = (mixed[:, :128] + bias[0]).astype(LOW) * LOW(0.125)
    k = mixed[:, 128:256].astype(LOW)
    v = (mixed[:, 256:] + bias[1]).astype(LOW)
    lanes = lax.broadcasted_iota(jnp.int32, (rows, 128), 1) % 64
    protein = jnp.where(codes >= 4, codes - 4, codes)
    q_marks = jnp.where((lanes < 5) & (lanes != protein), -FAR, 0.0).astype(LOW)
    k_marks = jnp.where(lanes == jnp.minimum(codes, 4), 1.0, 0.0).astype(LOW)
    mine = first_lanes((rows, 128))
    return (
        (jnp.where(mine, q, q_marks), jnp.where(mine, q_marks, q)),
        (jnp.where(mine, k, k_marks), jnp.where(mine, k_marks, k)),
        v,
    )


def spread_vectors(small, par, hid):
    for i in range(8):
        for j in range(4):
            row = small[j, i : i + 1].astype(HIGH)
            at = (i * 4 + j) * 32
            for k in range(8):
                par[k : k + 1, at : at + 32] = row[:, k * 32 : k * 32 + 32]
            hid[:, at * 4 : at * 4 + 128] = row[:, 256:384]


def front_kernel(
    x,
    segment,
    present,
    input_weight,
    gains,
    biases,
    hidden_bias,
    expand,
    out_w_in,
    w2,
    X_out,
    W1,
    W2,
    act_out,
    slope_out,
    wfull,
    small,
    qh,
    kh,
    v,
    att,
    lse,
    branch_in,
    n1,
    r1,
    normed_t,
    par,
    normed_low,
    X,
    W,
    win,
    w1,
    rows_att,
    w1v,
    act,
    slope,
    hid,
    send,
    recv,
    asend,
    arecv,
    lsem,
    osem,
    wsem,
    csem,
):
    b, z = position()
    bx, by, bd, bc = b ^ 2, b ^ 4, b ^ 6, b ^ 1
    count = X.shape[1] - 16
    hidden, width = expand.shape[1], x.shape[1]
    slots, rows = qh.shape[2:4]
    locs = []

    def local(src, dst):
        copy = pltpu.make_async_copy(src, dst, lsem.at[len(locs)])
        copy.start()
        locs.append(copy)

    local(x, X.at[b, pl.ds(0, count)])
    local(expand, w1.at[:, pl.ds(0, hidden)])
    local(out_w_in, w1.at[:, pl.ds(hidden, width)])
    local(w2, W2.at[b, z])
    shard = input_weight.shape[0]
    n = gains.shape[1]
    win[...] = jnp.zeros_like(win)
    for i in range(8):
        for k in range(3):
            at = k * width + i * 128
            win[i, 0:shard, k * 128 : (k + 1) * 128] = input_weight[:, at : at + 128]
    rows_small = [gains[k : k + 1] for k in range(2)] + [biases[k : k + 1] for k in range(6)]
    line = jnp.concatenate(rows_small + [hidden_bias[...]], axis=1)
    for i in range(8):
        win[i, shard : shard + 16] = jnp.broadcast_to(line, (16, line.shape[1]))
    W[z, b] = win[b]
    codes = (segment[...] + 4 * (1 - present[...])).astype(HIGH).astype(LOW)
    codes = jnp.concatenate([codes[k : k + 1] for k in range(slots)], axis=1)
    X[b, pl.ds(count, 16), 0:count] = jnp.broadcast_to(codes, (16, count))
    X[b, pl.ds(count, 16), count:width] = jnp.zeros((16, width - count), LOW)
    greet([(b ^ d, z) for d in range(1, 8)] + [(b, z ^ d) for d in range(1, 4)])
    s = Sender(send, recv)
    to_x, to_y, to_core = (bx, z), (by, z), (bc, z)

    def token_core(src, bb):
        return s.plan(src, X.at[bb], to_core, X.at[bb ^ 1])

    def to_z(d):
        return b, z ^ d

    def hops(F, src, zz):
        near = [
            s.plan(src, F.at[b, zz], to_x, F.at[bx, zz]),
            s.plan(src, F.at[b, zz], to_y, F.at[by, zz]),
        ]
        one, two = half(F.at[bx, zz], 0), half(F.at[by, zz], 1)
        far = [
            s.plan(one, one, to_y, half(F.at[bd, zz], 0)),
            s.plan(two, two, to_x, half(F.at[bd, zz], 1)),
        ]
        return near, far

    def planes(F, src, bb):
        pair = [s.plan(src, F.at[bb, z], to_z(d), F.at[bb, z ^ d]) for d in (1, 2)]
        on = F.at[bb, z ^ 2]
        return pair + [s.plan(on, on, to_z(1), F.at[bb, z ^ 3])]

    def to_sibling(F, src, bb, zz):
        return s.plan(src, F.at[bb, zz], to_core, F.at[bb ^ 1, zz])

    places = (b, bx, by, bd)
    z1 = planes(W1, w1, b)
    hop1 = [hops(W1, W1.at[b, z ^ d] if d else w1, z ^ d) for d in range(4)]
    hop2 = hops(W2, w2, z)
    z2 = [planes(W2, W2.at[bb, z] if i else w2, bb) for i, bb in enumerate(places)]
    core1, core2 = (
        {
            (i, d): to_sibling(F, F.at[bb, z ^ d] if i or d else own, bb, z ^ d)
            for i, bb in enumerate(places)
            for d in range(4)
        }
        for F, own in ((W1, w1), (W2, w2))
    )

    def start(*copies):
        for copy in copies:
            copy.go()

    def first(d):
        if d in (1, 3):
            z1[d - 1].wait_recv()
        start(*hop1[d][0], core1[0, d])

    def second(d):
        near, far = hop1[d]
        for i in (0, 1):
            near[i].wait_recv()
            start(far[i], core1[1 + i, d])

    def third(d):
        for copy in hop1[d][1]:
            copy.wait_recv()
        core1[3, d].go()

    def spread(i):
        start(z2[i][0], z2[i][1], core2[i, 0])

    def second2():
        near, far = hop2
        for i in (0, 1):
            near[i].wait_recv()
            far[i].go()
            spread(1 + i)

    def third2():
        for copy in hop2[1]:
            copy.wait_recv()
        spread(3)

    def arrive2(i):
        z2[i][1].wait_recv()
        start(z2[i][2], core2[i, 2])
        z2[i][0].wait_recv()
        core2[i, 1].go()

    def last2(i):
        z2[i][2].wait_recv()
        core2[i, 3].go()

    columns = [
        s.go(win.at[b ^ d], W.at[z, b], (b ^ d, z), W.at[z, b ^ d]) for d in range(1, 8)
    ]
    locs[0].wait()
    token_x = s.go(X.at[b], X.at[b], to_x, X.at[bx])
    token_y = s.go(X.at[b], X.at[b], to_y, X.at[by])
    token_c = token_core(X.at[b], b)
    token_c.go()
    for copy in locs[1:3]:
        copy.wait()
    local(w1, W1.at[b, z])
    start(z1[0], z1[1])
    for copy in columns:
        copy.wait_recv()
    for i in range(8):
        small[z, i : i + 1] = W[z, i, 32:33]
    trimmed = lambda zz: W.at[zz, :, pl.ds(0, 32)]
    columns, vectors = (
        [s.plan(at(z), at(z), to_z(d), at(z ^ d)) for d in (1, 2)]
        + [s.plan(at(z ^ 2), at(z ^ 2), to_z(1), at(z ^ 3))]
        for at in (trimmed, lambda zz: small.at[zz])
    )
    start(*columns[:2], *vectors[:2])
    spread(0)
    token_x.wait_recv()
    piece = half(X.at[bx], 0)
    token_one = s.go(piece, piece, to_y, half(X.at[bd], 0))
    token_xc = token_core(X.at[bx], bx)
    token_xc.go()
    token_y.wait_recv()
    piece = half(X.at[by], 1)
    token_two = s.go(piece, piece, to_x, half(X.at[bd], 1))
    token_yc = token_core(X.at[by], by)
    token_yc.go()
    token_dc = token_core(X.at[bd], bd)
    start(*hop2[0])
    columns[1].wait_recv()
    columns[2].go()
    vectors[1].wait_recv()
    vectors[2].go()
    z1[1].wait_recv()
    z1[2].go()
    for copy in (columns[0], columns[2], vectors[0], vectors[2]):
        copy.wait_recv()
    for i in range(8):
        for j in range(4):
            at = (i * 4 + j) * 32
            wfull[at : at + 32] = W[j, i, 0:32]
    spread_vectors(small, par, hid)
    chosen = lax.broadcasted_iota(jnp.int32, (16, 128), 0) == b
    bias = [[], []]
    for j in range(4):
        row = jnp.where(chosen, small[j, :, 0:128].astype(HIGH), 0.0)
        row = jnp.sum(row, axis=0, keepdims=True)
        bias[0].append(row[:, 64:96])
        bias[1].append(row[:, 96:128])
    bias = [jnp.concatenate(parts, axis=1) for parts in bias]

    def mix(i):
        pltpu.make_async_copy(X.at[i], X_out.at[i], osem.at[i]).start()
        mixed = product(X[i, 0:count], wfull[...])
        codes = jnp.broadcast_to(X[i, count : count + 1, 0:count].astype(HIGH), (128, count)).T
        queries, keys, values = split_heads(mixed, bias, codes.astype(jnp.int32))
        for head in (0, 1):
            qh[head, i] = queries[head].reshape(slots, rows, 128)
            kh[head, i] = keys[head].reshape(slots, rows, 128)
        v[i] = values.reshape(slots, rows, 128)

    mix(b)
    token_c.wait_recv()
    mix(bc)
    mix(bx)
    token_xc.wait_recv()
    mix(bx ^ 1)
    mix(by)
    token_one.wait_recv()
    token_two.wait_recv()
    token_dc.go()
    first(0)
    first(2)
    first(1)
    second2()
    first(3)
    token_yc.wait_recv()
    mix(by ^ 1)
    mix(bd)
    token_dc.wait_recv()
    mix(bd ^ 1)
    arrive2(0)

    def piece_of(slot):
        return pl.ds(pl.multiple_of(slot * rows, rows), rows)

    def send_att(slot, d):
        return pltpu.make_async_remote_copy(
            src_ref=att.at[b ^ d, slot],
            dst_ref=rows_att.at[b, piece_of(slot)],
            send_sem=asend.at[slot * 8 + d],
            recv_sem=arecv.at[slot * 8 + d],
            device_id=(b ^ d, z),
            device_id_type=MESH,
        )

    def keep_att(slot):
        return pltpu.make_async_copy(
            att.at[b, slot], rows_att.at[b, piece_of(slot)], osem.at[8 + slot]
        )

    events = {
        0: (second, 0),
        1: (third2,),
        2: (second, 2),
        4: (second, 1),
        5: (arrive2, 1),
        6: (arrive2, 2),
        7: (third, 0),
        9: (second, 3),
        10: (arrive2, 3),
        12: (third, 2),
        14: (third, 1),
    }
    late_events = {1: (last2, 0), 3: (last2, 1), 5: (last2, 2), 7: (last2, 3)}

    @pl.loop(0, 8 * slots)
    def _(step):
        slot, d = step // 8, (step + 1) % 8
        i = b ^ d
        keys = [rows_of(kh[head, :, slot]) for head in (0, 1)]
        out, logs = attend_tile([qh[head, i, slot] for head in (0, 1)], keys, rows_of(v[:, slot]))
        att[i, slot] = out
        lse[slot, :, pl.ds(pl.multiple_of(i * rows, rows), rows)] = logs

        @pl.when(d != 0)
        def _():
            send_att(slot, d).start()

        @pl.when(d == 0)
        def _():
            keep_att(slot).start()

        for at, (event, *what) in events.items():
            pl.when(step == at)(functools.partial(event, *what))

    third(3)
    for copy in core1.values():
        copy.wait_recv()
    locs[4].wait()
    chunk = 512
    steps = hidden // chunk

    def load(c, size=chunk):
        cols = pl.ds(pl.multiple_of(c * chunk, chunk), size)
        return pltpu.make_async_copy(W1.at[:, :, :, cols], w1v.at[:, :, :, cols], wsem.at[c])

    load(steps, width).start()
    for c in range(steps):
        load(c).start()
    for slot in range(slots):
        keep_att(slot).wait()
        for d in range(1, 8):
            pltpu.make_async_remote_copy(
                src_ref=rows_att.at[b ^ d, piece_of(slot)],
                dst_ref=rows_att.at[b ^ d, piece_of(slot)],
                send_sem=asend.at[slot * 8 + d],
                recv_sem=arecv.at[slot * 8 + d],
                device_id=(b ^ d, z),
                device_id_type=MESH,
            ).wait_recv()
    branch_in[...] = jnp.concatenate([rows_att[i] for i in range(8)], axis=1)
    load(steps, width).wait()
    out_w = w1v[:, :, :, hidden:].reshape(width, width)
    branch = product(branch_in[...], out_w) + par[4:5]
    normal, inverse = normalize(X[b, 0:count].astype(HIGH) + branch)
    n1[...] = normal
    r1[...] = jnp.broadcast_to(inverse, r1.shape)
    normed = (normal * par[0:1] + par[5:6]).astype(LOW)
    normed_low[...] = normed
    normed_t[...] = normed.T

    def store(c, ref, out, which):
        cols = pl.ds(pl.multiple_of(c * chunk, chunk), chunk)
        return pltpu.make_async_copy(ref.at[:, cols], out.at[:, cols], csem.at[which, c])

    @pl.loop(0, steps)
    def _(c):
        cols = pl.ds(pl.multiple_of(c * chunk, chunk), chunk)
        load(c).wait()
        pre = product(normed_low[...], w1v[:, :, :, cols].reshape(width, chunk))
        value, rate = gelu_parts(pre + hid[:, cols], quick_reciprocal)
        act[:, cols] = value.astype(LOW)
        slope[:, cols] = rate.astype(LOW)
        store(c, act, act_out, 0).start()
        store(c, slope, slope_out, 1).start()
        for at, (event, *what) in late_events.items():
            pl.when(c == at)(functools.partial(event, *what))

    for copy in core2.values():
        copy.wait_recv()
    for slot in range(slots):
        for d in range(1, 8):
            send_att(slot, d).wait_send()
    for c in range(steps):
        store(c, act, act_out, 0).wait()
        store(c, slope, slope_out, 1).wait()
    s.drain()
    locs[3].wait()
    for i in range(8):
        pltpu.make_async_copy(X.at[i], X_out.at[i], osem.at[i]).wait()


def in_hbm(count):
    return [pl.BlockSpec(memory_space=pl.ANY)] * count


def pair_of_semaphores(count):
    return [pltpu.SemaphoreType.DMA((count,)), pltpu.SemaphoreType.DMA((count,))]


def front(x, segment, present, input_weight, gains, biases, hidden_bias, expand, out_w, w2):
    slots = segment.shape[0]
    count, width = x.shape
    rows, hidden = count // slots, expand.shape[1]
    shard = expand.shape[0]
    shape = lambda *s: jax.ShapeDtypeStruct(s, LOW)
    wide = lambda *s: jax.ShapeDtypeStruct(s, HIGH)
    vmem = pl.BlockSpec(memory_space=pltpu.VMEM)
    return pl.pallas_call(
        front_kernel,
        out_shape=(
            shape(8, count + 16, width),
            shape(8, 4, shard, hidden + width),
            shape(8, 4, *w2.shape),
            shape(count, hidden),
            shape(count, hidden),
            shape(width, 384),
            shape(4, 16, 384),
            shape(2, 8, slots, rows, 128),
            shape(2, 8, slots, rows, 128),
            shape(8, slots, rows, 128),
            shape(8, slots, rows, 128),
            wide(slots, 8, 8 * rows),
            shape(count, width),
            wide(count, width),
            wide(count, 128),
            shape(width, count),
            wide(8, width),
        ),
        in_specs=in_hbm(1) + [vmem] * 6 + in_hbm(3),
        out_specs=tuple(in_hbm(5)) + (vmem,) * 12,
        scratch_shapes=[
            pltpu.VMEM((count, width), LOW),
            pltpu.VMEM((8, count + 16, width), LOW),
            pltpu.VMEM((4, 8, shard + 16, 384), LOW),
            pltpu.VMEM((8, shard + 16, 384), LOW),
            pltpu.VMEM((shard, hidden + width), LOW),
            pltpu.VMEM((8, count, 128), LOW),
            pltpu.VMEM((8, 4, shard, hidden + width), LOW),
            pltpu.VMEM((count, hidden), LOW),
            pltpu.VMEM((count, hidden), LOW),
            pltpu.VMEM((1, hidden), HIGH),
        ]
        + pair_of_semaphores(116)
        + pair_of_semaphores(8 * slots)
        + [pltpu.SemaphoreType.DMA((5,)), pltpu.SemaphoreType.DMA((8 + slots,))]
        + [pltpu.SemaphoreType.DMA((hidden // 512 + 1,)), pltpu.SemaphoreType.DMA((2, hidden // 512))],
        compiler_params=pltpu.CompilerParams(
            collective_id=1, has_side_effects=True, vmem_limit_bytes=VMEM_LIMIT
        ),
        name="front",
    )(x, segment, present, input_weight, gains, biases, hidden_bias, expand, out_w, w2)


def add_rows(out, one, two):
    @pl.loop(0, one.shape[0] // 16)
    def _(i):
        rows = pl.ds(pl.multiple_of(i * 16, 16), 16)
        out[rows, :] = one[rows, :] + two[rows, :]


def sum_rows(out, *terms):
    @pl.loop(0, out.shape[0] // 16)
    def _(i):
        rows = pl.ds(pl.multiple_of(i * 16, 16), 16)
        total = terms[0][rows, :].astype(HIGH)
        for term in terms[1:]:
            total = total + term[rows, :].astype(HIGH)
        out[rows, :] = total


class Reducer:
    ORDER = (3, 2, 1, 0)
    COPIES = 16 + 4 * 6 + 3

    def __init__(self, s, share, out, C, H, Q, Z=None, S=None, lsem=None):
        b, z = position()
        to_x, to_y, to_core = (b ^ 2, z), (b ^ 4, z), (b ^ 1, z)
        self.out, self.C, self.H, self.Q, self.Z = out, C, H, Q, Z
        self.at = at = lambda e, d: share(b ^ (2 * e), z ^ d) if S is None else S.at[e, d]
        self.mine, self.other, self.halves, self.ahead, self.rest, self.last = ({} for _ in range(6))
        for d in self.ORDER:
            for e in (3, 1, 2, 0):
                if S is not None:
                    self.mine[d, e] = pltpu.make_async_copy(
                        share(b ^ (2 * e), z ^ d), S.at[e, d], lsem.at[d * 4 + e]
                    )
                self.other[d, e] = s.plan(
                    share(b ^ 1 ^ (2 * e), z ^ d), C.at[e, d], to_core, C.at[e, d]
                )

            def send(e, part, to, where):
                return s.plan(half(at(e, d), part), where, to, where)

            self.halves[d] = [send(3, 0, to_x, H.at[d, 0]), send(3, 1, to_y, H.at[d, 1])]
            self.ahead[d] = [
                send(2, 1, to_y, half(Q.at[d, 1], 1)),
                send(1, 0, to_x, half(Q.at[d, 0], 0)),
            ]
            self.rest[d] = [
                send(2, 0, to_y, half(Q.at[d, 1], 0)),
                send(1, 1, to_x, half(Q.at[d, 0], 1)),
            ]
            if d and Z is not None:
                to = (b, z ^ (2 if d == 2 else 1))
                self.last[d] = s.plan(at(0, d), Z.at[d - 1], to, Z.at[d - 1])

    def keep_for_later(self, sems):
        self.keep = [
            pltpu.make_async_copy(self.at(*self.kept(d)), self.out.at[d], sems.at[d])
            for d in range(4)
        ]

    def kept(self, d):
        return 0, d

    def start(self):
        for d in self.ORDER:
            for e in (3, 1, 2, 0):
                self.mine[d, e].start()
                self.other[d, e].go()

    def give(self, e):
        for d in self.ORDER:
            self.other[d, e].go()

    def fold(self, d, chips=(3, 1, 2, 0)):
        for e in chips:
            if self.mine:
                self.mine[d, e].wait()
            self.other[d, e].wait_recv()
            add_rows(self.at(e, d), self.at(e, d), self.C.at[e, d])
            for copy in {3: self.halves[d], 1: self.ahead[d][1:], 2: self.ahead[d][:1], 0: []}[e]:
                copy.go()

    def fold_chip(self, e):
        for d in self.ORDER:
            self.fold(d, (e,))

    def relay(self, d):
        for i, e in ((0, 2), (1, 1)):
            self.halves[d][i].wait_recv()
            part = half(self.at(e, d), i)
            add_rows(part, part, self.H.at[d, i])
            self.rest[d][i].go()

    def collect(self, d):
        for copy in self.ahead[d] + self.rest[d]:
            copy.wait_recv()
        total = self.at(0, d)
        for i in (0, 1):
            add_rows(total, total, self.Q.at[d, i])
        if self.Z is None:
            self.keep[d].start()
            return
        if d == 2:
            self.last[3].wait_recv()
            add_rows(total, total, self.Z.at[2])
        if d:
            self.last[d].go()

    def total(self):
        for d in (1, 2):
            self.last[d].wait_recv()
        sum_rows(self.out, self.at(0, 0), self.Z.at[0], self.Z.at[1])

    LEAD = (((4, 4), 1), ((4, 2), 2), ((4, 2), 1), ((3,), 1))

    @classmethod
    def scratch(cls, rows, columns, in_place=False):
        shapes = [pltpu.VMEM((*n, rows // cut, columns), LOW) for n, cut in cls.LEAD]
        if in_place:
            return shapes
        return shapes + [pltpu.VMEM((4, 4, rows, columns), LOW), pltpu.SemaphoreType.DMA((16,))]


class ReducerAlongZ(Reducer):
    COPIES = 16 + 4 * 3 + 6

    def __init__(self, s, share, out, C, H, Q, Z, S=None, lsem=None):
        self.partial = H is None
        b, z = position()
        to_x, to_y, to_core = (b ^ 2, z), (b ^ 4, z), (b ^ 1, z)
        self.out, self.C, self.H, self.Q, self.Z = out, C, H, Q, Z
        self.at = at = lambda e, d: share(b ^ (2 * e), z ^ d) if S is None else S.at[e, d]
        self.mine, self.other, self.along = {}, {}, {}
        for e in (3, 1, 2, 0):
            for d in (3, 2, 1, 0):
                if S is not None:
                    self.mine[e, d] = pltpu.make_async_copy(
                        share(b ^ (2 * e), z ^ d), S.at[e, d], lsem.at[d * 4 + e]
                    )
                self.other[e, d] = s.plan(
                    share(b ^ 1 ^ (2 * e), z ^ d), C.at[e, d], to_core, C.at[e, d]
                )
                if d:
                    to = (b, z ^ (2 if d == 2 else 1))
                    self.along[e, d] = s.plan(at(e, d), Z.at[e, d - 1], to, Z.at[e, d - 1])

        if self.partial:
            return

        def send(e, part, to, where):
            return s.plan(half(at(e, 0), part), where, to, where)

        self.halves = [send(3, 0, to_x, H.at[0]), send(3, 1, to_y, H.at[1])]
        self.ahead = [
            send(2, 1, to_y, half(Q.at[1], 1)),
            send(1, 0, to_x, half(Q.at[0], 0)),
        ]
        self.rest = [
            send(2, 0, to_y, half(Q.at[1], 0)),
            send(1, 1, to_x, half(Q.at[0], 1)),
        ]

    def start(self):
        for at in self.mine:
            self.mine[at].start()
            self.other[at].go()

    def give(self, e):
        for d in (3, 2, 1, 0):
            self.other[e, d].go()

    def fold(self, e):
        for d in (3, 1, 2, 0):
            if self.mine:
                self.mine[e, d].wait()
            self.other[e, d].wait_recv()
            add_rows(self.at(e, d), self.at(e, d), self.C.at[e, d])
            if d in (1, 3):
                self.along[e, d].go()

    def relay(self, e):
        self.along[e, 3].wait_recv()
        add_rows(self.at(e, 2), self.at(e, 2), self.Z.at[e, 2])
        self.along[e, 2].go()

    def collect(self, e):
        total = self.at(e, 0)
        for d in (1, 2):
            self.along[e, d].wait_recv()
            add_rows(total, total, self.Z.at[e, d - 1])
        if self.partial:
            self.keep[e].start()
            return
        for copy in {3: self.halves, 1: self.ahead[1:], 2: self.ahead[:1], 0: []}[e]:
            copy.go()

    def kept(self, e):
        return e, 0

    def cross(self):
        for i, e in ((0, 2), (1, 1)):
            self.halves[i].wait_recv()
            part = half(self.at(e, 0), i)
            add_rows(part, part, self.H.at[i])
            self.rest[i].go()

    def total(self):
        for copy in self.ahead + self.rest:
            copy.wait_recv()
        sum_rows(self.out, self.at(0, 0), self.Q.at[0], self.Q.at[1])

    LEAD = (((4, 4), 1), ((2,), 2), ((2,), 1), ((4, 3), 1))


class PlaneSums:
    COPIES = 3

    def __init__(self, s, out, T, Z):
        b, z = position()
        self.out, self.T, self.Z = out, T, Z
        self.last = {
            d: s.plan(T.at[d], Z.at[d - 1], (b, z ^ (2 if d == 2 else 1)), Z.at[d - 1])
            for d in (3, 2, 1)
        }

    def start(self):
        self.last[3].go()
        self.last[1].go()

    def relay(self):
        self.last[3].wait_recv()
        add_rows(self.T.at[2], self.T.at[2], self.Z.at[2])
        self.last[2].go()

    def total(self):
        for d in (1, 2):
            self.last[d].wait_recv()
        sum_rows(self.out, self.T.at[0], self.Z.at[0], self.Z.at[1])

    @staticmethod
    def scratch(rows, columns):
        return [pltpu.VMEM((n, rows, columns), LOW) for n in (4, 3)]


class ChipSums:
    COPIES = 6

    def __init__(self, s, out, U, H, Q):
        b, z = position()
        to_x, to_y = (b ^ 2, z), (b ^ 4, z)
        self.out, self.U, self.H, self.Q = out, U, H, Q

        def send(e, part, to, where):
            return s.plan(half(U.at[e], part), where, to, where)

        self.halves = [send(3, 0, to_x, H.at[0]), send(3, 1, to_y, H.at[1])]
        self.ahead = [
            send(2, 1, to_y, half(Q.at[1], 1)),
            send(1, 0, to_x, half(Q.at[0], 0)),
        ]
        self.rest = [
            send(2, 0, to_y, half(Q.at[1], 0)),
            send(1, 1, to_x, half(Q.at[0], 1)),
        ]

    def start(self):
        for copy in self.halves + self.ahead:
            copy.go()

    def relay(self):
        for i, e in ((0, 2), (1, 1)):
            self.halves[i].wait_recv()
            part = half(self.U.at[e], i)
            add_rows(part, part, self.H.at[i])
            self.rest[i].go()

    def total(self):
        for copy in self.ahead + self.rest:
            copy.wait_recv()
        sum_rows(self.out, self.U.at[0], self.Q.at[0], self.Q.at[1])

    @staticmethod
    def scratch(rows, columns):
        shapes = (4, rows), (2, rows // 2), (2, rows)
        return [pltpu.VMEM((*n, columns), LOW) for n in shapes]


def attend_kernel(qh_ref, kh_ref, v_ref, out_ref, lse_ref):
    keys = [rows_of(kh_ref[head, :, 0]) for head in (0, 1)]
    out_ref[0, 0], lse_ref[0] = attend_tile(
        [qh_ref[head, 0, 0] for head in (0, 1)], keys, rows_of(v_ref[:, 0])
    )


def attend(qh, kh, v):
    blocks, slots, rows, lanes = v.shape
    tile = pl.BlockSpec((1, 1, rows, lanes), lambda s, i: (i, s, 0, 0))
    tiles = pl.BlockSpec((2, 1, 1, rows, lanes), lambda s, i: (0, i, s, 0, 0))
    whole = pl.BlockSpec((blocks, 1, rows, lanes), lambda s, i: (0, s, 0, 0))
    wholes = pl.BlockSpec((2, blocks, 1, rows, lanes), lambda s, i: (0, 0, s, 0, 0))
    return pl.pallas_call(
        attend_kernel,
        grid=(slots, blocks),
        out_shape=(
            jax.ShapeDtypeStruct(v.shape, LOW),
            jax.ShapeDtypeStruct((slots, 8, blocks * rows), HIGH),
        ),
        in_specs=[tiles, wholes, whole],
        out_specs=(tile, pl.BlockSpec((1, 8, rows), lambda s, i: (s, 0, i))),
        compiler_params=pltpu.CompilerParams(vmem_limit_bytes=VMEM_LIMIT),
        name="attend",
    )(qh, kh, v)


def row_products(out, grad):
    pick = (lax.broadcasted_iota(jnp.int32, (8, 128), 0) == 0) == first_lanes((8, 128))
    return lax.dot_general(
        pick.astype(HIGH),
        out.astype(HIGH) * grad.astype(HIGH),
        (((1,), (1,)), ((), ())),
        precision=lax.Precision.HIGHEST,
        preferred_element_type=HIGH,
    )


def attend_back_tile(queries, keys, values, grads, logs, delta, acc):
    zeros = jnp.zeros_like(grads)
    mine = first_lanes(grads.shape)
    dk, dv = [], 0.0
    for head in (0, 1):
        grad = jnp.where(mine == (head == 0), grads, zeros)
        probs = jnp.exp(product_nt(keys[head], queries[head]) - logs[head : head + 1])
        pushed = product_nt(values, grad)
        d_scores = (probs * (pushed - delta[head : head + 1])).astype(LOW)
        dv = dv + product(probs.astype(LOW), grad)
        dk.append(product(d_scores, queries[head]))
        keys_t = keys[head].T[head * 64 : head * 64 + 64]
        acc[head * 64 : head * 64 + 64, :] += product(keys_t, d_scores)
    return jnp.where(first_lanes(dk[0].shape), dk[0], dk[1]).astype(LOW), dv.astype(LOW)


def attend_back_kernel(
    qh_ref, o_ref, g_ref, lse_ref, kh_ref, v_ref, dq_ref, dk_ref, dv_ref, acc, delta
):
    tile = pl.program_id(1)
    blocks, _, rows, _ = g_ref.shape
    grads = rows_of(g_ref[:, 0])

    @pl.when(tile == 0)
    def _():
        acc[...] = jnp.zeros_like(acc)
        delta[...] = row_products(rows_of(o_ref[:, 0]), grads)

    dk_ref[0, 0], dv_ref[0, 0] = attend_back_tile(
        [rows_of(qh_ref[head, :, 0]) for head in (0, 1)],
        [kh_ref[head, 0, 0] for head in (0, 1)],
        v_ref[0, 0],
        grads,
        lse_ref[0],
        delta[...],
        acc,
    )

    @pl.when(tile == blocks - 1)
    def _():
        dq_ref[:, 0] = (acc[...].T * 0.125).astype(LOW).reshape(blocks, rows, 128)


def attend_back(qh, o, g, lse, kh, v):
    blocks, slots, rows, lanes = v.shape
    tile = pl.BlockSpec((1, 1, rows, lanes), lambda s, i: (i, s, 0, 0))
    tiles = pl.BlockSpec((2, 1, 1, rows, lanes), lambda s, i: (0, i, s, 0, 0))
    whole = pl.BlockSpec((blocks, 1, rows, lanes), lambda s, i: (0, s, 0, 0))
    wholes = pl.BlockSpec((2, blocks, 1, rows, lanes), lambda s, i: (0, 0, s, 0, 0))
    logs = pl.BlockSpec((1, 8, blocks * rows), lambda s, i: (s, 0, 0))
    shape = jax.ShapeDtypeStruct(v.shape, LOW)
    return pl.pallas_call(
        attend_back_kernel,
        grid=(slots, blocks),
        out_shape=(shape,) * 3,
        in_specs=[wholes, whole, whole, logs, tiles, tile],
        out_specs=(whole, tile, tile),
        scratch_shapes=[pltpu.VMEM((lanes, blocks * rows), HIGH), pltpu.VMEM((8, blocks * rows), HIGH)],
        compiler_params=pltpu.CompilerParams(vmem_limit_bytes=VMEM_LIMIT),
        name="attend_back",
    )(qh, o, g, lse, kh, v)


class TokenSums:
    COPIES = 4 + 2 + 4

    def __init__(self, s, piece, sent, C, S, H, Q, A):
        b, z = position()
        to_x, to_y, to_core = (b ^ 2, z), (b ^ 4, z), (b ^ 1, z)
        self.b, self.piece = b, piece
        self.sent, self.C, self.S, self.H, self.Q, self.A = sent, C, S, H, Q, A
        self.other = [s.plan(sent.at[e], C.at[e], to_core, C.at[e]) for e in range(4)]

        def send(e, part, to, where):
            return s.plan(half(S.at[e - 1], part), where, to, where)

        self.halves = [send(3, 0, to_x, H.at[0]), send(3, 1, to_y, H.at[1])]
        self.ahead = [
            send(2, 1, to_y, half(Q.at[1], 1)),
            send(1, 0, to_x, half(Q.at[0], 0)),
        ]
        self.rest = [
            send(2, 0, to_y, half(Q.at[1], 0)),
            send(1, 1, to_x, half(Q.at[0], 1)),
        ]

    def give(self, e):
        self.sent[e] = self.piece(self.b ^ 1 ^ (2 * e)).astype(LOW)
        self.other[e].go()

    def take(self, e):
        mine = self.piece(self.b ^ (2 * e))
        self.other[e].wait_recv()
        mine = mine + self.C[e].astype(HIGH)
        if e:
            self.S[e - 1] = mine.astype(LOW)
        else:
            self.A[...] = mine
        for copy in {3: self.halves, 1: self.ahead[1:], 2: self.ahead[:1], 0: []}[e]:
            copy.go()

    def relay(self):
        for i, e in ((0, 2), (1, 1)):
            self.halves[i].wait_recv()
            part = half(self.S.at[e - 1], i)
            add_rows(part, part, self.H.at[i])
            self.rest[i].go()

    def total(self):
        for copy in self.ahead + self.rest:
            copy.wait_recv()
        return self.A[...] + self.Q[0].astype(HIGH) + self.Q[1].astype(HIGH)

    @staticmethod
    def scratch(rows, width):
        low = lambda *s: pltpu.VMEM((*s, width), LOW)
        return [low(4, rows), low(4, rows), low(3, rows), low(2, rows // 2), low(2, rows)] + [
            pltpu.VMEM((rows, width), HIGH)
        ]


def back_kernel(
    d_att,
    qh_in,
    kh_in,
    v_in,
    att_in,
    lse_in,
    w_in,
    first,
    g1,
    g2_planes,
    g2_late,
    dq,
    dk,
    dv,
    o1,
    out_o,
    o2,
    tok,
    qh,
    kh,
    v,
    att,
    lse,
    w,
    first_rows,
    tail,
    grads,
    acc,
    delta,
    lsem,
    send,
    recv,
    *buffers,
):
    b, z = position()
    blocks, slots, rows, _ = v.shape
    loads = [
        pltpu.make_async_copy(src, dst, lsem.at[i])
        for i, (src, dst) in enumerate(
            (
                (d_att.at[b], grads.at[b]),
                (qh_in, qh),
                (kh_in, kh),
                (v_in, v),
                (att_in, att),
                (lse_in, lse),
                (w_in, w),
                (first.at[pl.ds(0, rows)], first_rows),
                (g2_planes, buffers[18]),
                (g2_late, buffers[20]),
            )
        )
    ]
    for load in loads:
        load.start()
    greet([(b ^ d, z) for d in range(1, 8)] + [(b, z ^ d) for d in (1, 2, 3)])
    s = Sender(send, recv)
    arriving = [
        [
            s.go(d_att.at[b ^ d, part], grads.at[b, part], (b ^ d, z), grads.at[b ^ d, part])
            for d in range(1, 8)
        ]
        for part in (pl.ds(slot * rows, rows) for slot in range(slots))
    ]

    def arrive(slot):
        for copy in arriving[slot]:
            copy.wait_recv()

    most = o1.shape[1] - tail.shape[1] + out_o.shape[1]
    sums = Reducer(
        s, lambda bb, zz: g1.at[bb, zz, :, pl.ds(0, most)], o1.at[:, pl.ds(0, most)], *buffers[:6]
    )
    late = ReducerAlongZ(
        s, lambda bb, zz: g1.at[bb, zz, :, pl.ds(most, tail.shape[1])], tail, *buffers[6:12]
    )

    def piece(i):
        mixed = jnp.concatenate([ref[i, 0] for ref in (dq, dk, dv)], axis=-1)
        return product_nt(mixed, w[...])

    tokens = TokenSums(s, piece, *buffers[12:18])
    cut = g2_planes.shape[1]
    planes = PlaneSums(s, o2.at[pl.ds(0, cut)], *buffers[18:20])
    chips = ChipSums(s, o2.at[pl.ds(cut, g2_late.shape[1])], *buffers[20:])
    late.start()
    sums.start()
    late.fold(3)
    late.fold(1)
    late.fold(2)
    sums.fold(3)
    arrive(0)
    for load in loads:
        load.wait()

    def grad_rows(slot):
        part = pl.ds(pl.multiple_of(slot * rows, rows), rows)
        return rows_of(grads[:, part])

    events = {
        0: [(late.fold, 0)],
        1: [(sums.fold, 2), (late.relay, 3)],
        2: [(late.relay, 1)],
        3: [(sums.fold, 1), (sums.relay, 3)],
        4: [(late.relay, 2)],
        5: [(late.relay, 0), (sums.relay, 2)],
        6: [(sums.fold, 0), (late.collect, 3), (arrive, 1)],
        7: [(sums.collect, 3), (late.collect, 1), (planes.start,), (chips.start,)],
        8: [(sums.relay, 1), (late.collect, 2), (tokens.give, 3), (tokens.give, 2)],
        9: [(sums.collect, 2), (tokens.give, 1), (tokens.take, 3), (chips.relay,)],
        10: [(tokens.give, 0), (tokens.take, 2)],
        11: [(sums.relay, 0), (late.cross,), (tokens.take, 1), (planes.relay,)],
        12: [(tokens.take, 0)],
        13: [(sums.collect, 1), (tokens.relay,)],
        15: [(late.collect, 0), (planes.total,), (chips.total,)],
    }

    @pl.loop(0, blocks * slots)
    def _(step):
        slot, tile = step // blocks, step % blocks
        slot_grads = grad_rows(slot)

        @pl.when(tile == 0)
        def _():
            acc[...] = jnp.zeros_like(acc)
            delta[...] = row_products(rows_of(att[:, slot]), slot_grads)

        dk[tile, slot], dv[tile, slot] = attend_back_tile(
            [rows_of(qh[head, :, slot]) for head in (0, 1)],
            [kh[head, tile, slot] for head in (0, 1)],
            v[tile, slot],
            slot_grads,
            lse[slot],
            delta[...],
            acc,
        )

        @pl.when(tile == blocks - 1)
        def _():
            dq[:, slot] = (acc[...].T * 0.125).astype(LOW).reshape(blocks, rows, 128)

        for at, some in events.items():

            @pl.when(step == at)
            def _(some=some):
                for event, *what in some:
                    event(*what)

    sums.collect(0)
    late.total()
    rest = o1.shape[1] - most
    o1[:, most:] = tail[:, :rest]
    out_o[...] = tail[:, rest:]
    sums.total()
    tok[...] = first_rows[...] + tokens.total()
    s.drain()


def back(d_att, qh, kh, v, att, lse, w, d_first, g1, g2_planes, g2_late):
    blocks, slots, rows, lanes = v.shape
    shape = jax.ShapeDtypeStruct
    shard, total = g1.shape[2:]
    width = w.shape[0]
    late = 2 * width
    vmem = pl.BlockSpec(memory_space=pltpu.VMEM)
    scratch = lambda a: pltpu.VMEM(a.shape, a.dtype)
    return pl.pallas_call(
        back_kernel,
        out_shape=(shape(v.shape, LOW),) * 3
        + (
            shape((shard, total - width), HIGH),
            shape((shard, width), HIGH),
            shape((g2_planes.shape[1] + g2_late.shape[1], width), HIGH),
            shape((rows, width), HIGH),
        ),
        in_specs=in_hbm(11),
        out_specs=(vmem,) * 7,
        scratch_shapes=[scratch(a) for a in (qh, kh, v, att, lse, w)]
        + [
            pltpu.VMEM((rows, width), HIGH),
            pltpu.VMEM((shard, late), HIGH),
            pltpu.VMEM(d_att.shape, LOW),
            pltpu.VMEM((lanes, blocks * rows), HIGH),
            pltpu.VMEM((8, blocks * rows), HIGH),
            pltpu.SemaphoreType.DMA((10,)),
        ]
        + pair_of_semaphores(
            7 * slots
            + sum(c.COPIES for c in (Reducer, ReducerAlongZ, TokenSums, PlaneSums, ChipSums))
        )
        + Reducer.scratch(shard, total - late)
        + ReducerAlongZ.scratch(shard, late)
        + TokenSums.scratch(rows, width)
        + PlaneSums.scratch(*g2_planes.shape[1:])
        + ChipSums.scratch(*g2_late.shape[1:]),
        compiler_params=pltpu.CompilerParams(
            collective_id=2, has_side_effects=True, vmem_limit_bytes=VMEM_LIMIT
        ),
        name="back",
    )(d_att, qh, kh, v, att, lse, w, d_first, g1, g2_planes, g2_late)


def column_sum(block):
    return jnp.sum(block.astype(HIGH), axis=0, keepdims=True)


def middle_kernel(
    chunk,
    small_rows,
    remote,
    att,
    n1,
    r1,
    normed_t,
    cot_ref,
    par_ref,
    act_hbm,
    slope_hbm,
    w1_hbm,
    w2_hbm,
    out_ref,
    first_ref,
    d_att_ref,
    small_ref,
    g1_hbm,
    g2_out,
    *rest,
):
    if remote:
        g2_late, *rest = rest
    w1, w2, act, slope, acc, low, sums_ref, d_hid_ref, wsem, gsem, *buffers = rest
    hidden, width = w2.shape
    steps = hidden // chunk
    pieces, _, held = d_att_ref.shape

    def columns(c):
        return pl.ds(pl.multiple_of(c * chunk, chunk), chunk)

    def load1(c):
        return pltpu.make_async_copy(w1_hbm.at[:, columns(c)], w1.at[:, columns(c)], wsem.at[0, c])

    def load2(c):
        return pltpu.make_async_copy(w2_hbm.at[columns(c)], w2.at[columns(c)], wsem.at[1, c])

    def load_act(c):
        return pltpu.make_async_copy(act_hbm.at[:, columns(c)], act.at[:, columns(c)], wsem.at[2, c])

    def load_slope(c):
        return pltpu.make_async_copy(
            slope_hbm.at[:, columns(c)], slope.at[:, columns(c)], wsem.at[3, c]
        )

    if remote:
        b, z = position()
        barrier = pltpu.get_barrier_semaphore()
        peers = [(b ^ d, z) for d in (1, 2, 4)] + [(b, z ^ d) for d in (1, 2)]
        for peer in peers:
            pl.semaphore_signal(barrier, inc=1, device_id=peer, device_id_type=MESH)
    last = pl.ds(hidden, width)
    for c in range(steps):
        load_act(c).start()
        load2(c).start()
    for c in range(steps):
        load_slope(c).start()
        load1(c).start()
    load_out = pltpu.make_async_copy(w1_hbm.at[:, last], w1.at[:, last], wsem.at[0, steps])
    load_out.start()
    gain1, gain2 = par_ref[0:1], par_ref[1:2]
    bias = lambda i: par_ref[2 + i : 3 + i]
    acc[...] = n1[...] * gain1 + (bias(3) + bias(4))

    @pl.loop(0, steps)
    def _(c):
        load_act(c).wait()
        load2(c).wait()
        acc[...] += product(act[:, columns(c)], w2[columns(c), :])

    normal, inverse2 = normalize(acc[...])
    out_ref[...] = (normal * gain2 + bias(5)).astype(LOW)
    cot = cot_ref[...].astype(HIGH)
    d_second = normalize_back(cot * gain2, normal, inverse2)
    low[...] = d_second.astype(LOW)
    acc[...] = d_second
    sums_ref[1:2] = column_sum(cot * normal)
    sums_ref[4:5] = column_sum(low[...])
    sums_ref[5:6] = column_sum(cot)

    def store1(c):
        return pltpu.make_async_copy(w1.at[:, columns(c)], g1_hbm.at[:, columns(c)], gsem.at[0, c])

    def store2(c):
        return pltpu.make_async_copy(w2.at[columns(c)], g2_out.at[columns(c)], gsem.at[1, c])

    first_events, second_events = {}, {}
    if remote:
        pl.semaphore_wait(barrier, len(peers))
        s = Sender(*buffers[:2])
        each = w2.shape[0] // (8 * 4)
        cut = buffers[2].shape[2]
        plain = lambda bb, zz: w2.at[pl.ds(pl.multiple_of((bb * 4 + zz) * each, each), cut)]
        upper = lambda bb, zz: w2.at[
            pl.ds(pl.multiple_of((bb * 4 + zz) * each + cut, 16), each - cut)
        ]
        sums = Reducer(s, plain, g2_out, *buffers[2:5])
        late = ReducerAlongZ(s, upper, g2_late, buffers[5], None, None, buffers[6])
        sums.keep_for_later(buffers[7])
        late.keep_for_later(buffers[8])
        first_events = {
            0: [(late.give, 3), (sums.give, 3)],
            2: [(late.give, 2), (sums.give, 2)],
            3: [(late.fold, 3), (sums.fold_chip, 3)],
            4: [(late.give, 1), (sums.give, 1)],
            5: [(late.fold, 2), (sums.fold_chip, 2)],
            6: [(late.give, 0), (sums.give, 0), (late.relay, 3)],
            7: [(late.fold, 1), (sums.fold_chip, 1)],
        }
        second_events = {
            0: [(late.relay, 2)],
            1: [(late.fold, 0), (sums.fold_chip, 0), (late.relay, 1)],
            2: [(sums.relay, 3), (sums.relay, 2)],
            3: [(late.relay, 0), (sums.relay, 1)],
            4: [(sums.relay, 0), (late.collect, 3)],
            5: [(late.collect, 2)],
            6: [(late.collect, 1), (sums.collect, 3)],
            7: [(sums.collect, 2)],
        }

    def run(events, step):
        for at, some in events.items():

            @pl.when(step == at)
            def _(some=some):
                for event, *what in some:
                    event(*what)

    @pl.loop(0, steps)
    def _(step):
        c = b ^ (7 - step) if remote else step
        load_slope(c).wait()
        d_act = product_nt(low[...], w2[columns(c), :])
        d_pre = (d_act * slope[:, columns(c)].astype(HIGH)).astype(LOW)
        d_hid_ref[:, columns(c)] = column_sum(d_pre)
        slope[:, columns(c)] = d_pre
        w2[columns(c), :] = product_tn(act[:, columns(c)], low[...]).astype(LOW)
        if not remote:
            store2(c).start()
        run(first_events, step)

    @pl.loop(0, steps)
    def _(c):
        load1(c).wait()
        d_pre = slope[:, columns(c)]
        acc[...] += product_nt(d_pre, w1[:, columns(c)])
        w1[:, columns(c)] = product(normed_t[...], d_pre).astype(LOW)
        store1(c).start()
        run(second_events, c)

    d_normed = acc[...]
    normal = n1[...]
    d_first = normalize_back(d_normed * gain1, normal, r1[:, 0:1])
    first_ref[...] = d_first
    low[...] = d_first.astype(LOW)
    sums_ref[0:1] = column_sum(d_normed * normal)
    sums_ref[2:3] = column_sum(low[...])
    sums_ref[3:4] = column_sum(d_normed)
    load_out.wait()
    d_att = product_nt(low[...], w1[:, hidden:]).astype(LOW)
    for i in range(pieces):
        d_att_ref[i] = d_att[:, i * held : (i + 1) * held]
    w1[:, hidden:] = product_tn(att[...], low[...]).astype(LOW)
    store_out = pltpu.make_async_copy(w1.at[:, last], g1_hbm.at[:, last], gsem.at[0, steps])
    store_out.start()
    blocks, planes, _ = small_ref.shape
    small_ref[...] = jnp.zeros_like(small_ref)
    owners = [(i, j) for i in range(blocks) for j in range(width // (blocks * small_rows))]
    for at, (i, j) in enumerate(owners):
        for k in range(6):
            small_ref[i, j : j + 1, k * small_rows : (k + 1) * small_rows] = sums_ref[
                k : k + 1, at * small_rows : (at + 1) * small_rows
            ]
        part = hidden // len(owners)
        small_ref[i, j : j + 1, 6 * small_rows : 6 * small_rows + part] = d_hid_ref[
            :, at * part : (at + 1) * part
        ]
    if remote:
        sums.collect(1)
        late.collect(0)
        sums.collect(0)
        for copy in sums.keep + late.keep:
            copy.wait()
        s.drain()
    for c in range(steps):
        store1(c).wait()
        if not remote:
            store2(c).wait()
    store_out.wait()


def middle(att, n1, r1, normed_t, cot, par, act, slope, w1, w2, pieces, planes, remote):
    count, width = cot.shape
    hidden = w2.shape[0]
    chunk = 512
    shape = jax.ShapeDtypeStruct
    vmem = pl.BlockSpec(memory_space=pltpu.VMEM)
    shard = hidden // (pieces * planes)
    late = shard // 4
    buffers, params = [], {}
    g2_shape = [shape(w2.shape, LOW)]
    if remote:
        g2_shape = [shape((4, shard - late, width), LOW), shape((4, late, width), LOW)]
        buffers = pair_of_semaphores(Reducer.COPIES + ReducerAlongZ.COPIES)
        buffers += Reducer.scratch(shard - late, width, in_place=True)[:3]
        buffers += ReducerAlongZ.scratch(late, width, in_place=True)[::3]
        buffers += [pltpu.SemaphoreType.DMA((4,)), pltpu.SemaphoreType.DMA((4,))]
        params = dict(collective_id=4, has_side_effects=True)
    return pl.pallas_call(
        functools.partial(middle_kernel, chunk, width // (pieces * planes), remote),
        out_shape=(
            shape((count, width), LOW),
            shape((count, width), HIGH),
            shape((pieces, count, width // pieces), LOW),
            shape((pieces, -(-planes // 8) * 8, 384), HIGH),
            shape(w1.shape, LOW),
            *g2_shape,
        ),
        in_specs=[vmem] * 6 + in_hbm(4),
        out_specs=(vmem,) * 4 + tuple(in_hbm(1 + len(g2_shape))),
        scratch_shapes=[
            pltpu.VMEM(w1.shape, LOW),
            pltpu.VMEM(w2.shape, LOW),
            pltpu.VMEM((count, hidden), LOW),
            pltpu.VMEM((count, hidden), LOW),
            pltpu.VMEM((count, width), HIGH),
            pltpu.VMEM((count, width), LOW),
            pltpu.VMEM((8, width), HIGH),
            pltpu.VMEM((1, hidden), HIGH),
            pltpu.SemaphoreType.DMA((4, hidden // chunk + 1)),
            pltpu.SemaphoreType.DMA((2, hidden // chunk + 1)),
        ]
        + buffers,
        compiler_params=pltpu.CompilerParams(vmem_limit_bytes=VMEM_LIMIT, **params),
        name="middle",
    )(att, n1, r1, normed_t, cot, par, act, slope, w1, w2)


def finish_kernel(
    dq,
    dk,
    dv,
    w,
    first,
    tok0,
    small,
    x_hbm,
    tok_out,
    in_out,
    gains_out,
    biases_out,
    hidden_out,
    first_rows,
    x,
    D,
    P,
    R,
    Z,
    M,
    N,
    T,
    lsem,
    send,
    recv,
    *buffers,
):
    b, z = position()
    rows, width = tok0.shape
    blocks = dq.shape[0]
    count = 2 * rows
    loads = [
        pltpu.make_async_copy(x_hbm.at[i, pl.ds(0, count)], x.at[i], lsem.at[i])
        for i in range(blocks)
    ]
    loads.append(pltpu.make_async_copy(first.at[pl.ds(rows, rows)], first_rows, lsem.at[blocks]))
    loads.append(pltpu.make_async_copy(tok0, tok_out.at[pl.ds(0, rows)], lsem.at[blocks + 1]))
    for load in loads:
        load.start()
    greet([(b ^ d, z) for d in range(1, 8)] + [(b, z ^ d) for d in (1, 2, 3)])
    s = Sender(send, recv)

    def piece(i):
        mixed = jnp.concatenate([ref[i, 1] for ref in (dq, dk, dv)], axis=-1)
        return product_nt(mixed, w[...])

    tokens = TokenSums(s, piece, *buffers)
    small_in = [
        s.go(small.at[b ^ d], M.at[d - 1], (b ^ d, z), M.at[d - 1]) for d in range(1, 8)
    ]
    total = jnp.zeros((width, w.shape[1]), HIGH)
    for i in range(blocks):
        loads[i].wait()
        mixed = jnp.concatenate([ref[i].reshape(count, -1) for ref in (dq, dk, dv)], axis=-1)
        total = total + product_tn(x[i], mixed)
    D[...] = total.astype(LOW).reshape(D.shape)
    share_rows = D.shape[1] // 4

    def share(d):
        return D.at[:, pl.ds(pl.multiple_of((z ^ d) * share_rows, share_rows), share_rows)]

    in_z = [s.go(share(d), Z.at[d - 1], (b, z ^ d), Z.at[d - 1]) for d in (1, 2, 3)]
    for e in (3, 2, 1, 0):
        tokens.give(e)
    for e in (3, 2, 1, 0):
        tokens.take(e)

    N[...] = small[b]
    for i in range(7):
        small_in[i].wait_recv()
        N[...] += M[i]
    for row, ref in ((4, dq), (5, dv)):
        whole = jnp.zeros((1, 128), HIGH)
        for i in range(blocks):
            whole = whole + column_sum(ref[i].reshape(count, -1))
        N[row : row + 1, 0:128] = whole
    small_z = [s.go(N, T.at[d - 1], (b, z ^ d), T.at[d - 1]) for d in (1, 2, 3)]

    for copy in in_z:
        copy.wait_recv()
    plane = share(0)[...].astype(HIGH)
    for i in range(3):
        plane = plane + Z[i].astype(HIGH)
    P[...] = plane
    grads_in = [
        s.go(P.at[b ^ d], R.at[b], (b ^ d, z), R.at[b ^ d]) for d in range(1, 8)
    ]
    R[b] = P[b]
    tokens.relay()
    for copy in small_z:
        copy.wait_recv()
    vectors = ((N[...] + T[0]) + T[1]) + T[2]
    planes = lax.broadcasted_iota(jnp.int32, vectors.shape, 0)
    row = jnp.sum(jnp.where(planes == z, vectors, 0.0), axis=0, keepdims=True)
    n = gains_out.shape[1]
    for k in range(2):
        gains_out[k : k + 1] = row[:, k * n : (k + 1) * n]
        own = vectors[4 + k : 5 + k]
        parts = [jnp.where(z == j, own[:, j * n : (j + 1) * n], 0.0) for j in range(4)]
        biases_out[k : k + 1] = (parts[0] + parts[1]) + (parts[2] + parts[3])
    for k in range(2, 6):
        biases_out[k : k + 1] = row[:, k * n : (k + 1) * n]
    hidden_out[...] = row[:, 6 * n : 6 * n + hidden_out.shape[1]]
    for copy in grads_in:
        copy.wait_recv()
    for i in range(blocks):
        for k in range(3):
            at = k * width + i * 128
            in_out[:, at : at + 128] = R[i, :, k * 128 : (k + 1) * 128]
    for load in loads[blocks:]:
        load.wait()
    tok_out[rows:] = first_rows[...] + tokens.total()
    s.drain()


def finish(dq, dk, dv, w, d_first, tok0, small, x):
    rows, width = tok0.shape
    blocks, columns = dq.shape[0], w.shape[1]
    share = width // (4 * blocks)
    vmem = pl.BlockSpec(memory_space=pltpu.VMEM)
    shape = lambda *s: jax.ShapeDtypeStruct(s, HIGH)
    low = lambda *s: pltpu.VMEM(s, LOW)
    wide = lambda *s: pltpu.VMEM(s, HIGH)
    tile = small.shape[1:]
    return pl.pallas_call(
        finish_kernel,
        out_shape=(
            shape(2 * rows, width),
            shape(share, 3 * width),
            shape(2, share),
            shape(6, share),
            shape(1, 4 * share),
        ),
        in_specs=[vmem] * 4 + in_hbm(2) + [vmem] + in_hbm(1),
        out_specs=(vmem,) * 5,
        scratch_shapes=[
            wide(rows, width),
            low(blocks, 2 * rows, width),
            low(blocks, 4 * share, columns),
            wide(blocks, share, columns),
            wide(blocks, share, columns),
            low(3, blocks, share, columns),
            wide(7, *tile),
            wide(*tile),
            wide(3, *tile),
            pltpu.SemaphoreType.DMA((blocks + 2,)),
        ]
        + pair_of_semaphores(20 + TokenSums.COPIES)
        + TokenSums.scratch(rows, width),
        compiler_params=pltpu.CompilerParams(
            collective_id=3, has_side_effects=True, vmem_limit_bytes=VMEM_LIMIT
        ),
        name="finish",
    )(dq, dk, dv, w, d_first, tok0, small, x)


def swap(pieces):
    return lax.all_to_all(pieces, "blk", 0, 0)


def by_slot(block, slots):
    blocks, count, held = block.shape
    block = block.reshape(blocks, slots, count // slots, held)
    return jnp.pad(block, ((0, 0),) * 3 + ((0, 128 - held),))


def front_apart(X, W, bias, slots):
    n_blk, count = X.shape[0], X.shape[1] - 16
    held = W.shape[1] // 3
    mixed = jnp.einsum("brd,dc->brc", X[:, :count], W, preferred_element_type=HIGH)
    parts = [mixed[..., i * held : (i + 1) * held] for i in range(3)]
    parts = [jnp.pad(p, ((0, 0), (0, 0), (0, 128 - held))).reshape(-1, 128) for p in parts]
    own = lax.dynamic_slice(bias[:2], (0, lax.axis_index("blk") * held), (2, held))
    own = jnp.pad(own, ((0, 0), (0, 128 - held)))
    codes = X[:, count, :count].reshape(-1, 1).astype(jnp.int32)
    codes = jnp.broadcast_to(codes, (n_blk * count, 128))
    queries, keys, values = split_heads(jnp.concatenate(parts, axis=1), (own[0], own[1]), codes)
    shape = (n_blk, slots, count // slots, 128)
    qh = jnp.stack(queries).reshape(2, *shape)
    kh = jnp.stack(keys).reshape(2, *shape)
    v = values.reshape(shape)
    att, lse = attend(qh, kh, v)
    rows_att = swap(att[..., :held].reshape(n_blk, count, held))
    return qh, kh, v, att, lse, rows_att


def on_device(
    tokens,
    input_weight,
    output_weight,
    expand_weight,
    reduce_weight,
    gains,
    biases,
    hidden_bias,
    segment,
    present,
    cotangent,
):
    slots, rows, width = tokens.shape
    n_blk, n_dp = lax.axis_size("blk"), lax.axis_size("dp")
    shards = n_blk * n_dp
    fast = (n_blk, n_dp) == (8, 4)
    held = width // n_blk
    shard = input_weight.shape[0]
    hidden = expand_weight.shape[1]
    count = slots * rows
    flat = tokens.reshape(count, width)

    if fast:
        front_out = front(
            flat,
            segment,
            present,
            input_weight,
            gains,
            biases,
            hidden_bias[None],
            expand_weight,
            output_weight,
            reduce_weight,
        )
        X, W1, W2, act, slope, W, _, qh, kh, v, att, lse = front_out[:12]
        attended, n1, r1, normed_t, cuts = front_out[12:]
        W1, W2 = W1.reshape(width, -1), W2.reshape(hidden, width)
    else:
        code = (segment + 4 * (1 - present)).reshape(1, count).astype(LOW)
        code_rows = jnp.pad(jnp.broadcast_to(code, (16, count)), ((0, 0), (0, width - count)))
        columns = input_weight.reshape(shard, 3, n_blk, held).transpose(2, 0, 1, 3)
        columns = columns.reshape(n_blk, shard, 3 * held)
        small = jnp.concatenate([gains.reshape(-1), biases.reshape(-1), hidden_bias])
        X = lax.all_gather(jnp.concatenate([flat, code_rows], axis=0), "blk")
        W = lax.all_gather(swap(columns), "dp", axis=1).reshape(width, 3 * held)
        small = lax.all_gather(small, BOTH)
        W1 = jnp.concatenate([expand_weight, output_weight], axis=1)
        W1 = lax.all_gather(W1, BOTH, axis=0, tiled=True)
        W2 = lax.all_gather(reduce_weight, BOTH, axis=0, tiled=True)
        part = width // shards
        cuts = small[:, : 8 * part].reshape(shards, 8, part).transpose(1, 0, 2)
        cuts = cuts.reshape(8, width).astype(HIGH)
        hidden_full = small[:, 8 * part :].reshape(hidden).astype(HIGH)
        gain, bias = cuts[:2], cuts[2:]
        qh, kh, v, att, lse, rows_att = front_apart(X, W, bias, slots)
        attended = rows_att.transpose(1, 0, 2).reshape(count, width)
        branch = product(attended, W1[:, hidden:]) + bias[2]
        n1, r1 = normalize(flat.astype(HIGH) + branch)
        r1 = jnp.broadcast_to(r1, (count, 128))
        normed_low = (n1 * gain[0] + bias[3]).astype(LOW)
        act, slope = gelu_parts(product(normed_low, W1[:, :hidden]) + hidden_full)
        act, slope = act.astype(LOW), slope.astype(LOW)
        normed_t = normed_low.T
    cot = cotangent.reshape(count, width)
    middle_out = middle(
        attended, n1, r1, normed_t, cot, cuts, act, slope, W1, W2, n_blk, n_dp, fast
    )
    output, d_first, d_att, small_rows, grad_both, grad_reduce = middle_out[:6]
    output = output.reshape(slots, rows, width)
    if fast:
        grad_both = grad_both.reshape(n_blk, n_dp, shard, -1)
        dq, dk, dv, sum_expand, sum_output, sum_reduce, tok0 = back(
            d_att, qh, kh, v, att, lse, W, d_first, grad_both, grad_reduce, middle_out[6]
        )
        grad_tokens, grad_input, d_gains, d_biases, d_hidden = finish(
            dq, dk, dv, W, d_first, tok0, small_rows, X
        )
        return (
            output,
            grad_tokens.reshape(slots, rows, width),
            grad_input,
            sum_output,
            sum_expand,
            sum_reduce,
            d_gains,
            d_biases,
            d_hidden.reshape(-1),
        )
    sum_both = lax.psum_scatter(grad_both, BOTH, scatter_dimension=0, tiled=True).astype(HIGH)
    sum_reduce = lax.psum_scatter(grad_reduce, BOTH, scatter_dimension=0, tiled=True)
    dq, dk, dv = attend_back(qh, att, by_slot(swap(d_att), slots), lse, kh, v)
    d_mixed = jnp.concatenate([dq[..., :held], dk[..., :held], dv[..., :held]], axis=-1)
    d_mixed = d_mixed.reshape(n_blk * count, 3 * held)
    all_tokens = X[:, :count].reshape(n_blk * count, width)
    d_input = product_tn(all_tokens, d_mixed).astype(LOW)
    d_tokens = product_nt(d_mixed, W).astype(LOW)
    d_tokens = lax.psum_scatter(d_tokens, "blk", scatter_dimension=0, tiled=True)
    grad_tokens = d_first + d_tokens.astype(HIGH)
    d_input = swap(d_input.reshape(n_blk, n_dp * shard, 3 * held))
    d_input = d_input.reshape(n_blk, n_dp, shard, 3, held).transpose(1, 2, 3, 0, 4)
    d_input = d_input.reshape(n_dp, shard, 3 * width).astype(HIGH)
    grad_input = lax.psum_scatter(d_input, "dp", scatter_dimension=0, tiled=False)
    col = lambda a: jnp.sum(a.astype(HIGH), axis=0)
    own_cols = jnp.stack([col(d_mixed[:, :held]), col(d_mixed[:, 2 * held :])])
    own_cols = lax.psum_scatter(own_cols, "dp", scatter_dimension=1, tiled=True)
    small_rows = small_rows[:, :n_dp].reshape(shards, -1)
    small_sum = lax.psum_scatter(small_rows, BOTH, scatter_dimension=0, tiled=False)
    vectors = small_sum[: 6 * part].reshape(6, part)
    return (
        output,
        grad_tokens.reshape(slots, rows, width),
        grad_input,
        sum_both[:, hidden:],
        sum_both[:, :hidden],
        sum_reduce.astype(HIGH),
        vectors[:2],
        jnp.concatenate([own_cols, vectors[2:]], axis=0),
        small_sum[6 * part : 6 * part + hidden // shards],
    )


def solution(mesh):
    rows, sharded = P("dp", "blk", None), P(BOTH, None)
    in_specs = (rows, sharded, sharded, sharded, sharded, P(None, BOTH), P(None, BOTH), P(BOTH))
    in_specs += (P("dp", "blk"), P("dp", "blk"), rows)
    out_specs = (rows, rows, sharded, sharded, sharded, sharded)
    out_specs += (P(None, BOTH), P(None, BOTH), P(BOTH))
    return jax.shard_map(
        on_device, mesh=mesh, in_specs=in_specs, out_specs=out_specs, check_vma=False
    )
```

```python
import functools

import jax
import jax.numpy as jnp
from jax import lax
from jax.experimental import pallas as pl
from jax.experimental.pallas import tpu as pltpu
from jax.sharding import PartitionSpec as P

HEADS = 16
EPSILON = 1e-12
FAR = 2.0**60
BOTH = ("blk", "dp")
MESH = pl.DeviceIdType.MESH
LOW = jnp.bfloat16
HIGH = jnp.float32
VMEM_LIMIT = 60 * 2**20


def product(left, right):
    return jnp.dot(left, right, preferred_element_type=HIGH)


def product_nt(left, right):
    return lax.dot_general(left, right, (((1,), (1,)), ((), ())), preferred_element_type=HIGH)


def product_tn(left, right):
    return lax.dot_general(left, right, (((0,), (0,)), ((), ())), preferred_element_type=HIGH)


def normalize(values):
    mean = jnp.mean(values, axis=-1, keepdims=True)
    centred = values - mean
    spread = jnp.mean(centred * centred, axis=-1, keepdims=True)
    inverse = lax.rsqrt(spread + EPSILON)
    return centred * inverse, inverse


def normalize_back(grad, normal, inverse):
    return inverse * (
        grad
        - jnp.mean(grad, axis=-1, keepdims=True)
        - normal * jnp.mean(grad * normal, axis=-1, keepdims=True)
    )


def quick_reciprocal(x):
    first = pl.reciprocal(x, approx=True)
    return first * (2.0 - x * first)


def gelu_parts(u, reciprocal=lambda x: 1.0 / x):
    bell = jnp.exp(-0.5 * u * u)
    below = 1.0 + (0.3275911 * 0.5**0.5) * jnp.abs(u)
    t = reciprocal(below)
    poly = 1.061405429 * t - 1.453152027
    poly = poly * t + 1.421413741
    poly = poly * t - 0.284496736
    poly = poly * t + 0.254829592
    tail = 0.5 * poly * t * bell
    below = jnp.where(u < 0.0, tail, 1.0 - tail)
    return u * below, below + u * bell * 0.3989422804014327


class Sender:
    def __init__(self, send, recv):
        self.send, self.recv, self.planned = send, recv, []

    def plan(self, src, dst, device, landing):
        at = len(self.planned)

        def copy(a, b):
            return pltpu.make_async_remote_copy(
                src_ref=a,
                dst_ref=b,
                send_sem=self.send.at[at],
                recv_sem=self.recv.at[at],
                device_id=device,
                device_id_type=MESH,
            )

        out = copy(src, dst)
        self.planned.append(out)
        landed = copy(landing, landing)
        landed.go = out.start
        return landed

    def go(self, *what):
        landed = self.plan(*what)
        landed.go()
        return landed

    def drain(self):
        for out in self.planned:
            out.wait_send()


def greet(peers):
    barrier = pltpu.get_barrier_semaphore()
    for peer in peers:
        pl.semaphore_signal(barrier, inc=1, device_id=peer, device_id_type=MESH)
    pl.semaphore_wait(barrier, len(peers))


def half(ref, which):
    rows = ref.shape[0]
    cut = rows // 32 * 16
    return ref.at[pl.ds(0, cut)] if which == 0 else ref.at[pl.ds(cut, rows - cut)]


def position():
    return lax.axis_index("blk"), lax.axis_index("dp")


def first_lanes(shape):
    return lax.broadcasted_iota(jnp.int32, shape, len(shape) - 1) < 64


def rows_of(block):
    return block.reshape(-1, block.shape[-1])


def attend_tile(queries, keys, values):
    rows = queries[0].shape[0]
    ones = jnp.ones_like(values)
    mine = first_lanes(values.shape)
    outs, logs = [], []
    for head in (0, 1):
        scores = product_nt(queries[head], keys[head])
        top = jnp.max(scores, axis=-1, keepdims=True)
        weights = jnp.exp(scores - top).astype(LOW)
        total = product(weights, jnp.where(mine == (head == 0), values, ones))
        mass = pltpu.roll(total, 64, 1)
        outs.append(total / mass)
        logs.append(top + jnp.log(mass))
    mine = first_lanes((rows, 128))
    flipped = jnp.where(mine, logs[0], logs[1]).T
    logs = jnp.concatenate([flipped[0:1], flipped[64:65], jnp.zeros((6, rows), HIGH)], axis=0)
    return jnp.where(mine, outs[0], outs[1]).astype(LOW), logs


def split_heads(mixed, bias, codes):
    rows = mixed.shape[0]
    q = (mixed[:, :128] + bias[0]).astype(LOW) * LOW(0.125)
    k = mixed[:, 128:256].astype(LOW)
    v = (mixed[:, 256:] + bias[1]).astype(LOW)
    lanes = lax.broadcasted_iota(jnp.int32, (rows, 128), 1) % 64
    protein = jnp.where(codes >= 4, codes - 4, codes)
    q_marks = jnp.where((lanes < 5) & (lanes != protein), -FAR, 0.0).astype(LOW)
    k_marks = jnp.where(lanes == jnp.minimum(codes, 4), 1.0, 0.0).astype(LOW)
    mine = first_lanes((rows, 128))
    return (
        (jnp.where(mine, q, q_marks), jnp.where(mine, q_marks, q)),
        (jnp.where(mine, k, k_marks), jnp.where(mine, k_marks, k)),
        v,
    )


def spread_vectors(small, par, hid):
    for i in range(8):
        for j in range(4):
            row = small[j, i : i + 1].astype(HIGH)
            at = (i * 4 + j) * 32
            for k in range(8):
                par[k : k + 1, at : at + 32] = row[:, k * 32 : k * 32 + 32]
            hid[:, at * 4 : at * 4 + 128] = row[:, 256:384]


def front_kernel(
    x,
    segment,
    present,
    input_weight,
    gains,
    biases,
    hidden_bias,
    expand,
    out_w_in,
    w2,
    X_out,
    W1,
    W2,
    act_out,
    slope_out,
    wfull,
    small,
    qh_out,
    kh_out,
    v_out,
    att_out,
    lse_out,
    branch_in_out,
    n1_out,
    r1_out,
    normed_t_out,
    par,
    qh,
    kh,
    v,
    att,
    lse,
    branch_in,
    n1,
    r1,
    normed_t,
    normed_low,
    X,
    W,
    win,
    w1,
    rows_att,
    w1v,
    act,
    slope,
    hid,
    send,
    recv,
    asend,
    arecv,
    lsem,
    osem,
    wsem,
    csem,
    fsem,
):
    b, z = position()
    bx, by, bd, bc = b ^ 2, b ^ 4, b ^ 6, b ^ 1
    count = X.shape[1] - 16
    hidden, width = expand.shape[1], x.shape[1]
    slots, rows = qh.shape[2:4]
    locs = []

    def local(src, dst):
        copy = pltpu.make_async_copy(src, dst, lsem.at[len(locs)])
        copy.start()
        locs.append(copy)

    local(x, X.at[b, pl.ds(0, count)])
    local(expand, w1.at[:, pl.ds(0, hidden)])
    local(out_w_in, w1.at[:, pl.ds(hidden, width)])
    local(w2, W2.at[b, z])
    shard = input_weight.shape[0]
    n = gains.shape[1]
    win[...] = jnp.zeros_like(win)
    for i in range(8):
        for k in range(3):
            at = k * width + i * 128
            win[i, 0:shard, k * 128 : (k + 1) * 128] = input_weight[:, at : at + 128]
    rows_small = [gains[k : k + 1] for k in range(2)] + [biases[k : k + 1] for k in range(6)]
    line = jnp.concatenate(rows_small + [hidden_bias[...]], axis=1)
    for i in range(8):
        win[i, shard : shard + 16] = jnp.broadcast_to(line, (16, line.shape[1]))
    W[z, b] = win[b]
    codes = (segment[...] + 4 * (1 - present[...])).astype(HIGH).astype(LOW)
    codes = jnp.concatenate([codes[k : k + 1] for k in range(slots)], axis=1)
    X[b, pl.ds(count, 16), 0:count] = jnp.broadcast_to(codes, (16, count))
    X[b, pl.ds(count, 16), count:width] = jnp.zeros((16, width - count), LOW)
    greet([(b ^ d, z) for d in range(1, 8)] + [(b, z ^ d) for d in range(1, 4)])
    s = Sender(send, recv)
    to_x, to_y, to_core = (bx, z), (by, z), (bc, z)

    def token_core(src, bb):
        return s.plan(src, X.at[bb], to_core, X.at[bb ^ 1])

    def to_z(d):
        return b, z ^ d

    def hops(F, src, zz):
        near = [
            s.plan(src, F.at[b, zz], to_x, F.at[bx, zz]),
            s.plan(src, F.at[b, zz], to_y, F.at[by, zz]),
        ]
        one, two = half(F.at[bx, zz], 0), half(F.at[by, zz], 1)
        far = [
            s.plan(one, one, to_y, half(F.at[bd, zz], 0)),
            s.plan(two, two, to_x, half(F.at[bd, zz], 1)),
        ]
        return near, far

    def planes(F, src, bb):
        pair = [s.plan(src, F.at[bb, z], to_z(d), F.at[bb, z ^ d]) for d in (1, 2)]
        on = F.at[bb, z ^ 2]
        return pair + [s.plan(on, on, to_z(1), F.at[bb, z ^ 3])]

    def to_sibling(F, src, bb, zz):
        return s.plan(src, F.at[bb, zz], to_core, F.at[bb ^ 1, zz])

    places = (b, bx, by, bd)
    z1 = planes(W1, w1, b)
    hop1 = [hops(W1, W1.at[b, z ^ d] if d else w1, z ^ d) for d in range(4)]
    hop2 = hops(W2, w2, z)
    z2 = [planes(W2, W2.at[bb, z] if i else w2, bb) for i, bb in enumerate(places)]
    core1, core2 = (
        {
            (i, d): to_sibling(F, F.at[bb, z ^ d] if i or d else own, bb, z ^ d)
            for i, bb in enumerate(places)
            for d in range(4)
        }
        for F, own in ((W1, w1), (W2, w2))
    )

    def start(*copies):
        for copy in copies:
            copy.go()

    def first(d):
        if d in (1, 3):
            z1[d - 1].wait_recv()
        start(*hop1[d][0], core1[0, d])

    def second(d):
        near, far = hop1[d]
        for i in (0, 1):
            near[i].wait_recv()
            start(far[i], core1[1 + i, d])

    def third(d):
        for copy in hop1[d][1]:
            copy.wait_recv()
        core1[3, d].go()

    def spread(i):
        start(z2[i][0], z2[i][1], core2[i, 0])

    def second2():
        near, far = hop2
        for i in (0, 1):
            near[i].wait_recv()
            far[i].go()
            spread(1 + i)

    def third2():
        for copy in hop2[1]:
            copy.wait_recv()
        spread(3)

    def arrive2(i):
        z2[i][1].wait_recv()
        start(z2[i][2], core2[i, 2])
        z2[i][0].wait_recv()
        core2[i, 1].go()

    def last2(i):
        z2[i][2].wait_recv()
        core2[i, 3].go()

    columns = [
        s.go(win.at[b ^ d], W.at[z, b], (b ^ d, z), W.at[z, b ^ d]) for d in range(1, 8)
    ]
    locs[0].wait()
    token_x = s.go(X.at[b], X.at[b], to_x, X.at[bx])
    token_y = s.go(X.at[b], X.at[b], to_y, X.at[by])
    token_c = token_core(X.at[b], b)
    token_c.go()
    for copy in locs[1:3]:
        copy.wait()
    local(w1, W1.at[b, z])
    start(z1[0], z1[1])
    for copy in columns:
        copy.wait_recv()
    for i in range(8):
        small[z, i : i + 1] = W[z, i, 32:33]
    trimmed = lambda zz: W.at[zz, :, pl.ds(0, 32)]
    columns, vectors = (
        [s.plan(at(z), at(z), to_z(d), at(z ^ d)) for d in (1, 2)]
        + [s.plan(at(z ^ 2), at(z ^ 2), to_z(1), at(z ^ 3))]
        for at in (trimmed, lambda zz: small.at[zz])
    )
    start(*columns[:2], *vectors[:2])
    spread(0)
    token_x.wait_recv()
    piece = half(X.at[bx], 0)
    token_one = s.go(piece, piece, to_y, half(X.at[bd], 0))
    token_xc = token_core(X.at[bx], bx)
    token_xc.go()
    token_y.wait_recv()
    piece = half(X.at[by], 1)
    token_two = s.go(piece, piece, to_x, half(X.at[bd], 1))
    token_yc = token_core(X.at[by], by)
    token_yc.go()
    token_dc = token_core(X.at[bd], bd)
    start(*hop2[0])
    columns[1].wait_recv()
    columns[2].go()
    vectors[1].wait_recv()
    vectors[2].go()
    z1[1].wait_recv()
    z1[2].go()
    for copy in (columns[0], columns[2], vectors[0], vectors[2]):
        copy.wait_recv()
    for i in range(8):
        for j in range(4):
            at = (i * 4 + j) * 32
            wfull[at : at + 32] = W[j, i, 0:32]
    spread_vectors(small, par, hid)
    chosen = lax.broadcasted_iota(jnp.int32, (16, 128), 0) == b
    bias = [[], []]
    for j in range(4):
        row = jnp.where(chosen, small[j, :, 0:128].astype(HIGH), 0.0)
        row = jnp.sum(row, axis=0, keepdims=True)
        bias[0].append(row[:, 64:96])
        bias[1].append(row[:, 96:128])
    bias = [jnp.concatenate(parts, axis=1) for parts in bias]

    def mix(i):
        pltpu.make_async_copy(X.at[i], X_out.at[i], osem.at[i]).start()
        mixed = product(X[i, 0:count], wfull[...])
        codes = jnp.broadcast_to(X[i, count : count + 1, 0:count].astype(HIGH), (128, count)).T
        queries, keys, values = split_heads(mixed, bias, codes.astype(jnp.int32))
        for head in (0, 1):
            qh[head, i] = queries[head].reshape(slots, rows, 128)
            kh[head, i] = keys[head].reshape(slots, rows, 128)
        v[i] = values.reshape(slots, rows, 128)

    mix(b)
    token_c.wait_recv()
    mix(bc)
    mix(bx)
    token_xc.wait_recv()
    mix(bx ^ 1)
    mix(by)
    token_one.wait_recv()
    token_two.wait_recv()
    token_dc.go()
    first(0)
    first(2)
    first(1)
    second2()
    first(3)
    token_yc.wait_recv()
    mix(by ^ 1)
    mix(bd)
    token_dc.wait_recv()
    mix(bd ^ 1)
    arrive2(0)

    def piece_of(slot):
        return pl.ds(pl.multiple_of(slot * rows, rows), rows)

    def send_att(slot, d):
        return pltpu.make_async_remote_copy(
            src_ref=att.at[b ^ d, slot],
            dst_ref=rows_att.at[b, piece_of(slot)],
            send_sem=asend.at[slot * 8 + d],
            recv_sem=arecv.at[slot * 8 + d],
            device_id=(b ^ d, z),
            device_id_type=MESH,
        )

    def keep_att(slot):
        return pltpu.make_async_copy(
            att.at[b, slot], rows_att.at[b, piece_of(slot)], osem.at[8 + slot]
        )

    events = {
        0: (second, 0),
        1: (third2,),
        2: (second, 2),
        4: (second, 1),
        5: (arrive2, 1),
        6: (arrive2, 2),
        7: (third, 0),
        9: (second, 3),
        10: (arrive2, 3),
        12: (third, 2),
        14: (third, 1),
    }
    late_events = {1: (last2, 0), 3: (last2, 1), 5: (last2, 2), 7: (last2, 3)}

    @pl.loop(0, 8 * slots)
    def _(step):
        slot, d = step // 8, (step + 1) % 8
        i = b ^ d
        keys = [rows_of(kh[head, :, slot]) for head in (0, 1)]
        out, logs = attend_tile([qh[head, i, slot] for head in (0, 1)], keys, rows_of(v[:, slot]))
        att[i, slot] = out
        lse[slot, :, pl.ds(pl.multiple_of(i * rows, rows), rows)] = logs

        @pl.when(d != 0)
        def _():
            send_att(slot, d).start()

        @pl.when(d == 0)
        def _():
            keep_att(slot).start()

        for at, (event, *what) in events.items():
            pl.when(step == at)(functools.partial(event, *what))

    early = [(qh, qh_out), (kh, kh_out), (v, v_out), (att, att_out), (lse, lse_out)]
    early += [(branch_in, branch_in_out), (n1, n1_out), (r1, r1_out), (normed_t, normed_t_out)]
    early = [pltpu.make_async_copy(*pair, fsem.at[i]) for i, pair in enumerate(early)]
    for copy in early[:5]:
        copy.start()

    third(3)
    for copy in core1.values():
        copy.wait_recv()
    locs[4].wait()
    chunk = 512
    steps = hidden // chunk

    def load(c, size=chunk):
        cols = pl.ds(pl.multiple_of(c * chunk, chunk), size)
        return pltpu.make_async_copy(W1.at[:, :, :, cols], w1v.at[:, :, :, cols], wsem.at[c])

    load(steps, width).start()
    for c in range(steps):
        load(c).start()
    for slot in range(slots):
        keep_att(slot).wait()
        for d in range(1, 8):
            pltpu.make_async_remote_copy(
                src_ref=rows_att.at[b ^ d, piece_of(slot)],
                dst_ref=rows_att.at[b ^ d, piece_of(slot)],
                send_sem=asend.at[slot * 8 + d],
                recv_sem=arecv.at[slot * 8 + d],
                device_id=(b ^ d, z),
                device_id_type=MESH,
            ).wait_recv()
    branch_in[...] = jnp.concatenate([rows_att[i] for i in range(8)], axis=1)
    load(steps, width).wait()
    out_w = w1v[:, :, :, hidden:].reshape(width, width)
    branch = product(branch_in[...], out_w) + par[4:5]
    normal, inverse = normalize(X[b, 0:count].astype(HIGH) + branch)
    n1[...] = normal
    r1[...] = jnp.broadcast_to(inverse, r1.shape)
    normed = (normal * par[0:1] + par[5:6]).astype(LOW)
    normed_low[...] = normed
    normed_t[...] = normed.T
    for copy in early[5:]:
        copy.start()

    def store(c, ref, out, which):
        cols = pl.ds(pl.multiple_of(c * chunk, chunk), chunk)
        return pltpu.make_async_copy(ref.at[:, cols], out.at[:, cols], csem.at[which, c])

    @pl.loop(0, steps)
    def _(c):
        cols = pl.ds(pl.multiple_of(c * chunk, chunk), chunk)
        load(c).wait()
        pre = product(normed_low[...], w1v[:, :, :, cols].reshape(width, chunk))
        value, rate = gelu_parts(pre + hid[:, cols], quick_reciprocal)
        act[:, cols] = value.astype(LOW)
        slope[:, cols] = rate.astype(LOW)
        store(c, act, act_out, 0).start()
        store(c, slope, slope_out, 1).start()
        for at, (event, *what) in late_events.items():
            pl.when(c == at)(functools.partial(event, *what))

    for copy in core2.values():
        copy.wait_recv()
    for slot in range(slots):
        for d in range(1, 8):
            send_att(slot, d).wait_send()
    for c in range(steps):
        store(c, act, act_out, 0).wait()
        store(c, slope, slope_out, 1).wait()
    s.drain()
    for copy in early:
        copy.wait()
    locs[3].wait()
    for i in range(8):
        pltpu.make_async_copy(X.at[i], X_out.at[i], osem.at[i]).wait()


def in_hbm(count):
    return [pl.BlockSpec(memory_space=pl.ANY)] * count


def pair_of_semaphores(count):
    return [pltpu.SemaphoreType.DMA((count,)), pltpu.SemaphoreType.DMA((count,))]


def front(x, segment, present, input_weight, gains, biases, hidden_bias, expand, out_w, w2):
    slots = segment.shape[0]
    count, width = x.shape
    rows, hidden = count // slots, expand.shape[1]
    shard = expand.shape[0]
    shape = lambda *s: jax.ShapeDtypeStruct(s, LOW)
    wide = lambda *s: jax.ShapeDtypeStruct(s, HIGH)
    vmem = pl.BlockSpec(memory_space=pltpu.VMEM)
    return pl.pallas_call(
        front_kernel,
        out_shape=(
            shape(8, count + 16, width),
            shape(8, 4, shard, hidden + width),
            shape(8, 4, *w2.shape),
            shape(count, hidden),
            shape(count, hidden),
            shape(width, 384),
            shape(4, 16, 384),
            shape(2, 8, slots, rows, 128),
            shape(2, 8, slots, rows, 128),
            shape(8, slots, rows, 128),
            shape(8, slots, rows, 128),
            wide(slots, 8, 8 * rows),
            shape(count, width),
            wide(count, width),
            wide(count, 128),
            shape(width, count),
            wide(8, width),
        ),
        in_specs=in_hbm(1) + [vmem] * 6 + in_hbm(3),
        out_specs=tuple(in_hbm(5)) + (vmem,) * 2 + tuple(in_hbm(9)) + (vmem,),
        scratch_shapes=[
            pltpu.VMEM((2, 8, slots, rows, 128), LOW),
            pltpu.VMEM((2, 8, slots, rows, 128), LOW),
            pltpu.VMEM((8, slots, rows, 128), LOW),
            pltpu.VMEM((8, slots, rows, 128), LOW),
            pltpu.VMEM((slots, 8, 8 * rows), HIGH),
            pltpu.VMEM((count, width), LOW),
            pltpu.VMEM((count, width), HIGH),
            pltpu.VMEM((count, 128), HIGH),
            pltpu.VMEM((width, count), LOW),
            pltpu.VMEM((count, width), LOW),
            pltpu.VMEM((8, count + 16, width), LOW),
            pltpu.VMEM((4, 8, shard + 16, 384), LOW),
            pltpu.VMEM((8, shard + 16, 384), LOW),
            pltpu.VMEM((shard, hidden + width), LOW),
            pltpu.VMEM((8, count, 128), LOW),
            pltpu.VMEM((8, 4, shard, hidden + width), LOW),
            pltpu.VMEM((count, hidden), LOW),
            pltpu.VMEM((count, hidden), LOW),
            pltpu.VMEM((1, hidden), HIGH),
        ]
        + pair_of_semaphores(116)
        + pair_of_semaphores(8 * slots)
        + [pltpu.SemaphoreType.DMA((5,)), pltpu.SemaphoreType.DMA((8 + slots,))]
        + [pltpu.SemaphoreType.DMA((hidden // 512 + 1,)), pltpu.SemaphoreType.DMA((2, hidden // 512))]
        + [pltpu.SemaphoreType.DMA((9,))],
        compiler_params=pltpu.CompilerParams(
            collective_id=1, has_side_effects=True, vmem_limit_bytes=VMEM_LIMIT
        ),
        name="front",
    )(x, segment, present, input_weight, gains, biases, hidden_bias, expand, out_w, w2)


def add_rows(out, one, two):
    @pl.loop(0, one.shape[0] // 16)
    def _(i):
        rows = pl.ds(pl.multiple_of(i * 16, 16), 16)
        out[rows, :] = one[rows, :] + two[rows, :]


def sum_rows(out, *terms):
    @pl.loop(0, out.shape[0] // 16)
    def _(i):
        rows = pl.ds(pl.multiple_of(i * 16, 16), 16)
        total = terms[0][rows, :].astype(HIGH)
        for term in terms[1:]:
            total = total + term[rows, :].astype(HIGH)
        out[rows, :] = total


class Reducer:
    ORDER = (3, 2, 1, 0)
    COPIES = 16 + 4 * 6 + 3

    def __init__(self, s, share, out, C, H, Q, Z=None, S=None, lsem=None):
        b, z = position()
        to_x, to_y, to_core = (b ^ 2, z), (b ^ 4, z), (b ^ 1, z)
        self.out, self.C, self.H, self.Q, self.Z = out, C, H, Q, Z
        self.at = at = lambda e, d: share(b ^ (2 * e), z ^ d) if S is None else S.at[e, d]
        self.mine, self.other, self.halves, self.ahead, self.rest, self.last = ({} for _ in range(6))
        for d in self.ORDER:
            for e in (3, 1, 2, 0):
                if S is not None:
                    self.mine[d, e] = pltpu.make_async_copy(
                        share(b ^ (2 * e), z ^ d), S.at[e, d], lsem.at[d * 4 + e]
                    )
                self.other[d, e] = s.plan(
                    share(b ^ 1 ^ (2 * e), z ^ d), C.at[e, d], to_core, C.at[e, d]
                )

            def send(e, part, to, where):
                return s.plan(half(at(e, d), part), where, to, where)

            self.halves[d] = [send(3, 0, to_x, H.at[d, 0]), send(3, 1, to_y, H.at[d, 1])]
            self.ahead[d] = [
                send(2, 1, to_y, half(Q.at[d, 1], 1)),
                send(1, 0, to_x, half(Q.at[d, 0], 0)),
            ]
            self.rest[d] = [
                send(2, 0, to_y, half(Q.at[d, 1], 0)),
                send(1, 1, to_x, half(Q.at[d, 0], 1)),
            ]
            if d and Z is not None:
                to = (b, z ^ (2 if d == 2 else 1))
                self.last[d] = s.plan(at(0, d), Z.at[d - 1], to, Z.at[d - 1])

    def keep_for_later(self, sems):
        self.keep = [
            pltpu.make_async_copy(self.at(*self.kept(d)), self.out.at[d], sems.at[d])
            for d in range(4)
        ]

    def kept(self, d):
        return 0, d

    def start(self):
        for d in self.ORDER:
            for e in (3, 1, 2, 0):
                self.mine[d, e].start()
                self.other[d, e].go()

    def give(self, e):
        for d in self.ORDER:
            self.other[d, e].go()

    def fold(self, d, chips=(3, 1, 2, 0)):
        for e in chips:
            if self.mine:
                self.mine[d, e].wait()
            self.other[d, e].wait_recv()
            add_rows(self.at(e, d), self.at(e, d), self.C.at[e, d])
            for copy in {3: self.halves[d], 1: self.ahead[d][1:], 2: self.ahead[d][:1], 0: []}[e]:
                copy.go()

    def fold_chip(self, e):
        for d in self.ORDER:
            self.fold(d, (e,))

    def relay(self, d):
        for i, e in ((0, 2), (1, 1)):
            self.halves[d][i].wait_recv()
            part = half(self.at(e, d), i)
            add_rows(part, part, self.H.at[d, i])
            self.rest[d][i].go()

    def collect(self, d):
        for copy in self.ahead[d] + self.rest[d]:
            copy.wait_recv()
        total = self.at(0, d)
        for i in (0, 1):
            add_rows(total, total, self.Q.at[d, i])
        if self.Z is None:
            self.keep[d].start()
            return
        if d == 2:
            self.last[3].wait_recv()
            add_rows(total, total, self.Z.at[2])
        if d:
            self.last[d].go()

    def total(self):
        for d in (1, 2):
            self.last[d].wait_recv()
        sum_rows(self.out, self.at(0, 0), self.Z.at[0], self.Z.at[1])

    LEAD = (((4, 4), 1), ((4, 2), 2), ((4, 2), 1), ((3,), 1))

    @classmethod
    def scratch(cls, rows, columns, in_place=False):
        shapes = [pltpu.VMEM((*n, rows // cut, columns), LOW) for n, cut in cls.LEAD]
        if in_place:
            return shapes
        return shapes + [pltpu.VMEM((4, 4, rows, columns), LOW), pltpu.SemaphoreType.DMA((16,))]


class ReducerAlongZ(Reducer):
    COPIES = 16 + 4 * 3 + 6

    def __init__(self, s, share, out, C, H, Q, Z, S=None, lsem=None):
        self.partial = H is None
        b, z = position()
        to_x, to_y, to_core = (b ^ 2, z), (b ^ 4, z), (b ^ 1, z)
        self.out, self.C, self.H, self.Q, self.Z = out, C, H, Q, Z
        self.at = at = lambda e, d: share(b ^ (2 * e), z ^ d) if S is None else S.at[e, d]
        self.mine, self.other, self.along = {}, {}, {}
        for e in (3, 1, 2, 0):
            for d in (3, 2, 1, 0):
                if S is not None:
                    self.mine[e, d] = pltpu.make_async_copy(
                        share(b ^ (2 * e), z ^ d), S.at[e, d], lsem.at[d * 4 + e]
                    )
                self.other[e, d] = s.plan(
                    share(b ^ 1 ^ (2 * e), z ^ d), C.at[e, d], to_core, C.at[e, d]
                )
                if d:
                    to = (b, z ^ (2 if d == 2 else 1))
                    self.along[e, d] = s.plan(at(e, d), Z.at[e, d - 1], to, Z.at[e, d - 1])

        if self.partial:
            return

        def send(e, part, to, where):
            return s.plan(half(at(e, 0), part), where, to, where)

        self.halves = [send(3, 0, to_x, H.at[0]), send(3, 1, to_y, H.at[1])]
        self.ahead = [
            send(2, 1, to_y, half(Q.at[1], 1)),
            send(1, 0, to_x, half(Q.at[0], 0)),
        ]
        self.rest = [
            send(2, 0, to_y, half(Q.at[1], 0)),
            send(1, 1, to_x, half(Q.at[0], 1)),
        ]

    def start(self):
        for at in self.mine:
            self.mine[at].start()
            self.other[at].go()

    def give(self, e):
        for d in (3, 2, 1, 0):
            self.other[e, d].go()

    def fold(self, e):
        for d in (3, 1, 2, 0):
            if self.mine:
                self.mine[e, d].wait()
            self.other[e, d].wait_recv()
            add_rows(self.at(e, d), self.at(e, d), self.C.at[e, d])
            if d in (1, 3):
                self.along[e, d].go()

    def relay(self, e):
        self.along[e, 3].wait_recv()
        add_rows(self.at(e, 2), self.at(e, 2), self.Z.at[e, 2])
        self.along[e, 2].go()

    def collect(self, e):
        total = self.at(e, 0)
        for d in (1, 2):
            self.along[e, d].wait_recv()
            add_rows(total, total, self.Z.at[e, d - 1])
        if self.partial:
            self.keep[e].start()
            return
        for copy in {3: self.halves, 1: self.ahead[1:], 2: self.ahead[:1], 0: []}[e]:
            copy.go()

    def kept(self, e):
        return e, 0

    def cross(self):
        for i, e in ((0, 2), (1, 1)):
            self.halves[i].wait_recv()
            part = half(self.at(e, 0), i)
            add_rows(part, part, self.H.at[i])
            self.rest[i].go()

    def total(self):
        for copy in self.ahead + self.rest:
            copy.wait_recv()
        sum_rows(self.out, self.at(0, 0), self.Q.at[0], self.Q.at[1])

    LEAD = (((4, 4), 1), ((2,), 2), ((2,), 1), ((4, 3), 1))


class PlaneSums:
    COPIES = 3

    def __init__(self, s, out, T, Z):
        b, z = position()
        self.out, self.T, self.Z = out, T, Z
        self.last = {
            d: s.plan(T.at[d], Z.at[d - 1], (b, z ^ (2 if d == 2 else 1)), Z.at[d - 1])
            for d in (3, 2, 1)
        }

    def start(self):
        self.last[3].go()
        self.last[1].go()

    def relay(self):
        self.last[3].wait_recv()
        add_rows(self.T.at[2], self.T.at[2], self.Z.at[2])
        self.last[2].go()

    def total(self):
        for d in (1, 2):
            self.last[d].wait_recv()
        sum_rows(self.out, self.T.at[0], self.Z.at[0], self.Z.at[1])

    @staticmethod
    def scratch(rows, columns):
        return [pltpu.VMEM((n, rows, columns), LOW) for n in (4, 3)]


class ChipSums:
    COPIES = 6

    def __init__(self, s, out, U, H, Q):
        b, z = position()
        to_x, to_y = (b ^ 2, z), (b ^ 4, z)
        self.out, self.U, self.H, self.Q = out, U, H, Q

        def send(e, part, to, where):
            return s.plan(half(U.at[e], part), where, to, where)

        self.halves = [send(3, 0, to_x, H.at[0]), send(3, 1, to_y, H.at[1])]
        self.ahead = [
            send(2, 1, to_y, half(Q.at[1], 1)),
            send(1, 0, to_x, half(Q.at[0], 0)),
        ]
        self.rest = [
            send(2, 0, to_y, half(Q.at[1], 0)),
            send(1, 1, to_x, half(Q.at[0], 1)),
        ]

    def start(self):
        for copy in self.halves + self.ahead:
            copy.go()

    def relay(self):
        for i, e in ((0, 2), (1, 1)):
            self.halves[i].wait_recv()
            part = half(self.U.at[e], i)
            add_rows(part, part, self.H.at[i])
            self.rest[i].go()

    def total(self):
        for copy in self.ahead + self.rest:
            copy.wait_recv()
        sum_rows(self.out, self.U.at[0], self.Q.at[0], self.Q.at[1])

    @staticmethod
    def scratch(rows, columns):
        shapes = (4, rows), (2, rows // 2), (2, rows)
        return [pltpu.VMEM((*n, columns), LOW) for n in shapes]


def attend_kernel(qh_ref, kh_ref, v_ref, out_ref, lse_ref):
    keys = [rows_of(kh_ref[head, :, 0]) for head in (0, 1)]
    out_ref[0, 0], lse_ref[0] = attend_tile(
        [qh_ref[head, 0, 0] for head in (0, 1)], keys, rows_of(v_ref[:, 0])
    )


def attend(qh, kh, v):
    blocks, slots, rows, lanes = v.shape
    tile = pl.BlockSpec((1, 1, rows, lanes), lambda s, i: (i, s, 0, 0))
    tiles = pl.BlockSpec((2, 1, 1, rows, lanes), lambda s, i: (0, i, s, 0, 0))
    whole = pl.BlockSpec((blocks, 1, rows, lanes), lambda s, i: (0, s, 0, 0))
    wholes = pl.BlockSpec((2, blocks, 1, rows, lanes), lambda s, i: (0, 0, s, 0, 0))
    return pl.pallas_call(
        attend_kernel,
        grid=(slots, blocks),
        out_shape=(
            jax.ShapeDtypeStruct(v.shape, LOW),
            jax.ShapeDtypeStruct((slots, 8, blocks * rows), HIGH),
        ),
        in_specs=[tiles, wholes, whole],
        out_specs=(tile, pl.BlockSpec((1, 8, rows), lambda s, i: (s, 0, i))),
        compiler_params=pltpu.CompilerParams(vmem_limit_bytes=VMEM_LIMIT),
        name="attend",
    )(qh, kh, v)


def row_products(out, grad):
    pick = (lax.broadcasted_iota(jnp.int32, (8, 128), 0) == 0) == first_lanes((8, 128))
    return lax.dot_general(
        pick.astype(HIGH),
        out.astype(HIGH) * grad.astype(HIGH),
        (((1,), (1,)), ((), ())),
        precision=lax.Precision.HIGHEST,
        preferred_element_type=HIGH,
    )


def attend_back_tile(queries, keys, values, grads, logs, delta, acc):
    zeros = jnp.zeros_like(grads)
    mine = first_lanes(grads.shape)
    dk, dv = [], 0.0
    for head in (0, 1):
        grad = jnp.where(mine == (head == 0), grads, zeros)
        probs = jnp.exp(product_nt(keys[head], queries[head]) - logs[head : head + 1])
        pushed = product_nt(values, grad)
        d_scores = (probs * (pushed - delta[head : head + 1])).astype(LOW)
        dv = dv + product(probs.astype(LOW), grad)
        dk.append(product(d_scores, queries[head]))
        keys_t = keys[head].T[head * 64 : head * 64 + 64]
        acc[head * 64 : head * 64 + 64, :] += product(keys_t, d_scores)
    return jnp.where(first_lanes(dk[0].shape), dk[0], dk[1]).astype(LOW), dv.astype(LOW)


def attend_back_kernel(
    qh_ref, o_ref, g_ref, lse_ref, kh_ref, v_ref, dq_ref, dk_ref, dv_ref, acc, delta
):
    tile = pl.program_id(1)
    blocks, _, rows, _ = g_ref.shape
    grads = rows_of(g_ref[:, 0])

    @pl.when(tile == 0)
    def _():
        acc[...] = jnp.zeros_like(acc)
        delta[...] = row_products(rows_of(o_ref[:, 0]), grads)

    dk_ref[0, 0], dv_ref[0, 0] = attend_back_tile(
        [rows_of(qh_ref[head, :, 0]) for head in (0, 1)],
        [kh_ref[head, 0, 0] for head in (0, 1)],
        v_ref[0, 0],
        grads,
        lse_ref[0],
        delta[...],
        acc,
    )

    @pl.when(tile == blocks - 1)
    def _():
        dq_ref[:, 0] = (acc[...].T * 0.125).astype(LOW).reshape(blocks, rows, 128)


def attend_back(qh, o, g, lse, kh, v):
    blocks, slots, rows, lanes = v.shape
    tile = pl.BlockSpec((1, 1, rows, lanes), lambda s, i: (i, s, 0, 0))
    tiles = pl.BlockSpec((2, 1, 1, rows, lanes), lambda s, i: (0, i, s, 0, 0))
    whole = pl.BlockSpec((blocks, 1, rows, lanes), lambda s, i: (0, s, 0, 0))
    wholes = pl.BlockSpec((2, blocks, 1, rows, lanes), lambda s, i: (0, 0, s, 0, 0))
    logs = pl.BlockSpec((1, 8, blocks * rows), lambda s, i: (s, 0, 0))
    shape = jax.ShapeDtypeStruct(v.shape, LOW)
    return pl.pallas_call(
        attend_back_kernel,
        grid=(slots, blocks),
        out_shape=(shape,) * 3,
        in_specs=[wholes, whole, whole, logs, tiles, tile],
        out_specs=(whole, tile, tile),
        scratch_shapes=[pltpu.VMEM((lanes, blocks * rows), HIGH), pltpu.VMEM((8, blocks * rows), HIGH)],
        compiler_params=pltpu.CompilerParams(vmem_limit_bytes=VMEM_LIMIT),
        name="attend_back",
    )(qh, o, g, lse, kh, v)


class TokenSums:
    COPIES = 4 + 2 + 4

    def __init__(self, s, piece, sent, C, S, H, Q, A):
        b, z = position()
        to_x, to_y, to_core = (b ^ 2, z), (b ^ 4, z), (b ^ 1, z)
        self.b, self.piece = b, piece
        self.sent, self.C, self.S, self.H, self.Q, self.A = sent, C, S, H, Q, A
        self.other = [s.plan(sent.at[e], C.at[e], to_core, C.at[e]) for e in range(4)]

        def send(e, part, to, where):
            return s.plan(half(S.at[e - 1], part), where, to, where)

        self.halves = [send(3, 0, to_x, H.at[0]), send(3, 1, to_y, H.at[1])]
        self.ahead = [
            send(2, 1, to_y, half(Q.at[1], 1)),
            send(1, 0, to_x, half(Q.at[0], 0)),
        ]
        self.rest = [
            send(2, 0, to_y, half(Q.at[1], 0)),
            send(1, 1, to_x, half(Q.at[0], 1)),
        ]

    def give(self, e):
        self.sent[e] = self.piece(self.b ^ 1 ^ (2 * e)).astype(LOW)
        self.other[e].go()

    def take(self, e):
        mine = self.piece(self.b ^ (2 * e))
        self.other[e].wait_recv()
        mine = mine + self.C[e].astype(HIGH)
        if e:
            self.S[e - 1] = mine.astype(LOW)
        else:
            self.A[...] = mine
        for copy in {3: self.halves, 1: self.ahead[1:], 2: self.ahead[:1], 0: []}[e]:
            copy.go()

    def relay(self):
        for i, e in ((0, 2), (1, 1)):
            self.halves[i].wait_recv()
            part = half(self.S.at[e - 1], i)
            add_rows(part, part, self.H.at[i])
            self.rest[i].go()

    def total(self):
        for copy in self.ahead + self.rest:
            copy.wait_recv()
        return self.A[...] + self.Q[0].astype(HIGH) + self.Q[1].astype(HIGH)

    @staticmethod
    def scratch(rows, width):
        low = lambda *s: pltpu.VMEM((*s, width), LOW)
        return [low(4, rows), low(4, rows), low(3, rows), low(2, rows // 2), low(2, rows)] + [
            pltpu.VMEM((rows, width), HIGH)
        ]


def back_kernel(
    d_att,
    qh_in,
    kh_in,
    v_in,
    att_in,
    lse_in,
    w_in,
    first,
    g1,
    g2_planes,
    g2_late,
    dq,
    dk,
    dv,
    o1,
    out_o,
    o2,
    tok,
    qh,
    kh,
    v,
    att,
    lse,
    w,
    first_rows,
    tail,
    grads,
    acc,
    delta,
    lsem,
    send,
    recv,
    *buffers,
):
    b, z = position()
    blocks, slots, rows, _ = v.shape
    loads = [
        pltpu.make_async_copy(src, dst, lsem.at[i])
        for i, (src, dst) in enumerate(
            (
                (d_att.at[b], grads.at[b]),
                (qh_in, qh),
                (kh_in, kh),
                (v_in, v),
                (att_in, att),
                (lse_in, lse),
                (w_in, w),
                (first.at[pl.ds(0, rows)], first_rows),
                (g2_planes, buffers[18]),
                (g2_late, buffers[20]),
            )
        )
    ]
    for load in loads:
        load.start()
    greet([(b ^ d, z) for d in range(1, 8)] + [(b, z ^ d) for d in (1, 2, 3)])
    s = Sender(send, recv)
    arriving = [
        [
            s.go(d_att.at[b ^ d, part], grads.at[b, part], (b ^ d, z), grads.at[b ^ d, part])
            for d in range(1, 8)
        ]
        for part in (pl.ds(slot * rows, rows) for slot in range(slots))
    ]

    def arrive(slot):
        for copy in arriving[slot]:
            copy.wait_recv()

    most = o1.shape[1] - tail.shape[1] + out_o.shape[1]
    sums = Reducer(
        s, lambda bb, zz: g1.at[bb, zz, :, pl.ds(0, most)], o1.at[:, pl.ds(0, most)], *buffers[:6]
    )
    late = ReducerAlongZ(
        s, lambda bb, zz: g1.at[bb, zz, :, pl.ds(most, tail.shape[1])], tail, *buffers[6:12]
    )

    def piece(i):
        mixed = jnp.concatenate([ref[i, 0] for ref in (dq, dk, dv)], axis=-1)
        return product_nt(mixed, w[...])

    tokens = TokenSums(s, piece, *buffers[12:18])
    cut = g2_planes.shape[1]
    planes = PlaneSums(s, o2.at[pl.ds(0, cut)], *buffers[18:20])
    chips = ChipSums(s, o2.at[pl.ds(cut, g2_late.shape[1])], *buffers[20:])
    late.start()
    sums.start()
    late.fold(3)
    late.fold(1)
    late.fold(2)
    sums.fold(3)
    arrive(0)
    for load in loads:
        load.wait()

    def grad_rows(slot):
        part = pl.ds(pl.multiple_of(slot * rows, rows), rows)
        return rows_of(grads[:, part])

    events = {
        0: [(late.fold, 0)],
        1: [(sums.fold, 2), (late.relay, 3)],
        2: [(late.relay, 1)],
        3: [(sums.fold, 1), (sums.relay, 3)],
        4: [(late.relay, 2)],
        5: [(late.relay, 0), (sums.relay, 2)],
        6: [(sums.fold, 0), (late.collect, 3), (arrive, 1)],
        7: [(sums.collect, 3), (late.collect, 1), (planes.start,), (chips.start,)],
        8: [(sums.relay, 1), (late.collect, 2), (tokens.give, 3), (tokens.give, 2)],
        9: [(sums.collect, 2), (tokens.give, 1), (tokens.take, 3), (chips.relay,)],
        10: [(tokens.give, 0), (tokens.take, 2)],
        11: [(sums.relay, 0), (late.cross,), (tokens.take, 1), (planes.relay,)],
        12: [(tokens.take, 0)],
        13: [(sums.collect, 1), (tokens.relay,)],
        15: [(late.collect, 0), (planes.total,), (chips.total,)],
    }

    @pl.loop(0, blocks * slots)
    def _(step):
        slot, tile = step // blocks, step % blocks
        slot_grads = grad_rows(slot)

        @pl.when(tile == 0)
        def _():
            acc[...] = jnp.zeros_like(acc)
            delta[...] = row_products(rows_of(att[:, slot]), slot_grads)

        dk[tile, slot], dv[tile, slot] = attend_back_tile(
            [rows_of(qh[head, :, slot]) for head in (0, 1)],
            [kh[head, tile, slot] for head in (0, 1)],
            v[tile, slot],
            slot_grads,
            lse[slot],
            delta[...],
            acc,
        )

        @pl.when(tile == blocks - 1)
        def _():
            dq[:, slot] = (acc[...].T * 0.125).astype(LOW).reshape(blocks, rows, 128)

        for at, some in events.items():

            @pl.when(step == at)
            def _(some=some):
                for event, *what in some:
                    event(*what)

    sums.collect(0)
    late.total()
    rest = o1.shape[1] - most
    o1[:, most:] = tail[:, :rest]
    out_o[...] = tail[:, rest:]
    sums.total()
    tok[...] = first_rows[...] + tokens.total()
    s.drain()


def back(d_att, qh, kh, v, att, lse, w, d_first, g1, g2_planes, g2_late):
    blocks, slots, rows, lanes = v.shape
    shape = jax.ShapeDtypeStruct
    shard, total = g1.shape[2:]
    width = w.shape[0]
    late = 2 * width
    vmem = pl.BlockSpec(memory_space=pltpu.VMEM)
    scratch = lambda a: pltpu.VMEM(a.shape, a.dtype)
    return pl.pallas_call(
        back_kernel,
        out_shape=(shape(v.shape, LOW),) * 3
        + (
            shape((shard, total - width), HIGH),
            shape((shard, width), HIGH),
            shape((g2_planes.shape[1] + g2_late.shape[1], width), HIGH),
            shape((rows, width), HIGH),
        ),
        in_specs=in_hbm(11),
        out_specs=(vmem,) * 7,
        scratch_shapes=[scratch(a) for a in (qh, kh, v, att, lse, w)]
        + [
            pltpu.VMEM((rows, width), HIGH),
            pltpu.VMEM((shard, late), HIGH),
            pltpu.VMEM(d_att.shape, LOW),
            pltpu.VMEM((lanes, blocks * rows), HIGH),
            pltpu.VMEM((8, blocks * rows), HIGH),
            pltpu.SemaphoreType.DMA((10,)),
        ]
        + pair_of_semaphores(
            7 * slots
            + sum(c.COPIES for c in (Reducer, ReducerAlongZ, TokenSums, PlaneSums, ChipSums))
        )
        + Reducer.scratch(shard, total - late)
        + ReducerAlongZ.scratch(shard, late)
        + TokenSums.scratch(rows, width)
        + PlaneSums.scratch(*g2_planes.shape[1:])
        + ChipSums.scratch(*g2_late.shape[1:]),
        compiler_params=pltpu.CompilerParams(
            collective_id=2, has_side_effects=True, vmem_limit_bytes=VMEM_LIMIT
        ),
        name="back",
    )(d_att, qh, kh, v, att, lse, w, d_first, g1, g2_planes, g2_late)


def column_sum(block):
    return jnp.sum(block.astype(HIGH), axis=0, keepdims=True)


def middle_kernel(
    chunk,
    small_rows,
    remote,
    att_in,
    n1,
    r1_in,
    normed_in,
    cot_in,
    par_ref,
    act_hbm,
    slope_hbm,
    w1_hbm,
    w2_hbm,
    out_ref,
    first_ref,
    d_att_ref,
    small_ref,
    g1_hbm,
    g2_out,
    *rest,
):
    if remote:
        g2_late, *rest = rest
    w1, w2, act, slope, acc, low, sums_ref, d_hid_ref, wsem, gsem, *rest = rest
    att, r1, normed_t, cot_ref, isem, *buffers = rest
    inputs = ((cot_in, cot_ref), (normed_in, normed_t), (r1_in, r1), (att_in, att))
    inputs = [pltpu.make_async_copy(*pair, isem.at[i]) for i, pair in enumerate(inputs)]
    hidden, width = w2.shape
    steps = hidden // chunk
    pieces, _, held = d_att_ref.shape

    def columns(c):
        return pl.ds(pl.multiple_of(c * chunk, chunk), chunk)

    def load1(c):
        return pltpu.make_async_copy(w1_hbm.at[:, columns(c)], w1.at[:, columns(c)], wsem.at[0, c])

    def load2(c):
        return pltpu.make_async_copy(w2_hbm.at[columns(c)], w2.at[columns(c)], wsem.at[1, c])

    def load_act(c):
        return pltpu.make_async_copy(act_hbm.at[:, columns(c)], act.at[:, columns(c)], wsem.at[2, c])

    def load_slope(c):
        return pltpu.make_async_copy(
            slope_hbm.at[:, columns(c)], slope.at[:, columns(c)], wsem.at[3, c]
        )

    if remote:
        b, z = position()
        barrier = pltpu.get_barrier_semaphore()
        peers = [(b ^ d, z) for d in (1, 2, 4)] + [(b, z ^ d) for d in (1, 2)]
        for peer in peers:
            pl.semaphore_signal(barrier, inc=1, device_id=peer, device_id_type=MESH)
    last = pl.ds(hidden, width)
    for c in range(steps):
        load_act(c).start()
        load2(c).start()
    inputs[0].start()
    for c in range(steps):
        load_slope(c).start()
    for copy in inputs[1:]:
        copy.start()
    for c in range(steps):
        load1(c).start()
    load_out = pltpu.make_async_copy(w1_hbm.at[:, last], w1.at[:, last], wsem.at[0, steps])
    load_out.start()
    gain1, gain2 = par_ref[0:1], par_ref[1:2]
    bias = lambda i: par_ref[2 + i : 3 + i]
    acc[...] = n1[...] * gain1 + (bias(3) + bias(4))

    @pl.loop(0, steps)
    def _(c):
        load_act(c).wait()
        load2(c).wait()
        acc[...] += product(act[:, columns(c)], w2[columns(c), :])

    normal, inverse2 = normalize(acc[...])
    inputs[0].wait()
    out_ref[...] = (normal * gain2 + bias(5)).astype(LOW)
    cot = cot_ref[...].astype(HIGH)
    d_second = normalize_back(cot * gain2, normal, inverse2)
    low[...] = d_second.astype(LOW)
    acc[...] = d_second
    sums_ref[1:2] = column_sum(cot * normal)
    sums_ref[4:5] = column_sum(low[...])
    sums_ref[5:6] = column_sum(cot)

    def store1(c):
        return pltpu.make_async_copy(w1.at[:, columns(c)], g1_hbm.at[:, columns(c)], gsem.at[0, c])

    def store2(c):
        return pltpu.make_async_copy(w2.at[columns(c)], g2_out.at[columns(c)], gsem.at[1, c])

    first_events, second_events = {}, {}
    if remote:
        pl.semaphore_wait(barrier, len(peers))
        s = Sender(*buffers[:2])
        each = w2.shape[0] // (8 * 4)
        cut = buffers[2].shape[2]
        plain = lambda bb, zz: w2.at[pl.ds(pl.multiple_of((bb * 4 + zz) * each, each), cut)]
        upper = lambda bb, zz: w2.at[
            pl.ds(pl.multiple_of((bb * 4 + zz) * each + cut, 16), each - cut)
        ]
        sums = Reducer(s, plain, g2_out, *buffers[2:5])
        late = ReducerAlongZ(s, upper, g2_late, buffers[5], None, None, buffers[6])
        sums.keep_for_later(buffers[7])
        late.keep_for_later(buffers[8])
        first_events = {
            0: [(late.give, 3), (sums.give, 3)],
            2: [(late.give, 2), (sums.give, 2)],
            3: [(late.fold, 3), (sums.fold_chip, 3)],
            4: [(late.give, 1), (sums.give, 1)],
            5: [(late.fold, 2), (sums.fold_chip, 2)],
            6: [(late.give, 0), (sums.give, 0), (late.relay, 3)],
            7: [(late.fold, 1), (sums.fold_chip, 1)],
        }
        second_events = {
            0: [(late.relay, 2)],
            1: [(late.fold, 0), (sums.fold_chip, 0), (late.relay, 1)],
            2: [(sums.relay, 3), (sums.relay, 2)],
            3: [(late.relay, 0), (sums.relay, 1)],
            4: [(sums.relay, 0), (late.collect, 3)],
            5: [(late.collect, 2)],
            6: [(late.collect, 1), (sums.collect, 3)],
            7: [(sums.collect, 2)],
        }

    def run(events, step):
        for at, some in events.items():

            @pl.when(step == at)
            def _(some=some):
                for event, *what in some:
                    event(*what)

    @pl.loop(0, steps)
    def _(step):
        c = b ^ (7 - step) if remote else step
        load_slope(c).wait()
        d_act = product_nt(low[...], w2[columns(c), :])
        d_pre = (d_act * slope[:, columns(c)].astype(HIGH)).astype(LOW)
        d_hid_ref[:, columns(c)] = column_sum(d_pre)
        slope[:, columns(c)] = d_pre
        w2[columns(c), :] = product_tn(act[:, columns(c)], low[...]).astype(LOW)
        if not remote:
            store2(c).start()
        run(first_events, step)

    for copy in inputs[1:]:
        copy.wait()

    @pl.loop(0, steps)
    def _(c):
        load1(c).wait()
        d_pre = slope[:, columns(c)]
        acc[...] += product_nt(d_pre, w1[:, columns(c)])
        w1[:, columns(c)] = product(normed_t[...], d_pre).astype(LOW)
        store1(c).start()
        run(second_events, c)

    d_normed = acc[...]
    normal = n1[...]
    d_first = normalize_back(d_normed * gain1, normal, r1[:, 0:1])
    first_ref[...] = d_first
    low[...] = d_first.astype(LOW)
    sums_ref[0:1] = column_sum(d_normed * normal)
    sums_ref[2:3] = column_sum(low[...])
    sums_ref[3:4] = column_sum(d_normed)
    load_out.wait()
    d_att = product_nt(low[...], w1[:, hidden:]).astype(LOW)
    for i in range(pieces):
        d_att_ref[i] = d_att[:, i * held : (i + 1) * held]
    w1[:, hidden:] = product_tn(att[...], low[...]).astype(LOW)
    store_out = pltpu.make_async_copy(w1.at[:, last], g1_hbm.at[:, last], gsem.at[0, steps])
    store_out.start()
    blocks, planes, _ = small_ref.shape
    small_ref[...] = jnp.zeros_like(small_ref)
    owners = [(i, j) for i in range(blocks) for j in range(width // (blocks * small_rows))]
    for at, (i, j) in enumerate(owners):
        for k in range(6):
            small_ref[i, j : j + 1, k * small_rows : (k + 1) * small_rows] = sums_ref[
                k : k + 1, at * small_rows : (at + 1) * small_rows
            ]
        part = hidden // len(owners)
        small_ref[i, j : j + 1, 6 * small_rows : 6 * small_rows + part] = d_hid_ref[
            :, at * part : (at + 1) * part
        ]
    if remote:
        sums.collect(1)
        late.collect(0)
        sums.collect(0)
        for copy in sums.keep + late.keep:
            copy.wait()
        s.drain()
    for c in range(steps):
        store1(c).wait()
        if not remote:
            store2(c).wait()
    store_out.wait()


def middle(att, n1, r1, normed_t, cot, par, act, slope, w1, w2, pieces, planes, remote):
    count, width = cot.shape
    hidden = w2.shape[0]
    chunk = 512
    shape = jax.ShapeDtypeStruct
    vmem = pl.BlockSpec(memory_space=pltpu.VMEM)
    shard = hidden // (pieces * planes)
    late = shard // 4
    buffers, params = [], {}
    g2_shape = [shape(w2.shape, LOW)]
    if remote:
        g2_shape = [shape((4, shard - late, width), LOW), shape((4, late, width), LOW)]
        buffers = pair_of_semaphores(Reducer.COPIES + ReducerAlongZ.COPIES)
        buffers += Reducer.scratch(shard - late, width, in_place=True)[:3]
        buffers += ReducerAlongZ.scratch(late, width, in_place=True)[::3]
        buffers += [pltpu.SemaphoreType.DMA((4,)), pltpu.SemaphoreType.DMA((4,))]
        params = dict(collective_id=4, has_side_effects=True)
    return pl.pallas_call(
        functools.partial(middle_kernel, chunk, width // (pieces * planes), remote),
        out_shape=(
            shape((count, width), LOW),
            shape((count, width), HIGH),
            shape((pieces, count, width // pieces), LOW),
            shape((pieces, -(-planes // 8) * 8, 384), HIGH),
            shape(w1.shape, LOW),
            *g2_shape,
        ),
        in_specs=in_hbm(1) + [vmem] + in_hbm(3) + [vmem] + in_hbm(4),
        out_specs=(vmem,) * 4 + tuple(in_hbm(1 + len(g2_shape))),
        scratch_shapes=[
            pltpu.VMEM(w1.shape, LOW),
            pltpu.VMEM(w2.shape, LOW),
            pltpu.VMEM((count, hidden), LOW),
            pltpu.VMEM((count, hidden), LOW),
            pltpu.VMEM((count, width), HIGH),
            pltpu.VMEM((count, width), LOW),
            pltpu.VMEM((8, width), HIGH),
            pltpu.VMEM((1, hidden), HIGH),
            pltpu.SemaphoreType.DMA((4, hidden // chunk + 1)),
            pltpu.SemaphoreType.DMA((2, hidden // chunk + 1)),
            pltpu.VMEM(att.shape, LOW),
            pltpu.VMEM(r1.shape, HIGH),
            pltpu.VMEM(normed_t.shape, LOW),
            pltpu.VMEM(cot.shape, LOW),
            pltpu.SemaphoreType.DMA((4,)),
        ]
        + buffers,
        compiler_params=pltpu.CompilerParams(vmem_limit_bytes=VMEM_LIMIT, **params),
        name="middle",
    )(att, n1, r1, normed_t, cot, par, act, slope, w1, w2)


def finish_kernel(
    dq,
    dk,
    dv,
    w,
    first,
    tok0,
    small,
    x_hbm,
    tok_out,
    in_out,
    gains_out,
    biases_out,
    hidden_out,
    first_rows,
    x,
    D,
    P,
    R,
    Z,
    M,
    N,
    T,
    lsem,
    send,
    recv,
    *buffers,
):
    b, z = position()
    rows, width = tok0.shape
    blocks = dq.shape[0]
    count = 2 * rows
    loads = [
        pltpu.make_async_copy(x_hbm.at[i, pl.ds(0, count)], x.at[i], lsem.at[i])
        for i in range(blocks)
    ]
    loads.append(pltpu.make_async_copy(first.at[pl.ds(rows, rows)], first_rows, lsem.at[blocks]))
    loads.append(pltpu.make_async_copy(tok0, tok_out.at[pl.ds(0, rows)], lsem.at[blocks + 1]))
    for load in loads:
        load.start()
    greet([(b ^ d, z) for d in range(1, 8)] + [(b, z ^ d) for d in (1, 2, 3)])
    s = Sender(send, recv)

    def piece(i):
        mixed = jnp.concatenate([ref[i, 1] for ref in (dq, dk, dv)], axis=-1)
        return product_nt(mixed, w[...])

    tokens = TokenSums(s, piece, *buffers)
    small_in = [
        s.go(small.at[b ^ d], M.at[d - 1], (b ^ d, z), M.at[d - 1]) for d in range(1, 8)
    ]
    total = jnp.zeros((width, w.shape[1]), HIGH)
    for i in range(blocks):
        loads[i].wait()
        mixed = jnp.concatenate([ref[i].reshape(count, -1) for ref in (dq, dk, dv)], axis=-1)
        total = total + product_tn(x[i], mixed)
    D[...] = total.astype(LOW).reshape(D.shape)
    share_rows = D.shape[1] // 4

    def share(d):
        return D.at[:, pl.ds(pl.multiple_of((z ^ d) * share_rows, share_rows), share_rows)]

    in_z = {
        d: s.plan(share(d), Z.at[d - 1], (b, z ^ (2 if d == 2 else 1)), Z.at[d - 1])
        for d in (3, 1, 2)
    }
    in_z[3].go()
    in_z[1].go()
    for e in (3, 2, 1, 0):
        tokens.give(e)
    tokens.take(3)
    in_z[3].wait_recv()
    onward = share(2)
    onward[...] = onward[...] + Z[2]
    in_z[2].go()
    for e in (2, 1, 0):
        tokens.take(e)

    N[...] = small[b]
    for i in range(7):
        small_in[i].wait_recv()
        N[...] += M[i]
    for row, ref in ((4, dq), (5, dv)):
        whole = jnp.zeros((1, 128), HIGH)
        for i in range(blocks):
            whole = whole + column_sum(ref[i].reshape(count, -1))
        N[row : row + 1, 0:128] = whole
    small_z = [s.go(N, T.at[d - 1], (b, z ^ d), T.at[d - 1]) for d in (1, 2, 3)]

    in_z[1].wait_recv()
    in_z[2].wait_recv()
    plane = share(0)[...].astype(HIGH)
    for i in range(2):
        plane = plane + Z[i].astype(HIGH)
    P[...] = plane
    grads_in = [
        s.go(P.at[b ^ d], R.at[b], (b ^ d, z), R.at[b ^ d]) for d in range(1, 8)
    ]
    R[b] = P[b]
    tokens.relay()
    for copy in small_z:
        copy.wait_recv()
    vectors = ((N[...] + T[0]) + T[1]) + T[2]
    planes = lax.broadcasted_iota(jnp.int32, vectors.shape, 0)
    row = jnp.sum(jnp.where(planes == z, vectors, 0.0), axis=0, keepdims=True)
    n = gains_out.shape[1]
    for k in range(2):
        gains_out[k : k + 1] = row[:, k * n : (k + 1) * n]
        own = vectors[4 + k : 5 + k]
        parts = [jnp.where(z == j, own[:, j * n : (j + 1) * n], 0.0) for j in range(4)]
        biases_out[k : k + 1] = (parts[0] + parts[1]) + (parts[2] + parts[3])
    for k in range(2, 6):
        biases_out[k : k + 1] = row[:, k * n : (k + 1) * n]
    hidden_out[...] = row[:, 6 * n : 6 * n + hidden_out.shape[1]]
    for copy in grads_in:
        copy.wait_recv()
    for i in range(blocks):
        for k in range(3):
            at = k * width + i * 128
            in_out[:, at : at + 128] = R[i, :, k * 128 : (k + 1) * 128]
    for load in loads[blocks:]:
        load.wait()
    tok_out[rows:] = first_rows[...] + tokens.total()
    s.drain()


def finish(dq, dk, dv, w, d_first, tok0, small, x):
    rows, width = tok0.shape
    blocks, columns = dq.shape[0], w.shape[1]
    share = width // (4 * blocks)
    vmem = pl.BlockSpec(memory_space=pltpu.VMEM)
    shape = lambda *s: jax.ShapeDtypeStruct(s, HIGH)
    low = lambda *s: pltpu.VMEM(s, LOW)
    wide = lambda *s: pltpu.VMEM(s, HIGH)
    tile = small.shape[1:]
    return pl.pallas_call(
        finish_kernel,
        out_shape=(
            shape(2 * rows, width),
            shape(share, 3 * width),
            shape(2, share),
            shape(6, share),
            shape(1, 4 * share),
        ),
        in_specs=[vmem] * 4 + in_hbm(2) + [vmem] + in_hbm(1),
        out_specs=(vmem,) * 5,
        scratch_shapes=[
            wide(rows, width),
            low(blocks, 2 * rows, width),
            low(blocks, 4 * share, columns),
            wide(blocks, share, columns),
            wide(blocks, share, columns),
            low(3, blocks, share, columns),
            wide(7, *tile),
            wide(*tile),
            wide(3, *tile),
            pltpu.SemaphoreType.DMA((blocks + 2,)),
        ]
        + pair_of_semaphores(20 + TokenSums.COPIES)
        + TokenSums.scratch(rows, width),
        compiler_params=pltpu.CompilerParams(
            collective_id=3, has_side_effects=True, vmem_limit_bytes=VMEM_LIMIT
        ),
        name="finish",
    )(dq, dk, dv, w, d_first, tok0, small, x)


def swap(pieces):
    return lax.all_to_all(pieces, "blk", 0, 0)


def by_slot(block, slots):
    blocks, count, held = block.shape
    block = block.reshape(blocks, slots, count // slots, held)
    return jnp.pad(block, ((0, 0),) * 3 + ((0, 128 - held),))


def front_apart(X, W, bias, slots):
    n_blk, count = X.shape[0], X.shape[1] - 16
    held = W.shape[1] // 3
    mixed = jnp.einsum("brd,dc->brc", X[:, :count], W, preferred_element_type=HIGH)
    parts = [mixed[..., i * held : (i + 1) * held] for i in range(3)]
    parts = [jnp.pad(p, ((0, 0), (0, 0), (0, 128 - held))).reshape(-1, 128) for p in parts]
    own = lax.dynamic_slice(bias[:2], (0, lax.axis_index("blk") * held), (2, held))
    own = jnp.pad(own, ((0, 0), (0, 128 - held)))
    codes = X[:, count, :count].reshape(-1, 1).astype(jnp.int32)
    codes = jnp.broadcast_to(codes, (n_blk * count, 128))
    queries, keys, values = split_heads(jnp.concatenate(parts, axis=1), (own[0], own[1]), codes)
    shape = (n_blk, slots, count // slots, 128)
    qh = jnp.stack(queries).reshape(2, *shape)
    kh = jnp.stack(keys).reshape(2, *shape)
    v = values.reshape(shape)
    att, lse = attend(qh, kh, v)
    rows_att = swap(att[..., :held].reshape(n_blk, count, held))
    return qh, kh, v, att, lse, rows_att


def on_device(
    tokens,
    input_weight,
    output_weight,
    expand_weight,
    reduce_weight,
    gains,
    biases,
    hidden_bias,
    segment,
    present,
    cotangent,
):
    slots, rows, width = tokens.shape
    n_blk, n_dp = lax.axis_size("blk"), lax.axis_size("dp")
    shards = n_blk * n_dp
    fast = (n_blk, n_dp) == (8, 4)
    held = width // n_blk
    shard = input_weight.shape[0]
    hidden = expand_weight.shape[1]
    count = slots * rows
    flat = tokens.reshape(count, width)

    if fast:
        front_out = front(
            flat,
            segment,
            present,
            input_weight,
            gains,
            biases,
            hidden_bias[None],
            expand_weight,
            output_weight,
            reduce_weight,
        )
        X, W1, W2, act, slope, W, _, qh, kh, v, att, lse = front_out[:12]
        attended, n1, r1, normed_t, cuts = front_out[12:]
        W1, W2 = W1.reshape(width, -1), W2.reshape(hidden, width)
    else:
        code = (segment + 4 * (1 - present)).reshape(1, count).astype(LOW)
        code_rows = jnp.pad(jnp.broadcast_to(code, (16, count)), ((0, 0), (0, width - count)))
        columns = input_weight.reshape(shard, 3, n_blk, held).transpose(2, 0, 1, 3)
        columns = columns.reshape(n_blk, shard, 3 * held)
        small = jnp.concatenate([gains.reshape(-1), biases.reshape(-1), hidden_bias])
        X = lax.all_gather(jnp.concatenate([flat, code_rows], axis=0), "blk")
        W = lax.all_gather(swap(columns), "dp", axis=1).reshape(width, 3 * held)
        small = lax.all_gather(small, BOTH)
        W1 = jnp.concatenate([expand_weight, output_weight], axis=1)
        W1 = lax.all_gather(W1, BOTH, axis=0, tiled=True)
        W2 = lax.all_gather(reduce_weight, BOTH, axis=0, tiled=True)
        part = width // shards
        cuts = small[:, : 8 * part].reshape(shards, 8, part).transpose(1, 0, 2)
        cuts = cuts.reshape(8, width).astype(HIGH)
        hidden_full = small[:, 8 * part :].reshape(hidden).astype(HIGH)
        gain, bias = cuts[:2], cuts[2:]
        qh, kh, v, att, lse, rows_att = front_apart(X, W, bias, slots)
        attended = rows_att.transpose(1, 0, 2).reshape(count, width)
        branch = product(attended, W1[:, hidden:]) + bias[2]
        n1, r1 = normalize(flat.astype(HIGH) + branch)
        r1 = jnp.broadcast_to(r1, (count, 128))
        normed_low = (n1 * gain[0] + bias[3]).astype(LOW)
        act, slope = gelu_parts(product(normed_low, W1[:, :hidden]) + hidden_full)
        act, slope = act.astype(LOW), slope.astype(LOW)
        normed_t = normed_low.T
    cot = cotangent.reshape(count, width)
    middle_out = middle(
        attended, n1, r1, normed_t, cot, cuts, act, slope, W1, W2, n_blk, n_dp, fast
    )
    output, d_first, d_att, small_rows, grad_both, grad_reduce = middle_out[:6]
    output = output.reshape(slots, rows, width)
    if fast:
        grad_both = grad_both.reshape(n_blk, n_dp, shard, -1)
        dq, dk, dv, sum_expand, sum_output, sum_reduce, tok0 = back(
            d_att, qh, kh, v, att, lse, W, d_first, grad_both, grad_reduce, middle_out[6]
        )
        grad_tokens, grad_input, d_gains, d_biases, d_hidden = finish(
            dq, dk, dv, W, d_first, tok0, small_rows, X
        )
        return (
            output,
            grad_tokens.reshape(slots, rows, width),
            grad_input,
            sum_output,
            sum_expand,
            sum_reduce,
            d_gains,
            d_biases,
            d_hidden.reshape(-1),
        )
    sum_both = lax.psum_scatter(grad_both, BOTH, scatter_dimension=0, tiled=True).astype(HIGH)
    sum_reduce = lax.psum_scatter(grad_reduce, BOTH, scatter_dimension=0, tiled=True)
    dq, dk, dv = attend_back(qh, att, by_slot(swap(d_att), slots), lse, kh, v)
    d_mixed = jnp.concatenate([dq[..., :held], dk[..., :held], dv[..., :held]], axis=-1)
    d_mixed = d_mixed.reshape(n_blk * count, 3 * held)
    all_tokens = X[:, :count].reshape(n_blk * count, width)
    d_input = product_tn(all_tokens, d_mixed).astype(LOW)
    d_tokens = product_nt(d_mixed, W).astype(LOW)
    d_tokens = lax.psum_scatter(d_tokens, "blk", scatter_dimension=0, tiled=True)
    grad_tokens = d_first + d_tokens.astype(HIGH)
    d_input = swap(d_input.reshape(n_blk, n_dp * shard, 3 * held))
    d_input = d_input.reshape(n_blk, n_dp, shard, 3, held).transpose(1, 2, 3, 0, 4)
    d_input = d_input.reshape(n_dp, shard, 3 * width).astype(HIGH)
    grad_input = lax.psum_scatter(d_input, "dp", scatter_dimension=0, tiled=False)
    col = lambda a: jnp.sum(a.astype(HIGH), axis=0)
    own_cols = jnp.stack([col(d_mixed[:, :held]), col(d_mixed[:, 2 * held :])])
    own_cols = lax.psum_scatter(own_cols, "dp", scatter_dimension=1, tiled=True)
    small_rows = small_rows[:, :n_dp].reshape(shards, -1)
    small_sum = lax.psum_scatter(small_rows, BOTH, scatter_dimension=0, tiled=False)
    vectors = small_sum[: 6 * part].reshape(6, part)
    return (
        output,
        grad_tokens.reshape(slots, rows, width),
        grad_input,
        sum_both[:, hidden:],
        sum_both[:, :hidden],
        sum_reduce.astype(HIGH),
        vectors[:2],
        jnp.concatenate([own_cols, vectors[2:]], axis=0),
        small_sum[6 * part : 6 * part + hidden // shards],
    )


def solution(mesh):
    rows, sharded = P("dp", "blk", None), P(BOTH, None)
    in_specs = (rows, sharded, sharded, sharded, sharded, P(None, BOTH), P(None, BOTH), P(BOTH))
    in_specs += (P("dp", "blk"), P("dp", "blk"), rows)
    out_specs = (rows, rows, sharded, sharded, sharded, sharded)
    out_specs += (P(None, BOTH), P(None, BOTH), P(BOTH))
    return jax.shard_map(
        on_device, mesh=mesh, in_specs=in_specs, out_specs=out_specs, check_vma=False
    )
```

```python
import functools

import jax
import jax.numpy as jnp
from jax import lax
from jax.experimental import pallas as pl
from jax.experimental.pallas import tpu as pltpu
from jax.sharding import PartitionSpec as P

HEADS = 16
EPSILON = 1e-12
FAR = 2.0**60
BOTH = ("blk", "dp")
MESH = pl.DeviceIdType.MESH
LOW = jnp.bfloat16
HIGH = jnp.float32
VMEM_LIMIT = 60 * 2**20


def product(left, right):
    return jnp.dot(left, right, preferred_element_type=HIGH)


def product_nt(left, right):
    return lax.dot_general(left, right, (((1,), (1,)), ((), ())), preferred_element_type=HIGH)


def product_tn(left, right):
    return lax.dot_general(left, right, (((0,), (0,)), ((), ())), preferred_element_type=HIGH)


def normalize(values):
    mean = jnp.mean(values, axis=-1, keepdims=True)
    centred = values - mean
    spread = jnp.mean(centred * centred, axis=-1, keepdims=True)
    inverse = lax.rsqrt(spread + EPSILON)
    return centred * inverse, inverse


def normalize_back(grad, normal, inverse):
    return inverse * (
        grad
        - jnp.mean(grad, axis=-1, keepdims=True)
        - normal * jnp.mean(grad * normal, axis=-1, keepdims=True)
    )


def quick_reciprocal(x):
    first = pl.reciprocal(x, approx=True)
    return first * (2.0 - x * first)


def gelu_parts(u, reciprocal=lambda x: 1.0 / x):
    bell = jnp.exp(-0.5 * u * u)
    below = 1.0 + (0.3275911 * 0.5**0.5) * jnp.abs(u)
    t = reciprocal(below)
    poly = 1.061405429 * t - 1.453152027
    poly = poly * t + 1.421413741
    poly = poly * t - 0.284496736
    poly = poly * t + 0.254829592
    tail = 0.5 * poly * t * bell
    below = jnp.where(u < 0.0, tail, 1.0 - tail)
    return u * below, below + u * bell * 0.3989422804014327


class Sender:
    def __init__(self, send, recv):
        self.send, self.recv, self.planned = send, recv, []

    def plan(self, src, dst, device, landing):
        at = len(self.planned)

        def copy(a, b):
            return pltpu.make_async_remote_copy(
                src_ref=a,
                dst_ref=b,
                send_sem=self.send.at[at],
                recv_sem=self.recv.at[at],
                device_id=device,
                device_id_type=MESH,
            )

        out = copy(src, dst)
        self.planned.append(out)
        landed = copy(landing, landing)
        landed.go = out.start
        return landed

    def go(self, *what):
        landed = self.plan(*what)
        landed.go()
        return landed

    def drain(self):
        for out in self.planned:
            out.wait_send()


def greet(peers):
    barrier = pltpu.get_barrier_semaphore()
    for peer in peers:
        pl.semaphore_signal(barrier, inc=1, device_id=peer, device_id_type=MESH)
    pl.semaphore_wait(barrier, len(peers))


def half(ref, which):
    rows = ref.shape[0]
    cut = rows // 32 * 16
    return ref.at[pl.ds(0, cut)] if which == 0 else ref.at[pl.ds(cut, rows - cut)]


def position():
    return lax.axis_index("blk"), lax.axis_index("dp")


def first_lanes(shape):
    return lax.broadcasted_iota(jnp.int32, shape, len(shape) - 1) < 64


def rows_of(block):
    return block.reshape(-1, block.shape[-1])


def attend_tile(queries, keys, values):
    rows = queries[0].shape[0]
    ones = jnp.ones_like(values)
    mine = first_lanes(values.shape)
    outs, logs = [], []
    for head in (0, 1):
        scores = product_nt(queries[head], keys[head])
        top = jnp.max(scores, axis=-1, keepdims=True)
        weights = jnp.exp(scores - top).astype(LOW)
        total = product(weights, jnp.where(mine == (head == 0), values, ones))
        mass = pltpu.roll(total, 64, 1)
        outs.append(total / mass)
        logs.append(top + jnp.log(mass))
    mine = first_lanes((rows, 128))
    flipped = jnp.where(mine, logs[0], logs[1]).T
    logs = jnp.concatenate([flipped[0:1], flipped[64:65], jnp.zeros((6, rows), HIGH)], axis=0)
    return jnp.where(mine, outs[0], outs[1]).astype(LOW), logs


def split_heads(mixed, bias, codes):
    rows = mixed.shape[0]
    q = (mixed[:, :128] + bias[0]).astype(LOW) * LOW(0.125)
    k = mixed[:, 128:256].astype(LOW)
    v = (mixed[:, 256:] + bias[1]).astype(LOW)
    lanes = lax.broadcasted_iota(jnp.int32, (rows, 128), 1) % 64
    protein = jnp.where(codes >= 4, codes - 4, codes)
    q_marks = jnp.where((lanes < 5) & (lanes != protein), -FAR, 0.0).astype(LOW)
    k_marks = jnp.where(lanes == jnp.minimum(codes, 4), 1.0, 0.0).astype(LOW)
    mine = first_lanes((rows, 128))
    return (
        (jnp.where(mine, q, q_marks), jnp.where(mine, q_marks, q)),
        (jnp.where(mine, k, k_marks), jnp.where(mine, k_marks, k)),
        v,
    )


def spread_vectors(small, par, hid):
    for i in range(8):
        for j in range(4):
            row = small[j, i : i + 1].astype(HIGH)
            at = (i * 4 + j) * 32
            for k in range(8):
                par[k : k + 1, at : at + 32] = row[:, k * 32 : k * 32 + 32]
            hid[:, at * 4 : at * 4 + 128] = row[:, 256:384]


def front_kernel(
    x,
    segment,
    present,
    input_weight,
    gains,
    biases,
    hidden_bias,
    expand,
    out_w_in,
    w2,
    X_out,
    W1,
    W2,
    act_out,
    slope_out,
    wfull,
    small,
    qh_out,
    kh_out,
    v_out,
    att_out,
    lse_out,
    branch_in_out,
    n1_out,
    r1_out,
    normed_t_out,
    par,
    qh,
    kh,
    v,
    att,
    lse,
    branch_in,
    n1,
    r1,
    normed_t,
    normed_low,
    X,
    W,
    win,
    w1,
    rows_att,
    w1v,
    act,
    slope,
    hid,
    send,
    recv,
    asend,
    arecv,
    lsem,
    osem,
    wsem,
    csem,
    fsem,
):
    b, z = position()
    bx, by, bd, bc = b ^ 2, b ^ 4, b ^ 6, b ^ 1
    count = X.shape[1] - 16
    hidden, width = expand.shape[1], x.shape[1]
    slots, rows = qh.shape[2:4]
    locs = []

    def local(src, dst):
        copy = pltpu.make_async_copy(src, dst, lsem.at[len(locs)])
        copy.start()
        locs.append(copy)

    local(x, X.at[b, pl.ds(0, count)])
    local(expand, w1.at[:, pl.ds(0, hidden)])
    local(out_w_in, w1.at[:, pl.ds(hidden, width)])
    local(w2, W2.at[b, z])
    shard = input_weight.shape[0]
    n = gains.shape[1]
    win[...] = jnp.zeros_like(win)
    for i in range(8):
        for k in range(3):
            at = k * width + i * 128
            win[i, 0:shard, k * 128 : (k + 1) * 128] = input_weight[:, at : at + 128]
    rows_small = [gains[k : k + 1] for k in range(2)] + [biases[k : k + 1] for k in range(6)]
    line = jnp.concatenate(rows_small + [hidden_bias[...]], axis=1)
    for i in range(8):
        win[i, shard : shard + 16] = jnp.broadcast_to(line, (16, line.shape[1]))
    W[z, b] = win[b]
    codes = (segment[...] + 4 * (1 - present[...])).astype(HIGH).astype(LOW)
    codes = jnp.concatenate([codes[k : k + 1] for k in range(slots)], axis=1)
    X[b, pl.ds(count, 16), 0:count] = jnp.broadcast_to(codes, (16, count))
    X[b, pl.ds(count, 16), count:width] = jnp.zeros((16, width - count), LOW)
    greet([(b ^ d, z) for d in range(1, 8)] + [(b, z ^ d) for d in range(1, 4)])
    s = Sender(send, recv)
    to_x, to_y, to_core = (bx, z), (by, z), (bc, z)

    def token_core(src, bb):
        return s.plan(src, X.at[bb], to_core, X.at[bb ^ 1])

    def to_z(d):
        return b, z ^ d

    def hops(F, src, zz):
        near = [
            s.plan(src, F.at[b, zz], to_x, F.at[bx, zz]),
            s.plan(src, F.at[b, zz], to_y, F.at[by, zz]),
        ]
        one, two = half(F.at[bx, zz], 0), half(F.at[by, zz], 1)
        far = [
            s.plan(one, one, to_y, half(F.at[bd, zz], 0)),
            s.plan(two, two, to_x, half(F.at[bd, zz], 1)),
        ]
        return near, far

    def planes(F, src, bb):
        pair = [s.plan(src, F.at[bb, z], to_z(d), F.at[bb, z ^ d]) for d in (1, 2)]
        on = F.at[bb, z ^ 2]
        return pair + [s.plan(on, on, to_z(1), F.at[bb, z ^ 3])]

    def to_sibling(F, src, bb, zz):
        return s.plan(src, F.at[bb, zz], to_core, F.at[bb ^ 1, zz])

    places = (b, bx, by, bd)
    z1 = planes(W1, w1, b)
    hop1 = [hops(W1, W1.at[b, z ^ d] if d else w1, z ^ d) for d in range(4)]
    hop2 = hops(W2, w2, z)
    z2 = [planes(W2, W2.at[bb, z] if i else w2, bb) for i, bb in enumerate(places)]
    core1, core2 = (
        {
            (i, d): to_sibling(F, F.at[bb, z ^ d] if i or d else own, bb, z ^ d)
            for i, bb in enumerate(places)
            for d in range(4)
        }
        for F, own in ((W1, w1), (W2, w2))
    )

    def start(*copies):
        for copy in copies:
            copy.go()

    def first(d):
        if d in (1, 3):
            z1[d - 1].wait_recv()
        start(*hop1[d][0], core1[0, d])

    def second(d):
        near, far = hop1[d]
        for i in (0, 1):
            near[i].wait_recv()
            start(far[i], core1[1 + i, d])

    def third(d):
        for copy in hop1[d][1]:
            copy.wait_recv()
        core1[3, d].go()

    def spread(i):
        start(z2[i][0], z2[i][1], core2[i, 0])

    def second2():
        near, far = hop2
        for i in (0, 1):
            near[i].wait_recv()
            far[i].go()
            spread(1 + i)

    def third2():
        for copy in hop2[1]:
            copy.wait_recv()
        spread(3)

    def arrive2(i):
        z2[i][1].wait_recv()
        start(z2[i][2], core2[i, 2])
        z2[i][0].wait_recv()
        core2[i, 1].go()

    def last2(i):
        z2[i][2].wait_recv()
        core2[i, 3].go()

    columns = [
        s.go(win.at[b ^ d], W.at[z, b], (b ^ d, z), W.at[z, b ^ d]) for d in range(1, 8)
    ]
    locs[0].wait()
    token_x = s.go(X.at[b], X.at[b], to_x, X.at[bx])
    token_y = s.go(X.at[b], X.at[b], to_y, X.at[by])
    token_c = token_core(X.at[b], b)
    token_c.go()
    for copy in locs[1:3]:
        copy.wait()
    local(w1, W1.at[b, z])
    start(z1[0], z1[1])
    for copy in columns:
        copy.wait_recv()
    for i in range(8):
        small[z, i : i + 1] = W[z, i, 32:33]
    trimmed = lambda zz: W.at[zz, :, pl.ds(0, 32)]
    columns, vectors = (
        [s.plan(at(z), at(z), to_z(d), at(z ^ d)) for d in (1, 2)]
        + [s.plan(at(z ^ 2), at(z ^ 2), to_z(1), at(z ^ 3))]
        for at in (trimmed, lambda zz: small.at[zz])
    )
    start(*columns[:2], *vectors[:2])
    spread(0)
    token_x.wait_recv()
    piece = half(X.at[bx], 0)
    token_one = s.go(piece, piece, to_y, half(X.at[bd], 0))
    token_xc = token_core(X.at[bx], bx)
    token_xc.go()
    token_y.wait_recv()
    piece = half(X.at[by], 1)
    token_two = s.go(piece, piece, to_x, half(X.at[bd], 1))
    token_yc = token_core(X.at[by], by)
    token_yc.go()
    token_dc = token_core(X.at[bd], bd)
    start(*hop2[0])
    columns[1].wait_recv()
    columns[2].go()
    vectors[1].wait_recv()
    vectors[2].go()
    z1[1].wait_recv()
    z1[2].go()
    for copy in (columns[0], columns[2], vectors[0], vectors[2]):
        copy.wait_recv()
    for i in range(8):
        for j in range(4):
            at = (i * 4 + j) * 32
            wfull[at : at + 32] = W[j, i, 0:32]
    spread_vectors(small, par, hid)
    chosen = lax.broadcasted_iota(jnp.int32, (16, 128), 0) == b
    bias = [[], []]
    for j in range(4):
        row = jnp.where(chosen, small[j, :, 0:128].astype(HIGH), 0.0)
        row = jnp.sum(row, axis=0, keepdims=True)
        bias[0].append(row[:, 64:96])
        bias[1].append(row[:, 96:128])
    bias = [jnp.concatenate(parts, axis=1) for parts in bias]

    def mix(i):
        pltpu.make_async_copy(X.at[i], X_out.at[i], osem.at[i]).start()
        mixed = product(X[i, 0:count], wfull[...])
        codes = jnp.broadcast_to(X[i, count : count + 1, 0:count].astype(HIGH), (128, count)).T
        queries, keys, values = split_heads(mixed, bias, codes.astype(jnp.int32))
        for head in (0, 1):
            qh[head, i] = queries[head].reshape(slots, rows, 128)
            kh[head, i] = keys[head].reshape(slots, rows, 128)
        v[i] = values.reshape(slots, rows, 128)

    mix(b)
    token_c.wait_recv()
    mix(bc)
    mix(bx)
    token_xc.wait_recv()
    mix(bx ^ 1)
    mix(by)
    token_one.wait_recv()
    token_two.wait_recv()
    token_dc.go()
    first(0)
    first(2)
    first(1)
    second2()
    first(3)
    token_yc.wait_recv()
    mix(by ^ 1)
    mix(bd)
    token_dc.wait_recv()
    mix(bd ^ 1)
    arrive2(0)

    def piece_of(slot):
        return pl.ds(pl.multiple_of(slot * rows, rows), rows)

    def send_att(slot, d):
        return pltpu.make_async_remote_copy(
            src_ref=att.at[b ^ d, slot],
            dst_ref=rows_att.at[b, piece_of(slot)],
            send_sem=asend.at[slot * 8 + d],
            recv_sem=arecv.at[slot * 8 + d],
            device_id=(b ^ d, z),
            device_id_type=MESH,
        )

    def keep_att(slot):
        return pltpu.make_async_copy(
            att.at[b, slot], rows_att.at[b, piece_of(slot)], osem.at[8 + slot]
        )

    events = {
        0: (second, 0),
        1: (third2,),
        2: (second, 2),
        4: (second, 1),
        5: (arrive2, 1),
        6: (arrive2, 2),
        7: (third, 0),
        9: (second, 3),
        10: (arrive2, 3),
        12: (third, 2),
        14: (third, 1),
    }
    late_events = {1: (last2, 0), 3: (last2, 1), 5: (last2, 2), 7: (last2, 3)}

    @pl.loop(0, 8 * slots)
    def _(step):
        slot, d = step // 8, (step + 1) % 8
        i = b ^ d
        keys = [rows_of(kh[head, :, slot]) for head in (0, 1)]
        out, logs = attend_tile([qh[head, i, slot] for head in (0, 1)], keys, rows_of(v[:, slot]))
        att[i, slot] = out
        lse[slot, :, pl.ds(pl.multiple_of(i * rows, rows), rows)] = logs

        @pl.when(d != 0)
        def _():
            send_att(slot, d).start()

        @pl.when(d == 0)
        def _():
            keep_att(slot).start()

        for at, (event, *what) in events.items():
            pl.when(step == at)(functools.partial(event, *what))

    early = [(qh, qh_out), (kh, kh_out), (v, v_out), (att, att_out), (lse, lse_out)]
    early += [(branch_in, branch_in_out), (n1, n1_out), (r1, r1_out), (normed_t, normed_t_out)]
    early = [pltpu.make_async_copy(*pair, fsem.at[i]) for i, pair in enumerate(early)]
    for copy in early[:5]:
        copy.start()

    third(3)
    for copy in core1.values():
        copy.wait_recv()
    locs[4].wait()
    chunk = 512
    steps = hidden // chunk

    def load(c, size=chunk):
        cols = pl.ds(pl.multiple_of(c * chunk, chunk), size)
        return pltpu.make_async_copy(W1.at[:, :, :, cols], w1v.at[:, :, :, cols], wsem.at[c])

    load(steps, width).start()
    for c in range(steps):
        load(c).start()
    for slot in range(slots):
        keep_att(slot).wait()
        for d in range(1, 8):
            pltpu.make_async_remote_copy(
                src_ref=rows_att.at[b ^ d, piece_of(slot)],
                dst_ref=rows_att.at[b ^ d, piece_of(slot)],
                send_sem=asend.at[slot * 8 + d],
                recv_sem=arecv.at[slot * 8 + d],
                device_id=(b ^ d, z),
                device_id_type=MESH,
            ).wait_recv()
    branch_in[...] = jnp.concatenate([rows_att[i] for i in range(8)], axis=1)
    load(steps, width).wait()
    out_w = w1v[:, :, :, hidden:].reshape(width, width)
    branch = product(branch_in[...], out_w) + par[4:5]
    normal, inverse = normalize(X[b, 0:count].astype(HIGH) + branch)
    n1[...] = normal
    r1[...] = jnp.broadcast_to(inverse, r1.shape)
    normed = (normal * par[0:1] + par[5:6]).astype(LOW)
    normed_low[...] = normed
    normed_t[...] = normed.T
    for copy in early[5:]:
        copy.start()

    def store(c, ref, out, which):
        cols = pl.ds(pl.multiple_of(c * chunk, chunk), chunk)
        return pltpu.make_async_copy(ref.at[:, cols], out.at[:, cols], csem.at[which, c])

    @pl.loop(0, steps)
    def _(c):
        cols = pl.ds(pl.multiple_of(c * chunk, chunk), chunk)
        load(c).wait()
        pre = product(normed_low[...], w1v[:, :, :, cols].reshape(width, chunk))
        value, rate = gelu_parts(pre + hid[:, cols], quick_reciprocal)
        act[:, cols] = value.astype(LOW)
        slope[:, cols] = rate.astype(LOW)
        store(c, act, act_out, 0).start()
        store(c, slope, slope_out, 1).start()
        for at, (event, *what) in late_events.items():
            pl.when(c == at)(functools.partial(event, *what))

    for copy in core2.values():
        copy.wait_recv()
    for slot in range(slots):
        for d in range(1, 8):
            send_att(slot, d).wait_send()
    for c in range(steps):
        store(c, act, act_out, 0).wait()
        store(c, slope, slope_out, 1).wait()
    s.drain()
    for copy in early:
        copy.wait()
    locs[3].wait()
    for i in range(8):
        pltpu.make_async_copy(X.at[i], X_out.at[i], osem.at[i]).wait()


def in_hbm(count):
    return [pl.BlockSpec(memory_space=pl.ANY)] * count


def pair_of_semaphores(count):
    return [pltpu.SemaphoreType.DMA((count,)), pltpu.SemaphoreType.DMA((count,))]


def front(x, segment, present, input_weight, gains, biases, hidden_bias, expand, out_w, w2):
    slots = segment.shape[0]
    count, width = x.shape
    rows, hidden = count // slots, expand.shape[1]
    shard = expand.shape[0]
    shape = lambda *s: jax.ShapeDtypeStruct(s, LOW)
    wide = lambda *s: jax.ShapeDtypeStruct(s, HIGH)
    vmem = pl.BlockSpec(memory_space=pltpu.VMEM)
    return pl.pallas_call(
        front_kernel,
        out_shape=(
            shape(8, count + 16, width),
            shape(8, 4, shard, hidden + width),
            shape(8, 4, *w2.shape),
            shape(count, hidden),
            shape(count, hidden),
            shape(width, 384),
            shape(4, 16, 384),
            shape(2, 8, slots, rows, 128),
            shape(2, 8, slots, rows, 128),
            shape(8, slots, rows, 128),
            shape(8, slots, rows, 128),
            wide(slots, 8, 8 * rows),
            shape(count, width),
            wide(count, width),
            wide(count, 128),
            shape(width, count),
            wide(8, width),
        ),
        in_specs=in_hbm(1) + [vmem] * 6 + in_hbm(3),
        out_specs=tuple(in_hbm(5)) + (vmem,) * 2 + tuple(in_hbm(9)) + (vmem,),
        scratch_shapes=[
            pltpu.VMEM((2, 8, slots, rows, 128), LOW),
            pltpu.VMEM((2, 8, slots, rows, 128), LOW),
            pltpu.VMEM((8, slots, rows, 128), LOW),
            pltpu.VMEM((8, slots, rows, 128), LOW),
            pltpu.VMEM((slots, 8, 8 * rows), HIGH),
            pltpu.VMEM((count, width), LOW),
            pltpu.VMEM((count, width), HIGH),
            pltpu.VMEM((count, 128), HIGH),
            pltpu.VMEM((width, count), LOW),
            pltpu.VMEM((count, width), LOW),
            pltpu.VMEM((8, count + 16, width), LOW),
            pltpu.VMEM((4, 8, shard + 16, 384), LOW),
            pltpu.VMEM((8, shard + 16, 384), LOW),
            pltpu.VMEM((shard, hidden + width), LOW),
            pltpu.VMEM((8, count, 128), LOW),
            pltpu.VMEM((8, 4, shard, hidden + width), LOW),
            pltpu.VMEM((count, hidden), LOW),
            pltpu.VMEM((count, hidden), LOW),
            pltpu.VMEM((1, hidden), HIGH),
        ]
        + pair_of_semaphores(116)
        + pair_of_semaphores(8 * slots)
        + [pltpu.SemaphoreType.DMA((5,)), pltpu.SemaphoreType.DMA((8 + slots,))]
        + [pltpu.SemaphoreType.DMA((hidden // 512 + 1,)), pltpu.SemaphoreType.DMA((2, hidden // 512))]
        + [pltpu.SemaphoreType.DMA((9,))],
        compiler_params=pltpu.CompilerParams(
            collective_id=1, has_side_effects=True, vmem_limit_bytes=VMEM_LIMIT
        ),
        name="front",
    )(x, segment, present, input_weight, gains, biases, hidden_bias, expand, out_w, w2)


def add_rows(out, one, two):
    @pl.loop(0, one.shape[0] // 16)
    def _(i):
        rows = pl.ds(pl.multiple_of(i * 16, 16), 16)
        out[rows, :] = one[rows, :] + two[rows, :]


def sum_rows(out, *terms):
    @pl.loop(0, out.shape[0] // 16)
    def _(i):
        rows = pl.ds(pl.multiple_of(i * 16, 16), 16)
        total = terms[0][rows, :].astype(HIGH)
        for term in terms[1:]:
            total = total + term[rows, :].astype(HIGH)
        out[rows, :] = total


class Reducer:
    ORDER = (3, 2, 1, 0)
    COPIES = 16 + 4 * 6 + 3

    def __init__(self, s, share, out, C, H, Q, Z=None, S=None, lsem=None):
        b, z = position()
        to_x, to_y, to_core = (b ^ 2, z), (b ^ 4, z), (b ^ 1, z)
        self.out, self.C, self.H, self.Q, self.Z = out, C, H, Q, Z
        self.at = at = lambda e, d: share(b ^ (2 * e), z ^ d) if S is None else S.at[e, d]
        self.mine, self.other, self.halves, self.ahead, self.rest, self.last = ({} for _ in range(6))
        for d in self.ORDER:
            for e in (3, 1, 2, 0):
                if S is not None:
                    self.mine[d, e] = pltpu.make_async_copy(
                        share(b ^ (2 * e), z ^ d), S.at[e, d], lsem.at[d * 4 + e]
                    )
                self.other[d, e] = s.plan(
                    share(b ^ 1 ^ (2 * e), z ^ d), C.at[e, d], to_core, C.at[e, d]
                )

            def send(e, part, to, where):
                return s.plan(half(at(e, d), part), where, to, where)

            self.halves[d] = [send(3, 0, to_x, H.at[d, 0]), send(3, 1, to_y, H.at[d, 1])]
            self.ahead[d] = [
                send(2, 1, to_y, half(Q.at[d, 1], 1)),
                send(1, 0, to_x, half(Q.at[d, 0], 0)),
            ]
            self.rest[d] = [
                send(2, 0, to_y, half(Q.at[d, 1], 0)),
                send(1, 1, to_x, half(Q.at[d, 0], 1)),
            ]
            if d and Z is not None:
                to = (b, z ^ (2 if d == 2 else 1))
                self.last[d] = s.plan(at(0, d), Z.at[d - 1], to, Z.at[d - 1])

    def keep_for_later(self, sems):
        self.keep = [
            pltpu.make_async_copy(self.at(*self.kept(d)), self.out.at[d], sems.at[d])
            for d in range(4)
        ]

    def kept(self, d):
        return 0, d

    def start(self):
        for d in self.ORDER:
            for e in (3, 1, 2, 0):
                self.mine[d, e].start()
                self.other[d, e].go()

    def give(self, e):
        for d in self.ORDER:
            self.other[d, e].go()

    def fold(self, d, chips=(3, 1, 2, 0)):
        for e in chips:
            if self.mine:
                self.mine[d, e].wait()
            self.other[d, e].wait_recv()
            add_rows(self.at(e, d), self.at(e, d), self.C.at[e, d])
            for copy in {3: self.halves[d], 1: self.ahead[d][1:], 2: self.ahead[d][:1], 0: []}[e]:
                copy.go()

    def fold_chip(self, e):
        for d in self.ORDER:
            self.fold(d, (e,))

    def relay(self, d):
        for i, e in ((0, 2), (1, 1)):
            self.halves[d][i].wait_recv()
            part = half(self.at(e, d), i)
            add_rows(part, part, self.H.at[d, i])
            self.rest[d][i].go()

    def collect(self, d):
        for copy in self.ahead[d] + self.rest[d]:
            copy.wait_recv()
        total = self.at(0, d)
        for i in (0, 1):
            add_rows(total, total, self.Q.at[d, i])
        if self.Z is None:
            self.keep[d].start()
            return
        if d == 2:
            self.last[3].wait_recv()
            add_rows(total, total, self.Z.at[2])
        if d:
            self.last[d].go()

    def total(self):
        for d in (1, 2):
            self.last[d].wait_recv()
        sum_rows(self.out, self.at(0, 0), self.Z.at[0], self.Z.at[1])

    LEAD = (((4, 4), 1), ((4, 2), 2), ((4, 2), 1), ((3,), 1))

    @classmethod
    def scratch(cls, rows, columns, in_place=False):
        shapes = [pltpu.VMEM((*n, rows // cut, columns), LOW) for n, cut in cls.LEAD]
        if in_place:
            return shapes
        return shapes + [pltpu.VMEM((4, 4, rows, columns), LOW), pltpu.SemaphoreType.DMA((16,))]


class ReducerAlongZ(Reducer):
    COPIES = 16 + 4 * 3 + 6

    def __init__(self, s, share, out, C, H, Q, Z, S=None, lsem=None):
        self.partial = H is None
        b, z = position()
        to_x, to_y, to_core = (b ^ 2, z), (b ^ 4, z), (b ^ 1, z)
        self.out, self.C, self.H, self.Q, self.Z = out, C, H, Q, Z
        self.at = at = lambda e, d: share(b ^ (2 * e), z ^ d) if S is None else S.at[e, d]
        self.mine, self.other, self.along = {}, {}, {}
        for e in (3, 1, 2, 0):
            for d in (3, 2, 1, 0):
                if S is not None:
                    self.mine[e, d] = pltpu.make_async_copy(
                        share(b ^ (2 * e), z ^ d), S.at[e, d], lsem.at[d * 4 + e]
                    )
                self.other[e, d] = s.plan(
                    share(b ^ 1 ^ (2 * e), z ^ d), C.at[e, d], to_core, C.at[e, d]
                )
                if d:
                    to = (b, z ^ (2 if d == 2 else 1))
                    self.along[e, d] = s.plan(at(e, d), Z.at[e, d - 1], to, Z.at[e, d - 1])

        if self.partial:
            return

        def send(e, part, to, where):
            return s.plan(half(at(e, 0), part), where, to, where)

        self.halves = [send(3, 0, to_x, H.at[0]), send(3, 1, to_y, H.at[1])]
        self.ahead = [
            send(2, 1, to_y, half(Q.at[1], 1)),
            send(1, 0, to_x, half(Q.at[0], 0)),
        ]
        self.rest = [
            send(2, 0, to_y, half(Q.at[1], 0)),
            send(1, 1, to_x, half(Q.at[0], 1)),
        ]

    def start(self):
        for at in self.mine:
            self.mine[at].start()
            self.other[at].go()

    def give(self, e):
        for d in (3, 2, 1, 0):
            self.other[e, d].go()

    def fold(self, e):
        for d in (3, 1, 2, 0):
            if self.mine:
                self.mine[e, d].wait()
            self.other[e, d].wait_recv()
            add_rows(self.at(e, d), self.at(e, d), self.C.at[e, d])
            if d in (1, 3):
                self.along[e, d].go()

    def relay(self, e):
        self.along[e, 3].wait_recv()
        add_rows(self.at(e, 2), self.at(e, 2), self.Z.at[e, 2])
        self.along[e, 2].go()

    def collect(self, e):
        total = self.at(e, 0)
        for d in (1, 2):
            self.along[e, d].wait_recv()
            add_rows(total, total, self.Z.at[e, d - 1])
        if self.partial:
            self.keep[e].start()
            return
        for copy in {3: self.halves, 1: self.ahead[1:], 2: self.ahead[:1], 0: []}[e]:
            copy.go()

    def kept(self, e):
        return e, 0

    def cross(self):
        for i, e in ((0, 2), (1, 1)):
            self.halves[i].wait_recv()
            part = half(self.at(e, 0), i)
            add_rows(part, part, self.H.at[i])
            self.rest[i].go()

    def total(self):
        for copy in self.ahead + self.rest:
            copy.wait_recv()
        sum_rows(self.out, self.at(0, 0), self.Q.at[0], self.Q.at[1])

    LEAD = (((4, 4), 1), ((2,), 2), ((2,), 1), ((4, 3), 1))


class PlaneSums:
    COPIES = 3

    def __init__(self, s, out, T, Z):
        b, z = position()
        self.out, self.T, self.Z = out, T, Z
        self.last = {
            d: s.plan(T.at[d], Z.at[d - 1], (b, z ^ (2 if d == 2 else 1)), Z.at[d - 1])
            for d in (3, 2, 1)
        }

    def start(self):
        self.last[3].go()
        self.last[1].go()

    def relay(self):
        self.last[3].wait_recv()
        add_rows(self.T.at[2], self.T.at[2], self.Z.at[2])
        self.last[2].go()

    def total(self):
        for d in (1, 2):
            self.last[d].wait_recv()
        sum_rows(self.out, self.T.at[0], self.Z.at[0], self.Z.at[1])

    @staticmethod
    def scratch(rows, columns):
        return [pltpu.VMEM((n, rows, columns), LOW) for n in (4, 3)]


class ChipSums:
    COPIES = 6

    def __init__(self, s, out, U, H, Q):
        b, z = position()
        to_x, to_y = (b ^ 2, z), (b ^ 4, z)
        self.out, self.U, self.H, self.Q = out, U, H, Q

        def send(e, part, to, where):
            return s.plan(half(U.at[e], part), where, to, where)

        self.halves = [send(3, 0, to_x, H.at[0]), send(3, 1, to_y, H.at[1])]
        self.ahead = [
            send(2, 1, to_y, half(Q.at[1], 1)),
            send(1, 0, to_x, half(Q.at[0], 0)),
        ]
        self.rest = [
            send(2, 0, to_y, half(Q.at[1], 0)),
            send(1, 1, to_x, half(Q.at[0], 1)),
        ]

    def start(self):
        for copy in self.halves + self.ahead:
            copy.go()

    def relay(self):
        for i, e in ((0, 2), (1, 1)):
            self.halves[i].wait_recv()
            part = half(self.U.at[e], i)
            add_rows(part, part, self.H.at[i])
            self.rest[i].go()

    def total(self):
        for copy in self.ahead + self.rest:
            copy.wait_recv()
        sum_rows(self.out, self.U.at[0], self.Q.at[0], self.Q.at[1])

    @staticmethod
    def scratch(rows, columns):
        shapes = (4, rows), (2, rows // 2), (2, rows)
        return [pltpu.VMEM((*n, columns), LOW) for n in shapes]


def attend_kernel(qh_ref, kh_ref, v_ref, out_ref, lse_ref):
    keys = [rows_of(kh_ref[head, :, 0]) for head in (0, 1)]
    out_ref[0, 0], lse_ref[0] = attend_tile(
        [qh_ref[head, 0, 0] for head in (0, 1)], keys, rows_of(v_ref[:, 0])
    )


def attend(qh, kh, v):
    blocks, slots, rows, lanes = v.shape
    tile = pl.BlockSpec((1, 1, rows, lanes), lambda s, i: (i, s, 0, 0))
    tiles = pl.BlockSpec((2, 1, 1, rows, lanes), lambda s, i: (0, i, s, 0, 0))
    whole = pl.BlockSpec((blocks, 1, rows, lanes), lambda s, i: (0, s, 0, 0))
    wholes = pl.BlockSpec((2, blocks, 1, rows, lanes), lambda s, i: (0, 0, s, 0, 0))
    return pl.pallas_call(
        attend_kernel,
        grid=(slots, blocks),
        out_shape=(
            jax.ShapeDtypeStruct(v.shape, LOW),
            jax.ShapeDtypeStruct((slots, 8, blocks * rows), HIGH),
        ),
        in_specs=[tiles, wholes, whole],
        out_specs=(tile, pl.BlockSpec((1, 8, rows), lambda s, i: (s, 0, i))),
        compiler_params=pltpu.CompilerParams(vmem_limit_bytes=VMEM_LIMIT),
        name="attend",
    )(qh, kh, v)


def row_products(out, grad):
    pick = (lax.broadcasted_iota(jnp.int32, (8, 128), 0) == 0) == first_lanes((8, 128))
    return lax.dot_general(
        pick.astype(HIGH),
        out.astype(HIGH) * grad.astype(HIGH),
        (((1,), (1,)), ((), ())),
        precision=lax.Precision.HIGHEST,
        preferred_element_type=HIGH,
    )


def attend_back_tile(queries, keys, values, grads, logs, delta, acc):
    zeros = jnp.zeros_like(grads)
    mine = first_lanes(grads.shape)
    dk, dv = [], 0.0
    for head in (0, 1):
        grad = jnp.where(mine == (head == 0), grads, zeros)
        probs = jnp.exp(product_nt(keys[head], queries[head]) - logs[head : head + 1])
        pushed = product_nt(values, grad)
        d_scores = (probs * (pushed - delta[head : head + 1])).astype(LOW)
        dv = dv + product(probs.astype(LOW), grad)
        dk.append(product(d_scores, queries[head]))
        keys_t = keys[head].T[head * 64 : head * 64 + 64]
        acc[head * 64 : head * 64 + 64, :] += product(keys_t, d_scores)
    return jnp.where(first_lanes(dk[0].shape), dk[0], dk[1]).astype(LOW), dv.astype(LOW)


def attend_back_kernel(
    qh_ref, o_ref, g_ref, lse_ref, kh_ref, v_ref, dq_ref, dk_ref, dv_ref, acc, delta
):
    tile = pl.program_id(1)
    blocks, _, rows, _ = g_ref.shape
    grads = rows_of(g_ref[:, 0])

    @pl.when(tile == 0)
    def _():
        acc[...] = jnp.zeros_like(acc)
        delta[...] = row_products(rows_of(o_ref[:, 0]), grads)

    dk_ref[0, 0], dv_ref[0, 0] = attend_back_tile(
        [rows_of(qh_ref[head, :, 0]) for head in (0, 1)],
        [kh_ref[head, 0, 0] for head in (0, 1)],
        v_ref[0, 0],
        grads,
        lse_ref[0],
        delta[...],
        acc,
    )

    @pl.when(tile == blocks - 1)
    def _():
        dq_ref[:, 0] = (acc[...].T * 0.125).astype(LOW).reshape(blocks, rows, 128)


def attend_back(qh, o, g, lse, kh, v):
    blocks, slots, rows, lanes = v.shape
    tile = pl.BlockSpec((1, 1, rows, lanes), lambda s, i: (i, s, 0, 0))
    tiles = pl.BlockSpec((2, 1, 1, rows, lanes), lambda s, i: (0, i, s, 0, 0))
    whole = pl.BlockSpec((blocks, 1, rows, lanes), lambda s, i: (0, s, 0, 0))
    wholes = pl.BlockSpec((2, blocks, 1, rows, lanes), lambda s, i: (0, 0, s, 0, 0))
    logs = pl.BlockSpec((1, 8, blocks * rows), lambda s, i: (s, 0, 0))
    shape = jax.ShapeDtypeStruct(v.shape, LOW)
    return pl.pallas_call(
        attend_back_kernel,
        grid=(slots, blocks),
        out_shape=(shape,) * 3,
        in_specs=[wholes, whole, whole, logs, tiles, tile],
        out_specs=(whole, tile, tile),
        scratch_shapes=[pltpu.VMEM((lanes, blocks * rows), HIGH), pltpu.VMEM((8, blocks * rows), HIGH)],
        compiler_params=pltpu.CompilerParams(vmem_limit_bytes=VMEM_LIMIT),
        name="attend_back",
    )(qh, o, g, lse, kh, v)


class TokenSums:
    COPIES = 4 + 2 + 4

    def __init__(self, s, piece, sent, C, S, H, Q, A):
        b, z = position()
        to_x, to_y, to_core = (b ^ 2, z), (b ^ 4, z), (b ^ 1, z)
        self.b, self.piece = b, piece
        self.sent, self.C, self.S, self.H, self.Q, self.A = sent, C, S, H, Q, A
        self.other = [s.plan(sent.at[e], C.at[e], to_core, C.at[e]) for e in range(4)]

        def send(e, part, to, where):
            return s.plan(half(S.at[e - 1], part), where, to, where)

        self.halves = [send(3, 0, to_x, H.at[0]), send(3, 1, to_y, H.at[1])]
        self.ahead = [
            send(2, 1, to_y, half(Q.at[1], 1)),
            send(1, 0, to_x, half(Q.at[0], 0)),
        ]
        self.rest = [
            send(2, 0, to_y, half(Q.at[1], 0)),
            send(1, 1, to_x, half(Q.at[0], 1)),
        ]

    def give(self, e):
        self.sent[e] = self.piece(self.b ^ 1 ^ (2 * e)).astype(LOW)
        self.other[e].go()

    def take(self, e):
        mine = self.piece(self.b ^ (2 * e))
        self.other[e].wait_recv()
        mine = mine + self.C[e].astype(HIGH)
        if e:
            self.S[e - 1] = mine.astype(LOW)
        else:
            self.A[...] = mine
        for copy in {3: self.halves, 1: self.ahead[1:], 2: self.ahead[:1], 0: []}[e]:
            copy.go()

    def relay(self):
        for i, e in ((0, 2), (1, 1)):
            self.halves[i].wait_recv()
            part = half(self.S.at[e - 1], i)
            add_rows(part, part, self.H.at[i])
            self.rest[i].go()

    def total(self):
        for copy in self.ahead + self.rest:
            copy.wait_recv()
        return self.A[...] + self.Q[0].astype(HIGH) + self.Q[1].astype(HIGH)

    @staticmethod
    def scratch(rows, width):
        low = lambda *s: pltpu.VMEM((*s, width), LOW)
        return [low(4, rows), low(4, rows), low(3, rows), low(2, rows // 2), low(2, rows)] + [
            pltpu.VMEM((rows, width), HIGH)
        ]


def back_kernel(
    d_att,
    qh_in,
    kh_in,
    v_in,
    att_in,
    lse_in,
    w_in,
    first,
    g1,
    g2_planes,
    g2_late,
    dq_out,
    dk_out,
    dv_out,
    o1,
    out_o,
    o2,
    tok,
    dq,
    dk,
    dv,
    qsem,
    qh,
    kh,
    v,
    att,
    lse,
    w,
    first_rows,
    tail,
    grads,
    acc,
    delta,
    lsem,
    send,
    recv,
    *buffers,
):
    b, z = position()
    blocks, slots, rows, _ = v.shape
    loads = [
        pltpu.make_async_copy(src, dst, lsem.at[i])
        for i, (src, dst) in enumerate(
            (
                (d_att.at[b], grads.at[b]),
                (qh_in, qh),
                (kh_in, kh),
                (v_in, v),
                (att_in, att),
                (lse_in, lse),
                (w_in, w),
                (first.at[pl.ds(0, rows)], first_rows),
                (g2_planes, buffers[18]),
                (g2_late, buffers[20]),
            )
        )
    ]
    for load in loads:
        load.start()
    greet([(b ^ d, z) for d in range(1, 8)] + [(b, z ^ d) for d in (1, 2, 3)])
    s = Sender(send, recv)
    arriving = [
        [
            s.go(d_att.at[b ^ d, part], grads.at[b, part], (b ^ d, z), grads.at[b ^ d, part])
            for d in range(1, 8)
        ]
        for part in (pl.ds(slot * rows, rows) for slot in range(slots))
    ]

    def arrive(slot):
        for copy in arriving[slot]:
            copy.wait_recv()

    most = o1.shape[1] - tail.shape[1] + out_o.shape[1]
    sums = Reducer(
        s, lambda bb, zz: g1.at[bb, zz, :, pl.ds(0, most)], o1.at[:, pl.ds(0, most)], *buffers[:6]
    )
    late = ReducerAlongZ(
        s, lambda bb, zz: g1.at[bb, zz, :, pl.ds(most, tail.shape[1])], tail, *buffers[6:12]
    )

    def piece(i):
        mixed = jnp.concatenate([ref[i, 0] for ref in (dq, dk, dv)], axis=-1)
        return product_nt(mixed, w[...])

    tokens = TokenSums(s, piece, *buffers[12:18])
    cut = g2_planes.shape[1]
    planes = PlaneSums(s, o2.at[pl.ds(0, cut)], *buffers[18:20])
    chips = ChipSums(s, o2.at[pl.ds(cut, g2_late.shape[1])], *buffers[20:])
    late.start()
    sums.start()
    late.fold(3)
    late.fold(1)
    late.fold(2)
    sums.fold(3)
    arrive(0)
    for load in loads:
        load.wait()

    def grad_rows(slot):
        part = pl.ds(pl.multiple_of(slot * rows, rows), rows)
        return rows_of(grads[:, part])

    stores = [
        [
            pltpu.make_async_copy(src.at[:, slot], dst.at[:, slot], qsem.at[i, slot])
            for i, (src, dst) in enumerate(((dq, dq_out), (dk, dk_out), (dv, dv_out)))
        ]
        for slot in range(slots)
    ]

    def store(slot):
        for copy in stores[slot]:
            copy.start()

    events = {
        0: [(late.fold, 0)],
        1: [(sums.fold, 2), (late.relay, 3)],
        2: [(late.relay, 1)],
        3: [(sums.fold, 1), (sums.relay, 3)],
        4: [(late.relay, 2)],
        5: [(late.relay, 0), (sums.relay, 2)],
        6: [(sums.fold, 0), (late.collect, 3), (arrive, 1)],
        7: [(sums.collect, 3), (late.collect, 1), (planes.start,), (chips.start,)],
        8: [(store, 0), (sums.relay, 1), (late.collect, 2), (tokens.give, 3), (tokens.give, 2)],
        9: [(sums.collect, 2), (tokens.give, 1), (tokens.take, 3), (chips.relay,)],
        10: [(tokens.give, 0), (tokens.take, 2)],
        11: [(sums.relay, 0), (late.cross,), (tokens.take, 1), (planes.relay,)],
        12: [(tokens.take, 0)],
        13: [(sums.collect, 1), (tokens.relay,)],
        15: [(late.collect, 0), (planes.total,), (chips.total,)],
    }

    @pl.loop(0, blocks * slots)
    def _(step):
        slot, tile = step // blocks, step % blocks
        slot_grads = grad_rows(slot)

        @pl.when(tile == 0)
        def _():
            acc[...] = jnp.zeros_like(acc)
            delta[...] = row_products(rows_of(att[:, slot]), slot_grads)

        dk[tile, slot], dv[tile, slot] = attend_back_tile(
            [rows_of(qh[head, :, slot]) for head in (0, 1)],
            [kh[head, tile, slot] for head in (0, 1)],
            v[tile, slot],
            slot_grads,
            lse[slot],
            delta[...],
            acc,
        )

        @pl.when(tile == blocks - 1)
        def _():
            dq[:, slot] = (acc[...].T * 0.125).astype(LOW).reshape(blocks, rows, 128)

        for at, some in events.items():

            @pl.when(step == at)
            def _(some=some):
                for event, *what in some:
                    event(*what)

    store(slots - 1)
    sums.collect(0)
    late.total()
    rest = o1.shape[1] - most
    o1[:, most:] = tail[:, :rest]
    out_o[...] = tail[:, rest:]
    sums.total()
    tok[...] = first_rows[...] + tokens.total()
    for copy in stores[0] + stores[1]:
        copy.wait()
    s.drain()


def back(d_att, qh, kh, v, att, lse, w, d_first, g1, g2_planes, g2_late):
    blocks, slots, rows, lanes = v.shape
    shape = jax.ShapeDtypeStruct
    shard, total = g1.shape[2:]
    width = w.shape[0]
    late = 2 * width
    vmem = pl.BlockSpec(memory_space=pltpu.VMEM)
    scratch = lambda a: pltpu.VMEM(a.shape, a.dtype)
    return pl.pallas_call(
        back_kernel,
        out_shape=(shape(v.shape, LOW),) * 3
        + (
            shape((shard, total - width), HIGH),
            shape((shard, width), HIGH),
            shape((g2_planes.shape[1] + g2_late.shape[1], width), HIGH),
            shape((rows, width), HIGH),
        ),
        in_specs=in_hbm(11),
        out_specs=tuple(in_hbm(3)) + (vmem,) * 4,
        scratch_shapes=[pltpu.VMEM(v.shape, LOW)] * 3
        + [pltpu.SemaphoreType.DMA((3, slots))]
        + [scratch(a) for a in (qh, kh, v, att, lse, w)]
        + [
            pltpu.VMEM((rows, width), HIGH),
            pltpu.VMEM((shard, late), HIGH),
            pltpu.VMEM(d_att.shape, LOW),
            pltpu.VMEM((lanes, blocks * rows), HIGH),
            pltpu.VMEM((8, blocks * rows), HIGH),
            pltpu.SemaphoreType.DMA((10,)),
        ]
        + pair_of_semaphores(
            7 * slots
            + sum(c.COPIES for c in (Reducer, ReducerAlongZ, TokenSums, PlaneSums, ChipSums))
        )
        + Reducer.scratch(shard, total - late)
        + ReducerAlongZ.scratch(shard, late)
        + TokenSums.scratch(rows, width)
        + PlaneSums.scratch(*g2_planes.shape[1:])
        + ChipSums.scratch(*g2_late.shape[1:]),
        compiler_params=pltpu.CompilerParams(
            collective_id=2, has_side_effects=True, vmem_limit_bytes=VMEM_LIMIT
        ),
        name="back",
    )(d_att, qh, kh, v, att, lse, w, d_first, g1, g2_planes, g2_late)


def column_sum(block):
    return jnp.sum(block.astype(HIGH), axis=0, keepdims=True)


def middle_kernel(
    chunk,
    small_rows,
    remote,
    att_in,
    n1,
    r1_in,
    normed_in,
    cot_in,
    par_ref,
    act_hbm,
    slope_hbm,
    w1_hbm,
    w2_hbm,
    out_ref,
    first_ref,
    d_att_ref,
    small_ref,
    g1_hbm,
    g2_out,
    *rest,
):
    if remote:
        g2_late, *rest = rest
    w1, w2, act, slope, acc, low, sums_ref, d_hid_ref, wsem, gsem, *rest = rest
    att, r1, normed_t, cot_ref, isem, *buffers = rest
    inputs = ((cot_in, cot_ref), (normed_in, normed_t), (r1_in, r1), (att_in, att))
    inputs = [pltpu.make_async_copy(*pair, isem.at[i]) for i, pair in enumerate(inputs)]
    hidden, width = w2.shape
    steps = hidden // chunk
    pieces, _, held = d_att_ref.shape

    def columns(c):
        return pl.ds(pl.multiple_of(c * chunk, chunk), chunk)

    def load1(c):
        return pltpu.make_async_copy(w1_hbm.at[:, columns(c)], w1.at[:, columns(c)], wsem.at[0, c])

    def load2(c):
        return pltpu.make_async_copy(w2_hbm.at[columns(c)], w2.at[columns(c)], wsem.at[1, c])

    def load_act(c):
        return pltpu.make_async_copy(act_hbm.at[:, columns(c)], act.at[:, columns(c)], wsem.at[2, c])

    def load_slope(c):
        return pltpu.make_async_copy(
            slope_hbm.at[:, columns(c)], slope.at[:, columns(c)], wsem.at[3, c]
        )

    if remote:
        b, z = position()
        barrier = pltpu.get_barrier_semaphore()
        peers = [(b ^ d, z) for d in (1, 2, 4)] + [(b, z ^ d) for d in (1, 2)]
        for peer in peers:
            pl.semaphore_signal(barrier, inc=1, device_id=peer, device_id_type=MESH)
    last = pl.ds(hidden, width)
    for c in range(steps):
        load_act(c).start()
        load2(c).start()
    inputs[0].start()
    for c in range(steps):
        load_slope(c).start()
    for copy in inputs[1:]:
        copy.start()
    for c in range(steps):
        load1(c).start()
    load_out = pltpu.make_async_copy(w1_hbm.at[:, last], w1.at[:, last], wsem.at[0, steps])
    load_out.start()
    gain1, gain2 = par_ref[0:1], par_ref[1:2]
    bias = lambda i: par_ref[2 + i : 3 + i]
    acc[...] = n1[...] * gain1 + (bias(3) + bias(4))

    @pl.loop(0, steps)
    def _(c):
        load_act(c).wait()
        load2(c).wait()
        acc[...] += product(act[:, columns(c)], w2[columns(c), :])

    normal, inverse2 = normalize(acc[...])
    inputs[0].wait()
    out_ref[...] = (normal * gain2 + bias(5)).astype(LOW)
    cot = cot_ref[...].astype(HIGH)
    d_second = normalize_back(cot * gain2, normal, inverse2)
    low[...] = d_second.astype(LOW)
    acc[...] = d_second
    sums_ref[1:2] = column_sum(cot * normal)
    sums_ref[4:5] = column_sum(low[...])
    sums_ref[5:6] = column_sum(cot)

    def store1(c):
        return pltpu.make_async_copy(w1.at[:, columns(c)], g1_hbm.at[:, columns(c)], gsem.at[0, c])

    def store2(c):
        return pltpu.make_async_copy(w2.at[columns(c)], g2_out.at[columns(c)], gsem.at[1, c])

    first_events, second_events = {}, {}
    if remote:
        pl.semaphore_wait(barrier, len(peers))
        s = Sender(*buffers[:2])
        each = w2.shape[0] // (8 * 4)
        cut = buffers[2].shape[2]
        plain = lambda bb, zz: w2.at[pl.ds(pl.multiple_of((bb * 4 + zz) * each, each), cut)]
        upper = lambda bb, zz: w2.at[
            pl.ds(pl.multiple_of((bb * 4 + zz) * each + cut, 16), each - cut)
        ]
        sums = Reducer(s, plain, g2_out, *buffers[2:5])
        late = ReducerAlongZ(s, upper, g2_late, buffers[5], None, None, buffers[6])
        sums.keep_for_later(buffers[7])
        late.keep_for_later(buffers[8])
        first_events = {
            0: [(late.give, 3), (sums.give, 3)],
            2: [(late.give, 2), (sums.give, 2)],
            3: [(late.fold, 3), (sums.fold_chip, 3)],
            4: [(late.give, 1), (sums.give, 1)],
            5: [(late.fold, 2), (sums.fold_chip, 2)],
            6: [(late.give, 0), (sums.give, 0), (late.relay, 3)],
            7: [(late.fold, 1), (sums.fold_chip, 1)],
        }
        second_events = {
            0: [(late.relay, 2)],
            1: [(late.fold, 0), (sums.fold_chip, 0), (late.relay, 1)],
            2: [(sums.relay, 3), (sums.relay, 2)],
            3: [(late.relay, 0), (sums.relay, 1)],
            4: [(sums.relay, 0), (late.collect, 3)],
            5: [(late.collect, 2)],
            6: [(late.collect, 1), (sums.collect, 3)],
            7: [(sums.collect, 2)],
        }

    def run(events, step):
        for at, some in events.items():

            @pl.when(step == at)
            def _(some=some):
                for event, *what in some:
                    event(*what)

    @pl.loop(0, steps)
    def _(step):
        c = b ^ (7 - step) if remote else step
        load_slope(c).wait()
        d_act = product_nt(low[...], w2[columns(c), :])
        d_pre = (d_act * slope[:, columns(c)].astype(HIGH)).astype(LOW)
        d_hid_ref[:, columns(c)] = column_sum(d_pre)
        slope[:, columns(c)] = d_pre
        w2[columns(c), :] = product_tn(act[:, columns(c)], low[...]).astype(LOW)
        if not remote:
            store2(c).start()
        run(first_events, step)

    for copy in inputs[1:]:
        copy.wait()

    @pl.loop(0, steps)
    def _(c):
        load1(c).wait()
        d_pre = slope[:, columns(c)]
        acc[...] += product_nt(d_pre, w1[:, columns(c)])
        w1[:, columns(c)] = product(normed_t[...], d_pre).astype(LOW)
        store1(c).start()
        run(second_events, c)

    d_normed = acc[...]
    normal = n1[...]
    d_first = normalize_back(d_normed * gain1, normal, r1[:, 0:1])
    first_ref[...] = d_first
    low[...] = d_first.astype(LOW)
    sums_ref[0:1] = column_sum(d_normed * normal)
    sums_ref[2:3] = column_sum(low[...])
    sums_ref[3:4] = column_sum(d_normed)
    load_out.wait()
    d_att = product_nt(low[...], w1[:, hidden:]).astype(LOW)
    for i in range(pieces):
        d_att_ref[i] = d_att[:, i * held : (i + 1) * held]
    w1[:, hidden:] = product_tn(att[...], low[...]).astype(LOW)
    store_out = pltpu.make_async_copy(w1.at[:, last], g1_hbm.at[:, last], gsem.at[0, steps])
    store_out.start()
    blocks, planes, _ = small_ref.shape
    small_ref[...] = jnp.zeros_like(small_ref)
    owners = [(i, j) for i in range(blocks) for j in range(width // (blocks * small_rows))]
    for at, (i, j) in enumerate(owners):
        for k in range(6):
            small_ref[i, j : j + 1, k * small_rows : (k + 1) * small_rows] = sums_ref[
                k : k + 1, at * small_rows : (at + 1) * small_rows
            ]
        part = hidden // len(owners)
        small_ref[i, j : j + 1, 6 * small_rows : 6 * small_rows + part] = d_hid_ref[
            :, at * part : (at + 1) * part
        ]
    if remote:
        sums.collect(1)
        late.collect(0)
        sums.collect(0)
        for copy in sums.keep + late.keep:
            copy.wait()
        s.drain()
    for c in range(steps):
        store1(c).wait()
        if not remote:
            store2(c).wait()
    store_out.wait()


def middle(att, n1, r1, normed_t, cot, par, act, slope, w1, w2, pieces, planes, remote):
    count, width = cot.shape
    hidden = w2.shape[0]
    chunk = 512
    shape = jax.ShapeDtypeStruct
    vmem = pl.BlockSpec(memory_space=pltpu.VMEM)
    shard = hidden // (pieces * planes)
    late = shard // 4
    buffers, params = [], {}
    g2_shape = [shape(w2.shape, LOW)]
    if remote:
        g2_shape = [shape((4, shard - late, width), LOW), shape((4, late, width), LOW)]
        buffers = pair_of_semaphores(Reducer.COPIES + ReducerAlongZ.COPIES)
        buffers += Reducer.scratch(shard - late, width, in_place=True)[:3]
        buffers += ReducerAlongZ.scratch(late, width, in_place=True)[::3]
        buffers += [pltpu.SemaphoreType.DMA((4,)), pltpu.SemaphoreType.DMA((4,))]
        params = dict(collective_id=4, has_side_effects=True)
    return pl.pallas_call(
        functools.partial(middle_kernel, chunk, width // (pieces * planes), remote),
        out_shape=(
            shape((count, width), LOW),
            shape((count, width), HIGH),
            shape((pieces, count, width // pieces), LOW),
            shape((pieces, -(-planes // 8) * 8, 384), HIGH),
            shape(w1.shape, LOW),
            *g2_shape,
        ),
        in_specs=in_hbm(1) + [vmem] + in_hbm(3) + [vmem] + in_hbm(4),
        out_specs=(vmem,) * 4 + tuple(in_hbm(1 + len(g2_shape))),
        scratch_shapes=[
            pltpu.VMEM(w1.shape, LOW),
            pltpu.VMEM(w2.shape, LOW),
            pltpu.VMEM((count, hidden), LOW),
            pltpu.VMEM((count, hidden), LOW),
            pltpu.VMEM((count, width), HIGH),
            pltpu.VMEM((count, width), LOW),
            pltpu.VMEM((8, width), HIGH),
            pltpu.VMEM((1, hidden), HIGH),
            pltpu.SemaphoreType.DMA((4, hidden // chunk + 1)),
            pltpu.SemaphoreType.DMA((2, hidden // chunk + 1)),
            pltpu.VMEM(att.shape, LOW),
            pltpu.VMEM(r1.shape, HIGH),
            pltpu.VMEM(normed_t.shape, LOW),
            pltpu.VMEM(cot.shape, LOW),
            pltpu.SemaphoreType.DMA((4,)),
        ]
        + buffers,
        compiler_params=pltpu.CompilerParams(vmem_limit_bytes=VMEM_LIMIT, **params),
        name="middle",
    )(att, n1, r1, normed_t, cot, par, act, slope, w1, w2)


def finish_kernel(
    dq,
    dk,
    dv,
    w,
    first,
    tok0,
    small,
    x_hbm,
    tok_out,
    in_out,
    gains_out,
    biases_out,
    hidden_out,
    first_rows,
    x,
    D,
    P,
    R,
    Z,
    M,
    N,
    T,
    lsem,
    send,
    recv,
    *buffers,
):
    b, z = position()
    rows, width = tok0.shape
    blocks = dq.shape[0]
    count = 2 * rows
    loads = [
        pltpu.make_async_copy(x_hbm.at[i, pl.ds(0, count)], x.at[i], lsem.at[i])
        for i in range(blocks)
    ]
    loads.append(pltpu.make_async_copy(first.at[pl.ds(rows, rows)], first_rows, lsem.at[blocks]))
    loads.append(pltpu.make_async_copy(tok0, tok_out.at[pl.ds(0, rows)], lsem.at[blocks + 1]))
    for load in loads:
        load.start()
    greet([(b ^ d, z) for d in range(1, 8)] + [(b, z ^ d) for d in (1, 2, 3)])
    s = Sender(send, recv)

    def piece(i):
        mixed = jnp.concatenate([ref[i, 1] for ref in (dq, dk, dv)], axis=-1)
        return product_nt(mixed, w[...])

    tokens = TokenSums(s, piece, *buffers)
    small_in = [
        s.go(small.at[b ^ d], M.at[d - 1], (b ^ d, z), M.at[d - 1]) for d in range(1, 8)
    ]
    total = jnp.zeros((width, w.shape[1]), HIGH)
    for i in range(blocks):
        loads[i].wait()
        mixed = jnp.concatenate([ref[i].reshape(count, -1) for ref in (dq, dk, dv)], axis=-1)
        total = total + product_tn(x[i], mixed)
    D[...] = total.astype(LOW).reshape(D.shape)
    share_rows = D.shape[1] // 4

    def share(d):
        return D.at[:, pl.ds(pl.multiple_of((z ^ d) * share_rows, share_rows), share_rows)]

    in_z = {
        d: s.plan(share(d), Z.at[d - 1], (b, z ^ (2 if d == 2 else 1)), Z.at[d - 1])
        for d in (3, 1, 2)
    }
    in_z[3].go()
    in_z[1].go()
    for e in (3, 2, 1, 0):
        tokens.give(e)
    tokens.take(3)
    in_z[3].wait_recv()
    onward = share(2)
    onward[...] = onward[...] + Z[2]
    in_z[2].go()
    for e in (2, 1, 0):
        tokens.take(e)

    N[...] = small[b]
    for i in range(7):
        small_in[i].wait_recv()
        N[...] += M[i]
    for row, ref in ((4, dq), (5, dv)):
        whole = jnp.zeros((1, 128), HIGH)
        for i in range(blocks):
            whole = whole + column_sum(ref[i].reshape(count, -1))
        N[row : row + 1, 0:128] = whole
    small_z = [s.go(N, T.at[d - 1], (b, z ^ d), T.at[d - 1]) for d in (1, 2, 3)]

    in_z[1].wait_recv()
    in_z[2].wait_recv()
    plane = share(0)[...].astype(HIGH)
    for i in range(2):
        plane = plane + Z[i].astype(HIGH)
    P[...] = plane
    grads_in = [
        s.go(P.at[b ^ d], R.at[b], (b ^ d, z), R.at[b ^ d]) for d in range(1, 8)
    ]
    R[b] = P[b]
    tokens.relay()
    for copy in small_z:
        copy.wait_recv()
    vectors = ((N[...] + T[0]) + T[1]) + T[2]
    planes = lax.broadcasted_iota(jnp.int32, vectors.shape, 0)
    row = jnp.sum(jnp.where(planes == z, vectors, 0.0), axis=0, keepdims=True)
    n = gains_out.shape[1]
    for k in range(2):
        gains_out[k : k + 1] = row[:, k * n : (k + 1) * n]
        own = vectors[4 + k : 5 + k]
        parts = [jnp.where(z == j, own[:, j * n : (j + 1) * n], 0.0) for j in range(4)]
        biases_out[k : k + 1] = (parts[0] + parts[1]) + (parts[2] + parts[3])
    for k in range(2, 6):
        biases_out[k : k + 1] = row[:, k * n : (k + 1) * n]
    hidden_out[...] = row[:, 6 * n : 6 * n + hidden_out.shape[1]]
    for copy in grads_in:
        copy.wait_recv()
    for i in range(blocks):
        for k in range(3):
            at = k * width + i * 128
            in_out[:, at : at + 128] = R[i, :, k * 128 : (k + 1) * 128]
    for load in loads[blocks:]:
        load.wait()
    tok_out[rows:] = first_rows[...] + tokens.total()
    s.drain()


def finish(dq, dk, dv, w, d_first, tok0, small, x):
    rows, width = tok0.shape
    blocks, columns = dq.shape[0], w.shape[1]
    share = width // (4 * blocks)
    vmem = pl.BlockSpec(memory_space=pltpu.VMEM)
    shape = lambda *s: jax.ShapeDtypeStruct(s, HIGH)
    low = lambda *s: pltpu.VMEM(s, LOW)
    wide = lambda *s: pltpu.VMEM(s, HIGH)
    tile = small.shape[1:]
    return pl.pallas_call(
        finish_kernel,
        out_shape=(
            shape(2 * rows, width),
            shape(share, 3 * width),
            shape(2, share),
            shape(6, share),
            shape(1, 4 * share),
        ),
        in_specs=[vmem] * 4 + in_hbm(2) + [vmem] + in_hbm(1),
        out_specs=(vmem,) * 5,
        scratch_shapes=[
            wide(rows, width),
            low(blocks, 2 * rows, width),
            low(blocks, 4 * share, columns),
            wide(blocks, share, columns),
            wide(blocks, share, columns),
            low(3, blocks, share, columns),
            wide(7, *tile),
            wide(*tile),
            wide(3, *tile),
            pltpu.SemaphoreType.DMA((blocks + 2,)),
        ]
        + pair_of_semaphores(20 + TokenSums.COPIES)
        + TokenSums.scratch(rows, width),
        compiler_params=pltpu.CompilerParams(
            collective_id=3, has_side_effects=True, vmem_limit_bytes=VMEM_LIMIT
        ),
        name="finish",
    )(dq, dk, dv, w, d_first, tok0, small, x)


def swap(pieces):
    return lax.all_to_all(pieces, "blk", 0, 0)


def by_slot(block, slots):
    blocks, count, held = block.shape
    block = block.reshape(blocks, slots, count // slots, held)
    return jnp.pad(block, ((0, 0),) * 3 + ((0, 128 - held),))


def front_apart(X, W, bias, slots):
    n_blk, count = X.shape[0], X.shape[1] - 16
    held = W.shape[1] // 3
    mixed = jnp.einsum("brd,dc->brc", X[:, :count], W, preferred_element_type=HIGH)
    parts = [mixed[..., i * held : (i + 1) * held] for i in range(3)]
    parts = [jnp.pad(p, ((0, 0), (0, 0), (0, 128 - held))).reshape(-1, 128) for p in parts]
    own = lax.dynamic_slice(bias[:2], (0, lax.axis_index("blk") * held), (2, held))
    own = jnp.pad(own, ((0, 0), (0, 128 - held)))
    codes = X[:, count, :count].reshape(-1, 1).astype(jnp.int32)
    codes = jnp.broadcast_to(codes, (n_blk * count, 128))
    queries, keys, values = split_heads(jnp.concatenate(parts, axis=1), (own[0], own[1]), codes)
    shape = (n_blk, slots, count // slots, 128)
    qh = jnp.stack(queries).reshape(2, *shape)
    kh = jnp.stack(keys).reshape(2, *shape)
    v = values.reshape(shape)
    att, lse = attend(qh, kh, v)
    rows_att = swap(att[..., :held].reshape(n_blk, count, held))
    return qh, kh, v, att, lse, rows_att


def on_device(
    tokens,
    input_weight,
    output_weight,
    expand_weight,
    reduce_weight,
    gains,
    biases,
    hidden_bias,
    segment,
    present,
    cotangent,
):
    slots, rows, width = tokens.shape
    n_blk, n_dp = lax.axis_size("blk"), lax.axis_size("dp")
    shards = n_blk * n_dp
    fast = (n_blk, n_dp) == (8, 4)
    held = width // n_blk
    shard = input_weight.shape[0]
    hidden = expand_weight.shape[1]
    count = slots * rows
    flat = tokens.reshape(count, width)

    if fast:
        front_out = front(
            flat,
            segment,
            present,
            input_weight,
            gains,
            biases,
            hidden_bias[None],
            expand_weight,
            output_weight,
            reduce_weight,
        )
        X, W1, W2, act, slope, W, _, qh, kh, v, att, lse = front_out[:12]
        attended, n1, r1, normed_t, cuts = front_out[12:]
        W1, W2 = W1.reshape(width, -1), W2.reshape(hidden, width)
    else:
        code = (segment + 4 * (1 - present)).reshape(1, count).astype(LOW)
        code_rows = jnp.pad(jnp.broadcast_to(code, (16, count)), ((0, 0), (0, width - count)))
        columns = input_weight.reshape(shard, 3, n_blk, held).transpose(2, 0, 1, 3)
        columns = columns.reshape(n_blk, shard, 3 * held)
        small = jnp.concatenate([gains.reshape(-1), biases.reshape(-1), hidden_bias])
        X = lax.all_gather(jnp.concatenate([flat, code_rows], axis=0), "blk")
        W = lax.all_gather(swap(columns), "dp", axis=1).reshape(width, 3 * held)
        small = lax.all_gather(small, BOTH)
        W1 = jnp.concatenate([expand_weight, output_weight], axis=1)
        W1 = lax.all_gather(W1, BOTH, axis=0, tiled=True)
        W2 = lax.all_gather(reduce_weight, BOTH, axis=0, tiled=True)
        part = width // shards
        cuts = small[:, : 8 * part].reshape(shards, 8, part).transpose(1, 0, 2)
        cuts = cuts.reshape(8, width).astype(HIGH)
        hidden_full = small[:, 8 * part :].reshape(hidden).astype(HIGH)
        gain, bias = cuts[:2], cuts[2:]
        qh, kh, v, att, lse, rows_att = front_apart(X, W, bias, slots)
        attended = rows_att.transpose(1, 0, 2).reshape(count, width)
        branch = product(attended, W1[:, hidden:]) + bias[2]
        n1, r1 = normalize(flat.astype(HIGH) + branch)
        r1 = jnp.broadcast_to(r1, (count, 128))
        normed_low = (n1 * gain[0] + bias[3]).astype(LOW)
        act, slope = gelu_parts(product(normed_low, W1[:, :hidden]) + hidden_full)
        act, slope = act.astype(LOW), slope.astype(LOW)
        normed_t = normed_low.T
    cot = cotangent.reshape(count, width)
    middle_out = middle(
        attended, n1, r1, normed_t, cot, cuts, act, slope, W1, W2, n_blk, n_dp, fast
    )
    output, d_first, d_att, small_rows, grad_both, grad_reduce = middle_out[:6]
    output = output.reshape(slots, rows, width)
    if fast:
        grad_both = grad_both.reshape(n_blk, n_dp, shard, -1)
        dq, dk, dv, sum_expand, sum_output, sum_reduce, tok0 = back(
            d_att, qh, kh, v, att, lse, W, d_first, grad_both, grad_reduce, middle_out[6]
        )
        grad_tokens, grad_input, d_gains, d_biases, d_hidden = finish(
            dq, dk, dv, W, d_first, tok0, small_rows, X
        )
        return (
            output,
            grad_tokens.reshape(slots, rows, width),
            grad_input,
            sum_output,
            sum_expand,
            sum_reduce,
            d_gains,
            d_biases,
            d_hidden.reshape(-1),
        )
    sum_both = lax.psum_scatter(grad_both, BOTH, scatter_dimension=0, tiled=True).astype(HIGH)
    sum_reduce = lax.psum_scatter(grad_reduce, BOTH, scatter_dimension=0, tiled=True)
    dq, dk, dv = attend_back(qh, att, by_slot(swap(d_att), slots), lse, kh, v)
    d_mixed = jnp.concatenate([dq[..., :held], dk[..., :held], dv[..., :held]], axis=-1)
    d_mixed = d_mixed.reshape(n_blk * count, 3 * held)
    all_tokens = X[:, :count].reshape(n_blk * count, width)
    d_input = product_tn(all_tokens, d_mixed).astype(LOW)
    d_tokens = product_nt(d_mixed, W).astype(LOW)
    d_tokens = lax.psum_scatter(d_tokens, "blk", scatter_dimension=0, tiled=True)
    grad_tokens = d_first + d_tokens.astype(HIGH)
    d_input = swap(d_input.reshape(n_blk, n_dp * shard, 3 * held))
    d_input = d_input.reshape(n_blk, n_dp, shard, 3, held).transpose(1, 2, 3, 0, 4)
    d_input = d_input.reshape(n_dp, shard, 3 * width).astype(HIGH)
    grad_input = lax.psum_scatter(d_input, "dp", scatter_dimension=0, tiled=False)
    col = lambda a: jnp.sum(a.astype(HIGH), axis=0)
    own_cols = jnp.stack([col(d_mixed[:, :held]), col(d_mixed[:, 2 * held :])])
    own_cols = lax.psum_scatter(own_cols, "dp", scatter_dimension=1, tiled=True)
    small_rows = small_rows[:, :n_dp].reshape(shards, -1)
    small_sum = lax.psum_scatter(small_rows, BOTH, scatter_dimension=0, tiled=False)
    vectors = small_sum[: 6 * part].reshape(6, part)
    return (
        output,
        grad_tokens.reshape(slots, rows, width),
        grad_input,
        sum_both[:, hidden:],
        sum_both[:, :hidden],
        sum_reduce.astype(HIGH),
        vectors[:2],
        jnp.concatenate([own_cols, vectors[2:]], axis=0),
        small_sum[6 * part : 6 * part + hidden // shards],
    )


def solution(mesh):
    rows, sharded = P("dp", "blk", None), P(BOTH, None)
    in_specs = (rows, sharded, sharded, sharded, sharded, P(None, BOTH), P(None, BOTH), P(BOTH))
    in_specs += (P("dp", "blk"), P("dp", "blk"), rows)
    out_specs = (rows, rows, sharded, sharded, sharded, sharded)
    out_specs += (P(None, BOTH), P(None, BOTH), P(BOTH))
    return jax.shard_map(
        on_device, mesh=mesh, in_specs=in_specs, out_specs=out_specs, check_vma=False
    )
```
